32 devices in a mesh: tm: 8 (over z, core), space: 4 (over y, x).
Axes of the slice: x: 2, y: 2, z: 4, core: 2. Of those that a mesh axis runs over, the one named last changes fastest.
Arguments:
- initial: float32 [64, 64, 2048], P('tm', 'space'), may hold values from -6 to 6
- source: float32 [64, 64, 2048], P('tm', 'space'), may hold values from -3 to 3.3
- diffusivity: float32 [64, 2048], P('space'), may hold values from 0.3 to 1
- growth: float32 [64, 2048], P('space'), may hold values from 0.5 to 4
Outputs:
- solution: float32 [64, 64, 2048], P('tm', 'space')
The draws below stay inside these ranges and needn't reach their ends.
All inputs are finite; a program needn't handle non-finite values.
Results may differ from the reference program's by a relative error of at most 0.00002.
Values sent between devices are 32-bit elements; how exact they have to be, the bound alone decides.
No kernel may reach another device: no remote copies, remote signals or barrier semaphores. Data moves between devices by JAX's collectives and lax.ppermute only.
A program may use at most 64 MiB of HBM per device.

```python
import math
import jax
import jax.numpy as jnp
from jax import lax

COLS = 2048
LEVELS = 4
STEPS_ALL = 64
GRID_ROWS = 64


def draw_source(key, part):
    second_key = jax.random.fold_in(key, 1)
    shape = (STEPS_ALL, GRID_ROWS, COLS)
    rough = 0.5 * jax.random.normal(second_key, shape, jnp.float32)
    return jnp.clip(rough, -3.0, 3.3)


def level_of(stream_key, shape, shards, low, high):
    def one(position, shards_of):
        steps = jax.random.uniform(jax.random.fold_in(jax.random.fold_in(stream_key, 6), position), (shards_of,), jnp.float32, low / len(shards), high / len(shards))
        return jnp.repeat(jnp.exp(steps), shape[position] // shards_of).reshape((-1,) + (1,) * (len(shape) - position - 1))

    level = one(*shards[0])
    for cut in shards[1:]:
        level = level * one(*cut)
    return level


def centred(rng, extent, deviation, bound, cuts=(), kind=jnp.bfloat16):
    values = jax.random.normal(rng, extent, jnp.float32) * deviation
    if len(cuts) > 0:
        values = level_of(rng, extent, cuts, -0.22, 0.18) * values
    return jnp.clip(values, min=-bound, max=bound).astype(kind)


def setup_inputs(seed: int = 0) -> dict:
    streams_of = jax.random.split(jax.random.key(seed), 5)
    return {
        "initial": centred(streams_of[0], (STEPS_ALL, GRID_ROWS, COLS), 1.0, 6.0, ((0, 8), (1, 4)), jnp.float32),
        "source": draw_source(jax.random.fold_in(streams_of[4], 71), 0),
        "diffusivity": jnp.clip(jnp.exp(math.log(1.0) - 1.2039728 * jax.random.uniform(streams_of[2], (GRID_ROWS, COLS), jnp.float32) ** level_of(streams_of[2], (GRID_ROWS, COLS), ((0, 4),), -0.2, 0.2)), 0.3, 1.0),
        "growth": jnp.clip(jnp.exp(math.log(4.0) - 2.0794415 * jax.random.uniform(streams_of[3], (GRID_ROWS, COLS), jnp.float32) ** level_of(streams_of[3], (GRID_ROWS, COLS), ((0, 4),), -0.2, 0.2)), 0.5, 4.0),
    }


diffusion_number = 0.03
time_step = 0.02


def propagate(fields, scales, diffusivity, growth):
    padded = jnp.pad(fields, ((0, 0), (1, 1), (1, 1)))
    beside_all = padded[:, :-2, 1:-1] + padded[:, 2:, 1:-1] + padded[:, 1:-1, :-2] + padded[:, 1:-1, 2:]
    laplace = beside_all - 4.0 * fields
    factor = scales[:, None, None]
    return fields + (diffusion_number * factor) * diffusivity * laplace + (time_step * factor) * growth * fields / (1.0 + fields * fields)


def uniform_scales(count, level_index):
    return jnp.full((count,), 2.0 ** level_index, jnp.float32)


def coarsest(states, forcing, diffusivity, growth):
    unit = uniform_scales(1, LEVELS - 1)

    def advance(prior, term):
        following = propagate(prior, unit, diffusivity, growth) + term[None]
        return following, following[0]

    final_state, chain = lax.scan(advance, states[-1:], forcing)
    return chain


def cycle(level_index, states, forcing, diffusivity, growth):
    if level_index == LEVELS - 1:
        return coarsest(states, forcing, diffusivity, growth)
    half = states.shape[0] // 2
    scales = uniform_scales(half, level_index)
    even_forcing = forcing[0::2]
    odd_forcing = forcing[1::2]
    even_points = states[0::2]
    odd_points = propagate(even_points, scales, diffusivity, growth) + odd_forcing
    shifted = jnp.concatenate([odd_points[-1:], odd_points[:-1]], axis=0)
    even_points = propagate(shifted, scales, diffusivity, growth) + even_forcing
    odd_points = propagate(even_points, scales, diffusivity, growth) + odd_forcing
    both_scales = jnp.concatenate([scales, uniform_scales(half, level_index + 1)])
    images = propagate(jnp.concatenate([odd_points, even_points], axis=0), both_scales, diffusivity, growth)
    pair_terms = images[:half] - images[half:]
    reduced_forcing = even_forcing + jnp.concatenate([pair_terms[-1:], pair_terms[:-1]], axis=0)
    coarse_points = cycle(level_index + 1, even_points, reduced_forcing, diffusivity, growth)
    odd_points = propagate(coarse_points, scales, diffusivity, growth) + odd_forcing
    return jnp.stack([coarse_points, odd_points], axis=1).reshape(states.shape)


def reference(initial, source, diffusivity, growth):
    return cycle(0, initial, source, diffusivity, growth)
```

```python
import functools

import jax
import jax.numpy as jnp
from jax import lax
from jax.experimental import pallas as pl
from jax.experimental.pallas import tpu as pltpu
from jax.sharding import PartitionSpec as P

LANES = 128
MARGIN = 4
REACH = 32
UP_RIM = 3
POINTS = 8
diffusion_number = 0.03
time_step = 0.02

RIMS_0 = (
    ("e0", 4), ("e1", 4), ("e2", 4),
    ("o0", 3), ("o1", 3), ("o2", 3), ("o3", 1),
    ("s0", 2), ("s1", 2), ("s2", 2), ("s3", 2),
    ("d", 3), ("g", 3),
)
CORES = ("e0", "e1", "e2", "o0", "o1", "o2", "o3", "s0", "s1", "s2", "s3", "d", "g")
BEHIND_0 = (("ep", 4), ("op", 3))
BEHIND = (("pair", 2), ("odd", 3))


def count(rims):
    return sum(rows for _, rows in rims)


def params(mib=16):
    return pltpu.CompilerParams(vmem_limit_bytes=mib * 2**20)


def call(kernel, outs, scratch, *args, mib=16):
    return pl.pallas_call(
        kernel,
        out_shape=tuple(jax.ShapeDtypeStruct(shape, jnp.float32) for shape in outs),
        in_specs=[pl.BlockSpec(memory_space=pltpu.VMEM)] * len(args),
        out_specs=tuple(pl.BlockSpec(memory_space=pltpu.VMEM) for _ in outs),
        scratch_shapes=[pltpu.VMEM(shape, jnp.float32) for shape in scratch],
        compiler_params=params(mib),
    )(*args)


def beside(mid):
    depth = mid.shape[1]
    lane = lax.broadcasted_iota(jnp.int32, mid.shape, 2)
    line = lax.broadcasted_iota(jnp.int32, mid.shape, 1)
    left = pltpu.roll(mid, 1, 2)
    left_turn = pltpu.roll(left, 1, 1)
    right = pltpu.roll(mid, LANES - 1, 2)
    right_turn = pltpu.roll(right, depth - 1, 1)
    left = jnp.where(lane == 0, jnp.where(line == 0, 0.0, left_turn), left)
    right = jnp.where(lane == LANES - 1, jnp.where(line == depth - 1, 0.0, right_turn), right)
    return left + right


def growth_of(ref, at, rows, diff, grow):
    wide = ref[pl.ds(at - 1, rows + 2)]
    mid = wide[1:-1]
    laplace = wide[:-2] + wide[2:] + beside(mid) - 4.0 * mid
    return mid, diff * laplace + grow * mid / (1.0 + mid * mid)


def over_rows(rows, rim, body, step=2):
    lax.fori_loop(
        0, (rows + 2 * rim) // step, lambda i, _: (body(MARGIN - rim + i * step), 0)[1], 0
    )


def flags():
    slab = lax.axis_index("space")
    low = jnp.where(slab > 0, 1.0, 0.0).astype(jnp.float32)
    high = jnp.where(slab < lax.axis_size("space") - 1, 1.0, 0.0).astype(jnp.float32)
    return low, high


def set_rims(buffer, rows, rim, low_rows, high_rows, low, high, inner=0):
    width = rim - inner
    buffer[pl.ds(MARGIN - rim, width)] = low_rows * low
    buffer[pl.ds(MARGIN + rows + inner, width)] = high_rows * high


def pieces(name, initial, source, diffusivity, growth):
    if name == "d":
        return lambda rows, cols: diffusivity[rows, cols] * diffusion_number
    if name == "g":
        return lambda rows, cols: growth[rows, cols] * time_step
    if name == "ep":
        return lambda rows, cols: initial[POINTS - 2, rows, cols]
    if name == "op":
        return lambda rows, cols: source[POINTS - 1, rows, cols]
    which = int(name[1])
    if name[0] == "e":
        return lambda rows, cols: initial[2 * which, rows, cols]
    return lambda rows, cols: source[2 * which + (name[0] == "o"), rows, cols]


def pack_kernel(initial, source, diffusivity, growth, down, up, turn, slant_down, slant_up):
    rows, cols = diffusivity.shape
    depth = cols // LANES
    for rims, low, high in ((RIMS_0, down, up), (BEHIND_0, slant_down, slant_up)):
        at = 0
        for name, rim in rims:
            get = pieces(name, initial, source, diffusivity, growth)
            for c in range(depth):
                lanes = pl.ds(c * LANES, LANES)
                place = pl.ds(at * depth + c, rim, stride=depth)
                low[place, :] = get(pl.ds(rows - rim, rim), lanes)
                high[place, :] = get(pl.ds(0, rim), lanes)
            at += rim
    for index, (name, _) in enumerate(BEHIND_0):
        get = pieces(name, initial, source, diffusivity, growth)
        for c in range(depth):
            for r in range(0, rows, 8):
                place = pl.ds((index * rows + r) * depth + c, 8, stride=depth)
                turn[place, :] = get(pl.ds(r, 8), pl.ds(c * LANES, LANES))


def window(get, first, depth):
    line, offset = first // LANES, first % LANES
    shape = get(0).shape
    source = lax.broadcasted_iota(jnp.int32, shape, 1) + (offset - REACH)
    shift = (REACH - offset) % LANES
    before = jnp.where(line > 0, pltpu.roll(get(jnp.maximum(line - 1, 0)), shift, 1), 0.0)
    here = pltpu.roll(get(line), shift, 1)
    after = jnp.where(
        line < depth - 1, pltpu.roll(get(jnp.minimum(line + 1, depth - 1)), shift, 1), 0.0
    )
    return jnp.where(source < 0, before, jnp.where(source >= LANES, after, here))


def core_kernel(share, initial, source, diffusivity, growth, core, back, windows):
    rows, cols = diffusivity.shape
    depth = cols // LANES
    for index, name in enumerate(CORES):
        get = pieces(name, initial, source, diffusivity, growth)
        for c in range(depth):
            for r in range(0, rows, 8):
                value = get(pl.ds(r, 8), pl.ds(c * LANES, LANES))
                core[pl.ds((index * rows + r) * depth + c, 8, stride=depth), :] = value
                if name == "s0":
                    back[pl.ds(r * depth + c, 8, stride=depth), :] = value
    block = lax.axis_index("tm") * lax.axis_size("space")
    for target in range(windows.shape[0]):
        first = (block + target) * share
        for which, name in enumerate(("d", "g")):
            start = CORES.index(name) * rows * depth
            get = lambda line: core[pl.ds(start + line, rows, stride=depth), :]
            windows[target, which] = window(get, first, depth)


def split(ref, rims):
    at, out = 0, {}
    for name, rim in rims:
        out[name] = ref[pl.ds(at, rim)]
        at += rim
    return out


def level0_kernel(
    core, above, below, behind, behind_above, behind_below,
    turn, down, up, slant_down, slant_up, state, forcing, first_forcing, coefs,
    fields, diff, grow,
):
    rows = core.shape[0] // len(CORES)
    low, high = flags()
    names = list(CORES) + ["ep", "op"]
    spots = {name: index for index, name in enumerate(names)}
    for rims, from_low, from_high in (
        (RIMS_0, above, below),
        (BEHIND_0, behind_above, behind_below),
    ):
        lows, highs = split(from_low, rims), split(from_high, rims)
        for name, rim in rims:
            if name in ("d", "g"):
                buffer = diff if name == "d" else grow
            else:
                buffer = fields.at[spots[name]]
            set_rims(buffer, rows, rim, lows[name], highs[name], low, high)
    for name in CORES:
        if name in ("d", "g"):
            buffer = diff if name == "d" else grow
        else:
            buffer = fields.at[spots[name]]
        buffer[pl.ds(MARGIN, rows)] = core[pl.ds(CORES.index(name) * rows, rows)]
    for index, (name, _) in enumerate(BEHIND_0):
        fields[spots[name], pl.ds(MARGIN, rows)] = behind[pl.ds(index * rows, rows)]
    extra = len(names)
    halves = POINTS // 2
    odd = [extra + i for i in range(halves)]
    even = [extra + halves + i for i in range(halves)]
    image = [extra + 2 * halves + i for i in range(halves)]

    def first(at):
        d, g = diff[pl.ds(at, 2)], grow[pl.ds(at, 2)]
        for i in range(halves):
            start, term = ("ep", "op") if i == 0 else (f"e{i - 1}", f"o{i - 1}")
            mid, slope = growth_of(fields.at[spots[start]], at, 2, d, g)
            fields[odd[i], pl.ds(at, 2)] = mid + slope + fields[spots[term], pl.ds(at, 2)]

    def second(at):
        d, g = diff[pl.ds(at, 2)], grow[pl.ds(at, 2)]
        for i in range(halves):
            mid, slope = growth_of(fields.at[odd[i]], at, 2, d, g)
            fields[even[i], pl.ds(at, 2)] = mid + slope + fields[spots[f"s{i}"], pl.ds(at, 2)]

    def third(at):
        d, g = diff[pl.ds(at, 2)], grow[pl.ds(at, 2)]
        for i in range(halves):
            mid, slope = growth_of(fields.at[even[i]], at, 2, d, g)
            fields[odd[i], pl.ds(at, 2)] = mid + slope + fields[spots[f"o{i}"], pl.ds(at, 2)]
            fields[image[i], pl.ds(at, 2)] = mid + 2.0 * slope

    def fourth(at):
        d, g = diff[pl.ds(at, 2)], grow[pl.ds(at, 2)]
        here = at - MARGIN
        for i in range(halves):
            mid, slope = growth_of(fields.at[odd[i]], at, 2, d, g)
            pair = mid + slope - fields[image[i], pl.ds(at, 2)]
            if i == halves - 1:
                turn[pl.ds(here, 2)] = pair
            else:
                term = fields[spots[f"s{i + 1}"], pl.ds(at, 2)] + pair
                forcing[pl.ds(i * rows + here, 2)] = term
                if i == halves - 2:
                    turn[pl.ds(rows + here, 2)] = fields[image[i], pl.ds(at, 2)] + term

    over_rows(rows, 3, first)
    over_rows(rows, 2, second)
    over_rows(rows, 1, third)
    over_rows(rows, 0, fourth)
    state[...] = fields[even[0], pl.ds(MARGIN - 2, rows + 4)]
    first_forcing[...] = fields[spots["s0"], pl.ds(MARGIN - 2, rows + 4)]
    coefs[pl.ds(0, rows + 6)] = diff[pl.ds(MARGIN - 3, rows + 6)]
    coefs[pl.ds(rows + 6, rows + 6)] = grow[pl.ds(MARGIN - 3, rows + 6)]
    send_behind(turn, slant_down, slant_up, rows)
    down[pl.ds(0, 2)] = fields[even[0], pl.ds(MARGIN + rows - 4, 2)]
    up[pl.ds(0, 2)] = fields[even[0], pl.ds(MARGIN + 2, 2)]
    at = 2
    for which, rim in ((0, 3), (2, 1), (1, 2)):
        down[pl.ds(at, rim)] = forcing[pl.ds((which + 1) * rows - rim, rim)]
        up[pl.ds(at, rim)] = forcing[pl.ds(which * rows, rim)]
        at += rim


RIMS_1 = (("state", 2), ("g1", 3), ("g3", 1), ("g2", 2))


def send_behind(turn, slant_down, slant_up, rows):
    at = 0
    for index, (_, rim) in enumerate(BEHIND):
        slant_down[pl.ds(at, rim)] = turn[pl.ds((index + 1) * rows - rim, rim)]
        slant_up[pl.ds(at, rim)] = turn[pl.ds(index * rows, rim)]
        at += rim


def take_behind(rows, buffers, behind, behind_above, behind_below, low, high):
    lows, highs = split(behind_above, BEHIND), split(behind_below, BEHIND)
    for index, (name, rim) in enumerate(BEHIND):
        buffer = buffers[index]
        set_rims(buffer, rows, rim, lows[name], highs[name], low, high)
        buffer[pl.ds(MARGIN, rows)] = behind[pl.ds(index * rows, rows)]


def take_coefs(rows, coefs, diff, grow):
    diff[pl.ds(MARGIN - 3, rows + 6)] = coefs[pl.ds(0, rows + 6)]
    grow[pl.ds(MARGIN - 3, rows + 6)] = coefs[pl.ds(rows + 6, rows + 6)]


def level1_kernel(
    state, forcing, first_forcing, coefs, above, below, behind, behind_above, behind_below,
    turn, down, up, slant_down, slant_up, next_first, next_forcing, late_a, late_b,
    fields, diff, grow,
):
    rows = forcing.shape[0] // 3
    low, high = flags()
    take_coefs(rows, coefs, diff, grow)
    v, g1, g3, g2, g0, pair, before, after, even0, even1, image0, image1, odd0, odd1 = range(14)
    lows, highs = split(above, RIMS_1), split(below, RIMS_1)
    for name, spot, rim, inner in (
        ("state", v, 4, 2), ("g1", g1, 3, 0), ("g3", g3, 1, 0), ("g2", g2, 2, 0),
    ):
        set_rims(fields.at[spot], rows, rim, lows[name], highs[name], low, high, inner)
    fields[v, pl.ds(MARGIN - 2, rows + 4)] = state[...]
    for which, spot in enumerate((g1, g2, g3)):
        fields[spot, pl.ds(MARGIN, rows)] = forcing[pl.ds(which * rows, rows)]
    take_behind(
        rows, (fields.at[pair], fields.at[before]), behind, behind_above, behind_below, low, high
    )
    fields[g0, pl.ds(MARGIN - 2, rows + 4)] = (
        first_forcing[...] + fields[pair, pl.ds(MARGIN - 2, rows + 4)]
    )

    def first(at):
        mid, slope = growth_of(fields.at[v], at, 2, diff[pl.ds(at, 2)], grow[pl.ds(at, 2)])
        fields[after, pl.ds(at, 2)] = mid + 2.0 * slope + fields[g1, pl.ds(at, 2)]

    def second(at):
        d, g = diff[pl.ds(at, 2)], grow[pl.ds(at, 2)]
        for start, term, end in ((before, g0, even0), (after, g2, even1)):
            mid, slope = growth_of(fields.at[start], at, 2, d, g)
            fields[end, pl.ds(at, 2)] = mid + 2.0 * slope + fields[term, pl.ds(at, 2)]

    def third(at):
        d, g = diff[pl.ds(at, 2)], grow[pl.ds(at, 2)]
        for start, term, end, image in ((even0, g1, odd0, image0), (even1, g3, odd1, image1)):
            mid, slope = growth_of(fields.at[start], at, 2, d, g)
            fields[end, pl.ds(at, 2)] = mid + 2.0 * slope + fields[term, pl.ds(at, 2)]
            fields[image, pl.ds(at, 2)] = mid + 4.0 * slope

    def fourth(at):
        d, g = diff[pl.ds(at, 2)], grow[pl.ds(at, 2)]
        here = at - MARGIN
        mid, slope = growth_of(fields.at[odd1], at, 2, d, g)
        turn[pl.ds(here, 2)] = mid + 2.0 * slope - fields[image1, pl.ds(at, 2)]
        mid, slope = growth_of(fields.at[odd0], at, 2, d, g)
        image = fields[image0, pl.ds(at, 2)]
        term = fields[g2, pl.ds(at, 2)] + (mid + 2.0 * slope - image)
        next_forcing[pl.ds(here, 2)] = term
        turn[pl.ds(rows + here, 2)] = image + term

    over_rows(rows, 3, first)
    over_rows(rows, 2, second)
    over_rows(rows, 1, third)
    over_rows(rows, 0, fourth)
    next_first[...] = fields[g0, pl.ds(MARGIN - 2, rows + 4)]
    late_a[...] = fields[g1, pl.ds(MARGIN - 1, rows + 2)]
    late_b[...] = fields[g3, pl.ds(MARGIN - 1, rows + 2)]
    send_behind(turn, slant_down, slant_up, rows)
    down[...] = next_forcing[pl.ds(rows - 2, 2)]
    up[...] = next_forcing[pl.ds(0, 2)]


def level2_kernel(
    share, next_first, next_forcing, coefs, above, below, behind, behind_above, behind_below,
    ahead, pair0, pair1, slots, wide_forcing, fields, diff, grow, flat,
):
    rows = next_forcing.shape[0]
    depth = next_forcing.shape[1]
    low, high = flags()
    take_coefs(rows, coefs, diff, grow)
    g1, g0, pair, before, even, image, odd = range(7)
    set_rims(fields.at[g1], rows, 2, above[...], below[...], low, high)
    fields[g1, pl.ds(MARGIN, rows)] = next_forcing[...]
    take_behind(
        rows, (fields.at[pair], fields.at[before]), behind, behind_above, behind_below, low, high
    )
    fields[g0, pl.ds(MARGIN - 2, rows + 4)] = (
        next_first[...] + fields[pair, pl.ds(MARGIN - 2, rows + 4)]
    )
    wide_forcing[...] = fields[g1, pl.ds(MARGIN - 2, rows + 4)]
    last = lax.axis_index("tm") == lax.axis_size("tm") - 1

    def second(at):
        mid, slope = growth_of(fields.at[before], at, 2, diff[pl.ds(at, 2)], grow[pl.ds(at, 2)])
        fields[even, pl.ds(at, 2)] = mid + 4.0 * slope + fields[g0, pl.ds(at, 2)]

    def third(at):
        mid, slope = growth_of(fields.at[even], at, 2, diff[pl.ds(at, 2)], grow[pl.ds(at, 2)])
        fields[odd, pl.ds(at, 2)] = mid + 4.0 * slope + fields[g1, pl.ds(at, 2)]
        fields[image, pl.ds(at, 2)] = mid + 8.0 * slope

    def fourth(at):
        here = at - MARGIN
        mid, slope = growth_of(fields.at[odd], at, 2, diff[pl.ds(at, 2)], grow[pl.ds(at, 2)])
        stepped = fields[image, pl.ds(at, 2)]
        term = (
            ahead[pl.ds(here, 2)]
            + pair0[pl.ds(here, 2)]
            + pair1[pl.ds(here, 2)]
            + (mid + 4.0 * slope - stepped)
        )
        term = term + jnp.where(last, stepped, 0.0)
        for i in range(2):
            flat[pl.ds(pl.multiple_of((here + i) * depth, depth), depth), :] = term[i]

    over_rows(rows, 2, second)
    over_rows(rows, 1, third)
    over_rows(rows, 0, fourth)
    lines = [flat[pl.ds(line, rows, stride=depth), :] for line in range(depth)]
    lane = lax.broadcasted_iota(jnp.int32, (rows, LANES), 1)
    for target in range(slots.shape[0]):
        line, offset = target * share // LANES, target * share % LANES
        shift = (REACH - offset) % LANES
        place = lane + (offset - REACH)
        value = pltpu.roll(lines[line], shift, 1)
        if offset < REACH:
            before_line = pltpu.roll(lines[line - 1], shift, 1) if line > 0 else 0.0
            value = jnp.where(place < 0, before_line, value)
        if offset - REACH + LANES > LANES:
            after_line = pltpu.roll(lines[line + 1], shift, 1) if line < depth - 1 else 0.0
            value = jnp.where(place >= LANES, after_line, value)
        slots[target] = value


def packing(rows, share):
    groups = LANES // share
    each = -(-(rows + 2 * UP_RIM) // groups)
    return groups, each, -(-each // 8) * 8


def sweep_kernel(share, slabs, arrived, windows, slots, padded):
    devices, rows, _ = arrived.shape
    blocks = devices // slabs
    total = slabs * rows
    groups, each, held = packing(rows, share)
    diff = jnp.concatenate([windows[slab, 0] for slab in range(slabs)], axis=0)
    grow = jnp.concatenate([windows[slab, 1] for slab in range(slabs)], axis=0)
    line = lax.broadcasted_iota(jnp.int32, (total, LANES), 0)
    lane = lax.broadcasted_iota(jnp.int32, (held, LANES), 1)
    padded[...] = jnp.zeros(padded.shape, jnp.float32)

    def block(index):
        return jnp.concatenate([arrived[index * slabs + slab] for slab in range(slabs)], axis=0)

    field = block(blocks - 1)
    for index in range(blocks):
        for group in range(groups):
            padded[group, pl.ds(8, total), :] = pltpu.roll(
                field, (group * share - REACH) % LANES, 1
            )
        for slab in range(slabs):
            start = 8 + slab * rows - UP_RIM
            value = padded[0, pl.ds(start, held), :]
            for group in range(1, groups):
                piece = padded[group, pl.ds(start + group * each, held), :]
                value = jnp.where(lane >= group * share, piece, value)
            slots[index * slabs + slab] = value
        if index < blocks - 1:
            north = jnp.where(line == 0, 0.0, pltpu.roll(field, 1, 0))
            south = jnp.where(line == total - 1, 0.0, pltpu.roll(field, total - 1, 0))
            sides = pltpu.roll(field, 1, 1) + pltpu.roll(field, LANES - 1, 1)
            laplace = north + south + sides - 4.0 * field
            slope = diff * laplace + grow * field / (1.0 + field * field)
            field = field + 8.0 * slope + block(index)


def up_kernel(
    share, arrived, wide_forcing, late_a, late_b, core, coefs, out, fields, diff, grow, flat
):
    rows = wide_forcing.shape[0] - 4
    depth = wide_forcing.shape[1]
    groups, each, held = packing(rows, share)
    take_coefs(rows, coefs, diff, grow)
    lane = lax.broadcasted_iota(jnp.int32, (depth, LANES), 1)
    for row in range(rows + 2 * UP_RIM):
        group, line = row // each, row % each
        value = None
        for part in range(groups):
            piece = arrived[pl.ds(part * held + line, depth, stride=groups * held), :]
            piece = pltpu.roll(piece, ((part - group) * share) % LANES, 1) if part != group else piece
            value = piece if value is None else jnp.where(lane >= part * share, piece, value)
        fields[0, MARGIN - UP_RIM + row] = value
    odd_first = CORES.index("o0") * rows

    def put(spot, here, value):
        for i in range(2):
            place = (spot * rows + here + i) * depth
            flat[pl.ds(pl.multiple_of(place, depth), depth), :] = value[i]

    def first(at):
        mid, slope = growth_of(fields.at[0], at, 2, diff[pl.ds(at, 2)], grow[pl.ds(at, 2)])
        fields[2, pl.ds(at, 2)] = mid + 4.0 * slope + wide_forcing[pl.ds(at - MARGIN + 2, 2)]

    def second(at):
        d, g = diff[pl.ds(at, 2)], grow[pl.ds(at, 2)]
        for start, late in ((0, late_a), (2, late_b)):
            mid, slope = growth_of(fields.at[start], at, 2, d, g)
            fields[start + 1, pl.ds(at, 2)] = mid + 2.0 * slope + late[pl.ds(at - MARGIN + 1, 2)]

    def third(at):
        d, g = diff[pl.ds(at, 2)], grow[pl.ds(at, 2)]
        here = at - MARGIN
        for i in range(POINTS // 2):
            mid, slope = growth_of(fields.at[i], at, 2, d, g)
            put(2 * i, here, mid)
            put(2 * i + 1, here, mid + slope + core[pl.ds(odd_first + i * rows + here, 2)])

    over_rows(rows, 2, first)
    over_rows(rows, 1, second)
    over_rows(rows, 0, third)
    for point in range(POINTS):
        for r in range(0, rows, 8):
            for c in range(depth):
                start = (point * rows + r) * depth + c
                out[point, pl.ds(r, 8), pl.ds(c * LANES, LANES)] = flat[
                    pl.ds(start, 8, stride=depth), :
                ]


def moved(array, blocks, slabs):
    tm, space = lax.axis_size("tm"), lax.axis_size("space")
    pairs = [
        (t * space + s, (t + blocks) % tm * space + (s + slabs) % space)
        for t in range(tm)
        for s in range(space)
    ]
    return lax.ppermute(array, ("tm", "space"), pairs)


def exchange(down, up, turn, slant_down, slant_up):
    return (
        moved(down, 0, 1), moved(up, 0, -1), moved(turn, 1, 0),
        moved(slant_down, 1, 1), moved(slant_up, 1, -1),
    )


def body(initial, source, diffusivity, growth):
    points, rows, cols = initial.shape
    assert points == POINTS and rows % 8 == 0 and cols % LANES == 0
    depth = cols // LANES
    tm, space = lax.axis_size("tm"), lax.axis_size("space")
    devices = tm * space
    share = cols // devices
    assert share * devices == cols and LANES % share == 0
    assert tm - 1 <= REACH and REACH + share + tm - 1 <= LANES
    groups, each, held = packing(rows, share)
    wide = rows + 2 * MARGIN

    def lines(n):
        return (n * depth, LANES)

    def field(n):
        return (n, depth, LANES)

    def as_rows(array):
        return array.reshape(-1, depth, LANES)

    sides, behind = count(RIMS_0), count(BEHIND_0)
    sends = call(
        pack_kernel,
        [lines(sides), lines(sides), lines(2 * rows), lines(behind), lines(behind)],
        [],
        initial, source, diffusivity, growth,
    )
    core, back, windows = call(
        functools.partial(core_kernel, share),
        [lines(len(CORES) * rows), lines(rows), (space, 2, rows, LANES)],
        [],
        initial, source, diffusivity, growth,
    )
    arrived = exchange(*(as_rows(part) for part in sends))
    ahead = as_rows(moved(back, -1, 0))
    core = as_rows(core)
    slab = lax.axis_index("space")
    kept = [lax.dynamic_index_in_dim(windows, slab, 0, keepdims=False)]
    for by in range(1, space):
        piece = lax.dynamic_index_in_dim(windows, (slab + by) % space, 0, keepdims=False)
        kept.append(moved(piece, 0, by))
    order = (slab - jnp.arange(space)) % space
    coef_windows = jnp.take(jnp.stack(kept), order, axis=0)

    buffers = [(wide, depth, LANES), (wide, depth, LANES)]
    rim1, rimb = count(RIMS_1), count(BEHIND)
    turn, down, up, slant_down, slant_up, state, forcing, first_forcing, coefs = call(
        level0_kernel,
        [
            field(2 * rows), field(rim1), field(rim1), field(rimb), field(rimb),
            field(rows + 4), field(3 * rows), field(rows + 4), field(2 * (rows + 6)),
        ],
        [(len(CORES) + 2 + 3 * (POINTS // 2), wide, depth, LANES)] + buffers,
        core, *arrived,
    )
    pair0 = turn[:rows]
    arrived = exchange(down, up, turn, slant_down, slant_up)
    turn, down, up, slant_down, slant_up, next_first, next_forcing, late_a, late_b = call(
        level1_kernel,
        [
            field(2 * rows), field(2), field(2), field(rimb), field(rimb),
            field(rows + 4), field(rows), field(rows + 2), field(rows + 2),
        ],
        [(14, wide, depth, LANES)] + buffers,
        state, forcing, first_forcing, coefs, *arrived,
    )
    pair1 = turn[:rows]
    arrived = exchange(down, up, turn, slant_down, slant_up)
    slots, wide_forcing = call(
        functools.partial(level2_kernel, share),
        [(devices, rows, LANES), field(rows + 4)],
        [(7, wide, depth, LANES)] + buffers + [(rows * depth, LANES)],
        next_first, next_forcing, coefs, *arrived, ahead, pair0, pair1,
    )
    slots = lax.all_to_all(slots, ("tm", "space"), 0, 0, tiled=True)
    (slots,) = call(
        functools.partial(sweep_kernel, share, space),
        [(devices, held, LANES)],
        [(groups, 8 + space * rows + 2 * rows + held, LANES)],
        slots, coef_windows,
    )
    slots = lax.all_to_all(slots, ("tm", "space"), 0, 0, tiled=True)
    (out,) = call(
        functools.partial(up_kernel, share),
        [(points, rows, cols)],
        [(4, wide, depth, LANES)] + buffers + [(points * rows * depth, LANES)],
        slots.reshape(devices * held, LANES), wide_forcing, late_a, late_b, core, coefs,
    )
    return out


def solution(mesh):
    placed = (P("tm", "space", None), P("tm", "space", None), P("space", None), P("space", None))
    return jax.shard_map(
        body, mesh=mesh, in_specs=placed, out_specs=P("tm", "space", None), check_vma=False
    )
```

```python
import functools

import jax
import jax.numpy as jnp
from jax import lax
from jax.experimental import pallas as pl
from jax.experimental.pallas import tpu as pltpu
from jax.sharding import PartitionSpec as P

LANES = 128
MARGIN = 4
REACH = 32
UP_RIM = 3
FIELDS = 3
POINTS = 8
diffusion_number = 0.03
time_step = 0.02

RIMS_0 = (
    ("e0", 4), ("e1", 4), ("e2", 4),
    ("o0", 3), ("o1", 3), ("o2", 3), ("o3", 1),
    ("s0", 2), ("s1", 2), ("s2", 2), ("s3", 2),
    ("d", 3), ("g", 3),
)
CORES = ("e0", "e1", "e2", "o0", "o1", "o2", "o3", "s0", "s1", "s2", "s3", "d", "g")
BEHIND_0 = (("ep", 4), ("op", 3))
BEHIND = (("pair", 2), ("odd", 3))


def count(rims):
    return sum(rows for _, rows in rims)


def params(mib=16):
    return pltpu.CompilerParams(vmem_limit_bytes=mib * 2**20)


def call(kernel, outs, scratch, *args, mib=16, place=pltpu.VMEM, sems=0):
    return pl.pallas_call(
        kernel,
        out_shape=tuple(jax.ShapeDtypeStruct(shape, jnp.float32) for shape in outs),
        in_specs=[pl.BlockSpec(memory_space=place)] * len(args),
        out_specs=tuple(pl.BlockSpec(memory_space=pltpu.VMEM) for _ in outs),
        scratch_shapes=[pltpu.VMEM(shape, jnp.float32) for shape in scratch]
        + ([pltpu.SemaphoreType.DMA((sems,))] if sems else []),
        compiler_params=params(mib),
    )(*args)


def beside(mid):
    depth = mid.shape[1]
    lane = lax.broadcasted_iota(jnp.int32, mid.shape, 2)
    line = lax.broadcasted_iota(jnp.int32, mid.shape, 1)
    left = pltpu.roll(mid, 1, 2)
    left_turn = pltpu.roll(left, 1, 1)
    right = pltpu.roll(mid, LANES - 1, 2)
    right_turn = pltpu.roll(right, depth - 1, 1)
    left = jnp.where(lane == 0, jnp.where(line == 0, 0.0, left_turn), left)
    right = jnp.where(lane == LANES - 1, jnp.where(line == depth - 1, 0.0, right_turn), right)
    return left + right


def growth_of(ref, at, rows, diff, grow):
    wide = ref[pl.ds(at - 1, rows + 2)]
    mid = wide[1:-1]
    laplace = wide[:-2] + wide[2:] + beside(mid) - 4.0 * mid
    return mid, diff * laplace + grow * mid / (1.0 + mid * mid)


def over_rows(rows, rim, body):
    body(MARGIN - rim, rows + 2 * rim)


def flags():
    slab = lax.axis_index("space")
    low = jnp.where(slab > 0, 1.0, 0.0).astype(jnp.float32)
    high = jnp.where(slab < lax.axis_size("space") - 1, 1.0, 0.0).astype(jnp.float32)
    return low, high


def set_rims(buffer, rows, rim, low_rows, high_rows, low, high, inner=0):
    width = rim - inner
    buffer[pl.ds(MARGIN - rim, width)] = low_rows * low
    buffer[pl.ds(MARGIN + rows + inner, width)] = high_rows * high


def pieces(name, evens, source, diffusivity, growth):
    if name == "d":
        return lambda rows, cols: diffusivity[rows, cols] * diffusion_number
    if name == "g":
        return lambda rows, cols: growth[rows, cols] * time_step
    if name == "ep":
        return lambda rows, cols: evens[POINTS // 2 - 1, rows, cols]
    if name == "op":
        return lambda rows, cols: source[POINTS - 1, rows, cols]
    which = int(name[1])
    if name[0] == "e":
        return lambda rows, cols: evens[which, rows, cols]
    return lambda rows, cols: source[2 * which + (name[0] == "o"), rows, cols]


def pack_kernel(
    initial_all, source_all, diffusivity_all, growth_all,
    down, up, turn, slant_down, slant_up, evens, source, diffusivity, growth, sems,
):
    pairs = [(initial_all.at[2 * i], evens.at[i]) for i in range(POINTS // 2)]
    pairs += [(source_all, source), (diffusivity_all, diffusivity), (growth_all, growth)]
    copies = [pltpu.make_async_copy(*pair, sems.at[i]) for i, pair in enumerate(pairs)]
    for copy in copies:
        copy.start()
    for copy in copies:
        copy.wait()
    rows, cols = diffusivity.shape
    depth = cols // LANES
    for rims, low, high in ((RIMS_0, down, up), (BEHIND_0, slant_down, slant_up)):
        at = 0
        for name, rim in rims:
            get = pieces(name, evens, source, diffusivity, growth)
            for c in range(depth):
                lanes = pl.ds(c * LANES, LANES)
                place = pl.ds(at * depth + c, rim, stride=depth)
                low[place, :] = get(pl.ds(rows - rim, rim), lanes)
                high[place, :] = get(pl.ds(0, rim), lanes)
            at += rim
    for index, (name, _) in enumerate(BEHIND_0):
        get = pieces(name, evens, source, diffusivity, growth)
        for c in range(depth):
            for r in range(0, rows, 8):
                place = pl.ds((index * rows + r) * depth + c, 8, stride=depth)
                turn[place, :] = get(pl.ds(r, 8), pl.ds(c * LANES, LANES))


def window(get, first, depth):
    line, offset = first // LANES, first % LANES
    shape = get(0).shape
    source = lax.broadcasted_iota(jnp.int32, shape, 1) + (offset - REACH)
    shift = (REACH - offset) % LANES
    before = jnp.where(line > 0, pltpu.roll(get(jnp.maximum(line - 1, 0)), shift, 1), 0.0)
    here = pltpu.roll(get(line), shift, 1)
    after = jnp.where(
        line < depth - 1, pltpu.roll(get(jnp.minimum(line + 1, depth - 1)), shift, 1), 0.0
    )
    return jnp.where(source < 0, before, jnp.where(source >= LANES, after, here))


def core_kernel(share, evens, source, diffusivity, growth, core, back, *windows):
    rows, cols = diffusivity.shape
    depth = cols // LANES
    for index, name in enumerate(CORES):
        get = pieces(name, evens, source, diffusivity, growth)
        for c in range(depth):
            for r in range(0, rows, 8):
                value = get(pl.ds(r, 8), pl.ds(c * LANES, LANES))
                core[pl.ds((index * rows + r) * depth + c, 8, stride=depth), :] = value
                if name == "s0":
                    back[pl.ds(r * depth + c, 8, stride=depth), :] = value
    slabs = lax.axis_size("space")
    for by, out in enumerate(windows):
        target = lax.axis_index("tm") * slabs + (lax.axis_index("space") + by) % slabs
        for which, name in enumerate(("d", "g")):
            start = CORES.index(name) * rows * depth
            get = lambda line: core[pl.ds(start + line, rows, stride=depth), :]
            out[which] = window(get, target * share, depth)


def split(ref, rims):
    at, out = 0, {}
    for name, rim in rims:
        out[name] = ref[pl.ds(at, rim)]
        at += rim
    return out


def level0_kernel(
    core, above, below, behind, behind_above, behind_below,
    turn, down, up, slant_down, slant_up, state, forcing, first_forcing, coefs,
    fields, diff, grow,
):
    rows = core.shape[0] // len(CORES)
    low, high = flags()
    names = list(CORES) + ["ep", "op"]
    spots = {name: index for index, name in enumerate(names)}
    for rims, from_low, from_high in (
        (RIMS_0, above, below),
        (BEHIND_0, behind_above, behind_below),
    ):
        lows, highs = split(from_low, rims), split(from_high, rims)
        for name, rim in rims:
            if name in ("d", "g"):
                buffer = diff if name == "d" else grow
            else:
                buffer = fields.at[spots[name]]
            set_rims(buffer, rows, rim, lows[name], highs[name], low, high)
    for name in CORES:
        if name in ("d", "g"):
            buffer = diff if name == "d" else grow
        else:
            buffer = fields.at[spots[name]]
        buffer[pl.ds(MARGIN, rows)] = core[pl.ds(CORES.index(name) * rows, rows)]
    for index, (name, _) in enumerate(BEHIND_0):
        fields[spots[name], pl.ds(MARGIN, rows)] = behind[pl.ds(index * rows, rows)]
    extra = len(names)
    halves = POINTS // 2
    odd = [extra + i for i in range(halves)]
    even = [extra + halves + i for i in range(halves)]
    image = [extra + 2 * halves + i for i in range(halves)]

    def first(at, n):
        d, g = diff[pl.ds(at, n)], grow[pl.ds(at, n)]
        for i in range(halves):
            start, term = ("ep", "op") if i == 0 else (f"e{i - 1}", f"o{i - 1}")
            mid, slope = growth_of(fields.at[spots[start]], at, n, d, g)
            fields[odd[i], pl.ds(at, n)] = mid + slope + fields[spots[term], pl.ds(at, n)]

    def second(at, n):
        d, g = diff[pl.ds(at, n)], grow[pl.ds(at, n)]
        for i in range(halves):
            mid, slope = growth_of(fields.at[odd[i]], at, n, d, g)
            fields[even[i], pl.ds(at, n)] = mid + slope + fields[spots[f"s{i}"], pl.ds(at, n)]

    def third(at, n):
        d, g = diff[pl.ds(at, n)], grow[pl.ds(at, n)]
        for i in range(halves):
            mid, slope = growth_of(fields.at[even[i]], at, n, d, g)
            fields[odd[i], pl.ds(at, n)] = mid + slope + fields[spots[f"o{i}"], pl.ds(at, n)]
            fields[image[i], pl.ds(at, n)] = mid + 2.0 * slope

    def fourth(at, n):
        d, g = diff[pl.ds(at, n)], grow[pl.ds(at, n)]
        here = at - MARGIN
        for i in range(halves):
            mid, slope = growth_of(fields.at[odd[i]], at, n, d, g)
            pair = mid + slope - fields[image[i], pl.ds(at, n)]
            if i == halves - 1:
                turn[pl.ds(here, n)] = pair
            else:
                term = fields[spots[f"s{i + 1}"], pl.ds(at, n)] + pair
                forcing[pl.ds(i * rows + here, n)] = term
                if i == halves - 2:
                    turn[pl.ds(rows + here, n)] = fields[image[i], pl.ds(at, n)] + term

    over_rows(rows, 3, first)
    over_rows(rows, 2, second)
    over_rows(rows, 1, third)
    over_rows(rows, 0, fourth)
    state[...] = fields[even[0], pl.ds(MARGIN - 2, rows + 4)]
    first_forcing[...] = fields[spots["s0"], pl.ds(MARGIN - 2, rows + 4)]
    coefs[pl.ds(0, rows + 6)] = diff[pl.ds(MARGIN - 3, rows + 6)]
    coefs[pl.ds(rows + 6, rows + 6)] = grow[pl.ds(MARGIN - 3, rows + 6)]
    send_behind(turn, slant_down, slant_up, rows)
    down[pl.ds(0, 2)] = fields[even[0], pl.ds(MARGIN + rows - 4, 2)]
    up[pl.ds(0, 2)] = fields[even[0], pl.ds(MARGIN + 2, 2)]
    at = 2
    for which, rim in ((0, 3), (2, 1), (1, 2)):
        down[pl.ds(at, rim)] = forcing[pl.ds((which + 1) * rows - rim, rim)]
        up[pl.ds(at, rim)] = forcing[pl.ds(which * rows, rim)]
        at += rim


RIMS_1 = (("state", 2), ("g1", 3), ("g3", 1), ("g2", 2))


def send_behind(turn, slant_down, slant_up, rows):
    at = 0
    for index, (_, rim) in enumerate(BEHIND):
        slant_down[pl.ds(at, rim)] = turn[pl.ds((index + 1) * rows - rim, rim)]
        slant_up[pl.ds(at, rim)] = turn[pl.ds(index * rows, rim)]
        at += rim


def take_behind(rows, buffers, behind, behind_above, behind_below, low, high):
    lows, highs = split(behind_above, BEHIND), split(behind_below, BEHIND)
    for index, (name, rim) in enumerate(BEHIND):
        buffer = buffers[index]
        set_rims(buffer, rows, rim, lows[name], highs[name], low, high)
        buffer[pl.ds(MARGIN, rows)] = behind[pl.ds(index * rows, rows)]


def take_coefs(rows, coefs, diff, grow):
    diff[pl.ds(MARGIN - 3, rows + 6)] = coefs[pl.ds(0, rows + 6)]
    grow[pl.ds(MARGIN - 3, rows + 6)] = coefs[pl.ds(rows + 6, rows + 6)]


def level1_kernel(
    share, state, forcing, first_forcing, coefs, last_pair, ahead,
    above, below, behind, behind_above, behind_below,
    slots, down, up, next_forcing, late_a, late_b,
    fields, diff, grow, flat,
):
    rows = forcing.shape[0] // 3
    low, high = flags()
    take_coefs(rows, coefs, diff, grow)
    v, g1, g3, g2, g0, pair, before, after, even0, even1, image0, image1, odd0, odd1 = range(14)
    lows, highs = split(above, RIMS_1), split(below, RIMS_1)
    for name, spot, rim, inner in (
        ("state", v, 4, 2), ("g1", g1, 3, 0), ("g3", g3, 1, 0), ("g2", g2, 2, 0),
    ):
        set_rims(fields.at[spot], rows, rim, lows[name], highs[name], low, high, inner)
    fields[v, pl.ds(MARGIN - 2, rows + 4)] = state[...]
    for which, spot in enumerate((g1, g2, g3)):
        fields[spot, pl.ds(MARGIN, rows)] = forcing[pl.ds(which * rows, rows)]
    take_behind(
        rows, (fields.at[pair], fields.at[before]), behind, behind_above, behind_below, low, high
    )
    fields[g0, pl.ds(MARGIN - 2, rows + 4)] = (
        first_forcing[...] + fields[pair, pl.ds(MARGIN - 2, rows + 4)]
    )

    def first(at, n):
        mid, slope = growth_of(fields.at[v], at, n, diff[pl.ds(at, n)], grow[pl.ds(at, n)])
        fields[after, pl.ds(at, n)] = mid + 2.0 * slope + fields[g1, pl.ds(at, n)]

    def second(at, n):
        d, g = diff[pl.ds(at, n)], grow[pl.ds(at, n)]
        for start, term, end in ((before, g0, even0), (after, g2, even1)):
            mid, slope = growth_of(fields.at[start], at, n, d, g)
            fields[end, pl.ds(at, n)] = mid + 2.0 * slope + fields[term, pl.ds(at, n)]

    def third(at, n):
        d, g = diff[pl.ds(at, n)], grow[pl.ds(at, n)]
        for start, term, end, image in ((even0, g1, odd0, image0), (even1, g3, odd1, image1)):
            mid, slope = growth_of(fields.at[start], at, n, d, g)
            fields[end, pl.ds(at, n)] = mid + 2.0 * slope + fields[term, pl.ds(at, n)]
            fields[image, pl.ds(at, n)] = mid + 4.0 * slope

    def fourth(at, n):
        d, g = diff[pl.ds(at, n)], grow[pl.ds(at, n)]
        here = at - MARGIN
        mid, slope = growth_of(fields.at[odd1], at, n, d, g)
        pair1 = mid + 2.0 * slope - fields[image1, pl.ds(at, n)]
        put_rows(flat, rows, ahead[...] + last_pair[pl.ds(0, rows)] + pair1)
        mid, slope = growth_of(fields.at[odd0], at, n, d, g)
        image = fields[image0, pl.ds(at, n)]
        term = fields[g2, pl.ds(at, n)] + (mid + 2.0 * slope - image)
        next_forcing[pl.ds(here, n)] = term
        put_rows(flat, 2 * rows, term)
        put_rows(flat, 0, image + term)

    over_rows(rows, 3, first)
    over_rows(rows, 2, second)
    over_rows(rows, 1, third)
    over_rows(rows, 0, fourth)
    late_a[...] = fields[g1, pl.ds(MARGIN - 1, rows + 2)]
    late_b[...] = fields[g3, pl.ds(MARGIN - 1, rows + 2)]
    down[...] = next_forcing[pl.ds(rows - 2, 2)]
    up[...] = next_forcing[pl.ds(0, 2)]
    depth = forcing.shape[1]
    if folded(rows, share, reach_of()):
        pack_folded(slots, flat, rows, depth, reach_of())
    else:
        pack_windows(slots, flat, rows, depth, share)


def put_rows(flat, first, value):
    depth = value.shape[1]
    for i in range(value.shape[0]):
        flat[pl.ds((first + i) * depth, depth), :] = value[i]


def reach_of():
    return lax.axis_size("tm") + 2


def folded(rows, share, reach):
    return rows == 16 and 2 * share == LANES and FIELDS * 2 * reach <= share


def pack_folded(slots, flat, rows, depth, reach):
    devices = slots.shape[0]
    lane = lax.broadcasted_iota(jnp.int32, (8, LANES), 1)
    place = lane % (LANES // 2)
    rims = [None] * devices
    for field in range(FIELDS):
        first = field * rows * depth
        cells = []
        for line in range(depth):
            top = flat[pl.ds(first + line, 8, stride=depth), :]
            low = flat[pl.ds(first + 8 * depth + line, 8, stride=depth), :]
            cells.append(jnp.where(lane < LANES // 2, top, pltpu.roll(low, LANES // 2, 1)))
            cells.append(jnp.where(lane < LANES // 2, pltpu.roll(top, LANES // 2, 1), low))
        for target in range(devices):
            slots[target, pl.ds(field * 8, 8)] = cells[target]
            left = cells[target - 1] if target > 0 else 0.0
            right = cells[target + 1] if target < devices - 1 else 0.0
            rim = jnp.where(
                place >= LANES // 2 - reach, left, jnp.where(place < reach, right, 0.0)
            )
            if field == 0:
                rims[target] = rim
            else:
                rims[target] = rims[target] + pltpu.roll(rim, 2 * reach * field, 1)
    for target in range(devices):
        slots[target, pl.ds(FIELDS * 8, 8)] = rims[target]


def unfold(slot, field, reach):
    cells, rims = slot[pl.ds(field * 8, 8)], slot[pl.ds(FIELDS * 8, 8)]
    lane = lax.broadcasted_iota(jnp.int32, (8, LANES), 1)
    half = LANES // 2
    near = pltpu.roll(rims, (REACH - 2 * reach * field) % LANES, 1)
    far = pltpu.roll(rims, (-REACH - 2 * reach * field) % LANES, 1)
    parts = []
    for shift, rim in ((REACH, far), (-REACH, near)):
        own = pltpu.roll(cells, shift % LANES, 1)
        value = jnp.where((lane >= REACH - reach) & (lane < REACH + half + reach), rim, 0.0)
        parts.append(jnp.where((lane >= REACH) & (lane < REACH + half), own, value))
    return jnp.concatenate(parts, axis=0)


def pack_windows(slots, flat, rows, depth, share):
    lane = lax.broadcasted_iota(jnp.int32, (rows, LANES), 1)
    for field in range(FIELDS):
        first = field * rows * depth
        lines = [flat[pl.ds(first + line, rows, stride=depth), :] for line in range(depth)]
        for target in range(slots.shape[0]):
            line, offset = target * share // LANES, target * share % LANES
            shift = (REACH - offset) % LANES
            place = lane + (offset - REACH)
            value = pltpu.roll(lines[line], shift, 1)
            if offset < REACH:
                before = pltpu.roll(lines[line - 1], shift, 1) if line > 0 else 0.0
                value = jnp.where(place < 0, before, value)
            if offset > REACH:
                after = pltpu.roll(lines[line + 1], shift, 1) if line < depth - 1 else 0.0
                value = jnp.where(place >= LANES, after, value)
            slots[target, pl.ds(field * rows, rows)] = value


def packing(rows, share):
    groups = LANES // share
    each = -(-(rows + 2 * UP_RIM) // groups)
    return groups, each, -(-each // 8) * 8


def sweep_kernel(share, rows, arrived, *refs):
    slabs = lax.axis_size("space")
    windows, (slots, diff, grow, terms, padded) = refs[:slabs], refs[slabs:]
    devices = arrived.shape[0]
    blocks = devices // slabs
    total = slabs * rows
    reach = reach_of()
    groups, each, held = packing(rows, share)
    for by, part in enumerate(windows):
        slab = (lax.axis_index("space") - by) % slabs
        start = pl.multiple_of(slab * rows, rows)
        diff[pl.ds(start, rows), :] = part[0]
        grow[pl.ds(start, rows), :] = part[1]
    line = lax.broadcasted_iota(jnp.int32, (total, LANES), 0)
    lane = lax.broadcasted_iota(jnp.int32, (held, LANES), 1)
    padded[...] = jnp.zeros(padded.shape, jnp.float32)

    def block(field, index):
        parts = []
        for slab in range(slabs):
            slot = arrived.at[index * slabs + slab]
            if folded(rows, share, reach):
                parts.append(unfold(slot, field, reach))
            else:
                parts.append(slot[pl.ds(field * rows, rows)])
        return jnp.concatenate(parts, axis=0)

    def slope_of(field):
        north = jnp.where(line == 0, 0.0, pltpu.roll(field, 1, 0))
        south = jnp.where(line == total - 1, 0.0, pltpu.roll(field, total - 1, 0))
        sides = pltpu.roll(field, 1, 1) + pltpu.roll(field, LANES - 1, 1)
        laplace = north + south + sides - 4.0 * field
        return diff[...] * laplace + grow[...] * field / (1.0 + field * field)

    field = None
    for index in range(blocks):
        behind = (index - 1) % blocks
        odd, term = block(0, behind), block(1, behind)
        even = odd + 4.0 * slope_of(odd) + term
        slope = slope_of(even)
        odd = even + 4.0 * slope + block(2, index)
        stepped = even + 8.0 * slope
        pair = odd + 4.0 * slope_of(odd) - stepped
        terms[index] = block(1, index) + pair
        if index == blocks - 1:
            field = stepped + terms[index]
    for index in range(blocks):
        for group in range(groups):
            padded[group, pl.ds(8, total), :] = pltpu.roll(
                field, (group * share - REACH) % LANES, 1
            )
        for slab in range(slabs):
            start = 8 + slab * rows - UP_RIM
            value = padded[0, pl.ds(start, held), :]
            for group in range(1, groups):
                piece = padded[group, pl.ds(start + group * each, held), :]
                value = jnp.where(lane >= group * share, piece, value)
            slots[index * slabs + slab] = value
        if index < blocks - 1:
            field = field + 8.0 * slope_of(field) + terms[index]


def up_kernel(
    share, arrived, next_forcing, above, below, late_a, late_b, core, coefs,
    out, fields, diff, grow, flat,
):
    rows = next_forcing.shape[0]
    depth = next_forcing.shape[1]
    low, high = flags()
    set_rims(fields.at[5], rows, 2, above[...], below[...], low, high)
    fields[5, pl.ds(MARGIN, rows)] = next_forcing[...]
    groups, each, held = packing(rows, share)
    take_coefs(rows, coefs, diff, grow)
    lane = lax.broadcasted_iota(jnp.int32, (depth, LANES), 1)
    for row in range(rows + 2 * UP_RIM):
        group, line = row // each, row % each
        value = None
        for part in range(groups):
            piece = arrived[pl.ds(part * held + line, depth, stride=groups * held), :]
            piece = pltpu.roll(piece, ((part - group) * share) % LANES, 1) if part != group else piece
            value = piece if value is None else jnp.where(lane >= part * share, piece, value)
        fields[0, MARGIN - UP_RIM + row] = value
    odd_first = CORES.index("o0") * rows

    def first(at, n):
        mid, slope = growth_of(fields.at[0], at, n, diff[pl.ds(at, n)], grow[pl.ds(at, n)])
        fields[2, pl.ds(at, n)] = mid + 4.0 * slope + fields[5, pl.ds(at, n)]

    def second(at, n):
        d, g = diff[pl.ds(at, n)], grow[pl.ds(at, n)]
        for start, late in ((0, late_a), (2, late_b)):
            mid, slope = growth_of(fields.at[start], at, n, d, g)
            fields[start + 1, pl.ds(at, n)] = mid + 2.0 * slope + late[pl.ds(at - MARGIN + 1, n)]

    def third(at, n):
        d, g = diff[pl.ds(at, n)], grow[pl.ds(at, n)]
        here = at - MARGIN
        for i in range(POINTS // 2):
            mid, slope = growth_of(fields.at[i], at, n, d, g)
            put_rows(flat, 2 * i * rows, mid)
            put_rows(flat, (2 * i + 1) * rows, mid + slope + core[pl.ds(odd_first + i * rows + here, n)])

    over_rows(rows, 2, first)
    over_rows(rows, 1, second)
    over_rows(rows, 0, third)
    for point in range(POINTS):
        for r in range(0, rows, 8):
            for c in range(depth):
                start = (point * rows + r) * depth + c
                out[point, pl.ds(r, 8), pl.ds(c * LANES, LANES)] = flat[
                    pl.ds(start, 8, stride=depth), :
                ]


def moved(array, blocks, slabs):
    tm, space = lax.axis_size("tm"), lax.axis_size("space")
    pairs = [
        (t * space + s, (t + blocks) % tm * space + (s + slabs) % space)
        for t in range(tm)
        for s in range(space)
    ]
    return lax.ppermute(array, ("tm", "space"), pairs)


def exchange(down, up, turn, slant_down, slant_up):
    return (
        moved(down, 0, 1), moved(up, 0, -1), moved(turn, 1, 0),
        moved(slant_down, 1, 1), moved(slant_up, 1, -1),
    )


def body(initial, source, diffusivity, growth):
    points, rows, cols = initial.shape
    assert points == POINTS and rows % 8 == 0 and cols % LANES == 0
    depth = cols // LANES
    tm, space = lax.axis_size("tm"), lax.axis_size("space")
    devices = tm * space
    share = cols // devices
    assert share * devices == cols and LANES % share == 0
    assert reach_of() <= REACH and REACH + share + reach_of() <= LANES
    _, _, held = packing(rows, share)
    wide = rows + 2 * MARGIN

    def lines(n):
        return (n * depth, LANES)

    def field(n):
        return (n, depth, LANES)

    def as_rows(array):
        return array.reshape(-1, depth, LANES)

    sides, behind = count(RIMS_0), count(BEHIND_0)
    *sends, evens, terms, diff, grow = call(
        pack_kernel,
        [lines(sides), lines(sides), lines(2 * rows), lines(behind), lines(behind)]
        + [(points // 2, rows, cols), source.shape, diffusivity.shape, growth.shape],
        [],
        initial, source, diffusivity, growth,
        place=pltpu.HBM, sems=points // 2 + 3,
    )
    core, back, *windows = call(
        functools.partial(core_kernel, share),
        [lines(len(CORES) * rows), lines(rows)] + [(2, rows, LANES)] * space,
        [],
        evens, terms, diff, grow,
    )
    arrived = exchange(*(as_rows(part) for part in sends))
    ahead = as_rows(moved(back, -1, 0))
    windows = [windows[0]] + [moved(windows[by], 0, by) for by in range(1, space)]
    core = as_rows(core)

    buffers = [(wide, depth, LANES), (wide, depth, LANES)]
    rim1, rimb = count(RIMS_1), count(BEHIND)
    turn, down, up, slant_down, slant_up, state, forcing, first_forcing, coefs = call(
        level0_kernel,
        [
            field(2 * rows), field(rim1), field(rim1), field(rimb), field(rimb),
            field(rows + 4), field(3 * rows), field(rows + 4), field(2 * (rows + 6)),
        ],
        [(len(CORES) + 2 + 3 * (POINTS // 2), wide, depth, LANES)] + buffers,
        core, *arrived,
    )
    arrived = exchange(down, up, turn, slant_down, slant_up)
    arrived, ahead, windows = lax.optimization_barrier((arrived, ahead, windows))
    held_rows = FIELDS * 8 + 8 if folded(rows, share, reach_of()) else FIELDS * rows
    slots, down, up, next_forcing, late_a, late_b = call(
        functools.partial(level1_kernel, share),
        [
            (devices, held_rows, LANES), field(2), field(2),
            field(rows), field(rows + 2), field(rows + 2),
        ],
        [(14, wide, depth, LANES)] + buffers + [(FIELDS * rows * depth, LANES)],
        state, forcing, first_forcing, coefs, turn, ahead, *arrived,
    )
    above, below = moved(down, 0, 1), moved(up, 0, -1)
    slots = lax.all_to_all(slots, ("tm", "space"), 0, 0, tiled=True)
    (slots,) = call(
        functools.partial(sweep_kernel, share, rows),
        [(devices, held, LANES)],
        [(space * rows, LANES), (space * rows, LANES), (tm, space * rows, LANES)]
        + [(LANES // share, 8 + space * rows + 2 * rows + held, LANES)],
        slots, *windows,
    )
    slots = lax.all_to_all(slots, ("tm", "space"), 0, 0, tiled=True)
    (out,) = call(
        functools.partial(up_kernel, share),
        [(points, rows, cols)],
        [(6, wide, depth, LANES)] + buffers + [(points * rows * depth, LANES)],
        slots.reshape(devices * held, LANES), next_forcing, above, below,
        late_a, late_b, core, coefs,
    )
    return out


def solution(mesh):
    placed = (P("tm", "space", None), P("tm", "space", None), P("space", None), P("space", None))
    return jax.shard_map(
        body, mesh=mesh, in_specs=placed, out_specs=P("tm", "space", None), check_vma=False
    )
```

```python
import functools

import jax
import jax.numpy as jnp
from jax import lax
from jax.experimental import pallas as pl
from jax.experimental.pallas import tpu as pltpu
from jax.sharding import PartitionSpec as P

LANES = 128
MARGIN = 4
REACH = 32
UP_RIM = 3
FIELDS = 3
POINTS = 8
diffusion_number = 0.03
time_step = 0.02

RIMS_0 = (
    ("e0", 2), ("e1", 2), ("e2", 2),
    ("o0", 1), ("o1", 1), ("o2", 1), ("o3", 1),
    ("s0", 2), ("s1", 2), ("s2", 2), ("s3", 2),
    ("d", 3), ("g", 3),
)
BEHIND_0 = (("ep", 2), ("op", 1))
STEPS_0 = (("e0", "o0"), ("e1", "o1"), ("e2", "o2"))
STEPS_BEHIND_0 = (("ep", "op"),)
CORES = ("e0", "e1", "e2", "o0", "o1", "o2", "o3", "s0", "s1", "s2", "s3", "d", "g")
RIMS_1 = (("next", 3), ("g1", 1), ("g3", 1), ("g2", 2))
BEHIND = (("pair", 2), ("odd", 3))


def count(rims):
    return sum(rows for _, rows in rims)


def params(mib=16):
    return pltpu.CompilerParams(vmem_limit_bytes=mib * 2**20)


def call(kernel, outs, scratch, *args, mib=16, place=pltpu.VMEM, sems=0):
    return pl.pallas_call(
        kernel,
        out_shape=tuple(jax.ShapeDtypeStruct(shape, jnp.float32) for shape in outs),
        in_specs=[pl.BlockSpec(memory_space=place)] * len(args),
        out_specs=tuple(pl.BlockSpec(memory_space=pltpu.VMEM) for _ in outs),
        scratch_shapes=[pltpu.VMEM(shape, jnp.float32) for shape in scratch]
        + ([pltpu.SemaphoreType.DMA((sems,))] if sems else []),
        compiler_params=params(mib),
    )(*args)


def beside(mid):
    depth = mid.shape[1]
    lane = lax.broadcasted_iota(jnp.int32, mid.shape, 2)
    line = lax.broadcasted_iota(jnp.int32, mid.shape, 1)
    left = pltpu.roll(mid, 1, 2)
    left_turn = pltpu.roll(left, 1, 1)
    right = pltpu.roll(mid, LANES - 1, 2)
    right_turn = pltpu.roll(right, depth - 1, 1)
    left = jnp.where(lane == 0, jnp.where(line == 0, 0.0, left_turn), left)
    right = jnp.where(lane == LANES - 1, jnp.where(line == depth - 1, 0.0, right_turn), right)
    return left + right


def slope_of_rows(wide, diff, grow):
    mid = wide[1:-1]
    laplace = wide[:-2] + wide[2:] + beside(mid) - 4.0 * mid
    return mid, diff * laplace + grow * mid / (1.0 + mid * mid)


def growth_of(ref, at, rows, diff, grow):
    return slope_of_rows(ref[pl.ds(at - 1, rows + 2)], diff, grow)


def over_rows(rows, rim, body):
    body(MARGIN - rim, rows + 2 * rim)


def flags():
    slab = lax.axis_index("space")
    low = jnp.where(slab > 0, 1.0, 0.0).astype(jnp.float32)
    high = jnp.where(slab < lax.axis_size("space") - 1, 1.0, 0.0).astype(jnp.float32)
    return low, high


def set_rims(buffer, rows, rim, low_rows, high_rows, low, high, inner=0):
    width = rim - inner
    buffer[pl.ds(MARGIN - rim, width)] = low_rows * low
    buffer[pl.ds(MARGIN + rows + inner, width)] = high_rows * high


def pieces(name, evens, source, diffusivity, growth):
    if name == "d":
        return lambda rows, cols: diffusivity[rows, cols] * diffusion_number
    if name == "g":
        return lambda rows, cols: growth[rows, cols] * time_step
    if name == "ep":
        return lambda rows, cols: evens[POINTS // 2 - 1, rows, cols]
    if name == "op":
        return lambda rows, cols: source[POINTS - 1, rows, cols]
    which = int(name[1])
    if name[0] == "e":
        return lambda rows, cols: evens[which, rows, cols]
    return lambda rows, cols: source[2 * which + (name[0] == "o"), rows, cols]


def pack_kernel(
    initial_all, source_all, diffusivity_all, growth_all,
    down, up, turn, slant_down, slant_up, evens, source, diffusivity, growth, edge, sems,
):
    pairs = [(initial_all.at[2 * i], evens.at[i]) for i in range(POINTS // 2)]
    pairs += [(source_all, source), (diffusivity_all, diffusivity), (growth_all, growth)]
    copies = [pltpu.make_async_copy(*pair, sems.at[i]) for i, pair in enumerate(pairs)]
    for copy in copies:
        copy.start()
    for copy in copies:
        copy.wait()
    rows, cols = diffusivity.shape
    depth = cols // LANES

    def put(ref, at, name, first, count):
        get = pieces(name, evens, source, diffusivity, growth)
        for c in range(depth):
            place = pl.ds(at * depth + c, count, stride=depth)
            ref[place, :] = get(pl.ds(first, count), pl.ds(c * LANES, LANES))

    def rows_of(at, count):
        return edge[pl.ds(at * depth, count * depth), :].reshape(count, depth, LANES)

    for rims, steps, low, high in (
        (RIMS_0, STEPS_0, down, up),
        (BEHIND_0, STEPS_BEHIND_0, slant_down, slant_up),
    ):
        for ref, outer, inner in ((low, rows - 4, rows - 3), (high, 0, 1)):
            at = 0
            for name, rim in rims:
                put(ref, at, name, rows - rim if ref is low else 0, rim)
                at += rim
            put(edge, 0, "d", inner, 2)
            put(edge, 2, "g", inner, 2)
            for start, term in steps:
                put(edge, 4, start, outer, 4)
                put(edge, 8, term, inner, 2)
                wide = rows_of(4, 4)
                mid, slope = slope_of_rows(wide, rows_of(0, 2), rows_of(2, 2))
                put_rows(ref, at, mid + slope + rows_of(8, 2))
                at += 2
    for index, (name, _) in enumerate(BEHIND_0):
        for r in range(0, rows, 8):
            put(turn, index * rows + r, name, r, 8)


def window(get, first, depth):
    line, offset = first // LANES, first % LANES
    shape = get(0).shape
    source = lax.broadcasted_iota(jnp.int32, shape, 1) + (offset - REACH)
    shift = (REACH - offset) % LANES
    before = jnp.where(line > 0, pltpu.roll(get(jnp.maximum(line - 1, 0)), shift, 1), 0.0)
    here = pltpu.roll(get(line), shift, 1)
    after = jnp.where(
        line < depth - 1, pltpu.roll(get(jnp.minimum(line + 1, depth - 1)), shift, 1), 0.0
    )
    return jnp.where(source < 0, before, jnp.where(source >= LANES, after, here))


def core_kernel(share, evens, source, diffusivity, growth, core, back, *windows):
    rows, cols = diffusivity.shape
    depth = cols // LANES
    for index, name in enumerate(CORES):
        get = pieces(name, evens, source, diffusivity, growth)
        for c in range(depth):
            for r in range(0, rows, 8):
                value = get(pl.ds(r, 8), pl.ds(c * LANES, LANES))
                core[pl.ds((index * rows + r) * depth + c, 8, stride=depth), :] = value
                if name == "s0":
                    back[pl.ds(r * depth + c, 8, stride=depth), :] = value
    slabs = lax.axis_size("space")
    for by, out in enumerate(windows):
        target = lax.axis_index("tm") * slabs + (lax.axis_index("space") + by) % slabs
        for which, name in enumerate(("d", "g")):
            start = CORES.index(name) * rows * depth
            get = lambda line: core[pl.ds(start + line, rows, stride=depth), :]
            out[which] = window(get, target * share, depth)


def split(ref, rims):
    at, out = 0, {}
    for name, rim in rims:
        out[name] = ref[pl.ds(at, rim)]
        at += rim
    return out


def level0_kernel(
    core, above, below, behind, behind_above, behind_below,
    turn, down, up, slant_down, slant_up, next_odd, forcing, first_forcing, coefs,
    fields, diff, grow,
):
    rows = core.shape[0] // len(CORES)
    low, high = flags()
    names = list(CORES) + ["ep", "op"]
    spots = {name: index for index, name in enumerate(names)}
    extra = len(names)
    halves = POINTS // 2
    odd = [extra + i for i in range(halves)]
    even = [extra + halves + i for i in range(halves)]
    image = [extra + 2 * halves + i for i in range(halves)]
    for rims, steps, from_low, from_high in (
        (RIMS_0, STEPS_0, above, below),
        (BEHIND_0, STEPS_BEHIND_0, behind_above, behind_below),
    ):
        lows, highs = split(from_low, rims), split(from_high, rims)
        for name, rim in rims:
            if name in ("d", "g"):
                buffer = diff if name == "d" else grow
            else:
                buffer = fields.at[spots[name]]
            set_rims(buffer, rows, rim, lows[name], highs[name], low, high)
        at = count(rims)
        for start, _ in steps:
            buffer = fields.at[odd[0 if start == "ep" else int(start[1]) + 1]]
            set_rims(
                buffer, rows, 3, from_low[pl.ds(at, 2)], from_high[pl.ds(at, 2)], low, high, 1
            )
            at += 2
    for name in CORES:
        if name in ("d", "g"):
            buffer = diff if name == "d" else grow
        else:
            buffer = fields.at[spots[name]]
        buffer[pl.ds(MARGIN, rows)] = core[pl.ds(CORES.index(name) * rows, rows)]
    for index, (name, _) in enumerate(BEHIND_0):
        fields[spots[name], pl.ds(MARGIN, rows)] = behind[pl.ds(index * rows, rows)]

    def first(at, n):
        d, g = diff[pl.ds(at, n)], grow[pl.ds(at, n)]
        for i in range(halves):
            start, term = ("ep", "op") if i == 0 else (f"e{i - 1}", f"o{i - 1}")
            mid, slope = growth_of(fields.at[spots[start]], at, n, d, g)
            fields[odd[i], pl.ds(at, n)] = mid + slope + fields[spots[term], pl.ds(at, n)]

    def second(at, n):
        d, g = diff[pl.ds(at, n)], grow[pl.ds(at, n)]
        for i in range(halves):
            mid, slope = growth_of(fields.at[odd[i]], at, n, d, g)
            fields[even[i], pl.ds(at, n)] = mid + slope + fields[spots[f"s{i}"], pl.ds(at, n)]

    def third(at, n):
        d, g = diff[pl.ds(at, n)], grow[pl.ds(at, n)]
        for i in range(halves):
            mid, slope = growth_of(fields.at[even[i]], at, n, d, g)
            fields[odd[i], pl.ds(at, n)] = mid + slope + fields[spots[f"o{i}"], pl.ds(at, n)]
            fields[image[i], pl.ds(at, n)] = mid + 2.0 * slope

    def fourth(at, n):
        d, g = diff[pl.ds(at, n)], grow[pl.ds(at, n)]
        here = at - MARGIN
        for i in range(halves):
            mid, slope = growth_of(fields.at[odd[i]], at, n, d, g)
            pair = mid + slope - fields[image[i], pl.ds(at, n)]
            if i == halves - 1:
                turn[pl.ds(here, n)] = pair
            else:
                term = fields[spots[f"s{i + 1}"], pl.ds(at, n)] + pair
                forcing[pl.ds(i * rows + here, n)] = term
                if i == 0:
                    next_odd[...] = fields[image[0], pl.ds(at, n)] + term
                if i == halves - 2:
                    turn[pl.ds(rows + here, n)] = fields[image[i], pl.ds(at, n)] + term

    over_rows(rows, 1, first)
    over_rows(rows, 2, second)
    over_rows(rows, 1, third)
    over_rows(rows, 0, fourth)
    first_forcing[...] = fields[spots["s0"], pl.ds(MARGIN - 2, rows + 4)]
    coefs[pl.ds(0, rows + 6)] = diff[pl.ds(MARGIN - 3, rows + 6)]
    coefs[pl.ds(rows + 6, rows + 6)] = grow[pl.ds(MARGIN - 3, rows + 6)]
    send_behind(turn, slant_down, slant_up, rows)
    at = 0
    for (name, rim), (ref, first_row) in zip(
        RIMS_1, ((next_odd, 0), (forcing, 0), (forcing, 2 * rows), (forcing, rows)), strict=True
    ):
        down[pl.ds(at, rim)] = ref[pl.ds(first_row + rows - rim, rim)]
        up[pl.ds(at, rim)] = ref[pl.ds(first_row, rim)]
        at += rim


def send_behind(turn, slant_down, slant_up, rows):
    at = 0
    for index, (_, rim) in enumerate(BEHIND):
        slant_down[pl.ds(at, rim)] = turn[pl.ds((index + 1) * rows - rim, rim)]
        slant_up[pl.ds(at, rim)] = turn[pl.ds(index * rows, rim)]
        at += rim


def take_behind(rows, buffers, behind, behind_above, behind_below, low, high):
    lows, highs = split(behind_above, BEHIND), split(behind_below, BEHIND)
    for index, (name, rim) in enumerate(BEHIND):
        buffer = buffers[index]
        set_rims(buffer, rows, rim, lows[name], highs[name], low, high)
        buffer[pl.ds(MARGIN, rows)] = behind[pl.ds(index * rows, rows)]


def take_coefs(rows, coefs, diff, grow):
    diff[pl.ds(MARGIN - 3, rows + 6)] = coefs[pl.ds(0, rows + 6)]
    grow[pl.ds(MARGIN - 3, rows + 6)] = coefs[pl.ds(rows + 6, rows + 6)]


def level1_kernel(
    share, next_odd, forcing, first_forcing, coefs, last_pair, ahead,
    above, below, behind, behind_above, behind_below,
    slots, next_forcing, late_a, late_b,
    fields, diff, grow, flat,
):
    rows = forcing.shape[0] // 3
    low, high = flags()
    take_coefs(rows, coefs, diff, grow)
    g1, g3, g2, g0, pair, before, after, even0, even1, image0, image1, odd0, odd1 = range(13)
    lows, highs = split(above, RIMS_1), split(below, RIMS_1)
    for (name, rim), spot in zip(RIMS_1, (after, g1, g3, g2), strict=True):
        set_rims(fields.at[spot], rows, rim, lows[name], highs[name], low, high)
    fields[after, pl.ds(MARGIN, rows)] = next_odd[...]
    for which, spot in enumerate((g1, g2, g3)):
        fields[spot, pl.ds(MARGIN, rows)] = forcing[pl.ds(which * rows, rows)]
    take_behind(
        rows, (fields.at[pair], fields.at[before]), behind, behind_above, behind_below, low, high
    )
    fields[g0, pl.ds(MARGIN - 2, rows + 4)] = (
        first_forcing[...] + fields[pair, pl.ds(MARGIN - 2, rows + 4)]
    )

    def second(at, n):
        d, g = diff[pl.ds(at, n)], grow[pl.ds(at, n)]
        for start, term, end in ((before, g0, even0), (after, g2, even1)):
            mid, slope = growth_of(fields.at[start], at, n, d, g)
            fields[end, pl.ds(at, n)] = mid + 2.0 * slope + fields[term, pl.ds(at, n)]

    def third(at, n):
        d, g = diff[pl.ds(at, n)], grow[pl.ds(at, n)]
        for start, term, end, image in ((even0, g1, odd0, image0), (even1, g3, odd1, image1)):
            mid, slope = growth_of(fields.at[start], at, n, d, g)
            fields[end, pl.ds(at, n)] = mid + 2.0 * slope + fields[term, pl.ds(at, n)]
            fields[image, pl.ds(at, n)] = mid + 4.0 * slope

    def fourth(at, n):
        d, g = diff[pl.ds(at, n)], grow[pl.ds(at, n)]
        here = at - MARGIN
        mid, slope = growth_of(fields.at[odd1], at, n, d, g)
        pair1 = mid + 2.0 * slope - fields[image1, pl.ds(at, n)]
        put_rows(flat, rows, ahead[...] + last_pair[pl.ds(0, rows)] + pair1)
        mid, slope = growth_of(fields.at[odd0], at, n, d, g)
        image = fields[image0, pl.ds(at, n)]
        term = fields[g2, pl.ds(at, n)] + (mid + 2.0 * slope - image)
        next_forcing[pl.ds(here, n)] = term
        put_rows(flat, 2 * rows, term)
        put_rows(flat, 0, image + term)

    over_rows(rows, 2, second)
    over_rows(rows, 1, third)
    over_rows(rows, 0, fourth)
    late_a[...] = fields[g1, pl.ds(MARGIN - 1, rows + 2)]
    late_b[...] = fields[g3, pl.ds(MARGIN - 1, rows + 2)]
    depth = forcing.shape[1]
    if folded(rows, share, reach_of()):
        pack_folded(slots, flat, rows, depth, reach_of())
    else:
        pack_windows(slots, flat, rows, depth, share)


def put_rows(flat, first, value):
    depth = value.shape[1]
    for i in range(value.shape[0]):
        flat[pl.ds((first + i) * depth, depth), :] = value[i]


def reach_of():
    return lax.axis_size("tm") + 2


def folded(rows, share, reach):
    return rows == 16 and 2 * share == LANES and FIELDS * 2 * reach <= share


def pack_folded(slots, flat, rows, depth, reach):
    devices = slots.shape[0]
    lane = lax.broadcasted_iota(jnp.int32, (8, LANES), 1)
    place = lane % (LANES // 2)
    rims = [None] * devices
    for field in range(FIELDS):
        first = field * rows * depth
        cells = []
        for line in range(depth):
            top = flat[pl.ds(first + line, 8, stride=depth), :]
            low = flat[pl.ds(first + 8 * depth + line, 8, stride=depth), :]
            cells.append(jnp.where(lane < LANES // 2, top, pltpu.roll(low, LANES // 2, 1)))
            cells.append(jnp.where(lane < LANES // 2, pltpu.roll(top, LANES // 2, 1), low))
        for target in range(devices):
            slots[target, pl.ds(field * 8, 8)] = cells[target]
            left = cells[target - 1] if target > 0 else 0.0
            right = cells[target + 1] if target < devices - 1 else 0.0
            rim = jnp.where(
                place >= LANES // 2 - reach, left, jnp.where(place < reach, right, 0.0)
            )
            if field == 0:
                rims[target] = rim
            else:
                rims[target] = rims[target] + pltpu.roll(rim, 2 * reach * field, 1)
    for target in range(devices):
        slots[target, pl.ds(FIELDS * 8, 8)] = rims[target]


def unfold(slot, field, reach):
    cells, rims = slot[pl.ds(field * 8, 8)], slot[pl.ds(FIELDS * 8, 8)]
    lane = lax.broadcasted_iota(jnp.int32, (8, LANES), 1)
    half = LANES // 2
    near = pltpu.roll(rims, (REACH - 2 * reach * field) % LANES, 1)
    far = pltpu.roll(rims, (-REACH - 2 * reach * field) % LANES, 1)
    parts = []
    for shift, rim in ((REACH, far), (-REACH, near)):
        own = pltpu.roll(cells, shift % LANES, 1)
        value = jnp.where((lane >= REACH - reach) & (lane < REACH + half + reach), rim, 0.0)
        parts.append(jnp.where((lane >= REACH) & (lane < REACH + half), own, value))
    return jnp.concatenate(parts, axis=0)


def pack_windows(slots, flat, rows, depth, share):
    lane = lax.broadcasted_iota(jnp.int32, (rows, LANES), 1)
    for field in range(FIELDS):
        first = field * rows * depth
        lines = [flat[pl.ds(first + line, rows, stride=depth), :] for line in range(depth)]
        for target in range(slots.shape[0]):
            line, offset = target * share // LANES, target * share % LANES
            shift = (REACH - offset) % LANES
            place = lane + (offset - REACH)
            value = pltpu.roll(lines[line], shift, 1)
            if offset < REACH:
                before = pltpu.roll(lines[line - 1], shift, 1) if line > 0 else 0.0
                value = jnp.where(place < 0, before, value)
            if offset > REACH:
                after = pltpu.roll(lines[line + 1], shift, 1) if line < depth - 1 else 0.0
                value = jnp.where(place >= LANES, after, value)
            slots[target, pl.ds(field * rows, rows)] = value


def late_rows(rows):
    return (-2, -1, rows, rows + 1)


def packing(rows, share):
    groups = LANES // share
    each = -(-(rows + 2 * UP_RIM) // groups)
    return groups, each, -(-(each + -(-4 // groups)) // 8) * 8


def sweep_kernel(share, rows, arrived, *refs):
    slabs = lax.axis_size("space")
    windows, (slots, diff, grow, terms, padded, kept) = refs[:slabs], refs[slabs:]
    devices = arrived.shape[0]
    blocks = devices // slabs
    total = slabs * rows
    reach = reach_of()
    groups, each, held = packing(rows, share)
    for by, part in enumerate(windows):
        slab = (lax.axis_index("space") - by) % slabs
        start = pl.multiple_of(slab * rows, rows)
        diff[pl.ds(start, rows), :] = part[0]
        grow[pl.ds(start, rows), :] = part[1]
    line = lax.broadcasted_iota(jnp.int32, (total, LANES), 0)
    lane = lax.broadcasted_iota(jnp.int32, (held, LANES), 1)
    padded[...] = jnp.zeros(padded.shape, jnp.float32)
    kept[...] = jnp.zeros(kept.shape, jnp.float32)

    def block(field, index):
        parts = []
        for slab in range(slabs):
            slot = arrived.at[index * slabs + slab]
            if folded(rows, share, reach):
                parts.append(unfold(slot, field, reach))
            else:
                parts.append(slot[pl.ds(field * rows, rows)])
        return jnp.concatenate(parts, axis=0)

    def slope_of(field):
        north = jnp.where(line == 0, 0.0, pltpu.roll(field, 1, 0))
        south = jnp.where(line == total - 1, 0.0, pltpu.roll(field, total - 1, 0))
        sides = pltpu.roll(field, 1, 1) + pltpu.roll(field, LANES - 1, 1)
        laplace = north + south + sides - 4.0 * field
        return diff[...] * laplace + grow[...] * field / (1.0 + field * field)

    field = None
    for index in range(blocks):
        behind = (index - 1) % blocks
        odd, term = block(0, behind), block(1, behind)
        even = odd + 4.0 * slope_of(odd) + term
        slope = slope_of(even)
        own_term = block(2, index)
        kept[index, pl.ds(8, total), :] = own_term
        odd = even + 4.0 * slope + own_term
        stepped = even + 8.0 * slope
        pair = odd + 4.0 * slope_of(odd) - stepped
        terms[index] = block(1, index) + pair
        if index == blocks - 1:
            field = stepped + terms[index]
    for index in range(blocks):
        for group in range(groups):
            padded[group, pl.ds(8, total), :] = pltpu.roll(
                field, (group * share - REACH) % LANES, 1
            )
        for slab in range(slabs):
            start = 8 + slab * rows - UP_RIM
            value = padded[0, pl.ds(start, held), :]
            for group in range(1, groups):
                piece = padded[group, pl.ds(start + group * each, held), :]
                value = jnp.where(lane >= group * share, piece, value)
            slots[index * slabs + slab] = value
            start = 8 + slab * rows
            for i, row in enumerate(late_rows(rows)):
                line_at, group = each + i // groups, i % groups
                piece = kept[index, pl.ds(start + row, 1), :]
                piece = pltpu.roll(piece, (group * share - REACH) % LANES, 1)
                if group > 0:
                    before = slots[index * slabs + slab, pl.ds(line_at, 1)]
                    piece = jnp.where(lane[:1] >= group * share, piece, before)
                slots[index * slabs + slab, pl.ds(line_at, 1)] = piece
        if index < blocks - 1:
            field = field + 8.0 * slope_of(field) + terms[index]


def up_kernel(
    share, arrived, next_forcing, late_a, late_b, core, coefs, out, fields, diff, grow, flat
):
    rows, depth, _ = next_forcing.shape
    groups, each, held = packing(rows, share)
    take_coefs(rows, coefs, diff, grow)
    lane = lax.broadcasted_iota(jnp.int32, (depth, LANES), 1)

    def whole(line, group):
        value = None
        for part in range(groups):
            piece = arrived[pl.ds(part * held + line, depth, stride=groups * held), :]
            if part != group:
                piece = pltpu.roll(piece, ((part - group) * share) % LANES, 1)
            value = piece if value is None else jnp.where(lane >= part * share, piece, value)
        return value

    for row in range(rows + 2 * UP_RIM):
        fields[0, MARGIN - UP_RIM + row] = whole(row % each, row // each)
    for i, row in enumerate(late_rows(rows)):
        fields[5, MARGIN + row] = whole(each + i // groups, i % groups)
    fields[5, pl.ds(MARGIN, rows)] = next_forcing[...]
    odd_first = CORES.index("o0") * rows

    def first(at, n):
        mid, slope = growth_of(fields.at[0], at, n, diff[pl.ds(at, n)], grow[pl.ds(at, n)])
        fields[2, pl.ds(at, n)] = mid + 4.0 * slope + fields[5, pl.ds(at, n)]

    def second(at, n):
        d, g = diff[pl.ds(at, n)], grow[pl.ds(at, n)]
        for start, late in ((0, late_a), (2, late_b)):
            mid, slope = growth_of(fields.at[start], at, n, d, g)
            fields[start + 1, pl.ds(at, n)] = mid + 2.0 * slope + late[pl.ds(at - MARGIN + 1, n)]

    def third(at, n):
        d, g = diff[pl.ds(at, n)], grow[pl.ds(at, n)]
        here = at - MARGIN
        for i in range(POINTS // 2):
            mid, slope = growth_of(fields.at[i], at, n, d, g)
            put_rows(flat, 2 * i * rows, mid)
            put_rows(flat, (2 * i + 1) * rows, mid + slope + core[pl.ds(odd_first + i * rows + here, n)])

    over_rows(rows, 2, first)
    over_rows(rows, 1, second)
    over_rows(rows, 0, third)
    for point in range(POINTS):
        for r in range(0, rows, 8):
            for c in range(depth):
                start = (point * rows + r) * depth + c
                out[point, pl.ds(r, 8), pl.ds(c * LANES, LANES)] = flat[
                    pl.ds(start, 8, stride=depth), :
                ]


def moved(array, blocks, slabs):
    tm, space = lax.axis_size("tm"), lax.axis_size("space")
    pairs = [
        (t * space + s, (t + blocks) % tm * space + (s + slabs) % space)
        for t in range(tm)
        for s in range(space)
    ]
    return lax.ppermute(array, ("tm", "space"), pairs)


def exchange(down, up, turn, slant_down, slant_up):
    return (
        moved(down, 0, 1), moved(up, 0, -1), moved(turn, 1, 0),
        moved(slant_down, 1, 1), moved(slant_up, 1, -1),
    )


def body(initial, source, diffusivity, growth):
    points, rows, cols = initial.shape
    assert points == POINTS and rows % 8 == 0 and cols % LANES == 0
    depth = cols // LANES
    tm, space = lax.axis_size("tm"), lax.axis_size("space")
    devices = tm * space
    share = cols // devices
    assert share * devices == cols and LANES % share == 0
    assert reach_of() <= REACH and REACH + share + reach_of() <= LANES
    _, _, held = packing(rows, share)
    wide = rows + 2 * MARGIN

    def lines(n):
        return (n * depth, LANES)

    def field(n):
        return (n, depth, LANES)

    def as_rows(array):
        return array.reshape(-1, depth, LANES)

    sides = count(RIMS_0) + 2 * len(STEPS_0)
    behind = count(BEHIND_0) + 2 * len(STEPS_BEHIND_0)
    *sends, evens, terms, diff, grow = call(
        pack_kernel,
        [lines(sides), lines(sides), lines(2 * rows), lines(behind), lines(behind)]
        + [(points // 2, rows, cols), source.shape, diffusivity.shape, growth.shape],
        [lines(10)],
        initial, source, diffusivity, growth,
        place=pltpu.HBM, sems=points // 2 + 3, mib=56,
    )
    core, back, *windows = call(
        functools.partial(core_kernel, share),
        [lines(len(CORES) * rows), lines(rows)] + [(2, rows, LANES)] * space,
        [],
        evens, terms, diff, grow,
    )
    arrived = exchange(*(as_rows(part) for part in sends))
    ahead = as_rows(moved(back, -1, 0))
    windows = [windows[0]] + [moved(windows[by], 0, by) for by in range(1, space)]
    core = as_rows(core)

    buffers = [(wide, depth, LANES), (wide, depth, LANES)]
    rim1, rimb = count(RIMS_1), count(BEHIND)
    arrived, ahead, windows = lax.optimization_barrier((arrived, ahead, windows))
    turn, down, up, slant_down, slant_up, next_odd, forcing, first_forcing, coefs = call(
        level0_kernel,
        [
            field(2 * rows), field(rim1), field(rim1), field(rimb), field(rimb),
            field(rows), field(3 * rows), field(rows + 4), field(2 * (rows + 6)),
        ],
        [(len(CORES) + 2 + 3 * (POINTS // 2), wide, depth, LANES)] + buffers,
        core, *arrived,
    )
    arrived = exchange(down, up, turn, slant_down, slant_up)
    held_rows = FIELDS * 8 + 8 if folded(rows, share, reach_of()) else FIELDS * rows
    slots, next_forcing, late_a, late_b = call(
        functools.partial(level1_kernel, share),
        [
            (devices, held_rows, LANES),
            field(rows), field(rows + 2), field(rows + 2),
        ],
        [(13, wide, depth, LANES)] + buffers + [(FIELDS * rows * depth, LANES)],
        next_odd, forcing, first_forcing, coefs, turn, ahead, *arrived,
    )
    slots = lax.all_to_all(slots, ("tm", "space"), 0, 0, tiled=True)
    (slots,) = call(
        functools.partial(sweep_kernel, share, rows),
        [(devices, held, LANES)],
        [(space * rows, LANES), (space * rows, LANES), (tm, space * rows, LANES)]
        + [(LANES // share, 8 + space * rows + 2 * rows + held, LANES)]
        + [(tm, 16 + space * rows, LANES)],
        slots, *windows,
    )
    slots = lax.all_to_all(slots, ("tm", "space"), 0, 0, tiled=True)
    (out,) = call(
        functools.partial(up_kernel, share),
        [(points, rows, cols)],
        [(6, wide, depth, LANES)] + buffers + [(points * rows * depth, LANES)],
        slots.reshape(devices * held, LANES), next_forcing, late_a, late_b, core, coefs,
    )
    return out


def solution(mesh):
    placed = (P("tm", "space", None), P("tm", "space", None), P("space", None), P("space", None))
    return jax.shard_map(
        body, mesh=mesh, in_specs=placed, out_specs=P("tm", "space", None), check_vma=False
    )
```

```python
import functools

import jax
import jax.numpy as jnp
from jax import lax
from jax.experimental import pallas as pl
from jax.experimental.pallas import tpu as pltpu
from jax.sharding import PartitionSpec as P

LANES = 128
MARGIN = 4
REACH = 32
UP_RIM = 3
FIELDS = 3
PACK_MIB = 62
CORE_COST = 30_000_000
POINTS = 8
diffusion_number = 0.03
time_step = 0.02

RIMS_0 = (
    ("e0", 2), ("e1", 2), ("e2", 2),
    ("o0", 1), ("o1", 1), ("o2", 1), ("o3", 1),
    ("s0", 2), ("s1", 2), ("s2", 2), ("s3", 2),
    ("d", 3), ("g", 3),
)
BEHIND_0 = (("ep", 2), ("op", 1))
STEPS_0 = (("e0", "o0"), ("e1", "o1"), ("e2", "o2"))
STEPS_BEHIND_0 = (("ep", "op"),)
CORES = ("e0", "e1", "e2", "o0", "o1", "o2", "o3", "s0", "s1", "s2", "s3", "d", "g")
RIMS_1 = (("next", 3), ("g1", 1), ("g3", 1), ("g2", 2))
BEHIND = (("pair", 2), ("odd", 3))


def count(rims):
    return sum(rows for _, rows in rims)


def params(mib):
    return pltpu.CompilerParams(vmem_limit_bytes=int(mib * 2**20))


def call(kernel, outs, scratch, *args, mib=16, place=pltpu.VMEM, sems=0, cost=None):
    return pl.pallas_call(
        kernel,
        out_shape=tuple(jax.ShapeDtypeStruct(shape, jnp.float32) for shape in outs),
        in_specs=[pl.BlockSpec(memory_space=place)] * len(args),
        out_specs=tuple(pl.BlockSpec(memory_space=pltpu.VMEM) for _ in outs),
        scratch_shapes=[pltpu.VMEM(shape, jnp.float32) for shape in scratch]
        + ([pltpu.SemaphoreType.DMA((sems,))] if sems else []),
        compiler_params=params(mib),
        cost_estimate=cost,
    )(*args)


def beside(mid):
    depth = mid.shape[1]
    lane = lax.broadcasted_iota(jnp.int32, mid.shape, 2)
    line = lax.broadcasted_iota(jnp.int32, mid.shape, 1)
    left = pltpu.roll(mid, 1, 2)
    left_turn = pltpu.roll(left, 1, 1)
    right = pltpu.roll(mid, LANES - 1, 2)
    right_turn = pltpu.roll(right, depth - 1, 1)
    left = jnp.where(lane == 0, jnp.where(line == 0, 0.0, left_turn), left)
    right = jnp.where(lane == LANES - 1, jnp.where(line == depth - 1, 0.0, right_turn), right)
    return left + right


def slope_of_rows(wide, diff, grow):
    mid = wide[1:-1]
    laplace = wide[:-2] + wide[2:] + beside(mid) - 4.0 * mid
    return mid, diff * laplace + grow * mid / (1.0 + mid * mid)


def growth_of(ref, at, rows, diff, grow):
    return slope_of_rows(ref[pl.ds(at - 1, rows + 2)], diff, grow)


def over_rows(rows, rim, body):
    body(MARGIN - rim, rows + 2 * rim)


def flags():
    slab = lax.axis_index("space")
    low = jnp.where(slab > 0, 1.0, 0.0).astype(jnp.float32)
    high = jnp.where(slab < lax.axis_size("space") - 1, 1.0, 0.0).astype(jnp.float32)
    return low, high


def set_rims(buffer, rows, rim, low_rows, high_rows, low, high, inner=0):
    width = rim - inner
    buffer[pl.ds(MARGIN - rim, width)] = low_rows * low
    buffer[pl.ds(MARGIN + rows + inner, width)] = high_rows * high


def pieces(name, evens, source, diffusivity, growth):
    if name == "d":
        return lambda rows, cols: diffusivity[rows, cols] * diffusion_number
    if name == "g":
        return lambda rows, cols: growth[rows, cols] * time_step
    if name == "ep":
        return lambda rows, cols: evens[POINTS // 2 - 1, rows, cols]
    if name == "op":
        return lambda rows, cols: source[POINTS - 1, rows, cols]
    which = int(name[1])
    if name[0] == "e":
        return lambda rows, cols: evens[which, rows, cols]
    return lambda rows, cols: source[2 * which + (name[0] == "o"), rows, cols]


def fetch(initial_all, source_all, diffusivity_all, growth_all, evens, source, coefs, sems):
    pairs = [(initial_all.at[2 * i], evens.at[i]) for i in range(POINTS // 2)]
    pairs += [(diffusivity_all, coefs.at[0]), (growth_all, coefs.at[1]), (source_all, source)]
    copies = [pltpu.make_async_copy(*pair, sems.at[i]) for i, pair in enumerate(pairs)]
    for copy in copies:
        copy.start()
    return copies[:-1], copies[-1]


def target_of(by):
    slabs = lax.axis_size("space")
    return lax.axis_index("tm") * slabs + (lax.axis_index("space") + by) % slabs


EDGE = 8


def pack_kernel(
    share, initial_all, source_all, diffusivity_all, growth_all,
    down, up, turn, slant_down, slant_up, back, evens, source, coefs, edge, cells, sems,
):
    waits, last = fetch(
        initial_all, source_all, diffusivity_all, growth_all, evens, source, coefs, sems
    )
    _, rows, cols = coefs.shape
    depth = cols // LANES
    diffusivity, growth = coefs.at[0], coefs.at[1]

    def put(ref, at, name, first, count):
        get = pieces(name, evens, source, diffusivity, growth)
        for c in range(depth):
            place = pl.ds(at * depth + c, count, stride=depth)
            ref[place, :] = get(pl.ds(first, count), pl.ds(c * LANES, LANES))

    def rows_of(at, count):
        return edge[pl.ds(at * depth, count * depth), :].reshape(count, depth, LANES)

    def put_sides(early):
        for rims, low, high in ((RIMS_0, down, up), (BEHIND_0, slant_down, slant_up)):
            at = 0
            for name, rim in rims:
                if early == (name[0] not in "os"):
                    put(low, at, name, rows - rim, rim)
                    put(high, at, name, 0, rim)
                at += rim

    for wait in waits:
        wait.wait()
    put_sides(True)
    for index, name in enumerate(("d", "g")):
        for r in range(0, rows, 8):
            put(cells, index * rows + r, name, r, 8)
    end = (count(RIMS_0) + 2 * len(STEPS_0)) * depth
    for ref, by, at in ((down, 1, end), (up, -1, end), (down, 2, end + 2 * rows)):
        if at < ref.shape[0]:
            for index in range(2):
                get = lambda line: cells[pl.ds(index * rows * depth + line, rows, stride=depth), :]
                ref[pl.ds(at + index * rows, rows), :] = window(
                    get, target_of(by) * share, depth
                )
    steps = [
        (start, term, sides, at + 2 * i)
        for group, sides, at in (
            (STEPS_0, (down, up), count(RIMS_0)),
            (STEPS_BEHIND_0, (slant_down, slant_up), count(BEHIND_0)),
        )
        for i, (start, term) in enumerate(group)
    ]
    for i, (start, _, _, _) in enumerate(steps):
        put(edge, 2 * EDGE * i, start, rows - 4, 4)
        put(edge, 2 * EDGE * i + EDGE, start, 0, 4)
    put(turn, 0, "ep", 0, 8)
    put(turn, 8, "ep", 8, 8)
    last.wait()
    put_sides(False)
    for i, (_, term, _, _) in enumerate(steps):
        put(edge, 2 * EDGE * i + 4, term, rows - 3, 2)
        put(edge, 2 * EDGE * i + EDGE + 4, term, 1, 2)
    for r in range(0, rows, 8):
        put(turn, rows + r, "op", r, 8)
        put(back, r, "s0", r, 8)
    for side, first in enumerate((rows - 3, 1)):
        diff, grow = (
            cells[pl.ds((index * rows + first) * depth, 2 * depth), :].reshape(2, depth, LANES)
            for index in range(2)
        )
        for i, (_, _, sides, at) in enumerate(steps):
            spot = (2 * i + side) * EDGE
            mid, slope = slope_of_rows(rows_of(spot, 4), diff, grow)
            put_rows(sides[side], at, mid + slope + rows_of(spot + 4, 2))


def window(get, first, depth):
    line, offset = first // LANES, first % LANES
    shape = get(0).shape
    source = lax.broadcasted_iota(jnp.int32, shape, 1) + (offset - REACH)
    shift = (REACH - offset) % LANES
    before = jnp.where(line > 0, pltpu.roll(get(jnp.maximum(line - 1, 0)), shift, 1), 0.0)
    here = pltpu.roll(get(line), shift, 1)
    after = jnp.where(
        line < depth - 1, pltpu.roll(get(jnp.minimum(line + 1, depth - 1)), shift, 1), 0.0
    )
    return jnp.where(source < 0, before, jnp.where(source >= LANES, after, here))


def core_kernel(
    share, initial_all, source_all, diffusivity_all, growth_all, core, *refs
):
    *windows, evens, source, coefs, sems = refs
    waits, last = fetch(
        initial_all, source_all, diffusivity_all, growth_all, evens, source, coefs, sems
    )
    for wait in (*waits, last):
        wait.wait()
    _, rows, cols = coefs.shape
    depth = cols // LANES
    for index, name in enumerate(CORES):
        get = pieces(name, evens, source, coefs.at[0], coefs.at[1])
        for c in range(depth):
            for r in range(0, rows, 8):
                value = get(pl.ds(r, 8), pl.ds(c * LANES, LANES))
                core[pl.ds((index * rows + r) * depth + c, 8, stride=depth), :] = value
    for by, out in zip(direct_windows(lax.axis_size("space")), windows, strict=True):
        for which, name in enumerate(("d", "g")):
            start = CORES.index(name) * rows * depth
            get = lambda line: core[pl.ds(start + line, rows, stride=depth), :]
            out[pl.ds(which * rows, rows)] = window(get, target_of(by) * share, depth)


def handed_on(slabs):
    return slabs == 4


def direct_windows(slabs):
    return [0] if handed_on(slabs) else [0] + list(range(2, slabs - 1))


def split(ref, rims):
    at, out = 0, {}
    for name, rim in rims:
        out[name] = ref[pl.ds(at, rim)]
        at += rim
    return out


def level0_kernel(
    apart, core, above, below, behind, behind_above, behind_below, *refs
):
    windows, refs = refs[: len(apart)], refs[len(apart) :]
    (
        turn, down, up, slant_down, slant_up, next_odd, forcing, first_forcing, coefs, held,
        fields, diff, grow,
    ) = refs
    rows = core.shape[0] // len(CORES)
    low, high = flags()
    depth = core.shape[1]
    names = list(CORES) + ["ep", "op"]
    spots = {name: index for index, name in enumerate(names)}
    extra = len(names)
    halves = POINTS // 2
    odd = [extra + i for i in range(halves)]
    even = [extra + halves + i for i in range(halves)]
    image = [extra + 2 * halves + i for i in range(halves)]
    for rims, steps, from_low, from_high in (
        (RIMS_0, STEPS_0, above, below),
        (BEHIND_0, STEPS_BEHIND_0, behind_above, behind_below),
    ):
        lows, highs = split(from_low, rims), split(from_high, rims)
        for name, rim in rims:
            if name in ("d", "g"):
                buffer = diff if name == "d" else grow
            else:
                buffer = fields.at[spots[name]]
            set_rims(buffer, rows, rim, lows[name], highs[name], low, high)
        at = count(rims)
        for start, _ in steps:
            buffer = fields.at[odd[0 if start == "ep" else int(start[1]) + 1]]
            set_rims(
                buffer, rows, 3, from_low[pl.ds(at, 2)], from_high[pl.ds(at, 2)], low, high, 1
            )
            at += 2
    for name in CORES:
        if name in ("d", "g"):
            buffer = diff if name == "d" else grow
        else:
            buffer = fields.at[spots[name]]
        buffer[pl.ds(MARGIN, rows)] = core[pl.ds(CORES.index(name) * rows, rows)]
    for index, (name, _) in enumerate(BEHIND_0):
        fields[spots[name], pl.ds(MARGIN, rows)] = behind[pl.ds(index * rows, rows)]

    def first(at, n):
        d, g = diff[pl.ds(at, n)], grow[pl.ds(at, n)]
        for i in range(halves):
            start, term = ("ep", "op") if i == 0 else (f"e{i - 1}", f"o{i - 1}")
            mid, slope = growth_of(fields.at[spots[start]], at, n, d, g)
            fields[odd[i], pl.ds(at, n)] = mid + slope + fields[spots[term], pl.ds(at, n)]

    def second(at, n):
        d, g = diff[pl.ds(at, n)], grow[pl.ds(at, n)]
        for i in range(halves):
            mid, slope = growth_of(fields.at[odd[i]], at, n, d, g)
            fields[even[i], pl.ds(at, n)] = mid + slope + fields[spots[f"s{i}"], pl.ds(at, n)]

    def third(at, n):
        d, g = diff[pl.ds(at, n)], grow[pl.ds(at, n)]
        for i in range(halves):
            mid, slope = growth_of(fields.at[even[i]], at, n, d, g)
            fields[odd[i], pl.ds(at, n)] = mid + slope + fields[spots[f"o{i}"], pl.ds(at, n)]
            fields[image[i], pl.ds(at, n)] = mid + 2.0 * slope

    def fourth(at, n):
        d, g = diff[pl.ds(at, n)], grow[pl.ds(at, n)]
        here = at - MARGIN
        for i in range(halves):
            mid, slope = growth_of(fields.at[odd[i]], at, n, d, g)
            pair = mid + slope - fields[image[i], pl.ds(at, n)]
            if i == halves - 1:
                turn[pl.ds(here, n)] = pair
            else:
                term = fields[spots[f"s{i + 1}"], pl.ds(at, n)] + pair
                forcing[pl.ds(i * rows + here, n)] = term
                if i == 0:
                    next_odd[...] = fields[image[0], pl.ds(at, n)] + term
                if i == halves - 2:
                    turn[pl.ds(rows + here, n)] = fields[image[i], pl.ds(at, n)] + term

    over_rows(rows, 1, first)
    over_rows(rows, 2, second)
    over_rows(rows, 1, third)
    over_rows(rows, 0, fourth)
    first_forcing[...] = fields[spots["s0"], pl.ds(MARGIN - 2, rows + 4)]
    coefs[pl.ds(0, rows + 6)] = diff[pl.ds(MARGIN - 3, rows + 6)]
    coefs[pl.ds(rows + 6, rows + 6)] = grow[pl.ds(MARGIN - 3, rows + 6)]
    send_behind(turn, slant_down, slant_up, rows)
    at = 0
    for (name, rim), (ref, first_row) in zip(
        RIMS_1, ((next_odd, 0), (forcing, 0), (forcing, 2 * rows), (forcing, rows)), strict=True
    ):
        down[pl.ds(at, rim)] = ref[pl.ds(first_row + rows - rim, rim)]
        up[pl.ds(at, rim)] = ref[pl.ds(first_row, rim)]
        at += rim
    extra_rows = down.shape[0] - at
    if extra_rows:
        down[pl.ds(at, extra_rows)] = above[pl.ds(above.shape[0] - extra_rows, extra_rows)]
    slab, slabs = lax.axis_index("space"), lax.axis_size("space")
    size = 2 * rows // depth
    at = count(RIMS_0) + 2 * len(STEPS_0)
    for by, part in (
        *zip(apart, windows, strict=True),
        (1, above.at[pl.ds(at, size)]),
        (slabs - 1, below.at[pl.ds(at, size)]),
    ):
        held[pl.ds((slab - by) % slabs * size, size)] = part[...]


def send_behind(turn, slant_down, slant_up, rows):
    at = 0
    for index, (_, rim) in enumerate(BEHIND):
        slant_down[pl.ds(at, rim)] = turn[pl.ds((index + 1) * rows - rim, rim)]
        slant_up[pl.ds(at, rim)] = turn[pl.ds(index * rows, rim)]
        at += rim


def take_behind(rows, buffers, behind, behind_above, behind_below, low, high):
    lows, highs = split(behind_above, BEHIND), split(behind_below, BEHIND)
    for index, (name, rim) in enumerate(BEHIND):
        buffer = buffers[index]
        set_rims(buffer, rows, rim, lows[name], highs[name], low, high)
        buffer[pl.ds(MARGIN, rows)] = behind[pl.ds(index * rows, rows)]


def take_coefs(rows, coefs, diff, grow):
    diff[pl.ds(MARGIN - 3, rows + 6)] = coefs[pl.ds(0, rows + 6)]
    grow[pl.ds(MARGIN - 3, rows + 6)] = coefs[pl.ds(rows + 6, rows + 6)]


def level1_kernel(
    share, next_odd, forcing, first_forcing, coefs, last_pair, held, ahead,
    above, below, behind, behind_above, behind_below,
    slots, next_forcing, late_a, late_b, windows,
    fields, diff, grow, flat,
):
    rows = forcing.shape[0] // 3
    low, high = flags()
    take_coefs(rows, coefs, diff, grow)
    windows[...] = held[...]
    size = above.shape[0] - count(RIMS_1)
    if size:
        slabs = lax.axis_size("space")
        slab = (lax.axis_index("space") - 2) % slabs
        windows[pl.ds(slab * size, size)] = above[pl.ds(count(RIMS_1), size)]
    g1, g3, g2, g0, pair, before, after, even0, even1, image0, image1, odd0, odd1 = range(13)
    lows, highs = split(above, RIMS_1), split(below, RIMS_1)
    for (name, rim), spot in zip(RIMS_1, (after, g1, g3, g2), strict=True):
        set_rims(fields.at[spot], rows, rim, lows[name], highs[name], low, high)
    fields[after, pl.ds(MARGIN, rows)] = next_odd[...]
    for which, spot in enumerate((g1, g2, g3)):
        fields[spot, pl.ds(MARGIN, rows)] = forcing[pl.ds(which * rows, rows)]
    take_behind(
        rows, (fields.at[pair], fields.at[before]), behind, behind_above, behind_below, low, high
    )
    fields[g0, pl.ds(MARGIN - 2, rows + 4)] = (
        first_forcing[...] + fields[pair, pl.ds(MARGIN - 2, rows + 4)]
    )

    def second(at, n):
        d, g = diff[pl.ds(at, n)], grow[pl.ds(at, n)]
        for start, term, end in ((before, g0, even0), (after, g2, even1)):
            mid, slope = growth_of(fields.at[start], at, n, d, g)
            fields[end, pl.ds(at, n)] = mid + 2.0 * slope + fields[term, pl.ds(at, n)]

    def third(at, n):
        d, g = diff[pl.ds(at, n)], grow[pl.ds(at, n)]
        for start, term, end, image in ((even0, g1, odd0, image0), (even1, g3, odd1, image1)):
            mid, slope = growth_of(fields.at[start], at, n, d, g)
            fields[end, pl.ds(at, n)] = mid + 2.0 * slope + fields[term, pl.ds(at, n)]
            fields[image, pl.ds(at, n)] = mid + 4.0 * slope

    def fourth(at, n):
        d, g = diff[pl.ds(at, n)], grow[pl.ds(at, n)]
        here = at - MARGIN
        mid, slope = growth_of(fields.at[odd1], at, n, d, g)
        pair1 = mid + 2.0 * slope - fields[image1, pl.ds(at, n)]
        put_rows(flat, rows, ahead[...] + last_pair[pl.ds(0, rows)] + pair1)
        mid, slope = growth_of(fields.at[odd0], at, n, d, g)
        image = fields[image0, pl.ds(at, n)]
        term = fields[g2, pl.ds(at, n)] + (mid + 2.0 * slope - image)
        next_forcing[pl.ds(here, n)] = term
        put_rows(flat, 2 * rows, term)
        put_rows(flat, 0, image + term)

    over_rows(rows, 2, second)
    over_rows(rows, 1, third)
    over_rows(rows, 0, fourth)
    late_a[...] = fields[g1, pl.ds(MARGIN - 1, rows + 2)]
    late_b[...] = fields[g3, pl.ds(MARGIN - 1, rows + 2)]
    depth = forcing.shape[1]
    if folded(rows, share, reach_of()):
        pack_folded(slots, flat, rows, depth, reach_of())
    else:
        pack_windows(slots, flat, rows, depth, share)


def put_rows(flat, first, value):
    depth = value.shape[1]
    for i in range(value.shape[0]):
        flat[pl.ds((first + i) * depth, depth), :] = value[i]


def reach_of():
    return lax.axis_size("tm") + 2


def folded(rows, share, reach):
    return rows == 16 and 2 * share == LANES and FIELDS * 2 * reach <= share


def pack_folded(slots, flat, rows, depth, reach):
    devices = slots.shape[0]
    lane = lax.broadcasted_iota(jnp.int32, (8, LANES), 1)
    place = lane % (LANES // 2)
    rims = [None] * devices
    for field in range(FIELDS):
        first = field * rows * depth
        cells = []
        for line in range(depth):
            top = flat[pl.ds(first + line, 8, stride=depth), :]
            low = flat[pl.ds(first + 8 * depth + line, 8, stride=depth), :]
            cells.append(jnp.where(lane < LANES // 2, top, pltpu.roll(low, LANES // 2, 1)))
            cells.append(jnp.where(lane < LANES // 2, pltpu.roll(top, LANES // 2, 1), low))
        for target in range(devices):
            slots[target, pl.ds(field * 8, 8)] = cells[target]
            left = cells[target - 1] if target > 0 else 0.0
            right = cells[target + 1] if target < devices - 1 else 0.0
            rim = jnp.where(
                place >= LANES // 2 - reach, left, jnp.where(place < reach, right, 0.0)
            )
            if field == 0:
                rims[target] = rim
            else:
                rims[target] = rims[target] + pltpu.roll(rim, 2 * reach * field, 1)
    for target in range(devices):
        slots[target, pl.ds(FIELDS * 8, 8)] = rims[target]


def unfold(slot, field, reach):
    cells, rims = slot[pl.ds(field * 8, 8)], slot[pl.ds(FIELDS * 8, 8)]
    lane = lax.broadcasted_iota(jnp.int32, (8, LANES), 1)
    half = LANES // 2
    near = pltpu.roll(rims, (REACH - 2 * reach * field) % LANES, 1)
    far = pltpu.roll(rims, (-REACH - 2 * reach * field) % LANES, 1)
    parts = []
    for shift, rim in ((REACH, far), (-REACH, near)):
        own = pltpu.roll(cells, shift % LANES, 1)
        value = jnp.where((lane >= REACH - reach) & (lane < REACH + half + reach), rim, 0.0)
        parts.append(jnp.where((lane >= REACH) & (lane < REACH + half), own, value))
    return jnp.concatenate(parts, axis=0)


def pack_windows(slots, flat, rows, depth, share):
    lane = lax.broadcasted_iota(jnp.int32, (rows, LANES), 1)
    for field in range(FIELDS):
        first = field * rows * depth
        lines = [flat[pl.ds(first + line, rows, stride=depth), :] for line in range(depth)]
        for target in range(slots.shape[0]):
            line, offset = target * share // LANES, target * share % LANES
            shift = (REACH - offset) % LANES
            place = lane + (offset - REACH)
            value = pltpu.roll(lines[line], shift, 1)
            if offset < REACH:
                before = pltpu.roll(lines[line - 1], shift, 1) if line > 0 else 0.0
                value = jnp.where(place < 0, before, value)
            if offset > REACH:
                after = pltpu.roll(lines[line + 1], shift, 1) if line < depth - 1 else 0.0
                value = jnp.where(place >= LANES, after, value)
            slots[target, pl.ds(field * rows, rows)] = value


def late_rows(rows):
    return (-2, -1, rows, rows + 1)


def packing(rows, share):
    groups = LANES // share
    each = -(-(rows + 2 * UP_RIM) // groups)
    return groups, each, -(-(each + -(-4 // groups)) // 8) * 8


def sweep_kernel(share, rows, arrived, windows, slots, diff, grow, terms, padded, kept):
    slabs = lax.axis_size("space")
    devices = arrived.shape[0]
    blocks = devices // slabs
    total = slabs * rows
    reach = reach_of()
    groups, each, held = packing(rows, share)
    for slab in range(slabs):
        diff[pl.ds(slab * rows, rows), :] = windows[pl.ds(2 * slab * rows, rows), :]
        grow[pl.ds(slab * rows, rows), :] = windows[pl.ds((2 * slab + 1) * rows, rows), :]
    line = lax.broadcasted_iota(jnp.int32, (total, LANES), 0)
    lane = lax.broadcasted_iota(jnp.int32, (held, LANES), 1)
    padded[...] = jnp.zeros(padded.shape, jnp.float32)
    kept[...] = jnp.zeros(kept.shape, jnp.float32)

    def block(field, index):
        parts = []
        for slab in range(slabs):
            slot = arrived.at[index * slabs + slab]
            if folded(rows, share, reach):
                parts.append(unfold(slot, field, reach))
            else:
                parts.append(slot[pl.ds(field * rows, rows)])
        return jnp.concatenate(parts, axis=0)

    def slope_of(field):
        north = jnp.where(line == 0, 0.0, pltpu.roll(field, 1, 0))
        south = jnp.where(line == total - 1, 0.0, pltpu.roll(field, total - 1, 0))
        sides = pltpu.roll(field, 1, 1) + pltpu.roll(field, LANES - 1, 1)
        laplace = north + south + sides - 4.0 * field
        return diff[...] * laplace + grow[...] * field / (1.0 + field * field)

    field = None
    for index in range(blocks):
        behind = (index - 1) % blocks
        odd, term = block(0, behind), block(1, behind)
        even = odd + 4.0 * slope_of(odd) + term
        slope = slope_of(even)
        own_term = block(2, index)
        kept[index, pl.ds(8, total), :] = own_term
        odd = even + 4.0 * slope + own_term
        stepped = even + 8.0 * slope
        pair = odd + 4.0 * slope_of(odd) - stepped
        terms[index] = block(1, index) + pair
        if index == blocks - 1:
            field = stepped + terms[index]
    for index in range(blocks):
        for group in range(groups):
            padded[group, pl.ds(8, total), :] = pltpu.roll(
                field, (group * share - REACH) % LANES, 1
            )
        for slab in range(slabs):
            start = 8 + slab * rows - UP_RIM
            value = padded[0, pl.ds(start, held), :]
            for group in range(1, groups):
                piece = padded[group, pl.ds(start + group * each, held), :]
                value = jnp.where(lane >= group * share, piece, value)
            slots[index * slabs + slab] = value
            start = 8 + slab * rows
            for i, row in enumerate(late_rows(rows)):
                line_at, group = each + i // groups, i % groups
                piece = kept[index, pl.ds(start + row, 1), :]
                piece = pltpu.roll(piece, (group * share - REACH) % LANES, 1)
                if group > 0:
                    before = slots[index * slabs + slab, pl.ds(line_at, 1)]
                    piece = jnp.where(lane[:1] >= group * share, piece, before)
                slots[index * slabs + slab, pl.ds(line_at, 1)] = piece
        if index < blocks - 1:
            field = field + 8.0 * slope_of(field) + terms[index]


def up_kernel(
    share, arrived, next_forcing, late_a, late_b, core, coefs, out, fields, diff, grow, flat
):
    rows, depth, _ = next_forcing.shape
    groups, each, held = packing(rows, share)
    take_coefs(rows, coefs, diff, grow)
    lane = lax.broadcasted_iota(jnp.int32, (depth, LANES), 1)

    def whole(line, group):
        value = None
        for part in range(groups):
            piece = arrived[pl.ds(part * held + line, depth, stride=groups * held), :]
            if part != group:
                piece = pltpu.roll(piece, ((part - group) * share) % LANES, 1)
            value = piece if value is None else jnp.where(lane >= part * share, piece, value)
        return value

    for row in range(rows + 2 * UP_RIM):
        fields[0, MARGIN - UP_RIM + row] = whole(row % each, row // each)
    for i, row in enumerate(late_rows(rows)):
        fields[5, MARGIN + row] = whole(each + i // groups, i % groups)
    fields[5, pl.ds(MARGIN, rows)] = next_forcing[...]
    odd_first = CORES.index("o0") * rows

    def first(at, n):
        mid, slope = growth_of(fields.at[0], at, n, diff[pl.ds(at, n)], grow[pl.ds(at, n)])
        fields[2, pl.ds(at, n)] = mid + 4.0 * slope + fields[5, pl.ds(at, n)]

    def second(at, n):
        d, g = diff[pl.ds(at, n)], grow[pl.ds(at, n)]
        for start, late in ((0, late_a), (2, late_b)):
            mid, slope = growth_of(fields.at[start], at, n, d, g)
            fields[start + 1, pl.ds(at, n)] = mid + 2.0 * slope + late[pl.ds(at - MARGIN + 1, n)]

    def third(at, n):
        d, g = diff[pl.ds(at, n)], grow[pl.ds(at, n)]
        here = at - MARGIN
        for i in range(POINTS // 2):
            mid, slope = growth_of(fields.at[i], at, n, d, g)
            put_rows(flat, 2 * i * rows, mid)
            put_rows(flat, (2 * i + 1) * rows, mid + slope + core[pl.ds(odd_first + i * rows + here, n)])

    over_rows(rows, 2, first)
    over_rows(rows, 1, second)
    over_rows(rows, 0, third)
    for point in range(POINTS):
        for r in range(0, rows, 8):
            for c in range(depth):
                start = (point * rows + r) * depth + c
                out[point, pl.ds(r, 8), pl.ds(c * LANES, LANES)] = flat[
                    pl.ds(start, 8, stride=depth), :
                ]


def moved(array, blocks, slabs):
    tm, space = lax.axis_size("tm"), lax.axis_size("space")
    pairs = [
        (t * space + s, (t + blocks) % tm * space + (s + slabs) % space)
        for t in range(tm)
        for s in range(space)
    ]
    return lax.ppermute(array, ("tm", "space"), pairs)


def exchange(down, up, turn, slant_down, slant_up):
    slanted = moved(slant_down, 1, 1), moved(slant_up, 1, -1)
    return moved(down, 0, 1), moved(up, 0, -1), moved(turn, 1, 0), *slanted


def body(initial, source, diffusivity, growth):
    points, rows, cols = initial.shape
    assert points == POINTS and rows % 8 == 0 and cols % LANES == 0
    depth = cols // LANES
    tm, space = lax.axis_size("tm"), lax.axis_size("space")
    devices = tm * space
    share = cols // devices
    assert share * devices == cols and LANES % share == 0
    assert reach_of() <= REACH and REACH + share + reach_of() <= LANES
    _, _, held = packing(rows, share)
    wide = rows + 2 * MARGIN

    def lines(n):
        return (n * depth, LANES)

    def field(n):
        return (n, depth, LANES)

    def as_rows(array):
        return array.reshape(-1, depth, LANES)

    window_rows = 2 * rows // depth
    assert window_rows * depth == 2 * rows
    raw = [(points // 2, rows, cols), source.shape, (2, rows, cols)]
    sides = count(RIMS_0) + 2 * len(STEPS_0) + window_rows
    behind = count(BEHIND_0) + 2 * len(STEPS_BEHIND_0)
    extra = window_rows if handed_on(space) else 0
    *sends, back = call(
        functools.partial(pack_kernel, share),
        [lines(sides + extra), lines(sides), lines(2 * rows), lines(behind), lines(behind)]
        + [lines(rows)],
        raw + [lines(2 * EDGE * (len(STEPS_0) + len(STEPS_BEHIND_0))), lines(2 * rows)],
        initial, source, diffusivity, growth,
        place=pltpu.HBM, sems=points // 2 + 3, mib=PACK_MIB,
    )
    apart = direct_windows(space)
    core, *windows = call(
        functools.partial(core_kernel, share),
        [lines(len(CORES) * rows)] + [(2 * rows, LANES)] * len(apart),
        raw,
        initial, source, diffusivity, growth,
        place=pltpu.HBM, sems=points // 2 + 3,
        cost=pl.CostEstimate(flops=0, transcendentals=0, bytes_accessed=CORE_COST),
    )
    above, below, turned, *slanted = exchange(*(as_rows(part) for part in sends))
    turned, back = lax.optimization_barrier((turned, back))
    ahead = as_rows(moved(back, -1, 0))
    windows = [moved(part, 0, by) if by else part for by, part in zip(apart, windows, strict=True)]
    windows = [as_rows(part) for part in windows]
    core = as_rows(core)
    above, below, turned, slanted, ahead, windows = lax.optimization_barrier(
        (above, below, turned, slanted, ahead, windows)
    )

    buffers = [(wide, depth, LANES), (wide, depth, LANES)]
    rim1, rimb = count(RIMS_1), count(BEHIND)
    turn, down, up, slant_down, slant_up, next_odd, forcing, first_forcing, coefs, held_windows = call(
        functools.partial(level0_kernel, tuple(apart)),
        [
            field(2 * rows), field(rim1 + extra), field(rim1), field(rimb), field(rimb),
            field(rows), field(3 * rows), field(rows + 4), field(2 * (rows + 6)),
            field(window_rows * space),
        ],
        [(len(CORES) + 2 + 3 * (POINTS // 2), wide, depth, LANES)] + buffers,
        core, above, below, turned, *slanted, *windows,
    )
    arrived = exchange(down, up, turn, slant_down, slant_up)
    held_rows = FIELDS * 8 + 8 if folded(rows, share, reach_of()) else FIELDS * rows
    slots, next_forcing, late_a, late_b, windows = call(
        functools.partial(level1_kernel, share),
        [
            (devices, held_rows, LANES),
            field(rows), field(rows + 2), field(rows + 2), field(window_rows * space),
        ],
        [(13, wide, depth, LANES)] + buffers + [(FIELDS * rows * depth, LANES)],
        next_odd, forcing, first_forcing, coefs, turn, held_windows, ahead, *arrived,
    )
    slots = lax.all_to_all(slots, ("tm", "space"), 0, 0, tiled=True)
    (slots,) = call(
        functools.partial(sweep_kernel, share, rows),
        [(devices, held, LANES)],
        [(space * rows, LANES), (space * rows, LANES), (tm, space * rows, LANES)]
        + [(LANES // share, 8 + space * rows + 2 * rows + held, LANES)]
        + [(tm, 16 + space * rows, LANES)],
        slots, windows.reshape(-1, LANES),
    )
    slots = lax.all_to_all(slots, ("tm", "space"), 0, 0, tiled=True)
    (out,) = call(
        functools.partial(up_kernel, share),
        [(points, rows, cols)],
        [(6, wide, depth, LANES)] + buffers + [(points * rows * depth, LANES)],
        slots.reshape(devices * held, LANES), next_forcing, late_a, late_b, core, coefs,
    )
    return out


def solution(mesh):
    placed = (P("tm", "space", None), P("tm", "space", None), P("space", None), P("space", None))
    return jax.shard_map(
        body, mesh=mesh, in_specs=placed, out_specs=P("tm", "space", None), check_vma=False
    )
```

```python
import functools

import jax
import jax.numpy as jnp
from jax import lax
from jax.experimental import pallas as pl
from jax.experimental.pallas import tpu as pltpu
from jax.sharding import PartitionSpec as P

LANES = 128
MARGIN = 4
REACH = 32
UP_RIM = 3
FIELDS = 3
CORE_COST = 30_000_000
POINTS = 8
diffusion_number = 0.03
time_step = 0.02

RIMS_0 = (
    ("e0", 2), ("e1", 2), ("e2", 2),
    ("o0", 1), ("o1", 1), ("o2", 1), ("o3", 1),
    ("s0", 2), ("s1", 2), ("s2", 2), ("s3", 2),
    ("d", 2), ("g", 2),
)
BEHIND_0 = (("ep", 2), ("op", 1))
STEPS_0 = (("e0", "o0"), ("e1", "o1"), ("e2", "o2"))
STEPS_BEHIND_0 = (("ep", "op"),)
CORES = ("e0", "e1", "e2", "o0", "o1", "o2", "o3", "s0", "s1", "s2", "s3", "d", "g")
RIMS_1 = (("next", 3), ("g1", 1), ("g3", 1), ("g2", 2))
BEHIND = (("pair", 2), ("odd", 3))


def count(rims):
    return sum(rows for _, rows in rims)


def params(mib):
    return pltpu.CompilerParams(vmem_limit_bytes=int(mib * 2**20))


def call(
    kernel, outs, scratch, *args, mib=16, place=pltpu.VMEM, to=pltpu.VMEM, sems=0, cost=None
):
    if place == pltpu.HBM:
        args = [pltpu.with_memory_space_constraint(arg, place) for arg in args]
    return pl.pallas_call(
        kernel,
        out_shape=tuple(jax.ShapeDtypeStruct(shape, jnp.float32) for shape in outs),
        in_specs=[pl.BlockSpec(memory_space=place)] * len(args),
        out_specs=tuple(pl.BlockSpec(memory_space=to) for _ in outs),
        scratch_shapes=[pltpu.VMEM(shape, jnp.float32) for shape in scratch]
        + ([pltpu.SemaphoreType.DMA((sems,))] if sems else []),
        compiler_params=params(mib),
        cost_estimate=cost,
    )(*args)


def beside(mid):
    depth = mid.shape[1]
    lane = lax.broadcasted_iota(jnp.int32, mid.shape, 2)
    line = lax.broadcasted_iota(jnp.int32, mid.shape, 1)
    left = pltpu.roll(mid, 1, 2)
    left_turn = pltpu.roll(left, 1, 1)
    right = pltpu.roll(mid, LANES - 1, 2)
    right_turn = pltpu.roll(right, depth - 1, 1)
    left = jnp.where(lane == 0, jnp.where(line == 0, 0.0, left_turn), left)
    right = jnp.where(lane == LANES - 1, jnp.where(line == depth - 1, 0.0, right_turn), right)
    return left + right


def slope_of_rows(wide, diff, grow):
    mid = wide[1:-1]
    laplace = wide[:-2] + wide[2:] + beside(mid) - 4.0 * mid
    return mid, diff * laplace + grow * mid / (1.0 + mid * mid)


def growth_of(ref, at, rows, diff, grow):
    return slope_of_rows(ref[pl.ds(at - 1, rows + 2)], diff, grow)


def over_rows(rows, rim, body):
    body(MARGIN - rim, rows + 2 * rim)


def flags():
    slab = lax.axis_index("space")
    low = jnp.where(slab > 0, 1.0, 0.0).astype(jnp.float32)
    high = jnp.where(slab < lax.axis_size("space") - 1, 1.0, 0.0).astype(jnp.float32)
    return low, high


def set_rims(buffer, rows, rim, low_rows, high_rows, low, high, inner=0):
    width = rim - inner
    buffer[pl.ds(MARGIN - rim, width)] = low_rows * low
    buffer[pl.ds(MARGIN + rows + inner, width)] = high_rows * high


def pieces(name, evens, source, diffusivity, growth):
    if name == "d":
        return lambda rows, cols: diffusivity[rows, cols] * diffusion_number
    if name == "g":
        return lambda rows, cols: growth[rows, cols] * time_step
    if name == "ep":
        return lambda rows, cols: evens[POINTS // 2 - 1, rows, cols]
    if name == "op":
        return lambda rows, cols: source[POINTS - 1, rows, cols]
    which = int(name[1])
    if name[0] == "e":
        return lambda rows, cols: evens[which, rows, cols]
    return lambda rows, cols: source[2 * which + (name[0] == "o"), rows, cols]


def fetch(initial_all, source_all, diffusivity_all, growth_all, evens, source, coefs, sems):
    pairs = [(initial_all.at[2 * i], evens.at[i]) for i in range(POINTS // 2)]
    pairs += [(diffusivity_all, coefs.at[0]), (growth_all, coefs.at[1]), (source_all, source)]
    copies = [pltpu.make_async_copy(*pair, sems.at[i]) for i, pair in enumerate(pairs)]
    for copy in copies:
        copy.start()
    return copies[:-1], copies[-1]


def target_of(by):
    slabs = lax.axis_size("space")
    return lax.axis_index("tm") * slabs + (lax.axis_index("space") + by) % slabs


EDGE = 8


def pack_kernel(
    share, initial_all, source_all, diffusivity_all, growth_all,
    down, up, turn, slant_down, slant_up, back, evens, source, coefs, edge, cells, sems,
):
    waits, last = fetch(
        initial_all, source_all, diffusivity_all, growth_all, evens, source, coefs, sems
    )
    _, rows, cols = coefs.shape
    depth = cols // LANES
    diffusivity, growth = coefs.at[0], coefs.at[1]

    def put(ref, at, name, first, count):
        get = pieces(name, evens, source, diffusivity, growth)
        for c in range(depth):
            place = pl.ds(at * depth + c, count, stride=depth)
            ref[place, :] = get(pl.ds(first, count), pl.ds(c * LANES, LANES))

    def rows_of(at, count):
        return edge[pl.ds(at * depth, count * depth), :].reshape(count, depth, LANES)

    def put_sides(early):
        for rims, low, high in ((RIMS_0, down, up), (BEHIND_0, slant_down, slant_up)):
            at = 0
            for name, rim in rims:
                if early == (name[0] not in "os"):
                    put(low, at, name, rows - rim, rim)
                    put(high, at, name, 0, rim)
                at += rim

    for wait in waits:
        wait.wait()
    put_sides(True)
    for index, name in enumerate(("d", "g")):
        for r in range(0, rows, 8):
            put(cells, index * rows + r, name, r, 8)
    end = (count(RIMS_0) + 2 * len(STEPS_0)) * depth
    for ref, by, at in ((down, 1, end), (up, -1, end), (down, 2, end + 2 * rows)):
        if at < ref.shape[0]:
            for index in range(2):
                get = lambda line: cells[pl.ds(index * rows * depth + line, rows, stride=depth), :]
                ref[pl.ds(at + index * rows, rows), :] = window(
                    get, target_of(by) * share, depth
                )
    steps = [
        (start, term, sides, at + 2 * i)
        for group, sides, at in (
            (STEPS_0, (down, up), count(RIMS_0)),
            (STEPS_BEHIND_0, (slant_down, slant_up), count(BEHIND_0)),
        )
        for i, (start, term) in enumerate(group)
    ]
    for i, (start, _, _, _) in enumerate(steps):
        put(edge, 2 * EDGE * i, start, rows - 4, 4)
        put(edge, 2 * EDGE * i + EDGE, start, 0, 4)
    put(turn, 0, "ep", 0, 8)
    put(turn, 8, "ep", 8, 8)
    last.wait()
    put_sides(False)
    for i, (_, term, _, _) in enumerate(steps):
        put(edge, 2 * EDGE * i + 4, term, rows - 3, 2)
        put(edge, 2 * EDGE * i + EDGE + 4, term, 1, 2)
    for r in range(0, rows, 8):
        put(turn, rows + r, "op", r, 8)
        put(back, r, "s0", r, 8)
    for side, first in enumerate((rows - 3, 1)):
        diff, grow = (
            cells[pl.ds((index * rows + first) * depth, 2 * depth), :].reshape(2, depth, LANES)
            for index in range(2)
        )
        for i, (_, _, sides, at) in enumerate(steps):
            spot = (2 * i + side) * EDGE
            mid, slope = slope_of_rows(rows_of(spot, 4), diff, grow)
            put_rows(sides[side], at, mid + slope + rows_of(spot + 4, 2))


def column_of(shape, offset):
    lane = lax.broadcasted_iota(jnp.int32, shape, len(shape) - 1)
    return jnp.where(lane < LANES - REACH, lane, lane - LANES) + offset


def window(get, first, depth):
    line, offset = first // LANES, first % LANES
    source = column_of(get(0).shape, offset)
    shift = (LANES - offset) % LANES
    before = jnp.where(line > 0, pltpu.roll(get(jnp.maximum(line - 1, 0)), shift, 1), 0.0)
    here = pltpu.roll(get(line), shift, 1)
    after = jnp.where(
        line < depth - 1, pltpu.roll(get(jnp.minimum(line + 1, depth - 1)), shift, 1), 0.0
    )
    return jnp.where(source < 0, before, jnp.where(source >= LANES, after, here))


def core_kernel(
    share, initial_all, source_all, diffusivity_all, growth_all, core, *refs
):
    *windows, evens, source, coefs, sems = refs
    waits, last = fetch(
        initial_all, source_all, diffusivity_all, growth_all, evens, source, coefs, sems
    )
    for wait in (*waits, last):
        wait.wait()
    _, rows, cols = coefs.shape
    depth = cols // LANES
    for index, name in enumerate(CORES):
        get = pieces(name, evens, source, coefs.at[0], coefs.at[1])
        for c in range(depth):
            for r in range(0, rows, 8):
                value = get(pl.ds(r, 8), pl.ds(c * LANES, LANES))
                core[pl.ds((index * rows + r) * depth + c, 8, stride=depth), :] = value
    for by, out in zip(direct_windows(lax.axis_size("space")), windows, strict=True):
        for which, name in enumerate(("d", "g")):
            start = CORES.index(name) * rows * depth
            get = lambda line: core[pl.ds(start + line, rows, stride=depth), :]
            out[pl.ds(which * rows, rows)] = window(get, target_of(by) * share, depth)


def handed_on(slabs):
    return slabs == 4


def direct_windows(slabs):
    return [0] if handed_on(slabs) else [0] + list(range(2, slabs - 1))


def split(ref, rims):
    at, out = 0, {}
    for name, rim in rims:
        out[name] = ref[pl.ds(at, rim)]
        at += rim
    return out


def level0_kernel(
    apart, core, above, below, behind, behind_above, behind_below, *refs
):
    windows, refs = refs[: len(apart)], refs[len(apart) :]
    (
        turn, down, up, slant_down, slant_up, next_odd, forcing, first_forcing, coefs, held,
        fields, diff, grow,
    ) = refs
    rows = core.shape[0] // len(CORES)
    low, high = flags()
    depth = core.shape[1]
    names = list(CORES) + ["ep", "op"]
    spots = {name: index for index, name in enumerate(names)}
    extra = len(names)
    halves = POINTS // 2
    odd = [extra + i for i in range(halves)]
    even = [extra + halves + i for i in range(halves)]
    image = [extra + 2 * halves + i for i in range(halves)]
    for rims, steps, from_low, from_high in (
        (RIMS_0, STEPS_0, above, below),
        (BEHIND_0, STEPS_BEHIND_0, behind_above, behind_below),
    ):
        lows, highs = split(from_low, rims), split(from_high, rims)
        for name, rim in rims:
            if name in ("d", "g"):
                buffer = diff if name == "d" else grow
            else:
                buffer = fields.at[spots[name]]
            set_rims(buffer, rows, rim, lows[name], highs[name], low, high)
        at = count(rims)
        for start, _ in steps:
            buffer = fields.at[odd[0 if start == "ep" else int(start[1]) + 1]]
            set_rims(
                buffer, rows, 3, from_low[pl.ds(at, 2)], from_high[pl.ds(at, 2)], low, high, 1
            )
            at += 2
    for name in CORES:
        if name in ("d", "g"):
            buffer = diff if name == "d" else grow
        else:
            buffer = fields.at[spots[name]]
        buffer[pl.ds(MARGIN, rows)] = core[pl.ds(CORES.index(name) * rows, rows)]
    for index, (name, _) in enumerate(BEHIND_0):
        fields[spots[name], pl.ds(MARGIN, rows)] = behind[pl.ds(index * rows, rows)]

    def first(at, n):
        d, g = diff[pl.ds(at, n)], grow[pl.ds(at, n)]
        for i in range(halves):
            start, term = ("ep", "op") if i == 0 else (f"e{i - 1}", f"o{i - 1}")
            mid, slope = growth_of(fields.at[spots[start]], at, n, d, g)
            fields[odd[i], pl.ds(at, n)] = mid + slope + fields[spots[term], pl.ds(at, n)]

    def second(at, n):
        d, g = diff[pl.ds(at, n)], grow[pl.ds(at, n)]
        for i in range(halves):
            mid, slope = growth_of(fields.at[odd[i]], at, n, d, g)
            fields[even[i], pl.ds(at, n)] = mid + slope + fields[spots[f"s{i}"], pl.ds(at, n)]

    def third(at, n):
        d, g = diff[pl.ds(at, n)], grow[pl.ds(at, n)]
        for i in range(halves):
            mid, slope = growth_of(fields.at[even[i]], at, n, d, g)
            fields[odd[i], pl.ds(at, n)] = mid + slope + fields[spots[f"o{i}"], pl.ds(at, n)]
            fields[image[i], pl.ds(at, n)] = mid + 2.0 * slope

    def fourth(at, n):
        d, g = diff[pl.ds(at, n)], grow[pl.ds(at, n)]
        here = at - MARGIN
        for i in range(halves):
            mid, slope = growth_of(fields.at[odd[i]], at, n, d, g)
            pair = mid + slope - fields[image[i], pl.ds(at, n)]
            if i == halves - 1:
                turn[pl.ds(here, n)] = pair
            else:
                term = fields[spots[f"s{i + 1}"], pl.ds(at, n)] + pair
                forcing[pl.ds(i * rows + here, n)] = term
                if i == 0:
                    next_odd[...] = fields[image[0], pl.ds(at, n)] + term
                if i == halves - 2:
                    turn[pl.ds(rows + here, n)] = fields[image[i], pl.ds(at, n)] + term

    over_rows(rows, 1, first)
    over_rows(rows, 2, second)
    over_rows(rows, 1, third)
    over_rows(rows, 0, fourth)
    first_forcing[...] = fields[spots["s0"], pl.ds(MARGIN - 2, rows + 4)]
    coefs[pl.ds(0, rows + 4)] = diff[pl.ds(MARGIN - 2, rows + 4)]
    coefs[pl.ds(rows + 4, rows + 4)] = grow[pl.ds(MARGIN - 2, rows + 4)]
    send_behind(turn, slant_down, slant_up, rows)
    at = 0
    for (name, rim), (ref, first_row) in zip(
        RIMS_1, ((next_odd, 0), (forcing, 0), (forcing, 2 * rows), (forcing, rows)), strict=True
    ):
        down[pl.ds(at, rim)] = ref[pl.ds(first_row + rows - rim, rim)]
        up[pl.ds(at, rim)] = ref[pl.ds(first_row, rim)]
        at += rim
    extra_rows = down.shape[0] - at
    if extra_rows:
        down[pl.ds(at, extra_rows)] = above[pl.ds(above.shape[0] - extra_rows, extra_rows)]
    slab, slabs = lax.axis_index("space"), lax.axis_size("space")
    size = 2 * rows // depth
    at = count(RIMS_0) + 2 * len(STEPS_0)
    for by, part in (
        *zip(apart, windows, strict=True),
        (1, above.at[pl.ds(at, size)]),
        (slabs - 1, below.at[pl.ds(at, size)]),
    ):
        held[pl.ds((slab - by) % slabs * size, size)] = part[...]


def send_behind(turn, slant_down, slant_up, rows):
    at = 0
    for index, (_, rim) in enumerate(BEHIND):
        slant_down[pl.ds(at, rim)] = turn[pl.ds((index + 1) * rows - rim, rim)]
        slant_up[pl.ds(at, rim)] = turn[pl.ds(index * rows, rim)]
        at += rim


def take_behind(rows, buffers, behind, behind_above, behind_below, low, high):
    lows, highs = split(behind_above, BEHIND), split(behind_below, BEHIND)
    for index, (name, rim) in enumerate(BEHIND):
        buffer = buffers[index]
        set_rims(buffer, rows, rim, lows[name], highs[name], low, high)
        buffer[pl.ds(MARGIN, rows)] = behind[pl.ds(index * rows, rows)]


def take_coefs(rows, coefs, diff, grow):
    diff[pl.ds(MARGIN - 2, rows + 4)] = coefs[pl.ds(0, rows + 4)]
    grow[pl.ds(MARGIN - 2, rows + 4)] = coefs[pl.ds(rows + 4, rows + 4)]


def level1_kernel(
    share, next_odd, forcing, first_forcing, coefs, last_pair, held, ahead,
    above, below, behind, behind_above, behind_below,
    slots, next_forcing, late_a, late_b, windows,
    fields, diff, grow, flat,
):
    rows = forcing.shape[0] // 3
    low, high = flags()
    take_coefs(rows, coefs, diff, grow)
    windows[...] = held[...]
    size = above.shape[0] - count(RIMS_1)
    if size:
        slabs = lax.axis_size("space")
        slab = (lax.axis_index("space") - 2) % slabs
        windows[pl.ds(slab * size, size)] = above[pl.ds(count(RIMS_1), size)]
    g1, g3, g2, g0, pair, before, after, even0, even1, image0, image1, odd0, odd1 = range(13)
    lows, highs = split(above, RIMS_1), split(below, RIMS_1)
    for (name, rim), spot in zip(RIMS_1, (after, g1, g3, g2), strict=True):
        set_rims(fields.at[spot], rows, rim, lows[name], highs[name], low, high)
    fields[after, pl.ds(MARGIN, rows)] = next_odd[...]
    for which, spot in enumerate((g1, g2, g3)):
        fields[spot, pl.ds(MARGIN, rows)] = forcing[pl.ds(which * rows, rows)]
    take_behind(
        rows, (fields.at[pair], fields.at[before]), behind, behind_above, behind_below, low, high
    )
    fields[g0, pl.ds(MARGIN - 2, rows + 4)] = (
        first_forcing[...] + fields[pair, pl.ds(MARGIN - 2, rows + 4)]
    )

    def second(at, n):
        d, g = diff[pl.ds(at, n)], grow[pl.ds(at, n)]
        for start, term, end in ((before, g0, even0), (after, g2, even1)):
            mid, slope = growth_of(fields.at[start], at, n, d, g)
            fields[end, pl.ds(at, n)] = mid + 2.0 * slope + fields[term, pl.ds(at, n)]

    def third(at, n):
        d, g = diff[pl.ds(at, n)], grow[pl.ds(at, n)]
        for start, term, end, image in ((even0, g1, odd0, image0), (even1, g3, odd1, image1)):
            mid, slope = growth_of(fields.at[start], at, n, d, g)
            fields[end, pl.ds(at, n)] = mid + 2.0 * slope + fields[term, pl.ds(at, n)]
            fields[image, pl.ds(at, n)] = mid + 4.0 * slope

    def fourth(at, n):
        d, g = diff[pl.ds(at, n)], grow[pl.ds(at, n)]
        here = at - MARGIN
        mid, slope = growth_of(fields.at[odd1], at, n, d, g)
        pair1 = mid + 2.0 * slope - fields[image1, pl.ds(at, n)]
        put_rows(flat, rows, ahead[...] + last_pair[pl.ds(0, rows)] + pair1)
        mid, slope = growth_of(fields.at[odd0], at, n, d, g)
        image = fields[image0, pl.ds(at, n)]
        term = fields[g2, pl.ds(at, n)] + (mid + 2.0 * slope - image)
        next_forcing[pl.ds(here, n)] = term
        put_rows(flat, 2 * rows, term)
        put_rows(flat, 0, image + term)

    over_rows(rows, 2, second)
    over_rows(rows, 1, third)
    over_rows(rows, 0, fourth)
    late_a[...] = fields[g1, pl.ds(MARGIN - 1, rows + 2)]
    late_b[...] = fields[g3, pl.ds(MARGIN - 1, rows + 2)]
    depth = forcing.shape[1]
    if folded(rows, share, reach_of()):
        pack_folded(slots, flat, rows, depth, reach_of())
    else:
        pack_windows(slots, flat, rows, depth, share)


def put_rows(flat, first, value):
    depth = value.shape[1]
    for i in range(value.shape[0]):
        flat[pl.ds((first + i) * depth, depth), :] = value[i]


def reach_of():
    return lax.axis_size("tm") + 2


def folded(rows, share, reach):
    return rows == 16 and 2 * share == LANES and FIELDS * 2 * reach <= share


def pack_folded(slots, flat, rows, depth, reach):
    devices = slots.shape[0]
    lane = lax.broadcasted_iota(jnp.int32, (8, LANES), 1)
    place = lane % (LANES // 2)
    rims = [None] * devices
    for field in range(FIELDS):
        first = field * rows * depth
        cells = []
        for line in range(depth):
            top = flat[pl.ds(first + line, 8, stride=depth), :]
            low = flat[pl.ds(first + 8 * depth + line, 8, stride=depth), :]
            cells.append(jnp.where(lane < LANES // 2, top, pltpu.roll(low, LANES // 2, 1)))
            cells.append(jnp.where(lane < LANES // 2, pltpu.roll(top, LANES // 2, 1), low))
        for target in range(devices):
            slots[target, pl.ds(field * 8, 8)] = cells[target]
            left = cells[target - 1] if target > 0 else 0.0
            right = cells[target + 1] if target < devices - 1 else 0.0
            rim = jnp.where(
                place >= LANES // 2 - reach, left, jnp.where(place < reach, right, 0.0)
            )
            if field == 0:
                rims[target] = rim
            else:
                rims[target] = rims[target] + pltpu.roll(rim, 2 * reach * field, 1)
    for target in range(devices):
        slots[target, pl.ds(FIELDS * 8, 8)] = rims[target]


def unfold(slot, field, reach):
    cells, rims = slot[pl.ds(field * 8, 8)], slot[pl.ds(FIELDS * 8, 8)]
    lane = lax.broadcasted_iota(jnp.int32, (8, LANES), 1)
    half = LANES // 2
    back = 2 * reach * field
    top = pltpu.roll(rims, (half - back) % LANES, 1)
    low = pltpu.roll(rims, (-back) % LANES, 1) if back else rims
    return jnp.concatenate(
        [
            jnp.where(lane < half, cells, top),
            jnp.where(lane < half, pltpu.roll(cells, half, 1), low),
        ],
        axis=0,
    )


def pack_windows(slots, flat, rows, depth, share):
    for field in range(FIELDS):
        first = field * rows * depth
        lines = [flat[pl.ds(first + line, rows, stride=depth), :] for line in range(depth)]
        for target in range(slots.shape[0]):
            line, offset = target * share // LANES, target * share % LANES
            shift = (LANES - offset) % LANES
            place = column_of((rows, LANES), offset)
            value = pltpu.roll(lines[line], shift, 1)
            if offset < REACH:
                before = pltpu.roll(lines[line - 1], shift, 1) if line > 0 else 0.0
                value = jnp.where(place < 0, before, value)
            if offset > REACH:
                after = pltpu.roll(lines[line + 1], shift, 1) if line < depth - 1 else 0.0
                value = jnp.where(place >= LANES, after, value)
            slots[target, pl.ds(field * rows, rows)] = value


def late_rows(rows):
    return (rows, -2, rows + 1, -1)


def packing(rows, share):
    groups = LANES // share
    each = -(-(rows + 2 * UP_RIM) // groups)
    return groups, each, -(-(each + -(-4 // groups)) // 8) * 8


def sweep_kernel(share, rows, arrived, windows, slots, diff, grow, terms, padded):
    slabs = lax.axis_size("space")
    devices = arrived.shape[0]
    blocks = devices // slabs
    total = slabs * rows
    reach = reach_of()
    groups, each, held = packing(rows, share)
    for slab in range(slabs):
        diff[pl.ds(slab * rows, rows), :] = windows[pl.ds(2 * slab * rows, rows), :]
        grow[pl.ds(slab * rows, rows), :] = windows[pl.ds((2 * slab + 1) * rows, rows), :]
    line = lax.broadcasted_iota(jnp.int32, (total, LANES), 0)
    lane = lax.broadcasted_iota(jnp.int32, (held, LANES), 1)
    padded[...] = jnp.zeros(padded.shape, jnp.float32)

    def block(field, index):
        parts = []
        for slab in range(slabs):
            slot = arrived.at[index * slabs + slab]
            if folded(rows, share, reach):
                parts.append(unfold(slot, field, reach))
            else:
                parts.append(slot[pl.ds(field * rows, rows)])
        return jnp.concatenate(parts, axis=0)

    def slope_of(field):
        north = jnp.where(line == 0, 0.0, pltpu.roll(field, 1, 0))
        south = jnp.where(line == total - 1, 0.0, pltpu.roll(field, total - 1, 0))
        sides = pltpu.roll(field, 1, 1) + pltpu.roll(field, LANES - 1, 1)
        laplace = north + south + sides - 4.0 * field
        return diff[...] * laplace + grow[...] * field / (1.0 + field * field)

    def put_late(index, slab):
        to = slots.at[index * slabs + slab]
        if folded(rows, share, reach):
            zero = jnp.zeros((2, LANES), jnp.float32)
            low = arrived[index * slabs + slab + 1, pl.ds(16, 2)] if slab < slabs - 1 else zero
            high = arrived[index * slabs + slab - 1, pl.ds(22, 2)] if slab > 0 else zero
            to[pl.ds(each, 2)] = jnp.where(lane[:2] < share, low, high)
            return
        for i, row in enumerate(late_rows(rows)):
            at, group = each + i // groups, i % groups
            beside_slab = slab + row // rows
            if 0 <= beside_slab < slabs:
                place = pl.ds(2 * rows + row % rows, 1)
                piece = arrived[index * slabs + beside_slab, place]
                piece = pltpu.roll(piece, group * share, 1)
            else:
                piece = jnp.zeros((1, LANES), jnp.float32)
            if group:
                piece = jnp.where(lane[:1] >= group * share, piece, to[pl.ds(at, 1)])
            to[pl.ds(at, 1)] = piece

    field = None
    for index in range(blocks):
        behind = (index - 1) % blocks
        odd, term = block(0, behind), block(1, behind)
        even = odd + 4.0 * slope_of(odd) + term
        slope = slope_of(even)
        odd = even + 4.0 * slope + block(2, index)
        stepped = even + 8.0 * slope
        pair = odd + 4.0 * slope_of(odd) - stepped
        terms[index] = block(1, index) + pair
        if index == blocks - 1:
            field = stepped + terms[index]
    for index in range(blocks):
        for group in range(groups):
            padded[group, pl.ds(8, total), :] = (
                pltpu.roll(field, group * share, 1) if group else field
            )
        for slab in range(slabs):
            start = 8 + slab * rows - UP_RIM
            value = padded[0, pl.ds(start, held), :]
            for group in range(1, groups):
                piece = padded[group, pl.ds(start + group * each, held), :]
                value = jnp.where(lane >= group * share, piece, value)
            slots[index * slabs + slab] = value
            put_late(index, slab)
        if index < blocks - 1:
            field = field + 8.0 * slope_of(field) + terms[index]


def up_kernel(
    share, arrived, next_forcing, late_a, late_b, core, coefs,
    out, fields, diff, grow, flat, ready, sems,
):
    rows, depth, _ = next_forcing.shape
    groups, each, held = packing(rows, share)
    take_coefs(rows, coefs, diff, grow)
    lane = lax.broadcasted_iota(jnp.int32, (depth, LANES), 1)

    def whole(line, group):
        value = None
        for part in range(groups):
            piece = arrived[pl.ds(part * held + line, depth, stride=groups * held), :]
            if part != group:
                piece = pltpu.roll(piece, ((part - group) * share) % LANES, 1)
            value = piece if value is None else jnp.where(lane >= part * share, piece, value)
        return value

    for row in range(rows + 2 * UP_RIM):
        fields[0, MARGIN - UP_RIM + row] = whole(row % each, row // each)
    for i, row in enumerate(late_rows(rows)):
        fields[5, MARGIN + row] = whole(each + i // groups, i % groups)
    fields[5, pl.ds(MARGIN, rows)] = next_forcing[...]
    odd_first = CORES.index("o0") * rows

    def first(at, n):
        mid, slope = growth_of(fields.at[0], at, n, diff[pl.ds(at, n)], grow[pl.ds(at, n)])
        fields[2, pl.ds(at, n)] = mid + 4.0 * slope + fields[5, pl.ds(at, n)]

    def second(at, n):
        d, g = diff[pl.ds(at, n)], grow[pl.ds(at, n)]
        for start, late in ((0, late_a), (2, late_b)):
            mid, slope = growth_of(fields.at[start], at, n, d, g)
            fields[start + 1, pl.ds(at, n)] = mid + 2.0 * slope + late[pl.ds(at - MARGIN + 1, n)]

    copies = []

    def emit(point, value):
        put_rows(flat, point * rows, value)
        for r in range(0, rows, 8):
            for c in range(depth):
                start = (point * rows + r) * depth + c
                ready[point, pl.ds(r, 8), pl.ds(c * LANES, LANES)] = flat[
                    pl.ds(start, 8, stride=depth), :
                ]
        copy = pltpu.make_async_copy(ready.at[point], out.at[point], sems.at[point])
        copy.start()
        copies.append(copy)

    def last(i):
        at, n = MARGIN, rows
        mid, slope = growth_of(fields.at[i], at, n, diff[pl.ds(at, n)], grow[pl.ds(at, n)])
        emit(2 * i + 1, mid + slope + core[pl.ds(odd_first + i * rows, n)])

    core_rows = pl.ds(MARGIN, rows)
    emit(0, fields[0, core_rows])
    over_rows(rows, 2, first)
    emit(4, fields[2, core_rows])
    over_rows(rows, 1, second)
    emit(2, fields[1, core_rows])
    emit(6, fields[3, core_rows])
    for i in (0, 2, 1, 3):
        last(i)
    for copy in copies:
        copy.wait()


def moved(array, blocks, slabs):
    tm, space = lax.axis_size("tm"), lax.axis_size("space")
    pairs = [
        (t * space + s, (t + blocks) % tm * space + (s + slabs) % space)
        for t in range(tm)
        for s in range(space)
    ]
    return lax.ppermute(array, ("tm", "space"), pairs)


def exchange(down, up, turn, slant_down, slant_up):
    slanted = moved(slant_down, 1, 1), moved(slant_up, 1, -1)
    return moved(down, 0, 1), moved(up, 0, -1), moved(turn, 1, 0), *slanted


def body(initial, source, diffusivity, growth):
    points, rows, cols = initial.shape
    assert points == POINTS and rows % 8 == 0 and cols % LANES == 0
    depth = cols // LANES
    tm, space = lax.axis_size("tm"), lax.axis_size("space")
    devices = tm * space
    share = cols // devices
    assert share * devices == cols and LANES % share == 0
    assert reach_of() <= REACH and REACH + share + reach_of() <= LANES
    _, _, held = packing(rows, share)
    wide = rows + 2 * MARGIN

    def lines(n):
        return (n * depth, LANES)

    def field(n):
        return (n, depth, LANES)

    def as_rows(array):
        return array.reshape(-1, depth, LANES)

    window_rows = 2 * rows // depth
    assert window_rows * depth == 2 * rows
    raw = [(points // 2, rows, cols), source.shape, (2, rows, cols)]
    sides = count(RIMS_0) + 2 * len(STEPS_0) + window_rows
    behind = count(BEHIND_0) + 2 * len(STEPS_BEHIND_0)
    extra = window_rows if handed_on(space) else 0
    *sends, back = call(
        functools.partial(pack_kernel, share),
        [lines(sides + extra), lines(sides), lines(2 * rows), lines(behind), lines(behind)]
        + [lines(rows)],
        raw + [lines(2 * EDGE * (len(STEPS_0) + len(STEPS_BEHIND_0))), lines(2 * rows)],
        initial, source, diffusivity, growth,
        place=pltpu.HBM, sems=points // 2 + 3,
    )
    apart = direct_windows(space)
    core, *windows = call(
        functools.partial(core_kernel, share),
        [lines(len(CORES) * rows)] + [(2 * rows, LANES)] * len(apart),
        raw,
        initial, source, diffusivity, growth,
        place=pltpu.HBM, sems=points // 2 + 3,
        cost=pl.CostEstimate(flops=0, transcendentals=0, bytes_accessed=CORE_COST),
    )
    above, below, turned, *slanted = exchange(*(as_rows(part) for part in sends))
    turned, back = lax.optimization_barrier((turned, back))
    ahead = as_rows(moved(back, -1, 0))
    windows = [moved(part, 0, by) if by else part for by, part in zip(apart, windows, strict=True)]
    windows = [as_rows(part) for part in windows]
    core = as_rows(core)
    above, below, turned, slanted, ahead, windows = lax.optimization_barrier(
        (above, below, turned, slanted, ahead, windows)
    )

    buffers = [(wide, depth, LANES), (wide, depth, LANES)]
    rim1, rimb = count(RIMS_1), count(BEHIND)
    turn, down, up, slant_down, slant_up, next_odd, forcing, first_forcing, coefs, held_windows = call(
        functools.partial(level0_kernel, tuple(apart)),
        [
            field(2 * rows), field(rim1 + extra), field(rim1), field(rimb), field(rimb),
            field(rows), field(3 * rows), field(rows + 4), field(2 * (rows + 4)),
            field(window_rows * space),
        ],
        [(len(CORES) + 2 + 3 * (POINTS // 2), wide, depth, LANES)] + buffers,
        core, above, below, turned, *slanted, *windows,
    )
    arrived = exchange(down, up, turn, slant_down, slant_up)
    held_rows = FIELDS * 8 + 8 if folded(rows, share, reach_of()) else FIELDS * rows
    slots, next_forcing, late_a, late_b, windows = call(
        functools.partial(level1_kernel, share),
        [
            (devices, held_rows, LANES),
            field(rows), field(rows + 2), field(rows + 2), field(window_rows * space),
        ],
        [(13, wide, depth, LANES)] + buffers + [(FIELDS * rows * depth, LANES)],
        next_odd, forcing, first_forcing, coefs, turn, held_windows, ahead, *arrived,
    )
    slots = lax.all_to_all(slots, ("tm", "space"), 0, 0, tiled=True)
    (slots,) = call(
        functools.partial(sweep_kernel, share, rows),
        [(devices, held, LANES)],
        [(space * rows, LANES), (space * rows, LANES), (tm, space * rows, LANES)]
        + [(LANES // share, 8 + space * rows + 2 * rows + held, LANES)],
        slots, windows.reshape(-1, LANES),
    )
    slots = lax.all_to_all(slots, ("tm", "space"), 0, 0, tiled=True)
    (out,) = call(
        functools.partial(up_kernel, share),
        [(points, rows, cols)],
        [(6, wide, depth, LANES)]
        + buffers
        + [(points * rows * depth, LANES), (points, rows, cols)],
        slots.reshape(devices * held, LANES), next_forcing, late_a, late_b, core, coefs,
        to=pltpu.HBM, sems=points,
    )
    return out


def solution(mesh):
    placed = (P("tm", "space", None), P("tm", "space", None), P("space", None), P("space", None))
    return jax.shard_map(
        body, mesh=mesh, in_specs=placed, out_specs=P("tm", "space", None), check_vma=False
    )
```

```python
import functools

import jax
import jax.numpy as jnp
from jax import lax
from jax.experimental import pallas as pl
from jax.experimental.pallas import tpu as pltpu
from jax.sharding import PartitionSpec as P

LANES = 128
MARGIN = 4
REACH = 32
UP_RIM = 3
POINTS = 8
FIELDS = 3
CORE_COST = 30_000_000
diffusion_number = 0.03
time_step = 0.02

CHAINS = POINTS // 2 - 1
EDGE_0 = 4 * CHAINS + 7
SLANT_0 = 4
EDGE_1 = 5
SLANT_1 = 3
CORES = ("e0", "e1", "e2", "o0", "o1", "o2", "o3", "s0", "s1", "s2", "s3", "d", "g")


def params(mib):
    return pltpu.CompilerParams(vmem_limit_bytes=int(mib * 2**20))


def call(
    kernel, outs, scratch, *args, mib=16, place=pltpu.VMEM, to=pltpu.VMEM, sems=0, cost=None
):
    if place == pltpu.HBM:
        args = [pltpu.with_memory_space_constraint(arg, place) for arg in args]
    return pl.pallas_call(
        kernel,
        out_shape=tuple(jax.ShapeDtypeStruct(shape, jnp.float32) for shape in outs),
        in_specs=[pl.BlockSpec(memory_space=place)] * len(args),
        out_specs=tuple(pl.BlockSpec(memory_space=to) for _ in outs),
        scratch_shapes=[pltpu.VMEM(shape, jnp.float32) for shape in scratch]
        + ([pltpu.SemaphoreType.DMA((sems,))] if sems else []),
        compiler_params=params(mib),
        cost_estimate=cost,
    )(*args)


def beside(mid):
    depth = mid.shape[1]
    lane = lax.broadcasted_iota(jnp.int32, mid.shape, 2)
    line = lax.broadcasted_iota(jnp.int32, mid.shape, 1)
    left = pltpu.roll(mid, 1, 2)
    left_turn = pltpu.roll(left, 1, 1)
    right = pltpu.roll(mid, LANES - 1, 2)
    right_turn = pltpu.roll(right, depth - 1, 1)
    left = jnp.where(lane == 0, jnp.where(line == 0, 0.0, left_turn), left)
    right = jnp.where(lane == LANES - 1, jnp.where(line == depth - 1, 0.0, right_turn), right)
    return left + right


def slope_of_rows(wide, diff, grow):
    mid = wide[1:-1]
    laplace = wide[:-2] + wide[2:] + beside(mid) - 4.0 * mid
    return mid, diff * laplace + grow * mid / (1.0 + mid * mid)


def growth_of(ref, at, rows, diff, grow):
    return slope_of_rows(ref[pl.ds(at - 1, rows + 2)], diff, grow)


def over_rows(rows, rim, body):
    body(MARGIN - rim, rows + 2 * rim)


def flags():
    slab = lax.axis_index("space")
    low = jnp.where(slab > 0, 1.0, 0.0).astype(jnp.float32)
    high = jnp.where(slab < lax.axis_size("space") - 1, 1.0, 0.0).astype(jnp.float32)
    return low, high


def rim_rows(rows, low, high):
    return (
        (lambda k: MARGIN - k, low),
        (lambda k: MARGIN + rows - 1 + k, high),
    )


def pieces(name, evens, source, diffusivity, growth):
    if name == "d":
        return lambda rows, cols: diffusivity[rows, cols] * diffusion_number
    if name == "g":
        return lambda rows, cols: growth[rows, cols] * time_step
    if name == "ep":
        return lambda rows, cols: evens[POINTS // 2 - 1, rows, cols]
    if name == "op":
        return lambda rows, cols: source[POINTS - 1, rows, cols]
    which = int(name[1])
    if name[0] == "e":
        return lambda rows, cols: evens[which, rows, cols]
    return lambda rows, cols: source[2 * which + (name[0] == "o"), rows, cols]


def fetch(initial_all, source_all, diffusivity_all, growth_all, evens, source, coefs, sems):
    pairs = [(initial_all.at[2 * i], evens.at[i]) for i in range(POINTS // 2)]
    pairs += [(diffusivity_all, coefs.at[0]), (growth_all, coefs.at[1]), (source_all, source)]
    copies = [pltpu.make_async_copy(*pair, sems.at[i]) for i, pair in enumerate(pairs)]
    for copy in copies:
        copy.start()
    return copies[:-1], copies[-1]


def target_of(by):
    slabs = lax.axis_size("space")
    return lax.axis_index("tm") * slabs + (lax.axis_index("space") + by) % slabs


SCRATCH = 10


def pack_kernel(
    share, initial_all, source_all, diffusivity_all, growth_all,
    down, up, turn, slant_down, slant_up, back, evens, source, coefs, edge, cells, sems,
):
    waits, last = fetch(
        initial_all, source_all, diffusivity_all, growth_all, evens, source, coefs, sems
    )
    _, rows, cols = coefs.shape
    depth = cols // LANES
    diffusivity, growth = coefs.at[0], coefs.at[1]

    def put(ref, at, name, first, count):
        get = pieces(name, evens, source, diffusivity, growth)
        for c in range(depth):
            place = pl.ds(at * depth + c, count, stride=depth)
            ref[place, :] = get(pl.ds(first, count), pl.ds(c * LANES, LANES))

    def rows_of(ref, at, count):
        return ref[pl.ds(at * depth, count * depth), :].reshape(count, depth, LANES)

    def coef_rows(which, first, count):
        return rows_of(cells, which * rows + first, count)

    chains = [(f"e{i}", f"o{i}", f"s{i + 1}", f"o{i + 1}") for i in range(CHAINS)]
    chains.append(("ep", "op", None, None))
    sides = ((down, slant_down, False), (up, slant_up, True))

    def near(upward, count):
        return 0 if upward else rows - count

    for wait in waits:
        wait.wait()
    for index, name in enumerate(("d", "g")):
        for r in range(0, rows, 8):
            put(cells, index * rows + r, name, r, 8)
    for side, (rim, slant, upward) in enumerate(sides):
        for i, (start, _, _, _) in enumerate(chains):
            put(edge, (2 * i + side) * SCRATCH, start, near(upward, 4), 4)
        for which in range(2):
            put_rows(rim, 4 * CHAINS + 3 + 2 * which, coef_rows(which, near(upward, 2), 2))
    end = EDGE_0 * depth
    for ref, by, at in ((down, 1, end), (up, -1, end), (down, 2, end + 2 * rows)):
        if at < ref.shape[0]:
            for index in range(2):
                get = lambda line: cells[pl.ds(index * rows * depth + line, rows, stride=depth), :]
                ref[pl.ds(at + index * rows, rows), :] = window(
                    get, target_of(by) * share, depth
                )
    put(turn, 0, "ep", 0, 8)
    put(turn, 8, "ep", 8, 8)
    last.wait()
    for side, (rim, slant, upward) in enumerate(sides):
        for i, (_, term, after, after_odd) in enumerate(chains):
            spot = (2 * i + side) * SCRATCH
            put(edge, spot + 4, term, near(upward, 3), 3)
            if after:
                put(edge, spot + 7, after, near(upward, 2), 2)
                put(edge, spot + 9, after_odd, near(upward, 1), 1)
        put(rim, 4 * CHAINS, "s0", near(upward, 2), 2)
        put(rim, 4 * CHAINS + 2, "o0", near(upward, 1), 1)
    for r in range(0, rows, 8):
        put(turn, rows + r, "op", r, 8)
        put(back, r, "s0", r, 8)
    for side, (rim, slant, upward) in enumerate(sides):
        n0, n1, inner = (0, 1, 1) if upward else (rows - 1, rows - 2, rows - 3)
        diff0, diff1, grow1 = coef_rows(0, n0, 1), coef_rows(0, n1, 1), coef_rows(1, n1, 1)
        nothing = jnp.zeros_like(diff0)

        def pick(value, k):
            place = k if upward else value.shape[0] - 1 - k
            return value[place : place + 1]

        for i, (_, _, after, _) in enumerate(chains):
            spot = (2 * i + side) * SCRATCH
            start, term = rows_of(edge, spot, 4), rows_of(edge, spot + 4, 3)
            mid, slope = slope_of_rows(start, coef_rows(0, inner, 2), coef_rows(1, inner, 2))
            inner_term = term[1:] if upward else term[:-1]
            odd = mid + slope + inner_term
            wide = [nothing, odd] if upward else [odd, nothing]
            mid, slope = slope_of_rows(jnp.concatenate(wide, axis=0), diff1, grow1)
            part = mid + slope
            odd1 = pick(odd, 0)
            to, at = (rim, 4 * i) if after else (slant, 0)
            put_rows(to, at, pick(start, 0))
            put_rows(to, at + 1, pick(term, 0) + diff0 * pick(start, 1))
            if after:
                follow = rows_of(edge, spot + 7, 2)
                put_rows(to, at + 2, pick(follow, 0) + diff0 * odd1)
                part = part + pick(follow, 1)
                put_rows(to, at + 3, rows_of(edge, spot + 9, 1) + diff0 * part)
            else:
                put_rows(to, at + 2, odd1)
                put_rows(to, at + 3, part)


def column_of(shape, offset):
    lane = lax.broadcasted_iota(jnp.int32, shape, len(shape) - 1)
    return jnp.where(lane < LANES - REACH, lane, lane - LANES) + offset


def window(get, first, depth):
    line, offset = first // LANES, first % LANES
    source = column_of(get(0).shape, offset)
    shift = (LANES - offset) % LANES
    before = jnp.where(line > 0, pltpu.roll(get(jnp.maximum(line - 1, 0)), shift, 1), 0.0)
    here = pltpu.roll(get(line), shift, 1)
    after = jnp.where(
        line < depth - 1, pltpu.roll(get(jnp.minimum(line + 1, depth - 1)), shift, 1), 0.0
    )
    return jnp.where(source < 0, before, jnp.where(source >= LANES, after, here))


def core_kernel(
    share, initial_all, source_all, diffusivity_all, growth_all, core, *refs
):
    *windows, evens, source, coefs, sems = refs
    waits, last = fetch(
        initial_all, source_all, diffusivity_all, growth_all, evens, source, coefs, sems
    )
    for wait in (*waits, last):
        wait.wait()
    _, rows, cols = coefs.shape
    depth = cols // LANES
    for index, name in enumerate(CORES):
        get = pieces(name, evens, source, coefs.at[0], coefs.at[1])
        for c in range(depth):
            for r in range(0, rows, 8):
                value = get(pl.ds(r, 8), pl.ds(c * LANES, LANES))
                core[pl.ds((index * rows + r) * depth + c, 8, stride=depth), :] = value
    for by, out in zip(direct_windows(lax.axis_size("space")), windows, strict=True):
        for which, name in enumerate(("d", "g")):
            start = CORES.index(name) * rows * depth
            get = lambda line: core[pl.ds(start + line, rows, stride=depth), :]
            out[pl.ds(which * rows, rows)] = window(get, target_of(by) * share, depth)


def handed_on(slabs):
    return slabs == 4


def direct_windows(slabs):
    return [0] if handed_on(slabs) else [0] + list(range(2, slabs - 1))


def level0_kernel(
    apart, core, above, below, behind, behind_above, behind_below, *refs
):
    windows, refs = refs[: len(apart)], refs[len(apart) :]
    (
        turn, down, up, slant_down, slant_up, next_odd, forcing, first_forcing, coefs, held,
        fields, diff, grow,
    ) = refs
    rows = core.shape[0] // len(CORES)
    low, high = flags()
    depth = core.shape[1]
    names = list(CORES) + ["ep", "op"]
    spots = {name: index for index, name in enumerate(names)}
    extra = len(names)
    halves = POINTS // 2
    odd = [extra + i for i in range(halves)]
    even = [extra + halves + i for i in range(halves)]
    image = [extra + 2 * halves + i for i in range(halves)]
    nothing = jnp.zeros((1, depth, LANES), jnp.float32)
    sides = rim_rows(rows, low, high)
    for (at, flag), rim, slant in zip(
        sides, (above, below), (behind_above, behind_below), strict=True
    ):

        def put(name, k, ref, row):
            fields[spots[name] if isinstance(name, str) else name, pl.ds(at(k), 1)] = (
                ref[pl.ds(row, 1)] * flag
            )

        for i in range(CHAINS):
            put(f"e{i}", 1, rim, 4 * i)
            put(f"o{i}", 1, rim, 4 * i + 1)
            put(f"s{i + 1}", 1, rim, 4 * i + 2)
            fields[spots[f"e{i}"], pl.ds(at(2), 1)] = nothing
            fields[odd[i + 1], pl.ds(at(2), 1)] = nothing
        put("ep", 1, slant, 0)
        put("op", 1, slant, 1)
        put(odd[0], 2, slant, 2)
        fields[spots["ep"], pl.ds(at(2), 1)] = nothing
        first_row = min(at(1), at(2))
        edge_at = 4 * CHAINS
        fields[spots["s0"], pl.ds(first_row, 2)] = rim[pl.ds(edge_at, 2)] * flag
        diff[pl.ds(first_row, 2)] = rim[pl.ds(edge_at + 3, 2)] * flag
        grow[pl.ds(first_row, 2)] = rim[pl.ds(edge_at + 5, 2)] * flag
    for name in CORES:
        if name in ("d", "g"):
            buffer = diff if name == "d" else grow
        else:
            buffer = fields.at[spots[name]]
        buffer[pl.ds(MARGIN, rows)] = core[pl.ds(CORES.index(name) * rows, rows)]
    for index, name in enumerate(("ep", "op")):
        fields[spots[name], pl.ds(MARGIN, rows)] = behind[pl.ds(index * rows, rows)]

    def first(at, n):
        d, g = diff[pl.ds(at, n)], grow[pl.ds(at, n)]
        for i in range(halves):
            start, term = ("ep", "op") if i == 0 else (f"e{i - 1}", f"o{i - 1}")
            mid, slope = growth_of(fields.at[spots[start]], at, n, d, g)
            fields[odd[i], pl.ds(at, n)] = mid + slope + fields[spots[term], pl.ds(at, n)]

    def second(at, n):
        d, g = diff[pl.ds(at, n)], grow[pl.ds(at, n)]
        for i in range(halves):
            mid, slope = growth_of(fields.at[odd[i]], at, n, d, g)
            fields[even[i], pl.ds(at, n)] = mid + slope + fields[spots[f"s{i}"], pl.ds(at, n)]

    def third(at, n):
        d, g = diff[pl.ds(at, n)], grow[pl.ds(at, n)]
        for i in range(halves):
            mid, slope = growth_of(fields.at[even[i]], at, n, d, g)
            fields[odd[i], pl.ds(at, n)] = mid + slope + fields[spots[f"o{i}"], pl.ds(at, n)]
            fields[image[i], pl.ds(at, n)] = mid + 2.0 * slope

    def fourth(at, n):
        d, g = diff[pl.ds(at, n)], grow[pl.ds(at, n)]
        here = at - MARGIN
        for i in range(halves):
            mid, slope = growth_of(fields.at[odd[i]], at, n, d, g)
            pair = mid + slope - fields[image[i], pl.ds(at, n)]
            if i == halves - 1:
                turn[pl.ds(here, n)] = pair
            else:
                term = fields[spots[f"s{i + 1}"], pl.ds(at, n)] + pair
                forcing[pl.ds(i * rows + here, n)] = term
                if i == 0:
                    next_odd[...] = fields[image[0], pl.ds(at, n)] + term
                if i == halves - 2:
                    turn[pl.ds(rows + here, n)] = fields[image[i], pl.ds(at, n)] + term

    over_rows(rows, 1, first)
    over_rows(rows, 1, second)
    for (at, flag), rim, slant in zip(
        sides, (above, below), (behind_above, behind_below), strict=True
    ):
        near, far = pl.ds(at(1), 1), pl.ds(at(2), 1)
        for i in range(halves):
            place = 4 * CHAINS + 2 if i == 0 else 4 * i - 1
            fields[spots[f"o{i}"], near] = rim[pl.ds(place, 1)] * flag
            value = diff[far] * fields[odd[i], near]
            if i == 0:
                value = value + fields[spots["s0"], far] + slant[pl.ds(3, 1)] * flag
            fields[even[i], far] = value
    over_rows(rows, 1, third)
    over_rows(rows, 0, fourth)
    first_forcing[...] = fields[spots["s0"], pl.ds(MARGIN - 2, rows + 4)]
    coefs[pl.ds(0, rows + 4)] = diff[pl.ds(MARGIN - 2, rows + 4)]
    coefs[pl.ds(rows + 4, rows + 4)] = grow[pl.ds(MARGIN - 2, rows + 4)]
    for rim, slant, n0, n1 in ((down, slant_down, rows - 1, rows - 2), (up, slant_up, 0, 1)):

        def row(ref, first, n):
            return ref[pl.ds(first + n, 1)]

        diff0 = 2.0 * row(diff, MARGIN, n0)
        around = [
            slope_of_rows(
                ref[pl.ds(first + n1 - 1, 3)], row(diff, MARGIN, n1), row(grow, MARGIN, n1)
            )
            for ref, first in ((next_odd, 0), (turn, rows))
        ]
        (mid, slope), (mid_last, slope_last) = around
        even1 = mid + 2.0 * slope + row(forcing, rows, n1)
        g3 = row(forcing, 2 * rows, n0)
        rim[pl.ds(0, 1)] = row(next_odd, 0, n0)
        rim[pl.ds(1, 1)] = row(forcing, rows, n0) + diff0 * mid
        rim[pl.ds(2, 1)] = g3 + diff0 * even1
        rim[pl.ds(3, 1)] = g3
        rim[pl.ds(4, 1)] = row(forcing, 0, n0)
        slant[pl.ds(0, 1)] = row(turn, rows, n0)
        slant[pl.ds(1, 1)] = row(turn, 0, n0) + diff0 * mid_last
        slant[pl.ds(2, 1)] = row(turn, 0, n1) + mid_last + 2.0 * slope_last
    at = EDGE_1
    extra_rows = down.shape[0] - at
    if extra_rows:
        down[pl.ds(at, extra_rows)] = above[pl.ds(above.shape[0] - extra_rows, extra_rows)]
    slab, slabs = lax.axis_index("space"), lax.axis_size("space")
    size = 2 * rows // depth
    for by, part in (
        *zip(apart, windows, strict=True),
        (1, above.at[pl.ds(EDGE_0, size)]),
        (slabs - 1, below.at[pl.ds(EDGE_0, size)]),
    ):
        held[pl.ds((slab - by) % slabs * size, size)] = part[...]


def take_coefs(rows, coefs, diff, grow):
    diff[pl.ds(MARGIN - 2, rows + 4)] = coefs[pl.ds(0, rows + 4)]
    grow[pl.ds(MARGIN - 2, rows + 4)] = coefs[pl.ds(rows + 4, rows + 4)]


def level1_kernel(
    share, next_odd, forcing, first_forcing, coefs, last_pair, held, ahead,
    above, below, behind, behind_above, behind_below,
    slots, next_forcing, late_a, late_b, windows,
    fields, diff, grow, flat,
):
    rows = forcing.shape[0] // 3
    low, high = flags()
    take_coefs(rows, coefs, diff, grow)
    windows[...] = held[...]
    size = above.shape[0] - EDGE_1
    if size:
        slabs = lax.axis_size("space")
        slab = (lax.axis_index("space") - 2) % slabs
        windows[pl.ds(slab * size, size)] = above[pl.ds(EDGE_1, size)]
    g1, g3, g2, g0, before, after, even0, even1, image0, image1, odd0, odd1 = range(12)
    nothing = jnp.zeros((1, *forcing.shape[1:]), jnp.float32)
    sides = rim_rows(rows, low, high)
    fields[after, pl.ds(MARGIN, rows)] = next_odd[...]
    for which, spot in enumerate((g1, g2, g3)):
        fields[spot, pl.ds(MARGIN, rows)] = forcing[pl.ds(which * rows, rows)]
    fields[before, pl.ds(MARGIN, rows)] = behind[pl.ds(rows, rows)]
    fields[g0, pl.ds(MARGIN, rows)] = first_forcing[pl.ds(2, rows)] + behind[pl.ds(0, rows)]
    for (at, flag), rim, slant in zip(
        sides, (above, below), (behind_above, behind_below), strict=True
    ):
        near, far = pl.ds(at(1), 1), pl.ds(at(2), 1)
        for spot, row in ((after, 0), (g2, 1), (g3, 2), (g1, 4)):
            fields[spot, near] = rim[pl.ds(row, 1)] * flag
        own = [first_forcing[pl.ds(at(k) - MARGIN + 2, 1)] for k in (1, 2)]
        fields[before, near] = slant[pl.ds(0, 1)] * flag
        fields[g0, near] = own[0] + slant[pl.ds(1, 1)] * flag
        fields[even0, far] = own[1] + slant[pl.ds(2, 1)] * flag
        for spot in (after, before, even1):
            fields[spot, far] = nothing

    def second(at, n):
        d, g = diff[pl.ds(at, n)], grow[pl.ds(at, n)]
        for start, term, end in ((before, g0, even0), (after, g2, even1)):
            mid, slope = growth_of(fields.at[start], at, n, d, g)
            fields[end, pl.ds(at, n)] = mid + 2.0 * slope + fields[term, pl.ds(at, n)]

    def third(at, n):
        d, g = diff[pl.ds(at, n)], grow[pl.ds(at, n)]
        for start, term, end, image in ((even0, g1, odd0, image0), (even1, g3, odd1, image1)):
            mid, slope = growth_of(fields.at[start], at, n, d, g)
            fields[end, pl.ds(at, n)] = mid + 2.0 * slope + fields[term, pl.ds(at, n)]
            fields[image, pl.ds(at, n)] = mid + 4.0 * slope

    def fourth(at, n):
        d, g = diff[pl.ds(at, n)], grow[pl.ds(at, n)]
        here = at - MARGIN
        mid, slope = growth_of(fields.at[odd1], at, n, d, g)
        pair1 = mid + 2.0 * slope - fields[image1, pl.ds(at, n)]
        put_rows(flat, rows, ahead[...] + last_pair[pl.ds(0, rows)] + pair1)
        mid, slope = growth_of(fields.at[odd0], at, n, d, g)
        image = fields[image0, pl.ds(at, n)]
        term = fields[g2, pl.ds(at, n)] + (mid + 2.0 * slope - image)
        next_forcing[pl.ds(here, n)] = term
        put_rows(flat, 2 * rows, term)
        put_rows(flat, 0, image + term)

    over_rows(rows, 1, second)
    over_rows(rows, 1, third)
    over_rows(rows, 0, fourth)
    late_a[...] = fields[g1, pl.ds(MARGIN - 1, rows + 2)]
    late_b[pl.ds(1, rows)] = fields[g3, pl.ds(MARGIN, rows)]
    late_b[pl.ds(0, 1)] = above[pl.ds(3, 1)] * low
    late_b[pl.ds(rows + 1, 1)] = below[pl.ds(3, 1)] * high
    depth = forcing.shape[1]
    if folded(rows, share, reach_of()):
        pack_folded(slots, flat, rows, depth, reach_of())
    else:
        pack_windows(slots, flat, rows, depth, share)


def put_rows(flat, first, value):
    depth = value.shape[1]
    for i in range(value.shape[0]):
        flat[pl.ds((first + i) * depth, depth), :] = value[i]


def reach_of():
    return lax.axis_size("tm") + 2


def folded(rows, share, reach):
    return rows == 16 and 2 * share == LANES and FIELDS * 2 * reach <= share


def pack_folded(slots, flat, rows, depth, reach):
    devices = slots.shape[0]
    lane = lax.broadcasted_iota(jnp.int32, (8, LANES), 1)
    place = lane % (LANES // 2)
    rims = [None] * devices
    for field in range(FIELDS):
        first = field * rows * depth
        cells = []
        for line in range(depth):
            top = flat[pl.ds(first + line, 8, stride=depth), :]
            low = flat[pl.ds(first + 8 * depth + line, 8, stride=depth), :]
            cells.append(jnp.where(lane < LANES // 2, top, pltpu.roll(low, LANES // 2, 1)))
            cells.append(jnp.where(lane < LANES // 2, pltpu.roll(top, LANES // 2, 1), low))
        for target in range(devices):
            slots[target, pl.ds(field * 8, 8)] = cells[target]
            left = cells[target - 1] if target > 0 else 0.0
            right = cells[target + 1] if target < devices - 1 else 0.0
            rim = jnp.where(
                place >= LANES // 2 - reach, left, jnp.where(place < reach, right, 0.0)
            )
            if field == 0:
                rims[target] = rim
            else:
                rims[target] = rims[target] + pltpu.roll(rim, 2 * reach * field, 1)
    for target in range(devices):
        slots[target, pl.ds(FIELDS * 8, 8)] = rims[target]


def unfold(slot, field, reach):
    cells, rims = slot[pl.ds(field * 8, 8)], slot[pl.ds(FIELDS * 8, 8)]
    lane = lax.broadcasted_iota(jnp.int32, (8, LANES), 1)
    half = LANES // 2
    back = 2 * reach * field
    top = pltpu.roll(rims, (half - back) % LANES, 1)
    low = pltpu.roll(rims, (-back) % LANES, 1) if back else rims
    return jnp.concatenate(
        [
            jnp.where(lane < half, cells, top),
            jnp.where(lane < half, pltpu.roll(cells, half, 1), low),
        ],
        axis=0,
    )


def pack_windows(slots, flat, rows, depth, share):
    for field in range(FIELDS):
        first = field * rows * depth
        lines = [flat[pl.ds(first + line, rows, stride=depth), :] for line in range(depth)]
        for target in range(slots.shape[0]):
            line, offset = target * share // LANES, target * share % LANES
            shift = (LANES - offset) % LANES
            place = column_of((rows, LANES), offset)
            value = pltpu.roll(lines[line], shift, 1)
            if offset < REACH:
                before = pltpu.roll(lines[line - 1], shift, 1) if line > 0 else 0.0
                value = jnp.where(place < 0, before, value)
            if offset > REACH:
                after = pltpu.roll(lines[line + 1], shift, 1) if line < depth - 1 else 0.0
                value = jnp.where(place >= LANES, after, value)
            slots[target, pl.ds(field * rows, rows)] = value


def late_rows(rows):
    return (rows, -2, rows + 1, -1)


def packing(rows, share):
    groups = LANES // share
    each = -(-(rows + 2 * UP_RIM) // groups)
    return groups, each, -(-(each + -(-4 // groups)) // 8) * 8


def sweep_kernel(share, rows, arrived, windows, slots, diff, grow, terms, padded):
    slabs = lax.axis_size("space")
    devices = arrived.shape[0]
    blocks = devices // slabs
    total = slabs * rows
    reach = reach_of()
    groups, each, held = packing(rows, share)
    for slab in range(slabs):
        diff[pl.ds(slab * rows, rows), :] = windows[pl.ds(2 * slab * rows, rows), :]
        grow[pl.ds(slab * rows, rows), :] = windows[pl.ds((2 * slab + 1) * rows, rows), :]
    line = lax.broadcasted_iota(jnp.int32, (total, LANES), 0)
    lane = lax.broadcasted_iota(jnp.int32, (held, LANES), 1)
    padded[...] = jnp.zeros(padded.shape, jnp.float32)

    def block(field, index):
        parts = []
        for slab in range(slabs):
            slot = arrived.at[index * slabs + slab]
            if folded(rows, share, reach):
                parts.append(unfold(slot, field, reach))
            else:
                parts.append(slot[pl.ds(field * rows, rows)])
        return jnp.concatenate(parts, axis=0)

    def slope_of(field):
        north = jnp.where(line == 0, 0.0, pltpu.roll(field, 1, 0))
        south = jnp.where(line == total - 1, 0.0, pltpu.roll(field, total - 1, 0))
        sides = pltpu.roll(field, 1, 1) + pltpu.roll(field, LANES - 1, 1)
        laplace = north + south + sides - 4.0 * field
        return diff[...] * laplace + grow[...] * field / (1.0 + field * field)

    def put_late(index, slab):
        to = slots.at[index * slabs + slab]
        if folded(rows, share, reach):
            zero = jnp.zeros((2, LANES), jnp.float32)
            low = arrived[index * slabs + slab + 1, pl.ds(16, 2)] if slab < slabs - 1 else zero
            high = arrived[index * slabs + slab - 1, pl.ds(22, 2)] if slab > 0 else zero
            to[pl.ds(each, 2)] = jnp.where(lane[:2] < share, low, high)
            return
        for i, row in enumerate(late_rows(rows)):
            at, group = each + i // groups, i % groups
            beside_slab = slab + row // rows
            if 0 <= beside_slab < slabs:
                place = pl.ds(2 * rows + row % rows, 1)
                piece = arrived[index * slabs + beside_slab, place]
                piece = pltpu.roll(piece, group * share, 1)
            else:
                piece = jnp.zeros((1, LANES), jnp.float32)
            if group:
                piece = jnp.where(lane[:1] >= group * share, piece, to[pl.ds(at, 1)])
            to[pl.ds(at, 1)] = piece

    field = None
    for index in range(blocks):
        behind = (index - 1) % blocks
        odd, term = block(0, behind), block(1, behind)
        even = odd + 4.0 * slope_of(odd) + term
        slope = slope_of(even)
        odd = even + 4.0 * slope + block(2, index)
        stepped = even + 8.0 * slope
        pair = odd + 4.0 * slope_of(odd) - stepped
        terms[index] = block(1, index) + pair
        if index == blocks - 1:
            field = stepped + terms[index]
    for index in range(blocks):
        for group in range(groups):
            padded[group, pl.ds(8, total), :] = (
                pltpu.roll(field, group * share, 1) if group else field
            )
        for slab in range(slabs):
            start = 8 + slab * rows - UP_RIM
            value = padded[0, pl.ds(start, held), :]
            for group in range(1, groups):
                piece = padded[group, pl.ds(start + group * each, held), :]
                value = jnp.where(lane >= group * share, piece, value)
            slots[index * slabs + slab] = value
            put_late(index, slab)
        if index < blocks - 1:
            field = field + 8.0 * slope_of(field) + terms[index]


def up_kernel(
    share, arrived, next_forcing, late_a, late_b, core, coefs,
    out, fields, diff, grow, flat, ready, sems,
):
    rows, depth, _ = next_forcing.shape
    groups, each, held = packing(rows, share)
    take_coefs(rows, coefs, diff, grow)
    lane = lax.broadcasted_iota(jnp.int32, (depth, LANES), 1)

    def whole(line, group):
        value = None
        for part in range(groups):
            piece = arrived[pl.ds(part * held + line, depth, stride=groups * held), :]
            if part != group:
                piece = pltpu.roll(piece, ((part - group) * share) % LANES, 1)
            value = piece if value is None else jnp.where(lane >= part * share, piece, value)
        return value

    for row in range(rows + 2 * UP_RIM):
        fields[0, MARGIN - UP_RIM + row] = whole(row % each, row // each)
    for i, row in enumerate(late_rows(rows)):
        fields[5, MARGIN + row] = whole(each + i // groups, i % groups)
    fields[5, pl.ds(MARGIN, rows)] = next_forcing[...]
    odd_first = CORES.index("o0") * rows

    def first(at, n):
        mid, slope = growth_of(fields.at[0], at, n, diff[pl.ds(at, n)], grow[pl.ds(at, n)])
        fields[2, pl.ds(at, n)] = mid + 4.0 * slope + fields[5, pl.ds(at, n)]

    def second(at, n):
        d, g = diff[pl.ds(at, n)], grow[pl.ds(at, n)]
        for start, late in ((0, late_a), (2, late_b)):
            mid, slope = growth_of(fields.at[start], at, n, d, g)
            fields[start + 1, pl.ds(at, n)] = mid + 2.0 * slope + late[pl.ds(at - MARGIN + 1, n)]

    copies = []

    def emit(point, value):
        put_rows(flat, point * rows, value)
        for r in range(0, rows, 8):
            for c in range(depth):
                start = (point * rows + r) * depth + c
                ready[point, pl.ds(r, 8), pl.ds(c * LANES, LANES)] = flat[
                    pl.ds(start, 8, stride=depth), :
                ]
        copy = pltpu.make_async_copy(ready.at[point], out.at[point], sems.at[point])
        copy.start()
        copies.append(copy)

    def last(i):
        at, n = MARGIN, rows
        mid, slope = growth_of(fields.at[i], at, n, diff[pl.ds(at, n)], grow[pl.ds(at, n)])
        emit(2 * i + 1, mid + slope + core[pl.ds(odd_first + i * rows, n)])

    core_rows = pl.ds(MARGIN, rows)
    emit(0, fields[0, core_rows])
    over_rows(rows, 2, first)
    emit(4, fields[2, core_rows])
    over_rows(rows, 1, second)
    emit(2, fields[1, core_rows])
    emit(6, fields[3, core_rows])
    for i in (0, 2, 1, 3):
        last(i)
    for copy in copies:
        copy.wait()


def moved(array, blocks, slabs):
    tm, space = lax.axis_size("tm"), lax.axis_size("space")
    pairs = [
        (t * space + s, (t + blocks) % tm * space + (s + slabs) % space)
        for t in range(tm)
        for s in range(space)
    ]
    return lax.ppermute(array, ("tm", "space"), pairs)


def exchange(down, up, turn, slant_down, slant_up):
    slanted = moved(slant_down, 1, 1), moved(slant_up, 1, -1)
    return moved(down, 0, 1), moved(up, 0, -1), moved(turn, 1, 0), *slanted


def body(initial, source, diffusivity, growth):
    points, rows, cols = initial.shape
    assert points == POINTS and rows % 8 == 0 and cols % LANES == 0
    depth = cols // LANES
    tm, space = lax.axis_size("tm"), lax.axis_size("space")
    devices = tm * space
    share = cols // devices
    assert share * devices == cols and LANES % share == 0
    assert reach_of() <= REACH and REACH + share + reach_of() <= LANES
    _, _, held = packing(rows, share)
    wide = rows + 2 * MARGIN

    def lines(n):
        return (n * depth, LANES)

    def field(n):
        return (n, depth, LANES)

    def as_rows(array):
        return array.reshape(-1, depth, LANES)

    window_rows = 2 * rows // depth
    assert window_rows * depth == 2 * rows
    raw = [(points // 2, rows, cols), source.shape, (2, rows, cols)]
    sides = EDGE_0 + window_rows
    extra = window_rows if handed_on(space) else 0
    *sends, back = call(
        functools.partial(pack_kernel, share),
        [lines(sides + extra), lines(sides), lines(2 * rows), lines(SLANT_0), lines(SLANT_0)]
        + [lines(rows)],
        raw + [lines(2 * SCRATCH * (CHAINS + 1)), lines(2 * rows)],
        initial, source, diffusivity, growth,
        place=pltpu.HBM, sems=points // 2 + 3,
    )
    apart = direct_windows(space)
    core, *windows = call(
        functools.partial(core_kernel, share),
        [lines(len(CORES) * rows)] + [(2 * rows, LANES)] * len(apart),
        raw,
        initial, source, diffusivity, growth,
        place=pltpu.HBM, sems=points // 2 + 3,
        cost=pl.CostEstimate(flops=0, transcendentals=0, bytes_accessed=CORE_COST),
    )
    above, below, turned, *slanted = exchange(*(as_rows(part) for part in sends))
    turned, back = lax.optimization_barrier((turned, back))
    ahead = as_rows(moved(back, -1, 0))
    windows = [moved(part, 0, by) if by else part for by, part in zip(apart, windows, strict=True)]
    windows = [as_rows(part) for part in windows]
    core = as_rows(core)
    above, below, turned, slanted, ahead, windows = lax.optimization_barrier(
        (above, below, turned, slanted, ahead, windows)
    )

    buffers = [(wide, depth, LANES), (wide, depth, LANES)]
    turn, down, up, slant_down, slant_up, next_odd, forcing, first_forcing, coefs, held_windows = call(
        functools.partial(level0_kernel, tuple(apart)),
        [
            field(2 * rows), field(EDGE_1 + extra), field(EDGE_1), field(SLANT_1), field(SLANT_1),
            field(rows), field(3 * rows), field(rows + 4), field(2 * (rows + 4)),
            field(window_rows * space),
        ],
        [(len(CORES) + 2 + 3 * (POINTS // 2), wide, depth, LANES)] + buffers,
        core, above, below, turned, *slanted, *windows,
    )
    arrived = exchange(down, up, turn, slant_down, slant_up)
    held_rows = FIELDS * 8 + 8 if folded(rows, share, reach_of()) else FIELDS * rows
    slots, next_forcing, late_a, late_b, windows = call(
        functools.partial(level1_kernel, share),
        [
            (devices, held_rows, LANES),
            field(rows), field(rows + 2), field(rows + 2), field(window_rows * space),
        ],
        [(12, wide, depth, LANES)] + buffers + [(FIELDS * rows * depth, LANES)],
        next_odd, forcing, first_forcing, coefs, turn, held_windows, ahead, *arrived,
    )
    slots = lax.all_to_all(slots, ("tm", "space"), 0, 0, tiled=True)
    (slots,) = call(
        functools.partial(sweep_kernel, share, rows),
        [(devices, held, LANES)],
        [(space * rows, LANES), (space * rows, LANES), (tm, space * rows, LANES)]
        + [(LANES // share, 8 + space * rows + 2 * rows + held, LANES)],
        slots, windows.reshape(-1, LANES),
    )
    slots = lax.all_to_all(slots, ("tm", "space"), 0, 0, tiled=True)
    (out,) = call(
        functools.partial(up_kernel, share),
        [(points, rows, cols)],
        [(6, wide, depth, LANES)]
        + buffers
        + [(points * rows * depth, LANES), (points, rows, cols)],
        slots.reshape(devices * held, LANES), next_forcing, late_a, late_b, core, coefs,
        to=pltpu.HBM, sems=points,
    )
    return out


def solution(mesh):
    placed = (P("tm", "space", None), P("tm", "space", None), P("space", None), P("space", None))
    return jax.shard_map(
        body, mesh=mesh, in_specs=placed, out_specs=P("tm", "space", None), check_vma=False
    )
```

```python
import functools

import jax
import jax.numpy as jnp
from jax import lax
from jax.experimental import pallas as pl
from jax.experimental.pallas import tpu as pltpu
from jax.sharding import PartitionSpec as P

LANES = 128
MARGIN = 4
REACH = 32
UP_RIM = 3
POINTS = 8
FIELDS = 3
CORE_COST = 30_000_000
diffusion_number = 0.03
time_step = 0.02

CHAINS = POINTS // 2 - 1
EDGE_0 = 4 * CHAINS + 7
SLANT_0 = 4
TURN = 2
EDGE_1 = 5
SLANT_1 = 3
CORES = ("e0", "e1", "e2", "o0", "o1", "o2", "o3", "s0", "s1", "s2", "s3", "d", "g")


def params(mib):
    return pltpu.CompilerParams(vmem_limit_bytes=int(mib * 2**20))


def call(
    kernel, outs, scratch, *args, mib=16, place=pltpu.VMEM, to=pltpu.VMEM, sems=0, cost=None
):
    if place == pltpu.HBM:
        args = [pltpu.with_memory_space_constraint(arg, place) for arg in args]
    return pl.pallas_call(
        kernel,
        out_shape=tuple(jax.ShapeDtypeStruct(shape, jnp.float32) for shape in outs),
        in_specs=[pl.BlockSpec(memory_space=place)] * len(args),
        out_specs=tuple(pl.BlockSpec(memory_space=to) for _ in outs),
        scratch_shapes=[pltpu.VMEM(shape, jnp.float32) for shape in scratch]
        + ([pltpu.SemaphoreType.DMA((sems,))] if sems else []),
        compiler_params=params(mib),
        cost_estimate=cost,
    )(*args)


def beside(mid):
    depth = mid.shape[1]
    lane = lax.broadcasted_iota(jnp.int32, mid.shape, 2)
    line = lax.broadcasted_iota(jnp.int32, mid.shape, 1)
    left = pltpu.roll(mid, 1, 2)
    left_turn = pltpu.roll(left, 1, 1)
    right = pltpu.roll(mid, LANES - 1, 2)
    right_turn = pltpu.roll(right, depth - 1, 1)
    left = jnp.where(lane == 0, jnp.where(line == 0, 0.0, left_turn), left)
    right = jnp.where(lane == LANES - 1, jnp.where(line == depth - 1, 0.0, right_turn), right)
    return left + right


def slope_of_rows(wide, diff, grow):
    mid = wide[1:-1]
    laplace = wide[:-2] + wide[2:] + beside(mid) - 4.0 * mid
    return mid, diff * laplace + grow * mid / (1.0 + mid * mid)


def growth_of(ref, at, rows, diff, grow):
    return slope_of_rows(ref[pl.ds(at - 1, rows + 2)], diff, grow)


def over_rows(rows, rim, body):
    body(MARGIN - rim, rows + 2 * rim)


def flags():
    slab = lax.axis_index("space")
    low = jnp.where(slab > 0, 1.0, 0.0).astype(jnp.float32)
    high = jnp.where(slab < lax.axis_size("space") - 1, 1.0, 0.0).astype(jnp.float32)
    return low, high


def rim_rows(rows, low, high):
    return (
        (lambda k: MARGIN - k, low),
        (lambda k: MARGIN + rows - 1 + k, high),
    )


def pieces(name, evens, source, diffusivity, growth):
    if name == "d":
        return lambda rows, cols: diffusivity[rows, cols] * diffusion_number
    if name == "g":
        return lambda rows, cols: growth[rows, cols] * time_step
    if name == "ep":
        return lambda rows, cols: evens[POINTS // 2 - 1, rows, cols]
    if name == "op":
        return lambda rows, cols: source[POINTS - 1, rows, cols]
    which = int(name[1])
    if name[0] == "e":
        return lambda rows, cols: evens[which, rows, cols]
    return lambda rows, cols: source[2 * which + (name[0] == "o"), rows, cols]


def fetch(initial_all, source_all, diffusivity_all, growth_all, evens, source, coefs, sems):
    pairs = [(initial_all.at[2 * i], evens.at[i]) for i in range(POINTS // 2)]
    pairs += [(diffusivity_all, coefs.at[0]), (growth_all, coefs.at[1]), (source_all, source)]
    copies = [pltpu.make_async_copy(*pair, sems.at[i]) for i, pair in enumerate(pairs)]
    for copy in copies:
        copy.start()
    return copies[:-1], copies[-1]


def target_of(by):
    slabs = lax.axis_size("space")
    return lax.axis_index("tm") * slabs + (lax.axis_index("space") + by) % slabs


SCRATCH = 10


def pack_kernel(
    share, initial_all, source_all, diffusivity_all, growth_all,
    down, up, slant_down, slant_up, inward, outward,
    evens, source, coefs, edge, cells, turn, sems,
):
    waits, last = fetch(
        initial_all, source_all, diffusivity_all, growth_all, evens, source, coefs, sems
    )
    _, rows, cols = coefs.shape
    depth = cols // LANES
    diffusivity, growth = coefs.at[0], coefs.at[1]

    def put(ref, at, name, first, count):
        get = pieces(name, evens, source, diffusivity, growth)
        for c in range(depth):
            place = pl.ds(at * depth + c, count, stride=depth)
            ref[place, :] = get(pl.ds(first, count), pl.ds(c * LANES, LANES))

    def rows_of(ref, at, count):
        return ref[pl.ds(at * depth, count * depth), :].reshape(count, depth, LANES)

    def coef_rows(which, first, count):
        return rows_of(cells, which * rows + first, count)

    chains = [(f"e{i}", f"o{i}", f"s{i + 1}", f"o{i + 1}") for i in range(CHAINS)]
    chains.append(("ep", "op", None, None))
    sides = ((down, slant_down, False), (up, slant_up, True))

    def near(upward, count):
        return 0 if upward else rows - count

    for wait in waits:
        wait.wait()
    for index, name in enumerate(("d", "g")):
        for r in range(0, rows, 8):
            put(cells, index * rows + r, name, r, 8)
    for side, (rim, slant, upward) in enumerate(sides):
        for i, (start, _, _, _) in enumerate(chains):
            put(edge, (2 * i + side) * SCRATCH, start, near(upward, 4), 4)
        for which in range(2):
            put_rows(rim, 4 * CHAINS + 3 + 2 * which, coef_rows(which, near(upward, 2), 2))
    end = EDGE_0 * depth
    for ref, by, at in ((down, 1, end), (up, -1, end), (down, 2, end + 2 * rows)):
        if at < ref.shape[0]:
            for index in range(2):
                get = lambda line: cells[pl.ds(index * rows * depth + line, rows, stride=depth), :]
                ref[pl.ds(at + index * rows, rows), :] = window(
                    get, target_of(by) * share, depth
                )
    put_rows(turn, 0, jnp.zeros((1, depth, LANES), jnp.float32))
    for r in range(0, rows, 8):
        put(turn, 1 + r, "ep", r, 8)
    put_rows(turn, rows + 1, jnp.zeros((1, depth, LANES), jnp.float32))
    last.wait()
    for side, (rim, slant, upward) in enumerate(sides):
        for i, (_, term, after, after_odd) in enumerate(chains):
            spot = (2 * i + side) * SCRATCH
            put(edge, spot + 4, term, near(upward, 3), 3)
            if after:
                put(edge, spot + 7, after, near(upward, 2), 2)
                put(edge, spot + 9, after_odd, near(upward, 1), 1)
        put(rim, 4 * CHAINS, "s0", near(upward, 2), 2)
        put(rim, 4 * CHAINS + 2, "o0", near(upward, 1), 1)
    for r in range(0, rows, 8):
        put(turn, rows + 2 + r, "op", r, 8)
        put(turn, 2 * rows + 2 + r, "s0", r, 8)
    ahead = lax.axis_index("tm") % 2 == 0
    wide = rows_of(turn, 0, rows + 2)
    mid, slope = slope_of_rows(wide, coef_rows(0, 0, rows), coef_rows(1, 0, rows))
    forward = mid + slope + rows_of(turn, rows + 2, rows)
    backward = rows_of(turn, 2 * rows + 2, rows)
    put_rows(inward, 0, jnp.where(ahead, forward, backward))
    put_rows(outward, 0, jnp.where(ahead, backward, forward))
    for i, row in enumerate((1, rows)):
        for to in (inward, outward):
            put_rows(to, rows + i, rows_of(turn, row, 1))
    for side, (rim, slant, upward) in enumerate(sides):
        n0, n1, inner = (0, 1, 1) if upward else (rows - 1, rows - 2, rows - 3)
        diff0, diff1, grow1 = coef_rows(0, n0, 1), coef_rows(0, n1, 1), coef_rows(1, n1, 1)
        nothing = jnp.zeros_like(diff0)

        def pick(value, k):
            place = k if upward else value.shape[0] - 1 - k
            return value[place : place + 1]

        for i, (_, _, after, _) in enumerate(chains):
            spot = (2 * i + side) * SCRATCH
            start, term = rows_of(edge, spot, 4), rows_of(edge, spot + 4, 3)
            mid, slope = slope_of_rows(start, coef_rows(0, inner, 2), coef_rows(1, inner, 2))
            inner_term = term[1:] if upward else term[:-1]
            odd = mid + slope + inner_term
            wide = [nothing, odd] if upward else [odd, nothing]
            mid, slope = slope_of_rows(jnp.concatenate(wide, axis=0), diff1, grow1)
            part = mid + slope
            odd1 = pick(odd, 0)
            to, at = (rim, 4 * i) if after else (slant, 0)
            put_rows(to, at, pick(start, 0))
            put_rows(to, at + 1, pick(term, 0) + diff0 * pick(start, 1))
            if after:
                follow = rows_of(edge, spot + 7, 2)
                put_rows(to, at + 2, pick(follow, 0) + diff0 * odd1)
                part = part + pick(follow, 1)
                put_rows(to, at + 3, rows_of(edge, spot + 9, 1) + diff0 * part)
            else:
                put_rows(to, at + 2, odd1)
                put_rows(to, at + 3, part)


def column_of(shape, offset):
    lane = lax.broadcasted_iota(jnp.int32, shape, len(shape) - 1)
    return jnp.where(lane < LANES - REACH, lane, lane - LANES) + offset


def window(get, first, depth):
    line, offset = first // LANES, first % LANES
    source = column_of(get(0).shape, offset)
    shift = (LANES - offset) % LANES
    before = jnp.where(line > 0, pltpu.roll(get(jnp.maximum(line - 1, 0)), shift, 1), 0.0)
    here = pltpu.roll(get(line), shift, 1)
    after = jnp.where(
        line < depth - 1, pltpu.roll(get(jnp.minimum(line + 1, depth - 1)), shift, 1), 0.0
    )
    return jnp.where(source < 0, before, jnp.where(source >= LANES, after, here))


def core_kernel(
    share, initial_all, source_all, diffusivity_all, growth_all, core, *refs
):
    *windows, evens, source, coefs, sems = refs
    waits, last = fetch(
        initial_all, source_all, diffusivity_all, growth_all, evens, source, coefs, sems
    )
    for wait in (*waits, last):
        wait.wait()
    _, rows, cols = coefs.shape
    depth = cols // LANES
    for index, name in enumerate(CORES):
        get = pieces(name, evens, source, coefs.at[0], coefs.at[1])
        for c in range(depth):
            for r in range(0, rows, 8):
                value = get(pl.ds(r, 8), pl.ds(c * LANES, LANES))
                core[pl.ds((index * rows + r) * depth + c, 8, stride=depth), :] = value
    for by, out in zip(direct_windows(lax.axis_size("space")), windows, strict=True):
        for which, name in enumerate(("d", "g")):
            start = CORES.index(name) * rows * depth
            get = lambda line: core[pl.ds(start + line, rows, stride=depth), :]
            out[pl.ds(which * rows, rows)] = window(get, target_of(by) * share, depth)


def handed_on(slabs):
    return slabs == 4


def direct_windows(slabs):
    return [0] if handed_on(slabs) else [0] + list(range(2, slabs - 1))


def level0_kernel(
    apart, core, above, below, behind_above, behind_below, inward, outward, *refs
):
    windows, refs = refs[: len(apart)], refs[len(apart) :]
    (
        turn, down, up, slant_down, slant_up, next_odd, forcing, first_forcing, coefs, held,
        behind_part, fields, diff, grow,
    ) = refs
    rows = core.shape[0] // len(CORES)
    low, high = flags()
    depth = core.shape[1]
    names = list(CORES) + ["ep", "op"]
    spots = {name: index for index, name in enumerate(names)}
    extra = len(names)
    halves = POINTS // 2
    odd = [extra + i for i in range(halves)]
    even = [extra + halves + i for i in range(halves)]
    image = [extra + 2 * halves + i for i in range(halves)]
    nothing = jnp.zeros((1, depth, LANES), jnp.float32)
    sides = rim_rows(rows, low, high)
    for (at, flag), rim, slant in zip(
        sides, (above, below), (behind_above, behind_below), strict=True
    ):

        def put(name, k, ref, row):
            fields[spots[name] if isinstance(name, str) else name, pl.ds(at(k), 1)] = (
                ref[pl.ds(row, 1)] * flag
            )

        for i in range(CHAINS):
            put(f"e{i}", 1, rim, 4 * i)
            put(f"o{i}", 1, rim, 4 * i + 1)
            put(f"s{i + 1}", 1, rim, 4 * i + 2)
            fields[spots[f"e{i}"], pl.ds(at(2), 1)] = nothing
            fields[odd[i + 1], pl.ds(at(2), 1)] = nothing
        put("ep", 1, slant, 0)
        put("op", 1, slant, 1)
        put(odd[0], 2, slant, 2)
        fields[spots["ep"], pl.ds(at(2), 1)] = nothing
        first_row = min(at(1), at(2))
        edge_at = 4 * CHAINS
        fields[spots["s0"], pl.ds(first_row, 2)] = rim[pl.ds(edge_at, 2)] * flag
        diff[pl.ds(first_row, 2)] = rim[pl.ds(edge_at + 3, 2)] * flag
        grow[pl.ds(first_row, 2)] = rim[pl.ds(edge_at + 5, 2)] * flag
    for name in CORES:
        if name in ("d", "g"):
            buffer = diff if name == "d" else grow
        else:
            buffer = fields.at[spots[name]]
        buffer[pl.ds(MARGIN, rows)] = core[pl.ds(CORES.index(name) * rows, rows)]
    even_block = lax.axis_index("tm") % 2 == 0
    cells = pl.ds(0, rows)
    from_behind = jnp.where(even_block, outward[cells], inward[cells])
    ahead = jnp.where(even_block, inward[cells], outward[cells])
    fields[odd[0], pl.ds(MARGIN, rows)] = from_behind
    for (at, _), row, edge_row in zip(sides, (0, 1), (0, rows - 1), strict=True):
        edge = pl.ds(rows + row, 1)
        fields[spots["ep"], pl.ds(MARGIN + edge_row, 1)] = jnp.where(
            even_block, outward[edge], inward[edge]
        )
        near, first = pl.ds(at(1), 1), pl.ds(MARGIN + edge_row, 1)
        mid, slope = growth_of(fields.at[spots["ep"]], at(1), 1, diff[near], grow[near])
        fields[odd[0], near] = mid + slope + fields[spots["op"], near]
        fields[odd[0], first] = fields[odd[0], first] + diff[first] * mid

    def first(at, n):
        d, g = diff[pl.ds(at, n)], grow[pl.ds(at, n)]
        for i in range(CHAINS):
            mid, slope = growth_of(fields.at[spots[f"e{i}"]], at, n, d, g)
            fields[odd[i + 1], pl.ds(at, n)] = mid + slope + fields[spots[f"o{i}"], pl.ds(at, n)]

    def second(at, n):
        d, g = diff[pl.ds(at, n)], grow[pl.ds(at, n)]
        for i in range(halves):
            mid, slope = growth_of(fields.at[odd[i]], at, n, d, g)
            fields[even[i], pl.ds(at, n)] = mid + slope + fields[spots[f"s{i}"], pl.ds(at, n)]

    def third(at, n):
        d, g = diff[pl.ds(at, n)], grow[pl.ds(at, n)]
        for i in range(halves):
            mid, slope = growth_of(fields.at[even[i]], at, n, d, g)
            fields[odd[i], pl.ds(at, n)] = mid + slope + fields[spots[f"o{i}"], pl.ds(at, n)]
            fields[image[i], pl.ds(at, n)] = mid + 2.0 * slope

    def fourth(at, n):
        d, g = diff[pl.ds(at, n)], grow[pl.ds(at, n)]
        here = at - MARGIN
        for i in range(halves):
            mid, slope = growth_of(fields.at[odd[i]], at, n, d, g)
            pair = mid + slope - fields[image[i], pl.ds(at, n)]
            if i == halves - 1:
                turn[pl.ds(here, n)] = pair
                behind_part[...] = ahead + pair
            else:
                term = fields[spots[f"s{i + 1}"], pl.ds(at, n)] + pair
                forcing[pl.ds(i * rows + here, n)] = term
                if i == 0:
                    next_odd[...] = fields[image[0], pl.ds(at, n)] + term
                if i == halves - 2:
                    turn[pl.ds(rows + here, n)] = fields[image[i], pl.ds(at, n)] + term

    over_rows(rows, 1, first)
    over_rows(rows, 1, second)
    for (at, flag), rim, slant in zip(
        sides, (above, below), (behind_above, behind_below), strict=True
    ):
        near, far = pl.ds(at(1), 1), pl.ds(at(2), 1)
        for i in range(halves):
            place = 4 * CHAINS + 2 if i == 0 else 4 * i - 1
            fields[spots[f"o{i}"], near] = rim[pl.ds(place, 1)] * flag
            value = diff[far] * fields[odd[i], near]
            if i == 0:
                value = value + fields[spots["s0"], far] + slant[pl.ds(3, 1)] * flag
            fields[even[i], far] = value
    over_rows(rows, 1, third)
    over_rows(rows, 0, fourth)
    first_forcing[...] = fields[spots["s0"], pl.ds(MARGIN - 2, rows + 4)]
    coefs[pl.ds(0, rows + 4)] = diff[pl.ds(MARGIN - 2, rows + 4)]
    coefs[pl.ds(rows + 4, rows + 4)] = grow[pl.ds(MARGIN - 2, rows + 4)]
    for rim, slant, n0, n1 in ((down, slant_down, rows - 1, rows - 2), (up, slant_up, 0, 1)):

        def row(ref, first, n):
            return ref[pl.ds(first + n, 1)]

        diff0 = 2.0 * row(diff, MARGIN, n0)
        around = [
            slope_of_rows(
                ref[pl.ds(first + n1 - 1, 3)], row(diff, MARGIN, n1), row(grow, MARGIN, n1)
            )
            for ref, first in ((next_odd, 0), (turn, rows))
        ]
        (mid, slope), (mid_last, slope_last) = around
        even1 = mid + 2.0 * slope + row(forcing, rows, n1)
        g3 = row(forcing, 2 * rows, n0)
        rim[pl.ds(0, 1)] = row(next_odd, 0, n0)
        rim[pl.ds(1, 1)] = row(forcing, rows, n0) + diff0 * mid
        rim[pl.ds(2, 1)] = g3 + diff0 * even1
        rim[pl.ds(3, 1)] = g3
        rim[pl.ds(4, 1)] = row(forcing, 0, n0)
        slant[pl.ds(0, 1)] = row(turn, rows, n0)
        slant[pl.ds(1, 1)] = row(turn, 0, n0) + diff0 * mid_last
        slant[pl.ds(2, 1)] = row(turn, 0, n1) + mid_last + 2.0 * slope_last
    at = EDGE_1
    extra_rows = down.shape[0] - at
    if extra_rows:
        down[pl.ds(at, extra_rows)] = above[pl.ds(above.shape[0] - extra_rows, extra_rows)]
    slab, slabs = lax.axis_index("space"), lax.axis_size("space")
    size = 2 * rows // depth
    for by, part in (
        *zip(apart, windows, strict=True),
        (1, above.at[pl.ds(EDGE_0, size)]),
        (slabs - 1, below.at[pl.ds(EDGE_0, size)]),
    ):
        held[pl.ds((slab - by) % slabs * size, size)] = part[...]


def take_coefs(rows, coefs, diff, grow):
    diff[pl.ds(MARGIN - 2, rows + 4)] = coefs[pl.ds(0, rows + 4)]
    grow[pl.ds(MARGIN - 2, rows + 4)] = coefs[pl.ds(rows + 4, rows + 4)]


def level1_kernel(
    share, next_odd, forcing, first_forcing, coefs, behind_part, held,
    above, below, behind, behind_above, behind_below,
    slots, next_forcing, late_a, late_b, windows,
    fields, diff, grow, flat,
):
    rows = forcing.shape[0] // 3
    low, high = flags()
    take_coefs(rows, coefs, diff, grow)
    windows[...] = held[...]
    size = above.shape[0] - EDGE_1
    if size:
        slabs = lax.axis_size("space")
        slab = (lax.axis_index("space") - 2) % slabs
        windows[pl.ds(slab * size, size)] = above[pl.ds(EDGE_1, size)]
    g1, g3, g2, g0, before, after, even0, even1, image0, image1, odd0, odd1 = range(12)
    nothing = jnp.zeros((1, *forcing.shape[1:]), jnp.float32)
    sides = rim_rows(rows, low, high)
    fields[after, pl.ds(MARGIN, rows)] = next_odd[...]
    for which, spot in enumerate((g1, g2, g3)):
        fields[spot, pl.ds(MARGIN, rows)] = forcing[pl.ds(which * rows, rows)]
    fields[before, pl.ds(MARGIN, rows)] = behind[pl.ds(rows, rows)]
    fields[g0, pl.ds(MARGIN, rows)] = first_forcing[pl.ds(2, rows)] + behind[pl.ds(0, rows)]
    for (at, flag), rim, slant in zip(
        sides, (above, below), (behind_above, behind_below), strict=True
    ):
        near, far = pl.ds(at(1), 1), pl.ds(at(2), 1)
        for spot, row in ((after, 0), (g2, 1), (g3, 2), (g1, 4)):
            fields[spot, near] = rim[pl.ds(row, 1)] * flag
        own = [first_forcing[pl.ds(at(k) - MARGIN + 2, 1)] for k in (1, 2)]
        fields[before, near] = slant[pl.ds(0, 1)] * flag
        fields[g0, near] = own[0] + slant[pl.ds(1, 1)] * flag
        fields[even0, far] = own[1] + slant[pl.ds(2, 1)] * flag
        for spot in (after, before, even1):
            fields[spot, far] = nothing

    def second(at, n):
        d, g = diff[pl.ds(at, n)], grow[pl.ds(at, n)]
        for start, term, end in ((before, g0, even0), (after, g2, even1)):
            mid, slope = growth_of(fields.at[start], at, n, d, g)
            fields[end, pl.ds(at, n)] = mid + 2.0 * slope + fields[term, pl.ds(at, n)]

    def third(at, n):
        d, g = diff[pl.ds(at, n)], grow[pl.ds(at, n)]
        for start, term, end, image in ((even0, g1, odd0, image0), (even1, g3, odd1, image1)):
            mid, slope = growth_of(fields.at[start], at, n, d, g)
            fields[end, pl.ds(at, n)] = mid + 2.0 * slope + fields[term, pl.ds(at, n)]
            fields[image, pl.ds(at, n)] = mid + 4.0 * slope

    def fourth(at, n):
        d, g = diff[pl.ds(at, n)], grow[pl.ds(at, n)]
        here = at - MARGIN
        mid, slope = growth_of(fields.at[odd1], at, n, d, g)
        pair1 = mid + 2.0 * slope - fields[image1, pl.ds(at, n)]
        put_rows(flat, rows, behind_part[...] + pair1)
        mid, slope = growth_of(fields.at[odd0], at, n, d, g)
        image = fields[image0, pl.ds(at, n)]
        term = fields[g2, pl.ds(at, n)] + (mid + 2.0 * slope - image)
        next_forcing[pl.ds(here, n)] = term
        put_rows(flat, 2 * rows, term)
        put_rows(flat, 0, image + term)

    over_rows(rows, 1, second)
    over_rows(rows, 1, third)
    over_rows(rows, 0, fourth)
    late_a[...] = fields[g1, pl.ds(MARGIN - 1, rows + 2)]
    late_b[pl.ds(1, rows)] = fields[g3, pl.ds(MARGIN, rows)]
    late_b[pl.ds(0, 1)] = above[pl.ds(3, 1)] * low
    late_b[pl.ds(rows + 1, 1)] = below[pl.ds(3, 1)] * high
    depth = forcing.shape[1]
    if folded(rows, share, reach_of()):
        pack_folded(slots, flat, rows, depth, reach_of())
    else:
        pack_windows(slots, flat, rows, depth, share)


def put_rows(flat, first, value):
    depth = value.shape[1]
    for i in range(value.shape[0]):
        flat[pl.ds((first + i) * depth, depth), :] = value[i]


def reach_of():
    return lax.axis_size("tm") + 2


def folded(rows, share, reach):
    return rows == 16 and 2 * share == LANES and FIELDS * 2 * reach <= share


def pack_folded(slots, flat, rows, depth, reach):
    devices = slots.shape[0]
    lane = lax.broadcasted_iota(jnp.int32, (8, LANES), 1)
    place = lane % (LANES // 2)
    rims = [None] * devices
    for field in range(FIELDS):
        first = field * rows * depth
        cells = []
        for line in range(depth):
            top = flat[pl.ds(first + line, 8, stride=depth), :]
            low = flat[pl.ds(first + 8 * depth + line, 8, stride=depth), :]
            cells.append(jnp.where(lane < LANES // 2, top, pltpu.roll(low, LANES // 2, 1)))
            cells.append(jnp.where(lane < LANES // 2, pltpu.roll(top, LANES // 2, 1), low))
        for target in range(devices):
            slots[target, pl.ds(field * 8, 8)] = cells[target]
            left = cells[target - 1] if target > 0 else 0.0
            right = cells[target + 1] if target < devices - 1 else 0.0
            rim = jnp.where(
                place >= LANES // 2 - reach, left, jnp.where(place < reach, right, 0.0)
            )
            if field == 0:
                rims[target] = rim
            else:
                rims[target] = rims[target] + pltpu.roll(rim, 2 * reach * field, 1)
    for target in range(devices):
        slots[target, pl.ds(FIELDS * 8, 8)] = rims[target]


def unfold(slot, field, reach):
    cells, rims = slot[pl.ds(field * 8, 8)], slot[pl.ds(FIELDS * 8, 8)]
    lane = lax.broadcasted_iota(jnp.int32, (8, LANES), 1)
    half = LANES // 2
    back = 2 * reach * field
    top = pltpu.roll(rims, (half - back) % LANES, 1)
    low = pltpu.roll(rims, (-back) % LANES, 1) if back else rims
    return jnp.concatenate(
        [
            jnp.where(lane < half, cells, top),
            jnp.where(lane < half, pltpu.roll(cells, half, 1), low),
        ],
        axis=0,
    )


def pack_windows(slots, flat, rows, depth, share):
    for field in range(FIELDS):
        first = field * rows * depth
        lines = [flat[pl.ds(first + line, rows, stride=depth), :] for line in range(depth)]
        for target in range(slots.shape[0]):
            line, offset = target * share // LANES, target * share % LANES
            shift = (LANES - offset) % LANES
            place = column_of((rows, LANES), offset)
            value = pltpu.roll(lines[line], shift, 1)
            if offset < REACH:
                before = pltpu.roll(lines[line - 1], shift, 1) if line > 0 else 0.0
                value = jnp.where(place < 0, before, value)
            if offset > REACH:
                after = pltpu.roll(lines[line + 1], shift, 1) if line < depth - 1 else 0.0
                value = jnp.where(place >= LANES, after, value)
            slots[target, pl.ds(field * rows, rows)] = value


def late_rows(rows):
    return (rows, -2, rows + 1, -1)


def packing(rows, share):
    groups = LANES // share
    each = -(-(rows + 2 * UP_RIM) // groups)
    return groups, each, each + -(-4 // groups)


def sweep_kernel(share, rows, arrived, windows, slots, diff, grow, terms, padded):
    slabs = lax.axis_size("space")
    devices = arrived.shape[0]
    blocks = devices // slabs
    total = slabs * rows
    reach = reach_of()
    groups, each, held = packing(rows, share)
    for slab in range(slabs):
        diff[pl.ds(slab * rows, rows), :] = windows[pl.ds(2 * slab * rows, rows), :]
        grow[pl.ds(slab * rows, rows), :] = windows[pl.ds((2 * slab + 1) * rows, rows), :]
    line = lax.broadcasted_iota(jnp.int32, (total, LANES), 0)
    lane = lax.broadcasted_iota(jnp.int32, (each, LANES), 1)
    padded[...] = jnp.zeros(padded.shape, jnp.float32)

    def block(field, index):
        parts = []
        for slab in range(slabs):
            slot = arrived.at[index * slabs + slab]
            if folded(rows, share, reach):
                parts.append(unfold(slot, field, reach))
            else:
                parts.append(slot[pl.ds(field * rows, rows)])
        return jnp.concatenate(parts, axis=0)

    def slope_of(field):
        north = jnp.where(line == 0, 0.0, pltpu.roll(field, 1, 0))
        south = jnp.where(line == total - 1, 0.0, pltpu.roll(field, total - 1, 0))
        sides = pltpu.roll(field, 1, 1) + pltpu.roll(field, LANES - 1, 1)
        laplace = north + south + sides - 4.0 * field
        return diff[...] * laplace + grow[...] * field / (1.0 + field * field)

    def put_late(index, slab):
        to = slots.at[pl.ds((index * slabs + slab) * held, held)]
        if folded(rows, share, reach):
            zero = jnp.zeros((2, LANES), jnp.float32)
            low = arrived[index * slabs + slab + 1, pl.ds(16, 2)] if slab < slabs - 1 else zero
            high = arrived[index * slabs + slab - 1, pl.ds(22, 2)] if slab > 0 else zero
            to[pl.ds(each, 2)] = jnp.where(lane[:2] < share, low, high)
            return
        for i, row in enumerate(late_rows(rows)):
            at, group = each + i // groups, i % groups
            beside_slab = slab + row // rows
            if 0 <= beside_slab < slabs:
                place = pl.ds(2 * rows + row % rows, 1)
                piece = arrived[index * slabs + beside_slab, place]
                piece = pltpu.roll(piece, group * share, 1)
            else:
                piece = jnp.zeros((1, LANES), jnp.float32)
            if group:
                piece = jnp.where(lane[:1] >= group * share, piece, to[pl.ds(at, 1)])
            to[pl.ds(at, 1)] = piece

    field = None
    for index in range(blocks):
        behind = (index - 1) % blocks
        odd, term = block(0, behind), block(1, behind)
        even = odd + 4.0 * slope_of(odd) + term
        slope = slope_of(even)
        odd = even + 4.0 * slope + block(2, index)
        stepped = even + 8.0 * slope
        pair = odd + 4.0 * slope_of(odd) - stepped
        terms[index] = block(1, index) + pair
        if index == blocks - 1:
            field = stepped + terms[index]
    for index in range(blocks):
        for group in range(groups):
            padded[group, pl.ds(8, total), :] = (
                pltpu.roll(field, group * share, 1) if group else field
            )
        for slab in range(slabs):
            start = 8 + slab * rows - UP_RIM
            value = padded[0, pl.ds(start, each), :]
            for group in range(1, groups):
                piece = padded[group, pl.ds(start + group * each, each), :]
                value = jnp.where(lane >= group * share, piece, value)
            slots[pl.ds((index * slabs + slab) * held, each), :] = value
            put_late(index, slab)
        if index < blocks - 1:
            field = field + 8.0 * slope_of(field) + terms[index]


def up_kernel(
    share, arrived, next_forcing, late_a, late_b, core, coefs,
    out, fields, diff, grow, flat, ready, sems,
):
    rows, depth, _ = next_forcing.shape
    groups, each, held = packing(rows, share)
    take_coefs(rows, coefs, diff, grow)
    lane = lax.broadcasted_iota(jnp.int32, (depth, LANES), 1)

    def whole(line, group):
        value = None
        for part in range(groups):
            piece = arrived[pl.ds(part * held + line, depth, stride=groups * held), :]
            if part != group:
                piece = pltpu.roll(piece, ((part - group) * share) % LANES, 1)
            value = piece if value is None else jnp.where(lane >= part * share, piece, value)
        return value

    for row in range(rows + 2 * UP_RIM):
        fields[0, MARGIN - UP_RIM + row] = whole(row % each, row // each)
    for i, row in enumerate(late_rows(rows)):
        fields[5, MARGIN + row] = whole(each + i // groups, i % groups)
    fields[5, pl.ds(MARGIN, rows)] = next_forcing[...]
    odd_first = CORES.index("o0") * rows

    def first(at, n):
        mid, slope = growth_of(fields.at[0], at, n, diff[pl.ds(at, n)], grow[pl.ds(at, n)])
        fields[2, pl.ds(at, n)] = mid + 4.0 * slope + fields[5, pl.ds(at, n)]

    def second(at, n):
        d, g = diff[pl.ds(at, n)], grow[pl.ds(at, n)]
        for start, late in ((0, late_a), (2, late_b)):
            mid, slope = growth_of(fields.at[start], at, n, d, g)
            fields[start + 1, pl.ds(at, n)] = mid + 2.0 * slope + late[pl.ds(at - MARGIN + 1, n)]

    copies = []

    def emit(point, value):
        put_rows(flat, point * rows, value)
        for r in range(0, rows, 8):
            for c in range(depth):
                start = (point * rows + r) * depth + c
                ready[point, pl.ds(r, 8), pl.ds(c * LANES, LANES)] = flat[
                    pl.ds(start, 8, stride=depth), :
                ]
        copy = pltpu.make_async_copy(ready.at[point], out.at[point], sems.at[point])
        copy.start()
        copies.append(copy)

    def last(i):
        at, n = MARGIN, rows
        mid, slope = growth_of(fields.at[i], at, n, diff[pl.ds(at, n)], grow[pl.ds(at, n)])
        emit(2 * i + 1, mid + slope + core[pl.ds(odd_first + i * rows, n)])

    core_rows = pl.ds(MARGIN, rows)
    emit(0, fields[0, core_rows])
    over_rows(rows, 2, first)
    emit(4, fields[2, core_rows])
    over_rows(rows, 1, second)
    emit(2, fields[1, core_rows])
    emit(6, fields[3, core_rows])
    for i in (0, 2, 1, 3):
        last(i)
    for copy in copies:
        copy.wait()


def moved(array, blocks, slabs):
    tm, space = lax.axis_size("tm"), lax.axis_size("space")
    pairs = [
        (t * space + s, (t + blocks) % tm * space + (s + slabs) % space)
        for t in range(tm)
        for s in range(space)
    ]
    return lax.ppermute(array, ("tm", "space"), pairs)


def swapped(array, offset):
    tm, space = lax.axis_size("tm"), lax.axis_size("space")
    pairs = [
        (t * space + s, ((((t - offset) % tm) ^ 1) + offset) % tm * space + s)
        for t in range(tm)
        for s in range(space)
    ]
    return lax.ppermute(array, ("tm", "space"), pairs)


def rims(down, up, slant_down, slant_up):
    slanted = moved(slant_down, 1, 1), moved(slant_up, 1, -1)
    return moved(down, 0, 1), moved(up, 0, -1), *slanted


def body(initial, source, diffusivity, growth):
    points, rows, cols = initial.shape
    assert points == POINTS and lax.axis_size("tm") % 2 == 0 and rows % 8 == 0 and cols % LANES == 0
    depth = cols // LANES
    tm, space = lax.axis_size("tm"), lax.axis_size("space")
    devices = tm * space
    share = cols // devices
    assert share * devices == cols and LANES % share == 0
    assert reach_of() <= REACH and REACH + share + reach_of() <= LANES
    _, _, held = packing(rows, share)
    wide = rows + 2 * MARGIN

    def lines(n):
        return (n * depth, LANES)

    def field(n):
        return (n, depth, LANES)

    def as_rows(array):
        return array.reshape(-1, depth, LANES)

    window_rows = 2 * rows // depth
    assert window_rows * depth == 2 * rows
    raw = [(points // 2, rows, cols), source.shape, (2, rows, cols)]
    sides = EDGE_0 + window_rows
    extra = window_rows if handed_on(space) else 0
    *sends, inward, outward = call(
        functools.partial(pack_kernel, share),
        [lines(sides + extra), lines(sides), lines(SLANT_0), lines(SLANT_0)]
        + [lines(rows + TURN)] * 2,
        raw + [lines(2 * SCRATCH * (CHAINS + 1)), lines(2 * rows), lines(3 * rows + 2)],
        initial, source, diffusivity, growth,
        place=pltpu.HBM, sems=points // 2 + 3,
    )
    apart = direct_windows(space)
    core, *windows = call(
        functools.partial(core_kernel, share),
        [lines(len(CORES) * rows)] + [(2 * rows, LANES)] * len(apart),
        raw,
        initial, source, diffusivity, growth,
        place=pltpu.HBM, sems=points // 2 + 3,
        cost=pl.CostEstimate(flops=0, transcendentals=0, bytes_accessed=CORE_COST),
    )
    sends, inward, outward = [as_rows(part) for part in sends], as_rows(inward), as_rows(outward)
    inward = swapped(inward, 0)
    inward, sends[2], sends[3] = lax.optimization_barrier((inward, sends[2], sends[3]))
    arrived = [*rims(*sends), inward, swapped(outward, 1)]
    windows = [moved(part, 0, by) if by else part for by, part in zip(apart, windows, strict=True)]
    windows = [as_rows(part) for part in windows]
    core = as_rows(core)
    arrived, windows = lax.optimization_barrier((arrived, windows))

    buffers = [(wide, depth, LANES), (wide, depth, LANES)]
    turn, down, up, slant_down, slant_up, next_odd, forcing, first_forcing, coefs, held_windows, behind_part = call(
        functools.partial(level0_kernel, tuple(apart)),
        [
            field(2 * rows), field(EDGE_1 + extra), field(EDGE_1), field(SLANT_1), field(SLANT_1),
            field(rows), field(3 * rows), field(rows + 4), field(2 * (rows + 4)),
            field(window_rows * space), field(rows),
        ],
        [(len(CORES) + 2 + 3 * (POINTS // 2), wide, depth, LANES)] + buffers,
        core, *arrived, *windows,
    )
    above, below, *slanted = rims(down, up, slant_down, slant_up)
    arrived = above, below, moved(turn, 1, 0), *slanted
    held_rows = FIELDS * 8 + 8 if folded(rows, share, reach_of()) else FIELDS * rows
    slots, next_forcing, late_a, late_b, windows = call(
        functools.partial(level1_kernel, share),
        [
            (devices, held_rows, LANES),
            field(rows), field(rows + 2), field(rows + 2), field(window_rows * space),
        ],
        [(12, wide, depth, LANES)] + buffers + [(FIELDS * rows * depth, LANES)],
        next_odd, forcing, first_forcing, coefs, behind_part, held_windows, *arrived,
    )
    slots = lax.all_to_all(slots, ("tm", "space"), 0, 0, tiled=True)
    (slots,) = call(
        functools.partial(sweep_kernel, share, rows),
        [(devices * held, LANES)],
        [(space * rows, LANES), (space * rows, LANES), (tm, space * rows, LANES)]
        + [(LANES // share, 8 + space * rows + 2 * rows + held, LANES)],
        slots, windows.reshape(-1, LANES),
    )
    slots = slots.reshape(devices, held, 1, LANES)
    slots = lax.all_to_all(slots, ("tm", "space"), 0, 0, tiled=True)
    (out,) = call(
        functools.partial(up_kernel, share),
        [(points, rows, cols)],
        [(6, wide, depth, LANES)]
        + buffers
        + [(points * rows * depth, LANES), (points, rows, cols)],
        slots.reshape(devices * held, LANES), next_forcing, late_a, late_b, core, coefs,
        to=pltpu.HBM, sems=points,
    )
    return out


def solution(mesh):
    placed = (P("tm", "space", None), P("tm", "space", None), P("space", None), P("space", None))
    return jax.shard_map(
        body, mesh=mesh, in_specs=placed, out_specs=P("tm", "space", None), check_vma=False
    )
```

```python
import functools

import jax
import jax.numpy as jnp
from jax import lax
from jax.experimental import pallas as pl
from jax.experimental.pallas import tpu as pltpu
from jax.sharding import PartitionSpec as P

LANES = 128
MARGIN = 4
REACH = 32
UP_RIM = 2
POINTS = 8
FIELDS = 3
CORE_COST = 30_000_000
diffusion_number = 0.03
time_step = 0.02

CHAINS = POINTS // 2 - 1
EDGE_0 = 4 * CHAINS + 6
SLANT_0 = 4
TURN = 2
EDGE_1 = 5
SLANT_1 = 3
CORES = ("e0", "e1", "e2", "o0", "o1", "o2", "o3", "s0", "s1", "s2", "s3", "d", "g")


def params(mib):
    return pltpu.CompilerParams(vmem_limit_bytes=int(mib * 2**20))


def call(
    kernel, outs, scratch, *args, mib=16, place=pltpu.VMEM, to=pltpu.VMEM, sems=0, cost=None
):
    if place == pltpu.HBM:
        args = [pltpu.with_memory_space_constraint(arg, place) for arg in args]
    return pl.pallas_call(
        kernel,
        out_shape=tuple(jax.ShapeDtypeStruct(shape, jnp.float32) for shape in outs),
        in_specs=[pl.BlockSpec(memory_space=place)] * len(args),
        out_specs=tuple(pl.BlockSpec(memory_space=to) for _ in outs),
        scratch_shapes=[pltpu.VMEM(shape, jnp.float32) for shape in scratch]
        + ([pltpu.SemaphoreType.DMA((sems,))] if sems else []),
        compiler_params=params(mib),
        cost_estimate=cost,
    )(*args)


def beside(mid):
    depth = mid.shape[1]
    lane = lax.broadcasted_iota(jnp.int32, mid.shape, 2)
    line = lax.broadcasted_iota(jnp.int32, mid.shape, 1)
    left = pltpu.roll(mid, 1, 2)
    left_turn = pltpu.roll(left, 1, 1)
    right = pltpu.roll(mid, LANES - 1, 2)
    right_turn = pltpu.roll(right, depth - 1, 1)
    left = jnp.where(lane == 0, jnp.where(line == 0, 0.0, left_turn), left)
    right = jnp.where(lane == LANES - 1, jnp.where(line == depth - 1, 0.0, right_turn), right)
    return left + right


def slope_of_rows(wide, diff, grow):
    mid = wide[1:-1]
    laplace = wide[:-2] + wide[2:] + beside(mid) - 4.0 * mid
    return mid, diff * laplace + grow * mid / (1.0 + mid * mid)


def growth_of(ref, at, rows, diff, grow):
    return slope_of_rows(ref[pl.ds(at - 1, rows + 2)], diff, grow)


def over_rows(rows, rim, body):
    body(MARGIN - rim, rows + 2 * rim)


def flags():
    slab = lax.axis_index("space")
    low = jnp.where(slab > 0, 1.0, 0.0).astype(jnp.float32)
    high = jnp.where(slab < lax.axis_size("space") - 1, 1.0, 0.0).astype(jnp.float32)
    return low, high


def rim_rows(rows, low, high):
    return (
        (lambda k: MARGIN - k, low),
        (lambda k: MARGIN + rows - 1 + k, high),
    )


def pieces(name, evens, source, diffusivity, growth):
    if name == "d":
        return lambda rows, cols: diffusivity[rows, cols] * diffusion_number
    if name == "g":
        return lambda rows, cols: growth[rows, cols] * time_step
    if name == "ep":
        return lambda rows, cols: evens[POINTS // 2 - 1, rows, cols]
    if name == "op":
        return lambda rows, cols: source[POINTS - 1, rows, cols]
    which = int(name[1])
    if name[0] == "e":
        return lambda rows, cols: evens[which, rows, cols]
    return lambda rows, cols: source[2 * which + (name[0] == "o"), rows, cols]


def fetch(initial_all, source_all, diffusivity_all, growth_all, evens, source, coefs, sems):
    pairs = [(initial_all.at[2 * i], evens.at[i]) for i in range(POINTS // 2)]
    pairs += [(diffusivity_all, coefs.at[0]), (growth_all, coefs.at[1]), (source_all, source)]
    copies = [pltpu.make_async_copy(*pair, sems.at[i]) for i, pair in enumerate(pairs)]
    for copy in copies:
        copy.start()
    return copies[:-1], copies[-1]


def target_of(by):
    slabs = lax.axis_size("space")
    return lax.axis_index("tm") * slabs + (lax.axis_index("space") + by) % slabs


SCRATCH = 10


def pack_kernel(
    share, initial_all, source_all, diffusivity_all, growth_all,
    down, up, slant_down, slant_up, inward, outward,
    evens, source, coefs, edge, cells, turn, sems,
):
    waits, last = fetch(
        initial_all, source_all, diffusivity_all, growth_all, evens, source, coefs, sems
    )
    _, rows, cols = coefs.shape
    depth = cols // LANES
    diffusivity, growth = coefs.at[0], coefs.at[1]

    def put(ref, at, name, first, count):
        get = pieces(name, evens, source, diffusivity, growth)
        for c in range(depth):
            place = pl.ds(at * depth + c, count, stride=depth)
            ref[place, :] = get(pl.ds(first, count), pl.ds(c * LANES, LANES))

    def rows_of(ref, at, count):
        return ref[pl.ds(at * depth, count * depth), :].reshape(count, depth, LANES)

    def coef_rows(which, first, count):
        return rows_of(cells, which * rows + first, count)

    chains = [(f"e{i}", f"o{i}", f"s{i + 1}", f"o{i + 1}") for i in range(CHAINS)]
    chains.append(("ep", "op", None, None))
    sides = ((down, slant_down, False), (up, slant_up, True))

    def near(upward, count):
        return 0 if upward else rows - count

    for wait in waits:
        wait.wait()
    for index, name in enumerate(("d", "g")):
        for r in range(0, rows, 8):
            put(cells, index * rows + r, name, r, 8)
    for side, (rim, slant, upward) in enumerate(sides):
        for i, (start, _, _, _) in enumerate(chains):
            put(edge, (2 * i + side) * SCRATCH, start, near(upward, 4), 4)
        put_rows(rim, 4 * CHAINS + 3, coef_rows(0, near(upward, 2), 2))
        put_rows(rim, 4 * CHAINS + 5, coef_rows(1, near(upward, 1), 1))
    end = EDGE_0 * depth
    if end < down.shape[0]:
        for index in range(2):
            get = lambda line: cells[pl.ds(index * rows * depth + line, rows, stride=depth), :]
            down[pl.ds(end + index * rows, rows), :] = window(get, target_of(2) * share, depth)
    put_rows(turn, 0, jnp.zeros((1, depth, LANES), jnp.float32))
    for r in range(0, rows, 8):
        put(turn, 1 + r, "ep", r, 8)
    put_rows(turn, rows + 1, jnp.zeros((1, depth, LANES), jnp.float32))
    last.wait()
    for side, (rim, slant, upward) in enumerate(sides):
        for i, (_, term, after, after_odd) in enumerate(chains):
            spot = (2 * i + side) * SCRATCH
            put(edge, spot + 4, term, near(upward, 3), 3)
            if after:
                put(edge, spot + 7, after, near(upward, 2), 2)
                put(edge, spot + 9, after_odd, near(upward, 1), 1)
        put(rim, 4 * CHAINS, "s0", near(upward, 2), 2)
        put(rim, 4 * CHAINS + 2, "o0", near(upward, 1), 1)
    for r in range(0, rows, 8):
        put(turn, rows + 2 + r, "op", r, 8)
        put(turn, 2 * rows + 2 + r, "s0", r, 8)
    ahead = lax.axis_index("tm") % 2 == 0
    wide = rows_of(turn, 0, rows + 2)
    mid, slope = slope_of_rows(wide, coef_rows(0, 0, rows), coef_rows(1, 0, rows))
    forward = mid + slope + rows_of(turn, rows + 2, rows)
    backward = rows_of(turn, 2 * rows + 2, rows)
    put_rows(inward, 0, jnp.where(ahead, forward, backward))
    put_rows(outward, 0, jnp.where(ahead, backward, forward))
    for i, row in enumerate((1, rows)):
        for to in (inward, outward):
            put_rows(to, rows + i, rows_of(turn, row, 1))
    for side, (rim, slant, upward) in enumerate(sides):
        n0, n1, inner = (0, 1, 1) if upward else (rows - 1, rows - 2, rows - 3)
        diff0, diff1, grow1 = coef_rows(0, n0, 1), coef_rows(0, n1, 1), coef_rows(1, n1, 1)
        nothing = jnp.zeros_like(diff0)

        def pick(value, k):
            place = k if upward else value.shape[0] - 1 - k
            return value[place : place + 1]

        for i, (_, _, after, _) in enumerate(chains):
            spot = (2 * i + side) * SCRATCH
            start, term = rows_of(edge, spot, 4), rows_of(edge, spot + 4, 3)
            mid, slope = slope_of_rows(start, coef_rows(0, inner, 2), coef_rows(1, inner, 2))
            inner_term = term[1:] if upward else term[:-1]
            odd = mid + slope + inner_term
            wide = [nothing, odd] if upward else [odd, nothing]
            mid, slope = slope_of_rows(jnp.concatenate(wide, axis=0), diff1, grow1)
            part = mid + slope
            odd1 = pick(odd, 0)
            to, at = (rim, 4 * i) if after else (slant, 0)
            put_rows(to, at, pick(start, 0))
            put_rows(to, at + 1, pick(term, 0) + diff0 * pick(start, 1))
            if after:
                follow = rows_of(edge, spot + 7, 2)
                put_rows(to, at + 2, pick(follow, 0) + diff0 * odd1)
                part = part + pick(follow, 1)
                put_rows(to, at + 3, rows_of(edge, spot + 9, 1) + diff0 * part)
            else:
                put_rows(to, at + 2, odd1)
                put_rows(to, at + 3, part)


def column_of(shape, offset):
    lane = lax.broadcasted_iota(jnp.int32, shape, len(shape) - 1)
    return jnp.where(lane < LANES - REACH, lane, lane - LANES) + offset


def window(get, first, depth):
    line, offset = first // LANES, first % LANES
    source = column_of(get(0).shape, offset)
    shift = (LANES - offset) % LANES
    before = jnp.where(line > 0, pltpu.roll(get(jnp.maximum(line - 1, 0)), shift, 1), 0.0)
    here = pltpu.roll(get(line), shift, 1)
    after = jnp.where(
        line < depth - 1, pltpu.roll(get(jnp.minimum(line + 1, depth - 1)), shift, 1), 0.0
    )
    return jnp.where(source < 0, before, jnp.where(source >= LANES, after, here))


def core_kernel(
    share, initial_all, source_all, diffusivity_all, growth_all, core, *refs
):
    *windows, evens, source, coefs, sems = refs
    waits, last = fetch(
        initial_all, source_all, diffusivity_all, growth_all, evens, source, coefs, sems
    )
    for wait in (*waits, last):
        wait.wait()
    _, rows, cols = coefs.shape
    depth = cols // LANES
    for index, name in enumerate(CORES):
        get = pieces(name, evens, source, coefs.at[0], coefs.at[1])
        for c in range(depth):
            for r in range(0, rows, 8):
                value = get(pl.ds(r, 8), pl.ds(c * LANES, LANES))
                core[pl.ds((index * rows + r) * depth + c, 8, stride=depth), :] = value
    for by, out in zip(sent_windows(lax.axis_size("space")), windows, strict=True):
        for which, name in enumerate(("d", "g")):
            start = CORES.index(name) * rows * depth
            get = lambda line: core[pl.ds(start + line, rows, stride=depth), :]
            out[pl.ds(which * rows, rows)] = window(get, target_of(by) * share, depth)


def handed_on(slabs):
    return slabs == 4


def far_windows(slabs):
    return [] if handed_on(slabs) else list(range(2, slabs - 1))


def sent_windows(slabs):
    return [0, 1, slabs - 1] + far_windows(slabs)


def level0_kernel(
    core, above, below, behind_above, behind_below, inward, outward, own, ahead_one, behind_one,
    *refs,
):
    distant = far_windows(lax.axis_size("space"))
    windows, refs = refs[: len(distant)], refs[len(distant) :]
    (
        turn, down, up, slant_down, slant_up, next_odd, forcing, first_forcing, coefs, held,
        behind_part, fields, diff, grow,
    ) = refs
    rows = core.shape[0] // len(CORES)
    low, high = flags()
    depth = core.shape[1]
    names = list(CORES) + ["ep", "op"]
    spots = {name: index for index, name in enumerate(names)}
    extra = len(names)
    halves = POINTS // 2
    odd = [extra + i for i in range(halves)]
    even = [extra + halves + i for i in range(halves)]
    image = [extra + 2 * halves + i for i in range(halves)]
    nothing = jnp.zeros((1, depth, LANES), jnp.float32)
    sides = rim_rows(rows, low, high)
    for (at, flag), rim, slant in zip(
        sides, (above, below), (behind_above, behind_below), strict=True
    ):

        def put(name, k, ref, row):
            fields[spots[name] if isinstance(name, str) else name, pl.ds(at(k), 1)] = (
                ref[pl.ds(row, 1)] * flag
            )

        for i in range(CHAINS):
            put(f"e{i}", 1, rim, 4 * i)
            put(f"o{i}", 1, rim, 4 * i + 1)
            put(f"s{i + 1}", 1, rim, 4 * i + 2)
            fields[spots[f"e{i}"], pl.ds(at(2), 1)] = nothing
            fields[odd[i + 1], pl.ds(at(2), 1)] = nothing
        put("ep", 1, slant, 0)
        put("op", 1, slant, 1)
        put(odd[0], 2, slant, 2)
        fields[spots["ep"], pl.ds(at(2), 1)] = nothing
        first_row = min(at(1), at(2))
        edge_at = 4 * CHAINS
        fields[spots["s0"], pl.ds(first_row, 2)] = rim[pl.ds(edge_at, 2)] * flag
        diff[pl.ds(first_row, 2)] = rim[pl.ds(edge_at + 3, 2)] * flag
        grow[pl.ds(at(1), 1)] = rim[pl.ds(edge_at + 5, 1)] * flag
        grow[pl.ds(at(2), 1)] = nothing
    for name in CORES:
        if name in ("d", "g"):
            buffer = diff if name == "d" else grow
        else:
            buffer = fields.at[spots[name]]
        buffer[pl.ds(MARGIN, rows)] = core[pl.ds(CORES.index(name) * rows, rows)]
    even_block = lax.axis_index("tm") % 2 == 0
    cells = pl.ds(0, rows)
    from_behind = jnp.where(even_block, outward[cells], inward[cells])
    ahead = jnp.where(even_block, inward[cells], outward[cells])
    fields[odd[0], pl.ds(MARGIN, rows)] = from_behind
    for (at, _), row, edge_row in zip(sides, (0, 1), (0, rows - 1), strict=True):
        edge = pl.ds(rows + row, 1)
        fields[spots["ep"], pl.ds(MARGIN + edge_row, 1)] = jnp.where(
            even_block, outward[edge], inward[edge]
        )
        near, first = pl.ds(at(1), 1), pl.ds(MARGIN + edge_row, 1)
        mid, slope = growth_of(fields.at[spots["ep"]], at(1), 1, diff[near], grow[near])
        fields[odd[0], near] = mid + slope + fields[spots["op"], near]
        fields[odd[0], first] = fields[odd[0], first] + diff[first] * mid

    def first(at, n):
        d, g = diff[pl.ds(at, n)], grow[pl.ds(at, n)]
        for i in range(CHAINS):
            mid, slope = growth_of(fields.at[spots[f"e{i}"]], at, n, d, g)
            fields[odd[i + 1], pl.ds(at, n)] = mid + slope + fields[spots[f"o{i}"], pl.ds(at, n)]

    def second(at, n):
        d, g = diff[pl.ds(at, n)], grow[pl.ds(at, n)]
        for i in range(halves):
            mid, slope = growth_of(fields.at[odd[i]], at, n, d, g)
            fields[even[i], pl.ds(at, n)] = mid + slope + fields[spots[f"s{i}"], pl.ds(at, n)]

    def third(at, n):
        d, g = diff[pl.ds(at, n)], grow[pl.ds(at, n)]
        for i in range(halves):
            mid, slope = growth_of(fields.at[even[i]], at, n, d, g)
            fields[odd[i], pl.ds(at, n)] = mid + slope + fields[spots[f"o{i}"], pl.ds(at, n)]
            fields[image[i], pl.ds(at, n)] = mid + 2.0 * slope

    def fourth(at, n):
        d, g = diff[pl.ds(at, n)], grow[pl.ds(at, n)]
        here = at - MARGIN
        for i in range(halves):
            mid, slope = growth_of(fields.at[odd[i]], at, n, d, g)
            pair = mid + slope - fields[image[i], pl.ds(at, n)]
            if i == halves - 1:
                turn[pl.ds(here, n)] = pair
                behind_part[...] = ahead + pair
            else:
                term = fields[spots[f"s{i + 1}"], pl.ds(at, n)] + pair
                forcing[pl.ds(i * rows + here, n)] = term
                if i == 0:
                    next_odd[...] = fields[image[0], pl.ds(at, n)] + term
                if i == halves - 2:
                    turn[pl.ds(rows + here, n)] = fields[image[i], pl.ds(at, n)] + term

    over_rows(rows, 1, first)
    over_rows(rows, 1, second)
    for (at, flag), rim, slant in zip(
        sides, (above, below), (behind_above, behind_below), strict=True
    ):
        near, far = pl.ds(at(1), 1), pl.ds(at(2), 1)
        for i in range(halves):
            place = 4 * CHAINS + 2 if i == 0 else 4 * i - 1
            fields[spots[f"o{i}"], near] = rim[pl.ds(place, 1)] * flag
            value = diff[far] * fields[odd[i], near]
            if i == 0:
                value = value + fields[spots["s0"], far] + slant[pl.ds(3, 1)] * flag
            fields[even[i], far] = value
    over_rows(rows, 1, third)
    over_rows(rows, 0, fourth)
    first_forcing[...] = fields[spots["s0"], pl.ds(MARGIN - 2, rows + 4)]
    coefs[pl.ds(0, rows + 4)] = diff[pl.ds(MARGIN - 2, rows + 4)]
    coefs[pl.ds(rows + 4, rows + 4)] = grow[pl.ds(MARGIN - 2, rows + 4)]
    for rim, slant, n0, n1 in ((down, slant_down, rows - 1, rows - 2), (up, slant_up, 0, 1)):

        def row(ref, first, n):
            return ref[pl.ds(first + n, 1)]

        diff0 = 2.0 * row(diff, MARGIN, n0)
        around = [
            slope_of_rows(
                ref[pl.ds(first + n1 - 1, 3)], row(diff, MARGIN, n1), row(grow, MARGIN, n1)
            )
            for ref, first in ((next_odd, 0), (turn, rows))
        ]
        (mid, slope), (mid_last, slope_last) = around
        even1 = mid + 2.0 * slope + row(forcing, rows, n1)
        g3 = row(forcing, 2 * rows, n0)
        rim[pl.ds(0, 1)] = row(next_odd, 0, n0)
        rim[pl.ds(1, 1)] = row(forcing, rows, n0) + diff0 * mid
        rim[pl.ds(2, 1)] = g3 + diff0 * even1
        rim[pl.ds(3, 1)] = g3
        rim[pl.ds(4, 1)] = row(forcing, 0, n0)
        slant[pl.ds(0, 1)] = row(turn, rows, n0)
        slant[pl.ds(1, 1)] = row(turn, 0, n0) + diff0 * mid_last
        slant[pl.ds(2, 1)] = row(turn, 0, n1) + mid_last + 2.0 * slope_last
    slab, slabs = lax.axis_index("space"), lax.axis_size("space")
    size = 2 * rows // depth
    down[pl.ds(EDGE_1, size)] = ahead_one[...]
    up[pl.ds(EDGE_1, size)] = behind_one[...]
    if handed_on(slabs):
        down[pl.ds(EDGE_1 + size, size)] = above[pl.ds(EDGE_0, size)]
    for by, part in zip([0] + distant, (own, *windows), strict=True):
        held[pl.ds((slab - by) % slabs * size, size)] = part[...]


def take_coefs(rows, coefs, diff, grow):
    diff[pl.ds(MARGIN - 2, rows + 4)] = coefs[pl.ds(0, rows + 4)]
    grow[pl.ds(MARGIN - 2, rows + 4)] = coefs[pl.ds(rows + 4, rows + 4)]


def level1_kernel(
    share, next_odd, forcing, first_forcing, coefs, behind_part, held,
    above, below, behind, behind_above, behind_below,
    slots, next_forcing, late_a, late_b, windows,
    fields, diff, grow, flat,
):
    rows = forcing.shape[0] // 3
    low, high = flags()
    take_coefs(rows, coefs, diff, grow)
    windows[...] = held[...]
    slab, slabs = lax.axis_index("space"), lax.axis_size("space")
    size = windows.shape[0] // slabs
    windows[pl.ds((slab - 1) % slabs * size, size)] = above[pl.ds(EDGE_1, size)]
    windows[pl.ds((slab + 1) % slabs * size, size)] = below[pl.ds(EDGE_1, size)]
    if handed_on(slabs):
        windows[pl.ds((slab - 2) % slabs * size, size)] = above[pl.ds(EDGE_1 + size, size)]
    g1, g3, g2, g0, before, after, even0, even1, image0, image1, odd0, odd1 = range(12)
    nothing = jnp.zeros((1, *forcing.shape[1:]), jnp.float32)
    sides = rim_rows(rows, low, high)
    fields[after, pl.ds(MARGIN, rows)] = next_odd[...]
    for which, spot in enumerate((g1, g2, g3)):
        fields[spot, pl.ds(MARGIN, rows)] = forcing[pl.ds(which * rows, rows)]
    fields[before, pl.ds(MARGIN, rows)] = behind[pl.ds(rows, rows)]
    fields[g0, pl.ds(MARGIN, rows)] = first_forcing[pl.ds(2, rows)] + behind[pl.ds(0, rows)]
    for (at, flag), rim, slant in zip(
        sides, (above, below), (behind_above, behind_below), strict=True
    ):
        near, far = pl.ds(at(1), 1), pl.ds(at(2), 1)
        for spot, row in ((after, 0), (g2, 1), (g3, 2), (g1, 4)):
            fields[spot, near] = rim[pl.ds(row, 1)] * flag
        own = [first_forcing[pl.ds(at(k) - MARGIN + 2, 1)] for k in (1, 2)]
        fields[before, near] = slant[pl.ds(0, 1)] * flag
        fields[g0, near] = own[0] + slant[pl.ds(1, 1)] * flag
        fields[even0, far] = own[1] + slant[pl.ds(2, 1)] * flag
        for spot in (after, before, even1):
            fields[spot, far] = nothing

    def second(at, n):
        d, g = diff[pl.ds(at, n)], grow[pl.ds(at, n)]
        for start, term, end in ((before, g0, even0), (after, g2, even1)):
            mid, slope = growth_of(fields.at[start], at, n, d, g)
            fields[end, pl.ds(at, n)] = mid + 2.0 * slope + fields[term, pl.ds(at, n)]

    def third(at, n):
        d, g = diff[pl.ds(at, n)], grow[pl.ds(at, n)]
        for start, term, end, image in ((even0, g1, odd0, image0), (even1, g3, odd1, image1)):
            mid, slope = growth_of(fields.at[start], at, n, d, g)
            fields[end, pl.ds(at, n)] = mid + 2.0 * slope + fields[term, pl.ds(at, n)]
            fields[image, pl.ds(at, n)] = mid + 4.0 * slope

    def fourth(at, n):
        d, g = diff[pl.ds(at, n)], grow[pl.ds(at, n)]
        here = at - MARGIN
        mid, slope = growth_of(fields.at[odd1], at, n, d, g)
        pair1 = mid + 2.0 * slope - fields[image1, pl.ds(at, n)]
        put_rows(flat, rows, behind_part[...] + pair1)
        mid, slope = growth_of(fields.at[odd0], at, n, d, g)
        image = fields[image0, pl.ds(at, n)]
        term = fields[g2, pl.ds(at, n)] + (mid + 2.0 * slope - image)
        next_forcing[pl.ds(here, n)] = term
        put_rows(flat, 2 * rows, term)
        put_rows(flat, 0, image + term)

    over_rows(rows, 1, second)
    over_rows(rows, 1, third)
    over_rows(rows, 0, fourth)
    late_a[...] = fields[g1, pl.ds(MARGIN - 1, rows + 2)]
    late_b[pl.ds(1, rows)] = fields[g3, pl.ds(MARGIN, rows)]
    late_b[pl.ds(0, 1)] = above[pl.ds(3, 1)] * low
    late_b[pl.ds(rows + 1, 1)] = below[pl.ds(3, 1)] * high
    depth = forcing.shape[1]
    if folded(rows, share, reach_of()):
        pack_folded(slots, flat, rows, depth, reach_of())
    else:
        pack_windows(slots, flat, rows, depth, share)


def put_rows(flat, first, value):
    depth = value.shape[1]
    for i in range(value.shape[0]):
        flat[pl.ds((first + i) * depth, depth), :] = value[i]


def reach_of():
    return lax.axis_size("tm") + 2


def folded(rows, share, reach):
    return rows == 16 and 2 * share == LANES and FIELDS * 2 * reach <= share


def pack_folded(slots, flat, rows, depth, reach):
    devices = slots.shape[0]
    lane = lax.broadcasted_iota(jnp.int32, (8, LANES), 1)
    place = lane % (LANES // 2)
    rims = [None] * devices
    for field in range(FIELDS):
        first = field * rows * depth
        cells = []
        for line in range(depth):
            top = flat[pl.ds(first + line, 8, stride=depth), :]
            low = flat[pl.ds(first + 8 * depth + line, 8, stride=depth), :]
            cells.append(jnp.where(lane < LANES // 2, top, pltpu.roll(low, LANES // 2, 1)))
            cells.append(jnp.where(lane < LANES // 2, pltpu.roll(top, LANES // 2, 1), low))
        for target in range(devices):
            slots[target, pl.ds(field * 8, 8)] = cells[target]
            left = cells[target - 1] if target > 0 else 0.0
            right = cells[target + 1] if target < devices - 1 else 0.0
            rim = jnp.where(
                place >= LANES // 2 - reach, left, jnp.where(place < reach, right, 0.0)
            )
            if field == 0:
                rims[target] = rim
            else:
                rims[target] = rims[target] + pltpu.roll(rim, 2 * reach * field, 1)
    for target in range(devices):
        slots[target, pl.ds(FIELDS * 8, 8)] = rims[target]


def unfold(slot, field, reach):
    cells, rims = slot[pl.ds(field * 8, 8)], slot[pl.ds(FIELDS * 8, 8)]
    lane = lax.broadcasted_iota(jnp.int32, (8, LANES), 1)
    half = LANES // 2
    back = 2 * reach * field
    top = pltpu.roll(rims, (half - back) % LANES, 1)
    low = pltpu.roll(rims, (-back) % LANES, 1) if back else rims
    return jnp.concatenate(
        [
            jnp.where(lane < half, cells, top),
            jnp.where(lane < half, pltpu.roll(cells, half, 1), low),
        ],
        axis=0,
    )


def pack_windows(slots, flat, rows, depth, share):
    for field in range(FIELDS):
        first = field * rows * depth
        lines = [flat[pl.ds(first + line, rows, stride=depth), :] for line in range(depth)]
        for target in range(slots.shape[0]):
            line, offset = target * share // LANES, target * share % LANES
            shift = (LANES - offset) % LANES
            place = column_of((rows, LANES), offset)
            value = pltpu.roll(lines[line], shift, 1)
            if offset < REACH:
                before = pltpu.roll(lines[line - 1], shift, 1) if line > 0 else 0.0
                value = jnp.where(place < 0, before, value)
            if offset > REACH:
                after = pltpu.roll(lines[line + 1], shift, 1) if line < depth - 1 else 0.0
                value = jnp.where(place >= LANES, after, value)
            slots[target, pl.ds(field * rows, rows)] = value


def late_rows(rows):
    return (("forcing", rows), ("forcing", -1), ("odd", rows + 1), ("odd", -2))


def packing(rows, share):
    groups = LANES // share
    each = -(-(rows + 2 * UP_RIM) // groups)
    return groups, each, each + -(-4 // groups)


def sweep_kernel(share, rows, arrived, windows, slots, diff, grow, terms, owns, padded, odds):
    slabs = lax.axis_size("space")
    devices = arrived.shape[0]
    blocks = devices // slabs
    total = slabs * rows
    reach = reach_of()
    groups, each, held = packing(rows, share)
    for slab in range(slabs):
        diff[pl.ds(slab * rows, rows), :] = windows[pl.ds(2 * slab * rows, rows), :]
        grow[pl.ds(slab * rows, rows), :] = windows[pl.ds((2 * slab + 1) * rows, rows), :]
    line = lax.broadcasted_iota(jnp.int32, (total, LANES), 0)
    lane = lax.broadcasted_iota(jnp.int32, (each, LANES), 1)
    padded[...] = jnp.zeros(padded.shape, jnp.float32)
    odds[...] = jnp.zeros(odds.shape, jnp.float32)

    def block(field, index):
        parts = []
        for slab in range(slabs):
            slot = arrived.at[index * slabs + slab]
            if folded(rows, share, reach):
                parts.append(unfold(slot, field, reach))
            else:
                parts.append(slot[pl.ds(field * rows, rows)])
        return jnp.concatenate(parts, axis=0)

    def slope_of(field):
        north = jnp.where(line == 0, 0.0, pltpu.roll(field, 1, 0))
        south = jnp.where(line == total - 1, 0.0, pltpu.roll(field, total - 1, 0))
        sides = pltpu.roll(field, 1, 1) + pltpu.roll(field, LANES - 1, 1)
        laplace = north + south + sides - 4.0 * field
        return diff[...] * laplace + grow[...] * field / (1.0 + field * field)

    def put_late(index, slab):
        to = slots.at[pl.ds((index * slabs + slab) * held, held)]
        if folded(rows, share, reach):
            zero = jnp.zeros((1, LANES), jnp.float32)
            low = arrived[index * slabs + slab + 1, pl.ds(16, 1)] if slab < slabs - 1 else zero
            high = arrived[index * slabs + slab - 1, pl.ds(23, 1)] if slab > 0 else zero
            to[pl.ds(each, 1)] = jnp.where(lane[:1] < share, low, high)
            low = odds[0, pl.ds(8 + slab * rows + rows + 1, 1)]
            high = odds[1, pl.ds(8 + slab * rows - 2, 1)]
            to[pl.ds(each + 1, 1)] = jnp.where(lane[:1] < share, low, high)
            return
        for i, (what, row) in enumerate(late_rows(rows)):
            at, group = each + i // groups, i % groups
            beside_slab = slab + row // rows
            if what == "odd":
                piece = odds[group, pl.ds(8 + slab * rows + row, 1)]
            elif 0 <= beside_slab < slabs:
                place = pl.ds(2 * rows + row % rows, 1)
                piece = arrived[index * slabs + beside_slab, place]
                piece = pltpu.roll(piece, group * share, 1)
            else:
                piece = jnp.zeros((1, LANES), jnp.float32)
            if group:
                piece = jnp.where(lane[:1] >= group * share, piece, to[pl.ds(at, 1)])
            to[pl.ds(at, 1)] = piece

    field = None
    for index in range(blocks):
        behind = (index - 1) % blocks
        odd, term = block(0, behind), block(1, behind)
        even = odd + 4.0 * slope_of(odd) + term
        slope = slope_of(even)
        own = block(2, index)
        owns[index] = own
        odd = even + 4.0 * slope + own
        stepped = even + 8.0 * slope
        pair = odd + 4.0 * slope_of(odd) - stepped
        terms[index] = block(1, index) + pair
        if index == blocks - 1:
            field = stepped + terms[index]
    for index in range(blocks):
        slope = slope_of(field)
        odd = field + 4.0 * slope + owns[index]
        for group in range(groups):
            for to, value in ((padded, field), (odds, odd)):
                to[group, pl.ds(8, total), :] = (
                    pltpu.roll(value, group * share, 1) if group else value
                )
        for slab in range(slabs):
            start = 8 + slab * rows - UP_RIM
            value = padded[0, pl.ds(start, each), :]
            for group in range(1, groups):
                piece = padded[group, pl.ds(start + group * each, each), :]
                value = jnp.where(lane >= group * share, piece, value)
            slots[pl.ds((index * slabs + slab) * held, each), :] = value
            put_late(index, slab)
        if index < blocks - 1:
            field = field + 8.0 * slope + terms[index]


def up_kernel(
    share, arrived, next_forcing, late_a, late_b, core, coefs,
    out, fields, diff, grow, flat, ready, sems,
):
    rows, depth, _ = next_forcing.shape
    groups, each, held = packing(rows, share)
    take_coefs(rows, coefs, diff, grow)
    lane = lax.broadcasted_iota(jnp.int32, (depth, LANES), 1)

    def whole(line, group):
        value = None
        for part in range(groups):
            piece = arrived[pl.ds(part * held + line, depth, stride=groups * held), :]
            if part != group:
                piece = pltpu.roll(piece, ((part - group) * share) % LANES, 1)
            value = piece if value is None else jnp.where(lane >= part * share, piece, value)
        return value

    for row in range(rows + 2 * UP_RIM):
        fields[0, MARGIN - UP_RIM + row] = whole(row % each, row // each)
    for i, (what, row) in enumerate(late_rows(rows)):
        spot = 5 if what == "forcing" else 2
        fields[spot, MARGIN + row] = whole(each + i // groups, i % groups)
    fields[5, pl.ds(MARGIN, rows)] = next_forcing[...]
    odd_first = CORES.index("o0") * rows

    def first(at, n):
        mid, slope = growth_of(fields.at[0], at, n, diff[pl.ds(at, n)], grow[pl.ds(at, n)])
        fields[2, pl.ds(at, n)] = mid + 4.0 * slope + fields[5, pl.ds(at, n)]

    def second(at, n):
        d, g = diff[pl.ds(at, n)], grow[pl.ds(at, n)]
        for start, late in ((0, late_a), (2, late_b)):
            mid, slope = growth_of(fields.at[start], at, n, d, g)
            fields[start + 1, pl.ds(at, n)] = mid + 2.0 * slope + late[pl.ds(at - MARGIN + 1, n)]

    copies = []

    def emit(point, value):
        put_rows(flat, point * rows, value)
        for r in range(0, rows, 8):
            for c in range(depth):
                start = (point * rows + r) * depth + c
                ready[point, pl.ds(r, 8), pl.ds(c * LANES, LANES)] = flat[
                    pl.ds(start, 8, stride=depth), :
                ]
        copy = pltpu.make_async_copy(ready.at[point], out.at[point], sems.at[point])
        copy.start()
        copies.append(copy)

    def last(i):
        at, n = MARGIN, rows
        mid, slope = growth_of(fields.at[i], at, n, diff[pl.ds(at, n)], grow[pl.ds(at, n)])
        emit(2 * i + 1, mid + slope + core[pl.ds(odd_first + i * rows, n)])

    core_rows = pl.ds(MARGIN, rows)
    emit(0, fields[0, core_rows])
    over_rows(rows, 1, first)
    emit(4, fields[2, core_rows])
    over_rows(rows, 1, second)
    emit(2, fields[1, core_rows])
    emit(6, fields[3, core_rows])
    for i in (0, 2, 1, 3):
        last(i)
    for copy in copies:
        copy.wait()


def moved(array, blocks, slabs):
    tm, space = lax.axis_size("tm"), lax.axis_size("space")
    pairs = [
        (t * space + s, (t + blocks) % tm * space + (s + slabs) % space)
        for t in range(tm)
        for s in range(space)
    ]
    return lax.ppermute(array, ("tm", "space"), pairs)


def swapped(array, offset):
    tm, space = lax.axis_size("tm"), lax.axis_size("space")
    pairs = [
        (t * space + s, ((((t - offset) % tm) ^ 1) + offset) % tm * space + s)
        for t in range(tm)
        for s in range(space)
    ]
    return lax.ppermute(array, ("tm", "space"), pairs)


def rims(down, up, slant_down, slant_up):
    slanted = moved(slant_down, 1, 1), moved(slant_up, 1, -1)
    return moved(down, 0, 1), moved(up, 0, -1), *slanted


def body(initial, source, diffusivity, growth):
    points, rows, cols = initial.shape
    assert points == POINTS and lax.axis_size("tm") % 2 == 0 and rows % 8 == 0 and cols % LANES == 0
    depth = cols // LANES
    tm, space = lax.axis_size("tm"), lax.axis_size("space")
    devices = tm * space
    share = cols // devices
    assert share * devices == cols and LANES % share == 0
    assert reach_of() <= REACH and REACH + share + reach_of() <= LANES
    _, _, held = packing(rows, share)
    wide = rows + 2 * MARGIN

    def lines(n):
        return (n * depth, LANES)

    def field(n):
        return (n, depth, LANES)

    def as_rows(array):
        return array.reshape(-1, depth, LANES)

    window_rows = 2 * rows // depth
    assert window_rows * depth == 2 * rows
    raw = [(points // 2, rows, cols), source.shape, (2, rows, cols)]
    extra = window_rows if handed_on(space) else 0
    *sends, inward, outward = call(
        functools.partial(pack_kernel, share),
        [lines(EDGE_0 + extra), lines(EDGE_0), lines(SLANT_0), lines(SLANT_0)]
        + [lines(rows + TURN)] * 2,
        raw + [lines(2 * SCRATCH * (CHAINS + 1)), lines(2 * rows), lines(3 * rows + 2)],
        initial, source, diffusivity, growth,
        place=pltpu.HBM, sems=points // 2 + 3,
    )
    core, *windows = call(
        functools.partial(core_kernel, share),
        [lines(len(CORES) * rows)] + [(2 * rows, LANES)] * len(sent_windows(space)),
        raw,
        initial, source, diffusivity, growth,
        place=pltpu.HBM, sems=points // 2 + 3,
        cost=pl.CostEstimate(flops=0, transcendentals=0, bytes_accessed=CORE_COST),
    )
    sends, inward, outward = [as_rows(part) for part in sends], as_rows(inward), as_rows(outward)
    inward = swapped(inward, 0)
    inward, sends[2], sends[3] = lax.optimization_barrier((inward, sends[2], sends[3]))
    arrived = [*rims(*sends), inward, swapped(outward, 1)]
    windows = [as_rows(part) for part in windows]
    for i, by in enumerate(far_windows(space), 3):
        windows[i] = moved(windows[i], 0, by)
    core = as_rows(core)
    arrived, windows = lax.optimization_barrier((arrived, windows))

    buffers = [(wide, depth, LANES), (wide, depth, LANES)]
    turn, down, up, slant_down, slant_up, next_odd, forcing, first_forcing, coefs, held_windows, behind_part = call(
        level0_kernel,
        [
            field(2 * rows), field(EDGE_1 + window_rows + extra), field(EDGE_1 + window_rows),
            field(SLANT_1), field(SLANT_1),
            field(rows), field(3 * rows), field(rows + 4), field(2 * (rows + 4)),
            field(window_rows * space), field(rows),
        ],
        [(len(CORES) + 2 + 3 * (POINTS // 2), wide, depth, LANES)] + buffers,
        core, *arrived, *windows,
    )
    above, below, *slanted = rims(down, up, slant_down, slant_up)
    arrived = above, below, moved(turn, 1, 0), *slanted
    held_rows = FIELDS * 8 + 8 if folded(rows, share, reach_of()) else FIELDS * rows
    slots, next_forcing, late_a, late_b, windows = call(
        functools.partial(level1_kernel, share),
        [
            (devices, held_rows, LANES),
            field(rows), field(rows + 2), field(rows + 2), field(window_rows * space),
        ],
        [(12, wide, depth, LANES)] + buffers + [(FIELDS * rows * depth, LANES)],
        next_odd, forcing, first_forcing, coefs, behind_part, held_windows, *arrived,
    )
    slots = lax.all_to_all(slots, ("tm", "space"), 0, 0, tiled=True)
    (slots,) = call(
        functools.partial(sweep_kernel, share, rows),
        [(devices * held, LANES)],
        [(space * rows, LANES)] * 2
        + [(tm, space * rows, LANES)] * 2
        + [(LANES // share, 8 + space * rows + 2 * rows + held, LANES)]
        + [(LANES // share, 16 + space * rows, LANES)],
        slots, windows.reshape(-1, LANES),
    )
    slots = slots.reshape(devices, held, 1, LANES)
    slots = lax.all_to_all(slots, ("tm", "space"), 0, 0, tiled=True)
    (out,) = call(
        functools.partial(up_kernel, share),
        [(points, rows, cols)],
        [(6, wide, depth, LANES)]
        + buffers
        + [(points * rows * depth, LANES), (points, rows, cols)],
        slots.reshape(devices * held, LANES), next_forcing, late_a, late_b, core, coefs,
        to=pltpu.HBM, sems=points,
    )
    return out


def solution(mesh):
    placed = (P("tm", "space", None), P("tm", "space", None), P("space", None), P("space", None))
    return jax.shard_map(
        body, mesh=mesh, in_specs=placed, out_specs=P("tm", "space", None), check_vma=False
    )
```

```python
import functools

import jax
import jax.numpy as jnp
from jax import lax
from jax.experimental import pallas as pl
from jax.experimental.pallas import tpu as pltpu
from jax.sharding import PartitionSpec as P

LANES = 128
MARGIN = 4
REACH = 32
UP_RIM = 2
POINTS = 8
FIELDS = 3
CORE_COST = 30_000_000
diffusion_number = 0.03
time_step = 0.02

CHAINS = POINTS // 2 - 1
EDGE_0 = 4 * CHAINS + 6
SLANT_0 = 4
TURN = 2
EDGE_1 = 8
CORES = ("e0", "e1", "e2", "o0", "o1", "o2", "o3", "s0", "s1", "s2", "s3", "d", "g")


def params(mib):
    return pltpu.CompilerParams(vmem_limit_bytes=int(mib * 2**20))


def call(
    kernel, outs, scratch, *args, mib=16, place=pltpu.VMEM, to=pltpu.VMEM, sems=0, cost=None
):
    if place == pltpu.HBM:
        args = [pltpu.with_memory_space_constraint(arg, place) for arg in args]
    return pl.pallas_call(
        kernel,
        out_shape=tuple(jax.ShapeDtypeStruct(shape, jnp.float32) for shape in outs),
        in_specs=[pl.BlockSpec(memory_space=place)] * len(args),
        out_specs=tuple(pl.BlockSpec(memory_space=to) for _ in outs),
        scratch_shapes=[pltpu.VMEM(shape, jnp.float32) for shape in scratch]
        + ([pltpu.SemaphoreType.DMA((sems,))] if sems else []),
        compiler_params=params(mib),
        cost_estimate=cost,
    )(*args)


def beside(mid):
    depth = mid.shape[1]
    lane = lax.broadcasted_iota(jnp.int32, mid.shape, 2)
    line = lax.broadcasted_iota(jnp.int32, mid.shape, 1)
    left = pltpu.roll(mid, 1, 2)
    left_turn = pltpu.roll(left, 1, 1)
    right = pltpu.roll(mid, LANES - 1, 2)
    right_turn = pltpu.roll(right, depth - 1, 1)
    left = jnp.where(lane == 0, jnp.where(line == 0, 0.0, left_turn), left)
    right = jnp.where(lane == LANES - 1, jnp.where(line == depth - 1, 0.0, right_turn), right)
    return left + right


def slope_of_rows(wide, diff, grow):
    mid = wide[1:-1]
    laplace = wide[:-2] + wide[2:] + beside(mid) - 4.0 * mid
    return mid, diff * laplace + grow * mid / (1.0 + mid * mid)


def growth_of(ref, at, rows, diff, grow):
    return slope_of_rows(ref[pl.ds(at - 1, rows + 2)], diff, grow)


def over_rows(rows, rim, body):
    body(MARGIN - rim, rows + 2 * rim)


def flags():
    slab = lax.axis_index("space")
    low = jnp.where(slab > 0, 1.0, 0.0).astype(jnp.float32)
    high = jnp.where(slab < lax.axis_size("space") - 1, 1.0, 0.0).astype(jnp.float32)
    return low, high


def rim_rows(rows, low, high):
    return (
        (lambda k: MARGIN - k, low),
        (lambda k: MARGIN + rows - 1 + k, high),
    )


def pieces(name, evens, source, diffusivity, growth):
    if name == "d":
        return lambda rows, cols: diffusivity[rows, cols] * diffusion_number
    if name == "g":
        return lambda rows, cols: growth[rows, cols] * time_step
    if name == "ep":
        return lambda rows, cols: evens[POINTS // 2 - 1, rows, cols]
    if name == "op":
        return lambda rows, cols: source[POINTS - 1, rows, cols]
    which = int(name[1])
    if name[0] == "e":
        return lambda rows, cols: evens[which, rows, cols]
    return lambda rows, cols: source[2 * which + (name[0] == "o"), rows, cols]


def fetch(initial_all, source_all, diffusivity_all, growth_all, evens, source, coefs, sems):
    pairs = [(initial_all.at[2 * i], evens.at[i]) for i in range(POINTS // 2)]
    pairs += [(diffusivity_all, coefs.at[0]), (growth_all, coefs.at[1]), (source_all, source)]
    copies = [pltpu.make_async_copy(*pair, sems.at[i]) for i, pair in enumerate(pairs)]
    for copy in copies:
        copy.start()
    return copies[:-1], copies[-1]


def target_of(by):
    slabs = lax.axis_size("space")
    return lax.axis_index("tm") * slabs + (lax.axis_index("space") + by) % slabs


SCRATCH = 10


def pack_kernel(
    share, initial_all, source_all, diffusivity_all, growth_all,
    down, up, slant_down, slant_up, inward, outward,
    evens, source, coefs, edge, cells, turn, sems,
):
    waits, last = fetch(
        initial_all, source_all, diffusivity_all, growth_all, evens, source, coefs, sems
    )
    _, rows, cols = coefs.shape
    depth = cols // LANES
    diffusivity, growth = coefs.at[0], coefs.at[1]

    def put(ref, at, name, first, count):
        get = pieces(name, evens, source, diffusivity, growth)
        for c in range(depth):
            place = pl.ds(at * depth + c, count, stride=depth)
            ref[place, :] = get(pl.ds(first, count), pl.ds(c * LANES, LANES))

    def rows_of(ref, at, count):
        return ref[pl.ds(at * depth, count * depth), :].reshape(count, depth, LANES)

    def coef_rows(which, first, count):
        return rows_of(cells, which * rows + first, count)

    chains = [(f"e{i}", f"o{i}", f"s{i + 1}", f"o{i + 1}") for i in range(CHAINS)]
    chains.append(("ep", "op", None, None))
    sides = ((down, slant_down, False), (up, slant_up, True))

    def near(upward, count):
        return 0 if upward else rows - count

    for wait in waits:
        wait.wait()
    for index, name in enumerate(("d", "g")):
        for r in range(0, rows, 8):
            put(cells, index * rows + r, name, r, 8)
    for side, (rim, slant, upward) in enumerate(sides):
        for i, (start, _, _, _) in enumerate(chains):
            put(edge, (2 * i + side) * SCRATCH, start, near(upward, 4), 4)
        put_rows(rim, 4 * CHAINS + 3, coef_rows(0, near(upward, 2), 2))
        put_rows(rim, 4 * CHAINS + 5, coef_rows(1, near(upward, 1), 1))
    end = EDGE_0 * depth
    if end < down.shape[0]:
        for index in range(2):
            get = lambda line: cells[pl.ds(index * rows * depth + line, rows, stride=depth), :]
            down[pl.ds(end + index * rows, rows), :] = window(get, target_of(2) * share, depth)
    put_rows(turn, 0, jnp.zeros((1, depth, LANES), jnp.float32))
    for r in range(0, rows, 8):
        put(turn, 1 + r, "ep", r, 8)
    put_rows(turn, rows + 1, jnp.zeros((1, depth, LANES), jnp.float32))
    last.wait()
    for side, (rim, slant, upward) in enumerate(sides):
        for i, (_, term, after, after_odd) in enumerate(chains):
            spot = (2 * i + side) * SCRATCH
            put(edge, spot + 4, term, near(upward, 3), 3)
            if after:
                put(edge, spot + 7, after, near(upward, 2), 2)
                put(edge, spot + 9, after_odd, near(upward, 1), 1)
        put(rim, 4 * CHAINS, "s0", near(upward, 2), 2)
        put(rim, 4 * CHAINS + 2, "o0", near(upward, 1), 1)
    for r in range(0, rows, 8):
        put(turn, rows + 2 + r, "op", r, 8)
        put(turn, 2 * rows + 2 + r, "s0", r, 8)
    ahead = lax.axis_index("tm") % 2 == 0
    wide = rows_of(turn, 0, rows + 2)
    mid, slope = slope_of_rows(wide, coef_rows(0, 0, rows), coef_rows(1, 0, rows))
    forward = mid + slope + rows_of(turn, rows + 2, rows)
    backward = rows_of(turn, 2 * rows + 2, rows)
    put_rows(inward, 0, jnp.where(ahead, forward, backward))
    put_rows(outward, 0, jnp.where(ahead, backward, forward))
    for i, row in enumerate((1, rows)):
        for to in (inward, outward):
            put_rows(to, rows + i, rows_of(turn, row, 1))
    for side, (rim, slant, upward) in enumerate(sides):
        n0, n1, inner = (0, 1, 1) if upward else (rows - 1, rows - 2, rows - 3)
        diff0, diff1, grow1 = coef_rows(0, n0, 1), coef_rows(0, n1, 1), coef_rows(1, n1, 1)
        nothing = jnp.zeros_like(diff0)

        def pick(value, k):
            place = k if upward else value.shape[0] - 1 - k
            return value[place : place + 1]

        for i, (_, _, after, _) in enumerate(chains):
            spot = (2 * i + side) * SCRATCH
            start, term = rows_of(edge, spot, 4), rows_of(edge, spot + 4, 3)
            mid, slope = slope_of_rows(start, coef_rows(0, inner, 2), coef_rows(1, inner, 2))
            inner_term = term[1:] if upward else term[:-1]
            odd = mid + slope + inner_term
            wide = [nothing, odd] if upward else [odd, nothing]
            mid, slope = slope_of_rows(jnp.concatenate(wide, axis=0), diff1, grow1)
            part = mid + slope
            odd1 = pick(odd, 0)
            to, at = (rim, 4 * i) if after else (slant, 0)
            put_rows(to, at, pick(start, 0))
            put_rows(to, at + 1, pick(term, 0) + diff0 * pick(start, 1))
            if after:
                follow = rows_of(edge, spot + 7, 2)
                put_rows(to, at + 2, pick(follow, 0) + diff0 * odd1)
                part = part + pick(follow, 1)
                put_rows(to, at + 3, rows_of(edge, spot + 9, 1) + diff0 * part)
            else:
                put_rows(to, at + 2, odd1)
                put_rows(to, at + 3, part)


def column_of(shape, offset):
    lane = lax.broadcasted_iota(jnp.int32, shape, len(shape) - 1)
    return jnp.where(lane < LANES - REACH, lane, lane - LANES) + offset


def window(get, first, depth):
    line, offset = first // LANES, first % LANES
    source = column_of(get(0).shape, offset)
    shift = (LANES - offset) % LANES
    before = jnp.where(line > 0, pltpu.roll(get(jnp.maximum(line - 1, 0)), shift, 1), 0.0)
    here = pltpu.roll(get(line), shift, 1)
    after = jnp.where(
        line < depth - 1, pltpu.roll(get(jnp.minimum(line + 1, depth - 1)), shift, 1), 0.0
    )
    return jnp.where(source < 0, before, jnp.where(source >= LANES, after, here))


def core_kernel(
    share, initial_all, source_all, diffusivity_all, growth_all, core, *refs
):
    *windows, evens, source, coefs, sems = refs
    waits, last = fetch(
        initial_all, source_all, diffusivity_all, growth_all, evens, source, coefs, sems
    )
    for wait in (*waits, last):
        wait.wait()
    _, rows, cols = coefs.shape
    depth = cols // LANES
    for index, name in enumerate(CORES):
        get = pieces(name, evens, source, coefs.at[0], coefs.at[1])
        for c in range(depth):
            for r in range(0, rows, 8):
                value = get(pl.ds(r, 8), pl.ds(c * LANES, LANES))
                core[pl.ds((index * rows + r) * depth + c, 8, stride=depth), :] = value
    for by, out in zip(sent_windows(lax.axis_size("space")), windows, strict=True):
        for which, name in enumerate(("d", "g")):
            start = CORES.index(name) * rows * depth
            get = lambda line: core[pl.ds(start + line, rows, stride=depth), :]
            out[pl.ds(which * rows, rows)] = window(get, target_of(by) * share, depth)


def handed_on(slabs):
    return slabs == 4


def far_windows(slabs):
    return [] if handed_on(slabs) else list(range(2, slabs - 1))


def sent_windows(slabs):
    return [0, 1, slabs - 1] + far_windows(slabs)


def level0_kernel(
    core, above, below, behind_above, behind_below, inward, outward, own, ahead_one, behind_one,
    *refs,
):
    distant = far_windows(lax.axis_size("space"))
    windows, refs = refs[: len(distant)], refs[len(distant) :]
    (
        turn, down, up, next_odd, last_odd, forcing, coefs, held, next_first,
        fields, diff, grow,
    ) = refs
    rows = core.shape[0] // len(CORES)
    low, high = flags()
    depth = core.shape[1]
    names = list(CORES) + ["ep", "op"]
    spots = {name: index for index, name in enumerate(names)}
    extra = len(names)
    halves = POINTS // 2
    odd = [extra + i for i in range(halves)]
    even = [extra + halves + i for i in range(halves)]
    image = [extra + 2 * halves + i for i in range(halves)]
    nothing = jnp.zeros((1, depth, LANES), jnp.float32)
    sides = rim_rows(rows, low, high)
    for (at, flag), rim, slant in zip(
        sides, (above, below), (behind_above, behind_below), strict=True
    ):

        def put(name, k, ref, row):
            fields[spots[name] if isinstance(name, str) else name, pl.ds(at(k), 1)] = (
                ref[pl.ds(row, 1)] * flag
            )

        for i in range(CHAINS):
            put(f"e{i}", 1, rim, 4 * i)
            put(f"o{i}", 1, rim, 4 * i + 1)
            put(f"s{i + 1}", 1, rim, 4 * i + 2)
            fields[spots[f"e{i}"], pl.ds(at(2), 1)] = nothing
            fields[odd[i + 1], pl.ds(at(2), 1)] = nothing
        put("ep", 1, slant, 0)
        put("op", 1, slant, 1)
        put(odd[0], 2, slant, 2)
        fields[spots["ep"], pl.ds(at(2), 1)] = nothing
        first_row = min(at(1), at(2))
        edge_at = 4 * CHAINS
        fields[spots["s0"], pl.ds(first_row, 2)] = rim[pl.ds(edge_at, 2)] * flag
        diff[pl.ds(first_row, 2)] = rim[pl.ds(edge_at + 3, 2)] * flag
        grow[pl.ds(at(1), 1)] = rim[pl.ds(edge_at + 5, 1)] * flag
        grow[pl.ds(at(2), 1)] = nothing
    for name in CORES:
        if name in ("d", "g"):
            buffer = diff if name == "d" else grow
        else:
            buffer = fields.at[spots[name]]
        buffer[pl.ds(MARGIN, rows)] = core[pl.ds(CORES.index(name) * rows, rows)]
    even_block = lax.axis_index("tm") % 2 == 0
    cells = pl.ds(0, rows)
    from_behind = jnp.where(even_block, outward[cells], inward[cells])
    ahead = jnp.where(even_block, inward[cells], outward[cells])
    fields[odd[0], pl.ds(MARGIN, rows)] = from_behind
    for (at, _), row, edge_row in zip(sides, (0, 1), (0, rows - 1), strict=True):
        edge = pl.ds(rows + row, 1)
        fields[spots["ep"], pl.ds(MARGIN + edge_row, 1)] = jnp.where(
            even_block, outward[edge], inward[edge]
        )
        near, first = pl.ds(at(1), 1), pl.ds(MARGIN + edge_row, 1)
        mid, slope = growth_of(fields.at[spots["ep"]], at(1), 1, diff[near], grow[near])
        fields[odd[0], near] = mid + slope + fields[spots["op"], near]
        fields[odd[0], first] = fields[odd[0], first] + diff[first] * mid

    def first(at, n):
        d, g = diff[pl.ds(at, n)], grow[pl.ds(at, n)]
        for i in range(CHAINS):
            mid, slope = growth_of(fields.at[spots[f"e{i}"]], at, n, d, g)
            fields[odd[i + 1], pl.ds(at, n)] = mid + slope + fields[spots[f"o{i}"], pl.ds(at, n)]

    def second(at, n):
        d, g = diff[pl.ds(at, n)], grow[pl.ds(at, n)]
        for i in range(halves):
            mid, slope = growth_of(fields.at[odd[i]], at, n, d, g)
            fields[even[i], pl.ds(at, n)] = mid + slope + fields[spots[f"s{i}"], pl.ds(at, n)]

    def third(at, n):
        d, g = diff[pl.ds(at, n)], grow[pl.ds(at, n)]
        for i in range(halves):
            mid, slope = growth_of(fields.at[even[i]], at, n, d, g)
            fields[odd[i], pl.ds(at, n)] = mid + slope + fields[spots[f"o{i}"], pl.ds(at, n)]
            fields[image[i], pl.ds(at, n)] = mid + 2.0 * slope

    def fourth(at, n):
        d, g = diff[pl.ds(at, n)], grow[pl.ds(at, n)]
        here = at - MARGIN
        for i in range(halves):
            mid, slope = growth_of(fields.at[odd[i]], at, n, d, g)
            pair = mid + slope - fields[image[i], pl.ds(at, n)]
            if i == halves - 1:
                next_first[...] = ahead + pair
            else:
                term = fields[spots[f"s{i + 1}"], pl.ds(at, n)] + pair
                forcing[pl.ds(i * rows + here, n)] = term
                if i < 2:
                    turn[pl.ds(i * rows + here, n)] = term
                if i == 0:
                    next_odd[...] = fields[image[0], pl.ds(at, n)] + term
                if i == halves - 2:
                    last_odd[...] = fields[image[i], pl.ds(at, n)] + term

    over_rows(rows, 1, first)
    over_rows(rows, 1, second)
    for (at, flag), rim, slant in zip(
        sides, (above, below), (behind_above, behind_below), strict=True
    ):
        near, far = pl.ds(at(1), 1), pl.ds(at(2), 1)
        for i in range(halves):
            place = 4 * CHAINS + 2 if i == 0 else 4 * i - 1
            fields[spots[f"o{i}"], near] = rim[pl.ds(place, 1)] * flag
            value = diff[far] * fields[odd[i], near]
            if i == 0:
                value = value + fields[spots["s0"], far] + slant[pl.ds(3, 1)] * flag
            fields[even[i], far] = value
    over_rows(rows, 1, third)
    over_rows(rows, 0, fourth)
    coefs[pl.ds(0, rows + 4)] = diff[pl.ds(MARGIN - 2, rows + 4)]
    coefs[pl.ds(rows + 4, rows + 4)] = grow[pl.ds(MARGIN - 2, rows + 4)]
    for rim, n0, n1 in ((down, rows - 1, rows - 2), (up, 0, 1)):

        def row(ref, first, n):
            return ref[pl.ds(first + n, 1)]

        diff0 = 2.0 * row(diff, MARGIN, n0)
        around = [
            slope_of_rows(
                ref[pl.ds(first + n1 - 1, 3)], row(diff, MARGIN, n1), row(grow, MARGIN, n1)
            )
            for ref, first in ((next_odd, 0), (last_odd, 0))
        ]
        (mid, slope), (mid_last, slope_last) = around
        even1 = mid + 2.0 * slope + row(forcing, rows, n1)
        g3 = row(forcing, 2 * rows, n0)
        rim[pl.ds(0, 1)] = row(next_odd, 0, n0)
        rim[pl.ds(1, 1)] = row(forcing, rows, n0) + diff0 * mid
        rim[pl.ds(2, 1)] = g3 + diff0 * even1
        rim[pl.ds(3, 1)] = g3
        rim[pl.ds(4, 1)] = row(forcing, 0, n0)
        rim[pl.ds(5, 1)] = row(last_odd, 0, n0)
        rim[pl.ds(6, 1)] = row(next_first, 0, n0) + diff0 * mid_last
        rim[pl.ds(7, 1)] = row(next_first, 0, n1) + mid_last + 2.0 * slope_last
    slab, slabs = lax.axis_index("space"), lax.axis_size("space")
    size = 2 * rows // depth
    down[pl.ds(EDGE_1, size)] = ahead_one[...]
    up[pl.ds(EDGE_1, size)] = behind_one[...]
    if handed_on(slabs):
        down[pl.ds(EDGE_1 + size, size)] = above[pl.ds(EDGE_0, size)]
    for by, part in zip([0] + distant, (own, *windows), strict=True):
        held[pl.ds((slab - by) % slabs * size, size)] = part[...]


def take_coefs(rows, coefs, diff, grow):
    diff[pl.ds(MARGIN - 2, rows + 4)] = coefs[pl.ds(0, rows + 4)]
    grow[pl.ds(MARGIN - 2, rows + 4)] = coefs[pl.ds(rows + 4, rows + 4)]


def level1_kernel(
    share, next_odd, last_odd, forcing, coefs, next_first, held, above, below, ahead_terms,
    slots, next_forcing, late_a, late_b, windows,
    fields, diff, grow, flat,
):
    rows = forcing.shape[0] // 3
    low, high = flags()
    take_coefs(rows, coefs, diff, grow)
    windows[...] = held[...]
    slab, slabs = lax.axis_index("space"), lax.axis_size("space")
    size = windows.shape[0] // slabs
    windows[pl.ds((slab - 1) % slabs * size, size)] = above[pl.ds(EDGE_1, size)]
    windows[pl.ds((slab + 1) % slabs * size, size)] = below[pl.ds(EDGE_1, size)]
    if handed_on(slabs):
        windows[pl.ds((slab - 2) % slabs * size, size)] = above[pl.ds(EDGE_1 + size, size)]
    g1, g3, g2, g0, before, after, even0, even1, image0, image1, odd0, odd1 = range(12)
    nothing = jnp.zeros((1, *forcing.shape[1:]), jnp.float32)
    sides = rim_rows(rows, low, high)
    core = pl.ds(MARGIN, rows)
    fields[after, core] = next_odd[...]
    fields[before, core] = last_odd[...]
    fields[g0, core] = next_first[...]
    fields[g1, core] = ahead_terms[pl.ds(0, rows)]
    fields[g2, core] = forcing[pl.ds(rows, rows)]
    fields[g3, core] = forcing[pl.ds(2 * rows, rows)]
    for (at, flag), rim in zip(sides, (above, below), strict=True):
        near, far = pl.ds(at(1), 1), pl.ds(at(2), 1)
        for spot, row in ((after, 0), (g2, 1), (g3, 2), (before, 5), (g0, 6)):
            fields[spot, near] = rim[pl.ds(row, 1)] * flag
        fields[even0, far] = rim[pl.ds(7, 1)] * flag
        fields[g1, near] = nothing
        for spot in (after, before, even1):
            fields[spot, far] = nothing

    def second(at, n):
        d, g = diff[pl.ds(at, n)], grow[pl.ds(at, n)]
        for start, term, end in ((before, g0, even0), (after, g2, even1)):
            mid, slope = growth_of(fields.at[start], at, n, d, g)
            fields[end, pl.ds(at, n)] = mid + 2.0 * slope + fields[term, pl.ds(at, n)]

    def third(at, n):
        d, g = diff[pl.ds(at, n)], grow[pl.ds(at, n)]
        for start, term, end, image in ((even0, g1, odd0, image0), (even1, g3, odd1, image1)):
            mid, slope = growth_of(fields.at[start], at, n, d, g)
            fields[end, pl.ds(at, n)] = mid + 2.0 * slope + fields[term, pl.ds(at, n)]
            fields[image, pl.ds(at, n)] = mid + 4.0 * slope

    def fourth(at, n):
        d, g = diff[pl.ds(at, n)], grow[pl.ds(at, n)]
        here = at - MARGIN
        mid, slope = growth_of(fields.at[odd1], at, n, d, g)
        pair1 = mid + 2.0 * slope - fields[image1, pl.ds(at, n)]
        put_rows(flat, rows, next_first[...] + pair1)
        mid, slope = growth_of(fields.at[odd0], at, n, d, g)
        image = fields[image0, pl.ds(at, n)]
        term = ahead_terms[pl.ds(rows, rows)] + (mid + 2.0 * slope - image)
        next_forcing[pl.ds(here, n)] = term
        put_rows(flat, 2 * rows, term)
        put_rows(flat, 0, image + term)

    over_rows(rows, 1, second)
    over_rows(rows, 1, third)
    over_rows(rows, 0, fourth)
    for late, which, row in ((late_a, 0, 4), (late_b, 2, 3)):
        late[pl.ds(1, rows)] = forcing[pl.ds(which * rows, rows)]
        late[pl.ds(0, 1)] = above[pl.ds(row, 1)] * low
        late[pl.ds(rows + 1, 1)] = below[pl.ds(row, 1)] * high
    depth = forcing.shape[1]
    put_rows(flat, FIELDS * rows, ahead_terms[pl.ds(0, 1)])
    put_rows(flat, FIELDS * rows + 1, ahead_terms[pl.ds(rows - 1, 1)])
    if folded(rows, share, reach_of()):
        pack_folded(slots, flat, rows, depth, reach_of())
    else:
        pack_windows(slots, flat, rows, depth, share)


def put_rows(flat, first, value):
    depth = value.shape[1]
    for i in range(value.shape[0]):
        flat[pl.ds((first + i) * depth, depth), :] = value[i]


def reach_of():
    return lax.axis_size("tm") + 2


def slot_lines(rows, share, reach):
    return (FIELDS * 8 + 8 if folded(rows, share, reach) else FIELDS * rows) + 2


def folded(rows, share, reach):
    return rows == 16 and 2 * share == LANES and FIELDS * 2 * reach <= share


def pack_folded(slots, flat, rows, depth, reach):
    lines = slot_lines(rows, LANES // 2, reach)
    devices = slots.shape[0] // lines
    lane = lax.broadcasted_iota(jnp.int32, (8, LANES), 1)
    place = lane % (LANES // 2)
    rims = [None] * devices
    for field in range(FIELDS):
        first = field * rows * depth
        cells = []
        for line in range(depth):
            top = flat[pl.ds(first + line, 8, stride=depth), :]
            low = flat[pl.ds(first + 8 * depth + line, 8, stride=depth), :]
            cells.append(jnp.where(lane < LANES // 2, top, pltpu.roll(low, LANES // 2, 1)))
            cells.append(jnp.where(lane < LANES // 2, pltpu.roll(top, LANES // 2, 1), low))
        for target in range(devices):
            slots[pl.ds(target * lines + field * 8, 8), :] = cells[target]
            left = cells[target - 1] if target > 0 else 0.0
            right = cells[target + 1] if target < devices - 1 else 0.0
            rim = jnp.where(
                place >= LANES // 2 - reach, left, jnp.where(place < reach, right, 0.0)
            )
            if field == 0:
                rims[target] = rim
            else:
                rims[target] = rims[target] + pltpu.roll(rim, 2 * reach * field, 1)
    for target in range(devices):
        slots[pl.ds(target * lines + FIELDS * 8, 8), :] = rims[target]
    top = flat[pl.ds(FIELDS * rows * depth, depth), :]
    low = flat[pl.ds((FIELDS * rows + 1) * depth, depth), :]
    lane = lax.broadcasted_iota(jnp.int32, (depth, LANES), 1)
    line = lax.broadcasted_iota(jnp.int32, (depth, LANES), 0)
    place = lane % (LANES // 2)
    evens = jnp.where(lane < LANES // 2, top, pltpu.roll(low, LANES // 2, 1))
    odds = jnp.where(lane < LANES // 2, pltpu.roll(top, LANES // 2, 1), low)
    before = jnp.where(line == 0, 0.0, pltpu.roll(odds, 1, 0))
    after = jnp.where(line == depth - 1, 0.0, pltpu.roll(evens, depth - 1, 0))
    for parity, cells, left, right in ((0, evens, before, odds), (1, odds, evens, after)):
        rim = jnp.where(place >= LANES // 2 - reach, left, jnp.where(place < reach, right, 0.0))
        for i, value in enumerate((cells, rim)):
            start = parity * lines + lines - 2 + i
            slots[pl.ds(start, depth, stride=2 * lines), :] = value


def unfold(slot, field, reach):
    cells, rims = slot[pl.ds(field * 8, 8)], slot[pl.ds(FIELDS * 8, 8)]
    lane = lax.broadcasted_iota(jnp.int32, (8, LANES), 1)
    half = LANES // 2
    back = 2 * reach * field
    top = pltpu.roll(rims, (half - back) % LANES, 1)
    low = pltpu.roll(rims, (-back) % LANES, 1) if back else rims
    return jnp.concatenate(
        [
            jnp.where(lane < half, cells, top),
            jnp.where(lane < half, pltpu.roll(cells, half, 1), low),
        ],
        axis=0,
    )


def unfold_row(slot, which):
    last = slot.shape[0] - 2
    cells, rims = slot[pl.ds(last, 1)], slot[pl.ds(last + 1, 1)]
    lane = lax.broadcasted_iota(jnp.int32, (1, LANES), 1)
    half = LANES // 2
    if which == 0:
        return jnp.where(lane < half, cells, pltpu.roll(rims, half, 1))
    return jnp.where(lane < half, pltpu.roll(cells, half, 1), rims)


def pack_windows(slots, flat, rows, depth, share):
    lines = slot_lines(rows, share, reach_of())
    for field in range(FIELDS + 1):
        first, count = field * rows * depth, rows if field < FIELDS else 2
        held = [flat[pl.ds(first + line, count, stride=depth), :] for line in range(depth)]
        for target in range(slots.shape[0] // lines):
            line, offset = target * share // LANES, target * share % LANES
            shift = (LANES - offset) % LANES
            place = column_of((count, LANES), offset)
            value = pltpu.roll(held[line], shift, 1)
            if offset < REACH:
                before = pltpu.roll(held[line - 1], shift, 1) if line > 0 else 0.0
                value = jnp.where(place < 0, before, value)
            if offset > REACH:
                after = pltpu.roll(held[line + 1], shift, 1) if line < depth - 1 else 0.0
                value = jnp.where(place >= LANES, after, value)
            slots[pl.ds(target * lines + field * rows, count), :] = value


def late_rows(rows):
    return (("forcing", rows), ("forcing", -1), ("odd", rows + 1), ("odd", -2))


def packing(rows, share):
    groups = LANES // share
    each = -(-(rows + 2 * UP_RIM) // groups)
    return groups, each, each + -(-4 // groups)


def sweep_kernel(share, rows, arrived, windows, slots, diff, grow, terms, owns, adds, padded, odds):
    slabs = lax.axis_size("space")
    reach = reach_of()
    lines = slot_lines(rows, share, reach)
    devices = arrived.shape[0] // lines
    blocks = devices // slabs
    total = slabs * rows
    groups, each, held = packing(rows, share)
    for slab in range(slabs):
        diff[pl.ds(slab * rows, rows), :] = windows[pl.ds(2 * slab * rows, rows), :]
        grow[pl.ds(slab * rows, rows), :] = windows[pl.ds((2 * slab + 1) * rows, rows), :]
    line = lax.broadcasted_iota(jnp.int32, (total, LANES), 0)
    lane = lax.broadcasted_iota(jnp.int32, (each, LANES), 1)
    padded[...] = jnp.zeros(padded.shape, jnp.float32)
    odds[...] = jnp.zeros(odds.shape, jnp.float32)

    def block(field, index):
        parts = []
        for slab in range(slabs):
            slot = arrived.at[pl.ds((index * slabs + slab) * lines, lines)]
            if folded(rows, share, reach):
                parts.append(unfold(slot, field, reach))
            else:
                parts.append(slot[pl.ds(field * rows, rows)])
        return jnp.concatenate(parts, axis=0)

    adds[...] = jnp.zeros(adds.shape, jnp.float32)

    def beyond(index):
        for slab in range(slabs):
            slot = arrived.at[pl.ds((index * slabs + slab) * lines, lines)]
            for which, at in ((0, slab * rows - 1), (1, (slab + 1) * rows)):
                if not 0 <= at < total:
                    continue
                if folded(rows, share, reach):
                    piece = unfold_row(slot, which)
                else:
                    piece = slot[pl.ds(FIELDS * rows + which, 1)]
                adds[index, pl.ds(at, 1), :] = 2.0 * diff[pl.ds(at, 1), :] * piece

    def slope_of(field):
        north = jnp.where(line == 0, 0.0, pltpu.roll(field, 1, 0))
        south = jnp.where(line == total - 1, 0.0, pltpu.roll(field, total - 1, 0))
        sides = pltpu.roll(field, 1, 1) + pltpu.roll(field, LANES - 1, 1)
        laplace = north + south + sides - 4.0 * field
        return diff[...] * laplace + grow[...] * field / (1.0 + field * field)

    def put_late(index, slab):
        to = slots.at[pl.ds((index * slabs + slab) * held, held)]
        for i, (what, row) in enumerate(late_rows(rows)):
            at, group = each + i // groups, i % groups
            place = slab * rows + row
            if what == "odd":
                piece = odds[group, pl.ds(8 + place, 1)]
            elif 0 <= place < total:
                piece = owns[index, pl.ds(place, 1)]
                piece = pltpu.roll(piece, group * share, 1) if group else piece
            else:
                piece = jnp.zeros((1, LANES), jnp.float32)
            if group:
                piece = jnp.where(lane[:1] >= group * share, piece, to[pl.ds(at, 1)])
            to[pl.ds(at, 1)] = piece

    field = None
    for index in range(blocks):
        beyond(index)
    for index in range(blocks):
        behind, twice = (index - 1) % blocks, (index - 2) % blocks
        odd, term = block(0, twice) + adds[twice], block(1, behind)
        even = odd + 4.0 * slope_of(odd) + term
        slope = slope_of(even)
        own = block(2, behind) + adds[behind]
        owns[index] = own
        odd = even + 4.0 * slope + own
        stepped = even + 8.0 * slope
        pair = odd + 4.0 * slope_of(odd) - stepped
        terms[index] = block(1, index) + pair
        if index == blocks - 1:
            field = stepped + terms[index]
    for index in range(blocks):
        slope = slope_of(field)
        odd = field + 4.0 * slope + owns[index]
        for group in range(groups):
            for to, value in ((padded, field), (odds, odd)):
                to[group, pl.ds(8, total), :] = (
                    pltpu.roll(value, group * share, 1) if group else value
                )
        for slab in range(slabs):
            start = 8 + slab * rows - UP_RIM
            value = padded[0, pl.ds(start, each), :]
            for group in range(1, groups):
                piece = padded[group, pl.ds(start + group * each, each), :]
                value = jnp.where(lane >= group * share, piece, value)
            slots[pl.ds((index * slabs + slab) * held, each), :] = value
            put_late(index, slab)
        if index < blocks - 1:
            field = field + 8.0 * slope + terms[index]


def up_kernel(
    share, arrived, next_forcing, late_a, late_b, core, coefs,
    out, fields, diff, grow, flat, ready, sems,
):
    rows, depth, _ = next_forcing.shape
    groups, each, held = packing(rows, share)
    take_coefs(rows, coefs, diff, grow)
    lane = lax.broadcasted_iota(jnp.int32, (depth, LANES), 1)

    def whole(line, group):
        value = None
        for part in range(groups):
            piece = arrived[pl.ds(part * held + line, depth, stride=groups * held), :]
            if part != group:
                piece = pltpu.roll(piece, ((part - group) * share) % LANES, 1)
            value = piece if value is None else jnp.where(lane >= part * share, piece, value)
        return value

    for row in range(rows + 2 * UP_RIM):
        fields[0, MARGIN - UP_RIM + row] = whole(row % each, row // each)
    for i, (what, row) in enumerate(late_rows(rows)):
        spot = 5 if what == "forcing" else 2
        fields[spot, MARGIN + row] = whole(each + i // groups, i % groups)
    fields[5, pl.ds(MARGIN, rows)] = next_forcing[...]
    for row, rim in ((0, 0), (rows - 1, rows + 1)):
        spot = pl.ds(MARGIN + row, 1)
        added = 2.0 * diff[spot] * late_a[pl.ds(rim, 1)]
        fields[5, spot] = next_forcing[pl.ds(row, 1)] + added
    odd_first = CORES.index("o0") * rows

    def first(at, n):
        mid, slope = growth_of(fields.at[0], at, n, diff[pl.ds(at, n)], grow[pl.ds(at, n)])
        fields[2, pl.ds(at, n)] = mid + 4.0 * slope + fields[5, pl.ds(at, n)]

    def second(at, n):
        d, g = diff[pl.ds(at, n)], grow[pl.ds(at, n)]
        for start, late in ((0, late_a), (2, late_b)):
            mid, slope = growth_of(fields.at[start], at, n, d, g)
            fields[start + 1, pl.ds(at, n)] = mid + 2.0 * slope + late[pl.ds(at - MARGIN + 1, n)]

    copies = []

    def emit(point, value):
        put_rows(flat, point * rows, value)
        for r in range(0, rows, 8):
            for c in range(depth):
                start = (point * rows + r) * depth + c
                ready[point, pl.ds(r, 8), pl.ds(c * LANES, LANES)] = flat[
                    pl.ds(start, 8, stride=depth), :
                ]
        copy = pltpu.make_async_copy(ready.at[point], out.at[point], sems.at[point])
        copy.start()
        copies.append(copy)

    def last(i):
        at, n = MARGIN, rows
        mid, slope = growth_of(fields.at[i], at, n, diff[pl.ds(at, n)], grow[pl.ds(at, n)])
        emit(2 * i + 1, mid + slope + core[pl.ds(odd_first + i * rows, n)])

    core_rows = pl.ds(MARGIN, rows)
    emit(0, fields[0, core_rows])
    over_rows(rows, 1, first)
    emit(4, fields[2, core_rows])
    over_rows(rows, 1, second)
    emit(2, fields[1, core_rows])
    emit(6, fields[3, core_rows])
    for i in (0, 2, 1, 3):
        last(i)
    for copy in copies:
        copy.wait()


def moved(array, blocks, slabs):
    tm, space = lax.axis_size("tm"), lax.axis_size("space")
    pairs = [
        (t * space + s, (t + blocks) % tm * space + (s + slabs) % space)
        for t in range(tm)
        for s in range(space)
    ]
    return lax.ppermute(array, ("tm", "space"), pairs)


def swapped(array, offset):
    tm, space = lax.axis_size("tm"), lax.axis_size("space")
    pairs = [
        (t * space + s, ((((t - offset) % tm) ^ 1) + offset) % tm * space + s)
        for t in range(tm)
        for s in range(space)
    ]
    return lax.ppermute(array, ("tm", "space"), pairs)


def rims(down, up, slant_down, slant_up):
    slanted = moved(slant_down, 1, 1), moved(slant_up, 1, -1)
    return moved(down, 0, 1), moved(up, 0, -1), *slanted


def body(initial, source, diffusivity, growth):
    points, rows, cols = initial.shape
    assert points == POINTS and lax.axis_size("tm") % 2 == 0 and rows % 8 == 0 and cols % LANES == 0
    depth = cols // LANES
    tm, space = lax.axis_size("tm"), lax.axis_size("space")
    devices = tm * space
    share = cols // devices
    assert share * devices == cols and LANES % share == 0
    assert reach_of() <= REACH and REACH + share + reach_of() <= LANES
    _, _, held = packing(rows, share)
    wide = rows + 2 * MARGIN

    def lines(n):
        return (n * depth, LANES)

    def field(n):
        return (n, depth, LANES)

    def as_rows(array):
        return array.reshape(-1, depth, LANES)

    window_rows = 2 * rows // depth
    assert window_rows * depth == 2 * rows
    raw = [(points // 2, rows, cols), source.shape, (2, rows, cols)]
    extra = window_rows if handed_on(space) else 0
    *sends, inward, outward = call(
        functools.partial(pack_kernel, share),
        [lines(EDGE_0 + extra), lines(EDGE_0), lines(SLANT_0), lines(SLANT_0)]
        + [lines(rows + TURN)] * 2,
        raw + [lines(2 * SCRATCH * (CHAINS + 1)), lines(2 * rows), lines(3 * rows + 2)],
        initial, source, diffusivity, growth,
        place=pltpu.HBM, sems=points // 2 + 3,
    )
    core, *windows = call(
        functools.partial(core_kernel, share),
        [lines(len(CORES) * rows)] + [(2 * rows, LANES)] * len(sent_windows(space)),
        raw,
        initial, source, diffusivity, growth,
        place=pltpu.HBM, sems=points // 2 + 3,
        cost=pl.CostEstimate(flops=0, transcendentals=0, bytes_accessed=CORE_COST),
    )
    sends, inward, outward = [as_rows(part) for part in sends], as_rows(inward), as_rows(outward)
    inward = swapped(inward, 0)
    inward, sends[2], sends[3] = lax.optimization_barrier((inward, sends[2], sends[3]))
    arrived = [*rims(*sends), inward, swapped(outward, 1)]
    windows = [as_rows(part) for part in windows]
    for i, by in enumerate(far_windows(space), 3):
        windows[i] = moved(windows[i], 0, by)
    core = as_rows(core)
    arrived, windows = lax.optimization_barrier((arrived, windows))

    buffers = [(wide, depth, LANES), (wide, depth, LANES)]
    turn, down, up, next_odd, last_odd, forcing, coefs, held_windows, next_first = call(
        level0_kernel,
        [
            field(2 * rows), field(EDGE_1 + window_rows + extra), field(EDGE_1 + window_rows),
            field(rows), field(rows), field(3 * rows), field(2 * (rows + 4)),
            field(window_rows * space), field(rows),
        ],
        [(len(CORES) + 2 + 3 * (POINTS // 2), wide, depth, LANES)] + buffers,
        core, *arrived, *windows,
    )
    above, below, ahead_terms = moved(down, 0, 1), moved(up, 0, -1), moved(turn, -1, 0)
    slot_rows = slot_lines(rows, share, reach_of())
    slots, next_forcing, late_a, late_b, windows = call(
        functools.partial(level1_kernel, share),
        [
            (devices * slot_rows, LANES),
            field(rows), field(rows + 2), field(rows + 2), field(window_rows * space),
        ],
        [(12, wide, depth, LANES)] + buffers + [((FIELDS * rows + 2) * depth, LANES)],
        next_odd, last_odd, forcing, coefs, next_first, held_windows, above, below, ahead_terms,
    )
    next_forcing = moved(next_forcing, 1, 0)
    slots = slots.reshape(devices, slot_rows, 1, LANES)
    slots = lax.all_to_all(slots, ("tm", "space"), 0, 0, tiled=True)
    slots = slots.reshape(devices * slot_rows, LANES)
    (slots,) = call(
        functools.partial(sweep_kernel, share, rows),
        [(devices * held, LANES)],
        [(space * rows, LANES)] * 2
        + [(tm, space * rows, LANES)] * 3
        + [(LANES // share, 8 + space * rows + 2 * rows + held, LANES)]
        + [(LANES // share, 16 + space * rows, LANES)],
        slots, windows.reshape(-1, LANES),
    )
    slots = slots.reshape(devices, held, 1, LANES)
    slots = lax.all_to_all(slots, ("tm", "space"), 0, 0, tiled=True)
    (out,) = call(
        functools.partial(up_kernel, share),
        [(points, rows, cols)],
        [(6, wide, depth, LANES)]
        + buffers
        + [(points * rows * depth, LANES), (points, rows, cols)],
        slots.reshape(devices * held, LANES), next_forcing, late_a, late_b, core, coefs,
        to=pltpu.HBM, sems=points,
    )
    return out


def solution(mesh):
    placed = (P("tm", "space", None), P("tm", "space", None), P("space", None), P("space", None))
    return jax.shard_map(
        body, mesh=mesh, in_specs=placed, out_specs=P("tm", "space", None), check_vma=False
    )
```

```python
import functools

import jax
import jax.numpy as jnp
from jax import lax
from jax.experimental import pallas as pl
from jax.experimental.pallas import tpu as pltpu
from jax.sharding import PartitionSpec as P

LANES = 128
MARGIN = 4
REACH = 32
UP_RIM = 2
POINTS = 8
FIELDS = 3
CORE_COST = 30_000_000
diffusion_number = 0.03
time_step = 0.02

CHAINS = POINTS // 2 - 1
EDGE_0 = 4 * CHAINS + 6
SLANT_0 = 4
TURN = 2
EDGE_1 = 8
CORES = ("e0", "e1", "e2", "o0", "o1", "o2", "o3", "s0", "s1", "s2", "s3", "d", "g")


def params(mib):
    return pltpu.CompilerParams(vmem_limit_bytes=int(mib * 2**20))


def call(
    kernel, outs, scratch, *args, mib=16, place=pltpu.VMEM, to=pltpu.VMEM, sems=0, cost=None
):
    if place == pltpu.HBM:
        args = [pltpu.with_memory_space_constraint(arg, place) for arg in args]
    return pl.pallas_call(
        kernel,
        out_shape=tuple(jax.ShapeDtypeStruct(shape, jnp.float32) for shape in outs),
        in_specs=[pl.BlockSpec(memory_space=place)] * len(args),
        out_specs=tuple(pl.BlockSpec(memory_space=to) for _ in outs),
        scratch_shapes=[pltpu.VMEM(shape, jnp.float32) for shape in scratch]
        + ([pltpu.SemaphoreType.DMA((sems,))] if sems else []),
        compiler_params=params(mib),
        cost_estimate=cost,
    )(*args)


def beside(mid):
    depth = mid.shape[1]
    lane = lax.broadcasted_iota(jnp.int32, mid.shape, 2)
    line = lax.broadcasted_iota(jnp.int32, mid.shape, 1)
    left = pltpu.roll(mid, 1, 2)
    left_turn = pltpu.roll(left, 1, 1)
    right = pltpu.roll(mid, LANES - 1, 2)
    right_turn = pltpu.roll(right, depth - 1, 1)
    left = jnp.where(lane == 0, jnp.where(line == 0, 0.0, left_turn), left)
    right = jnp.where(lane == LANES - 1, jnp.where(line == depth - 1, 0.0, right_turn), right)
    return left + right


def slope_of_rows(wide, diff, grow):
    mid = wide[1:-1]
    laplace = wide[:-2] + wide[2:] + beside(mid) - 4.0 * mid
    return mid, diff * laplace + grow * mid / (1.0 + mid * mid)


def growth_of(ref, at, rows, diff, grow):
    return slope_of_rows(ref[pl.ds(at - 1, rows + 2)], diff, grow)


def over_rows(rows, rim, body):
    body(MARGIN - rim, rows + 2 * rim)


def flags():
    slab = lax.axis_index("space")
    low = jnp.where(slab > 0, 1.0, 0.0).astype(jnp.float32)
    high = jnp.where(slab < lax.axis_size("space") - 1, 1.0, 0.0).astype(jnp.float32)
    return low, high


def rim_rows(rows, low, high):
    return (
        (lambda k: MARGIN - k, low),
        (lambda k: MARGIN + rows - 1 + k, high),
    )


def pieces(name, evens, source, diffusivity, growth):
    if name == "d":
        return lambda rows, cols: diffusivity[rows, cols] * diffusion_number
    if name == "g":
        return lambda rows, cols: growth[rows, cols] * time_step
    if name == "ep":
        return lambda rows, cols: evens[POINTS // 2 - 1, rows, cols]
    if name == "op":
        return lambda rows, cols: source[POINTS - 1, rows, cols]
    which = int(name[1])
    if name[0] == "e":
        return lambda rows, cols: evens[which, rows, cols]
    return lambda rows, cols: source[2 * which + (name[0] == "o"), rows, cols]


def fetch(initial_all, source_all, diffusivity_all, growth_all, evens, source, coefs, sems):
    pairs = [(initial_all.at[2 * i], evens.at[i]) for i in range(POINTS // 2)]
    pairs += [(diffusivity_all, coefs.at[0]), (growth_all, coefs.at[1]), (source_all, source)]
    copies = [pltpu.make_async_copy(*pair, sems.at[i]) for i, pair in enumerate(pairs)]
    for copy in copies:
        copy.start()
    return copies[:-1], copies[-1]


def target_of(by):
    slabs = lax.axis_size("space")
    return lax.axis_index("tm") * slabs + (lax.axis_index("space") + by) % slabs


SCRATCH = 10


def pack_kernel(
    share, initial_all, source_all, diffusivity_all, growth_all,
    down, up, slant_down, slant_up, inward, outward,
    evens, source, coefs, edge, cells, turn, sems,
):
    waits, last = fetch(
        initial_all, source_all, diffusivity_all, growth_all, evens, source, coefs, sems
    )
    _, rows, cols = coefs.shape
    depth = cols // LANES
    diffusivity, growth = coefs.at[0], coefs.at[1]

    def put(ref, at, name, first, count):
        get = pieces(name, evens, source, diffusivity, growth)
        for c in range(depth):
            place = pl.ds(at * depth + c, count, stride=depth)
            ref[place, :] = get(pl.ds(first, count), pl.ds(c * LANES, LANES))

    def rows_of(ref, at, count):
        return ref[pl.ds(at * depth, count * depth), :].reshape(count, depth, LANES)

    def coef_rows(which, first, count):
        return rows_of(cells, which * rows + first, count)

    chains = [(f"e{i}", f"o{i}", f"s{i + 1}", f"o{i + 1}") for i in range(CHAINS)]
    chains.append(("ep", "op", None, None))
    sides = ((down, slant_down, False), (up, slant_up, True))

    def near(upward, count):
        return 0 if upward else rows - count

    for wait in waits:
        wait.wait()
    for index, name in enumerate(("d", "g")):
        for r in range(0, rows, 8):
            put(cells, index * rows + r, name, r, 8)
    for side, (rim, slant, upward) in enumerate(sides):
        for i, (start, _, _, _) in enumerate(chains):
            put(edge, (2 * i + side) * SCRATCH, start, near(upward, 4), 4)
        put_rows(rim, 4 * CHAINS + 3, coef_rows(0, near(upward, 2), 2))
        put_rows(rim, 4 * CHAINS + 5, coef_rows(1, near(upward, 1), 1))
    end = EDGE_0 * depth
    if end < down.shape[0]:
        for index in range(2):
            get = lambda line: cells[pl.ds(index * rows * depth + line, rows, stride=depth), :]
            down[pl.ds(end + index * rows, rows), :] = window(get, target_of(2) * share, depth)
    put_rows(turn, 0, jnp.zeros((1, depth, LANES), jnp.float32))
    for r in range(0, rows, 8):
        put(turn, 1 + r, "ep", r, 8)
    put_rows(turn, rows + 1, jnp.zeros((1, depth, LANES), jnp.float32))
    last.wait()
    for side, (rim, slant, upward) in enumerate(sides):
        for i, (_, term, after, after_odd) in enumerate(chains):
            spot = (2 * i + side) * SCRATCH
            put(edge, spot + 4, term, near(upward, 3), 3)
            if after:
                put(edge, spot + 7, after, near(upward, 2), 2)
                put(edge, spot + 9, after_odd, near(upward, 1), 1)
        put(rim, 4 * CHAINS, "s0", near(upward, 2), 2)
        put(rim, 4 * CHAINS + 2, "o0", near(upward, 1), 1)
    for r in range(0, rows, 8):
        put(turn, rows + 2 + r, "op", r, 8)
        put(turn, 2 * rows + 2 + r, "s0", r, 8)
    ahead = lax.axis_index("tm") % 2 == 0
    wide = rows_of(turn, 0, rows + 2)
    mid, slope = slope_of_rows(wide, coef_rows(0, 0, rows), coef_rows(1, 0, rows))
    forward = mid + slope + rows_of(turn, rows + 2, rows)
    backward = rows_of(turn, 2 * rows + 2, rows)
    put_rows(inward, 0, jnp.where(ahead, forward, backward))
    put_rows(outward, 0, jnp.where(ahead, backward, forward))
    for i, row in enumerate((1, rows)):
        for to in (inward, outward):
            put_rows(to, rows + i, rows_of(turn, row, 1))
    for side, (rim, slant, upward) in enumerate(sides):
        n0, n1, inner = (0, 1, 1) if upward else (rows - 1, rows - 2, rows - 3)
        diff0, diff1, grow1 = coef_rows(0, n0, 1), coef_rows(0, n1, 1), coef_rows(1, n1, 1)
        nothing = jnp.zeros_like(diff0)

        def pick(value, k):
            place = k if upward else value.shape[0] - 1 - k
            return value[place : place + 1]

        for i, (_, _, after, _) in enumerate(chains):
            spot = (2 * i + side) * SCRATCH
            start, term = rows_of(edge, spot, 4), rows_of(edge, spot + 4, 3)
            mid, slope = slope_of_rows(start, coef_rows(0, inner, 2), coef_rows(1, inner, 2))
            inner_term = term[1:] if upward else term[:-1]
            odd = mid + slope + inner_term
            wide = [nothing, odd] if upward else [odd, nothing]
            mid, slope = slope_of_rows(jnp.concatenate(wide, axis=0), diff1, grow1)
            part = mid + slope
            odd1 = pick(odd, 0)
            to, at = (rim, 4 * i) if after else (slant, 0)
            put_rows(to, at, pick(start, 0))
            put_rows(to, at + 1, pick(term, 0) + diff0 * pick(start, 1))
            if after:
                follow = rows_of(edge, spot + 7, 2)
                put_rows(to, at + 2, pick(follow, 0) + diff0 * odd1)
                part = part + pick(follow, 1)
                put_rows(to, at + 3, rows_of(edge, spot + 9, 1) + diff0 * part)
            else:
                put_rows(to, at + 2, odd1)
                put_rows(to, at + 3, part)


def column_of(shape, offset):
    lane = lax.broadcasted_iota(jnp.int32, shape, len(shape) - 1)
    return jnp.where(lane < LANES - REACH, lane, lane - LANES) + offset


def window(get, first, depth):
    line, offset = first // LANES, first % LANES
    source = column_of(get(0).shape, offset)
    shift = (LANES - offset) % LANES
    before = jnp.where(line > 0, pltpu.roll(get(jnp.maximum(line - 1, 0)), shift, 1), 0.0)
    here = pltpu.roll(get(line), shift, 1)
    after = jnp.where(
        line < depth - 1, pltpu.roll(get(jnp.minimum(line + 1, depth - 1)), shift, 1), 0.0
    )
    return jnp.where(source < 0, before, jnp.where(source >= LANES, after, here))


def core_kernel(share, evens, source, coefs, core, *windows):
    _, rows, cols = coefs.shape
    depth = cols // LANES
    for index, name in enumerate(CORES):
        get = pieces(name, evens, source, coefs.at[0], coefs.at[1])
        for c in range(depth):
            for r in range(0, rows, 8):
                value = get(pl.ds(r, 8), pl.ds(c * LANES, LANES))
                core[pl.ds((index * rows + r) * depth + c, 8, stride=depth), :] = value
    for by, out in zip(sent_windows(lax.axis_size("space")), windows, strict=True):
        for which, name in enumerate(("d", "g")):
            start = CORES.index(name) * rows * depth
            get = lambda line: core[pl.ds(start + line, rows, stride=depth), :]
            out[pl.ds(which * rows, rows)] = window(get, target_of(by) * share, depth)


def handed_on(slabs):
    return slabs == 4


def far_windows(slabs):
    return [] if handed_on(slabs) else list(range(2, slabs - 1))


def sent_windows(slabs):
    return [0, 1, slabs - 1] + far_windows(slabs)


def level0_kernel(
    core, above, below, behind_above, behind_below, inward, outward, own, ahead_one, behind_one,
    *refs,
):
    distant = far_windows(lax.axis_size("space"))
    windows, refs = refs[: len(distant)], refs[len(distant) :]
    (
        turn, down, up, next_odd, last_odd, forcing, coefs, held, next_first,
        fields, diff, grow,
    ) = refs
    rows = core.shape[0] // len(CORES)
    low, high = flags()
    depth = core.shape[1]
    names = list(CORES) + ["ep", "op"]
    spots = {name: index for index, name in enumerate(names)}
    extra = len(names)
    halves = POINTS // 2
    odd = [extra + i for i in range(halves)]
    even = [extra + halves + i for i in range(halves)]
    image = [extra + 2 * halves + i for i in range(halves)]
    nothing = jnp.zeros((1, depth, LANES), jnp.float32)
    sides = rim_rows(rows, low, high)
    for (at, flag), rim, slant in zip(
        sides, (above, below), (behind_above, behind_below), strict=True
    ):

        def put(name, k, ref, row):
            fields[spots[name] if isinstance(name, str) else name, pl.ds(at(k), 1)] = (
                ref[pl.ds(row, 1)] * flag
            )

        for i in range(CHAINS):
            put(f"e{i}", 1, rim, 4 * i)
            put(f"o{i}", 1, rim, 4 * i + 1)
            put(f"s{i + 1}", 1, rim, 4 * i + 2)
            fields[spots[f"e{i}"], pl.ds(at(2), 1)] = nothing
            fields[odd[i + 1], pl.ds(at(2), 1)] = nothing
        put("ep", 1, slant, 0)
        put("op", 1, slant, 1)
        put(odd[0], 2, slant, 2)
        fields[spots["ep"], pl.ds(at(2), 1)] = nothing
        first_row = min(at(1), at(2))
        edge_at = 4 * CHAINS
        fields[spots["s0"], pl.ds(first_row, 2)] = rim[pl.ds(edge_at, 2)] * flag
        diff[pl.ds(first_row, 2)] = rim[pl.ds(edge_at + 3, 2)] * flag
        grow[pl.ds(at(1), 1)] = rim[pl.ds(edge_at + 5, 1)] * flag
        grow[pl.ds(at(2), 1)] = nothing
    for name in CORES:
        if name in ("d", "g"):
            buffer = diff if name == "d" else grow
        else:
            buffer = fields.at[spots[name]]
        buffer[pl.ds(MARGIN, rows)] = core[pl.ds(CORES.index(name) * rows, rows)]
    even_block = lax.axis_index("tm") % 2 == 0
    cells = pl.ds(0, rows)
    from_behind = jnp.where(even_block, outward[cells], inward[cells])
    ahead = jnp.where(even_block, inward[cells], outward[cells])
    fields[odd[0], pl.ds(MARGIN, rows)] = from_behind
    for (at, _), row, edge_row in zip(sides, (0, 1), (0, rows - 1), strict=True):
        edge = pl.ds(rows + row, 1)
        fields[spots["ep"], pl.ds(MARGIN + edge_row, 1)] = jnp.where(
            even_block, outward[edge], inward[edge]
        )
        near, first = pl.ds(at(1), 1), pl.ds(MARGIN + edge_row, 1)
        mid, slope = growth_of(fields.at[spots["ep"]], at(1), 1, diff[near], grow[near])
        fields[odd[0], near] = mid + slope + fields[spots["op"], near]
        fields[odd[0], first] = fields[odd[0], first] + diff[first] * mid

    def first(at, n):
        d, g = diff[pl.ds(at, n)], grow[pl.ds(at, n)]
        for i in range(CHAINS):
            mid, slope = growth_of(fields.at[spots[f"e{i}"]], at, n, d, g)
            fields[odd[i + 1], pl.ds(at, n)] = mid + slope + fields[spots[f"o{i}"], pl.ds(at, n)]

    def second(at, n):
        d, g = diff[pl.ds(at, n)], grow[pl.ds(at, n)]
        for i in range(halves):
            mid, slope = growth_of(fields.at[odd[i]], at, n, d, g)
            fields[even[i], pl.ds(at, n)] = mid + slope + fields[spots[f"s{i}"], pl.ds(at, n)]

    def third(at, n):
        d, g = diff[pl.ds(at, n)], grow[pl.ds(at, n)]
        for i in range(halves):
            mid, slope = growth_of(fields.at[even[i]], at, n, d, g)
            fields[odd[i], pl.ds(at, n)] = mid + slope + fields[spots[f"o{i}"], pl.ds(at, n)]
            fields[image[i], pl.ds(at, n)] = mid + 2.0 * slope

    def fourth(at, n):
        d, g = diff[pl.ds(at, n)], grow[pl.ds(at, n)]
        here = at - MARGIN
        for i in range(halves):
            mid, slope = growth_of(fields.at[odd[i]], at, n, d, g)
            pair = mid + slope - fields[image[i], pl.ds(at, n)]
            if i == halves - 1:
                next_first[...] = ahead + pair
            else:
                term = fields[spots[f"s{i + 1}"], pl.ds(at, n)] + pair
                forcing[pl.ds(i * rows + here, n)] = term
                if i < 2:
                    turn[pl.ds(i * rows + here, n)] = term
                if i == 0:
                    next_odd[...] = fields[image[0], pl.ds(at, n)] + term
                if i == halves - 2:
                    last_odd[...] = fields[image[i], pl.ds(at, n)] + term

    over_rows(rows, 1, first)
    over_rows(rows, 1, second)
    for (at, flag), rim, slant in zip(
        sides, (above, below), (behind_above, behind_below), strict=True
    ):
        near, far = pl.ds(at(1), 1), pl.ds(at(2), 1)
        for i in range(halves):
            place = 4 * CHAINS + 2 if i == 0 else 4 * i - 1
            fields[spots[f"o{i}"], near] = rim[pl.ds(place, 1)] * flag
            value = diff[far] * fields[odd[i], near]
            if i == 0:
                value = value + fields[spots["s0"], far] + slant[pl.ds(3, 1)] * flag
            fields[even[i], far] = value
    over_rows(rows, 1, third)
    over_rows(rows, 0, fourth)
    coefs[pl.ds(0, rows + 4)] = diff[pl.ds(MARGIN - 2, rows + 4)]
    coefs[pl.ds(rows + 4, rows + 4)] = grow[pl.ds(MARGIN - 2, rows + 4)]
    for rim, n0, n1 in ((down, rows - 1, rows - 2), (up, 0, 1)):

        def row(ref, first, n):
            return ref[pl.ds(first + n, 1)]

        diff0 = 2.0 * row(diff, MARGIN, n0)
        around = [
            slope_of_rows(
                ref[pl.ds(first + n1 - 1, 3)], row(diff, MARGIN, n1), row(grow, MARGIN, n1)
            )
            for ref, first in ((next_odd, 0), (last_odd, 0))
        ]
        (mid, slope), (mid_last, slope_last) = around
        even1 = mid + 2.0 * slope + row(forcing, rows, n1)
        g3 = row(forcing, 2 * rows, n0)
        rim[pl.ds(0, 1)] = row(next_odd, 0, n0)
        rim[pl.ds(1, 1)] = row(forcing, rows, n0) + diff0 * mid
        rim[pl.ds(2, 1)] = g3 + diff0 * even1
        rim[pl.ds(3, 1)] = g3
        rim[pl.ds(4, 1)] = row(forcing, 0, n0)
        rim[pl.ds(5, 1)] = row(last_odd, 0, n0)
        rim[pl.ds(6, 1)] = row(next_first, 0, n0) + diff0 * mid_last
        rim[pl.ds(7, 1)] = row(next_first, 0, n1) + mid_last + 2.0 * slope_last
    slab, slabs = lax.axis_index("space"), lax.axis_size("space")
    size = 2 * rows // depth
    down[pl.ds(EDGE_1, size)] = ahead_one[...]
    up[pl.ds(EDGE_1, size)] = behind_one[...]
    if handed_on(slabs):
        down[pl.ds(EDGE_1 + size, size)] = above[pl.ds(EDGE_0, size)]
    for by, part in zip([0] + distant, (own, *windows), strict=True):
        held[pl.ds((slab - by) % slabs * size, size)] = part[...]


def take_coefs(rows, coefs, diff, grow):
    diff[pl.ds(MARGIN - 2, rows + 4)] = coefs[pl.ds(0, rows + 4)]
    grow[pl.ds(MARGIN - 2, rows + 4)] = coefs[pl.ds(rows + 4, rows + 4)]


def level1_kernel(
    share, next_odd, last_odd, forcing, coefs, next_first, held, above, below, ahead_terms,
    slots, next_forcing, late_a, late_b, windows,
    fields, diff, grow, flat,
):
    rows = forcing.shape[0] // 3
    low, high = flags()
    take_coefs(rows, coefs, diff, grow)
    windows[...] = held[...]
    slab, slabs = lax.axis_index("space"), lax.axis_size("space")
    size = windows.shape[0] // slabs
    windows[pl.ds((slab - 1) % slabs * size, size)] = above[pl.ds(EDGE_1, size)]
    windows[pl.ds((slab + 1) % slabs * size, size)] = below[pl.ds(EDGE_1, size)]
    if handed_on(slabs):
        windows[pl.ds((slab - 2) % slabs * size, size)] = above[pl.ds(EDGE_1 + size, size)]
    g1, g3, g2, g0, before, after, even0, even1, image0, image1, odd0, odd1 = range(12)
    nothing = jnp.zeros((1, *forcing.shape[1:]), jnp.float32)
    sides = rim_rows(rows, low, high)
    core = pl.ds(MARGIN, rows)
    fields[after, core] = next_odd[...]
    fields[before, core] = last_odd[...]
    fields[g0, core] = next_first[...]
    fields[g1, core] = ahead_terms[pl.ds(0, rows)]
    fields[g2, core] = forcing[pl.ds(rows, rows)]
    fields[g3, core] = forcing[pl.ds(2 * rows, rows)]
    for (at, flag), rim in zip(sides, (above, below), strict=True):
        near, far = pl.ds(at(1), 1), pl.ds(at(2), 1)
        for spot, row in ((after, 0), (g2, 1), (g3, 2), (before, 5), (g0, 6)):
            fields[spot, near] = rim[pl.ds(row, 1)] * flag
        fields[even0, far] = rim[pl.ds(7, 1)] * flag
        fields[g1, near] = nothing
        for spot in (after, before, even1):
            fields[spot, far] = nothing

    def second(at, n):
        d, g = diff[pl.ds(at, n)], grow[pl.ds(at, n)]
        for start, term, end in ((before, g0, even0), (after, g2, even1)):
            mid, slope = growth_of(fields.at[start], at, n, d, g)
            fields[end, pl.ds(at, n)] = mid + 2.0 * slope + fields[term, pl.ds(at, n)]

    def third(at, n):
        d, g = diff[pl.ds(at, n)], grow[pl.ds(at, n)]
        for start, term, end, image in ((even0, g1, odd0, image0), (even1, g3, odd1, image1)):
            mid, slope = growth_of(fields.at[start], at, n, d, g)
            fields[end, pl.ds(at, n)] = mid + 2.0 * slope + fields[term, pl.ds(at, n)]
            fields[image, pl.ds(at, n)] = mid + 4.0 * slope

    def fourth(at, n):
        d, g = diff[pl.ds(at, n)], grow[pl.ds(at, n)]
        here = at - MARGIN
        mid, slope = growth_of(fields.at[odd1], at, n, d, g)
        pair1 = mid + 2.0 * slope - fields[image1, pl.ds(at, n)]
        put_rows(flat, rows, next_first[...] + pair1)
        mid, slope = growth_of(fields.at[odd0], at, n, d, g)
        image = fields[image0, pl.ds(at, n)]
        term = ahead_terms[pl.ds(rows, rows)] + (mid + 2.0 * slope - image)
        next_forcing[pl.ds(here, n)] = term
        put_rows(flat, 2 * rows, term)
        put_rows(flat, 0, image + term)

    over_rows(rows, 1, second)
    over_rows(rows, 1, third)
    over_rows(rows, 0, fourth)
    for late, which, row in ((late_a, 0, 4), (late_b, 2, 3)):
        late[pl.ds(1, rows)] = forcing[pl.ds(which * rows, rows)]
        late[pl.ds(0, 1)] = above[pl.ds(row, 1)] * low
        late[pl.ds(rows + 1, 1)] = below[pl.ds(row, 1)] * high
    depth = forcing.shape[1]
    put_rows(flat, FIELDS * rows, ahead_terms[pl.ds(0, 1)])
    put_rows(flat, FIELDS * rows + 1, ahead_terms[pl.ds(rows - 1, 1)])
    if folded(rows, share, reach_of()):
        pack_folded(slots, flat, rows, depth, reach_of())
    else:
        pack_windows(slots, flat, rows, depth, share)


def put_rows(flat, first, value):
    depth = value.shape[1]
    for i in range(value.shape[0]):
        flat[pl.ds((first + i) * depth, depth), :] = value[i]


def reach_of():
    return lax.axis_size("tm") + 2


def slot_lines(rows, share, reach):
    return (FIELDS * 8 + 8 if folded(rows, share, reach) else FIELDS * rows) + 2


def folded(rows, share, reach):
    return rows == 16 and 2 * share == LANES and FIELDS * 2 * reach <= share


def pack_folded(slots, flat, rows, depth, reach):
    lines = slot_lines(rows, LANES // 2, reach)
    devices = slots.shape[0] // lines
    lane = lax.broadcasted_iota(jnp.int32, (8, LANES), 1)
    place = lane % (LANES // 2)
    rims = [None] * devices
    for field in range(FIELDS):
        first = field * rows * depth
        cells = []
        for line in range(depth):
            top = flat[pl.ds(first + line, 8, stride=depth), :]
            low = flat[pl.ds(first + 8 * depth + line, 8, stride=depth), :]
            cells.append(jnp.where(lane < LANES // 2, top, pltpu.roll(low, LANES // 2, 1)))
            cells.append(jnp.where(lane < LANES // 2, pltpu.roll(top, LANES // 2, 1), low))
        for target in range(devices):
            slots[pl.ds(target * lines + field * 8, 8), :] = cells[target]
            left = cells[target - 1] if target > 0 else 0.0
            right = cells[target + 1] if target < devices - 1 else 0.0
            rim = jnp.where(
                place >= LANES // 2 - reach, left, jnp.where(place < reach, right, 0.0)
            )
            if field == 0:
                rims[target] = rim
            else:
                rims[target] = rims[target] + pltpu.roll(rim, 2 * reach * field, 1)
    for target in range(devices):
        slots[pl.ds(target * lines + FIELDS * 8, 8), :] = rims[target]
    top = flat[pl.ds(FIELDS * rows * depth, depth), :]
    low = flat[pl.ds((FIELDS * rows + 1) * depth, depth), :]
    lane = lax.broadcasted_iota(jnp.int32, (depth, LANES), 1)
    line = lax.broadcasted_iota(jnp.int32, (depth, LANES), 0)
    place = lane % (LANES // 2)
    evens = jnp.where(lane < LANES // 2, top, pltpu.roll(low, LANES // 2, 1))
    odds = jnp.where(lane < LANES // 2, pltpu.roll(top, LANES // 2, 1), low)
    before = jnp.where(line == 0, 0.0, pltpu.roll(odds, 1, 0))
    after = jnp.where(line == depth - 1, 0.0, pltpu.roll(evens, depth - 1, 0))
    for parity, cells, left, right in ((0, evens, before, odds), (1, odds, evens, after)):
        rim = jnp.where(place >= LANES // 2 - reach, left, jnp.where(place < reach, right, 0.0))
        for i, value in enumerate((cells, rim)):
            start = parity * lines + lines - 2 + i
            slots[pl.ds(start, depth, stride=2 * lines), :] = value


def unfold(slot, field, reach):
    cells, rims = slot[pl.ds(field * 8, 8)], slot[pl.ds(FIELDS * 8, 8)]
    lane = lax.broadcasted_iota(jnp.int32, (8, LANES), 1)
    half = LANES // 2
    back = 2 * reach * field
    top = pltpu.roll(rims, (half - back) % LANES, 1)
    low = pltpu.roll(rims, (-back) % LANES, 1) if back else rims
    return jnp.concatenate(
        [
            jnp.where(lane < half, cells, top),
            jnp.where(lane < half, pltpu.roll(cells, half, 1), low),
        ],
        axis=0,
    )


def unfold_row(slot, which):
    last = slot.shape[0] - 2
    cells, rims = slot[pl.ds(last, 1)], slot[pl.ds(last + 1, 1)]
    lane = lax.broadcasted_iota(jnp.int32, (1, LANES), 1)
    half = LANES // 2
    if which == 0:
        return jnp.where(lane < half, cells, pltpu.roll(rims, half, 1))
    return jnp.where(lane < half, pltpu.roll(cells, half, 1), rims)


def pack_windows(slots, flat, rows, depth, share):
    lines = slot_lines(rows, share, reach_of())
    for field in range(FIELDS + 1):
        first, count = field * rows * depth, rows if field < FIELDS else 2
        held = [flat[pl.ds(first + line, count, stride=depth), :] for line in range(depth)]
        for target in range(slots.shape[0] // lines):
            line, offset = target * share // LANES, target * share % LANES
            shift = (LANES - offset) % LANES
            place = column_of((count, LANES), offset)
            value = pltpu.roll(held[line], shift, 1)
            if offset < REACH:
                before = pltpu.roll(held[line - 1], shift, 1) if line > 0 else 0.0
                value = jnp.where(place < 0, before, value)
            if offset > REACH:
                after = pltpu.roll(held[line + 1], shift, 1) if line < depth - 1 else 0.0
                value = jnp.where(place >= LANES, after, value)
            slots[pl.ds(target * lines + field * rows, count), :] = value


def late_rows(rows):
    return (("forcing", rows), ("forcing", -1), ("odd", rows + 1), ("odd", -2))


def packing(rows, share):
    groups = LANES // share
    each = -(-(rows + 2 * UP_RIM) // groups)
    return groups, each, each + -(-4 // groups)


def sweep_kernel(share, rows, arrived, windows, slots, diff, grow, terms, owns, adds, padded, odds):
    slabs = lax.axis_size("space")
    reach = reach_of()
    lines = slot_lines(rows, share, reach)
    devices = arrived.shape[0] // lines
    blocks = devices // slabs
    total = slabs * rows
    groups, each, held = packing(rows, share)
    for slab in range(slabs):
        diff[pl.ds(slab * rows, rows), :] = windows[pl.ds(2 * slab * rows, rows), :]
        grow[pl.ds(slab * rows, rows), :] = windows[pl.ds((2 * slab + 1) * rows, rows), :]
    line = lax.broadcasted_iota(jnp.int32, (total, LANES), 0)
    lane = lax.broadcasted_iota(jnp.int32, (each, LANES), 1)
    padded[...] = jnp.zeros(padded.shape, jnp.float32)
    odds[...] = jnp.zeros(odds.shape, jnp.float32)

    def block(field, index):
        parts = []
        for slab in range(slabs):
            slot = arrived.at[pl.ds((index * slabs + slab) * lines, lines)]
            if folded(rows, share, reach):
                parts.append(unfold(slot, field, reach))
            else:
                parts.append(slot[pl.ds(field * rows, rows)])
        return jnp.concatenate(parts, axis=0)

    adds[...] = jnp.zeros(adds.shape, jnp.float32)

    def beyond(index):
        for slab in range(slabs):
            slot = arrived.at[pl.ds((index * slabs + slab) * lines, lines)]
            for which, at in ((0, slab * rows - 1), (1, (slab + 1) * rows)):
                if not 0 <= at < total:
                    continue
                if folded(rows, share, reach):
                    piece = unfold_row(slot, which)
                else:
                    piece = slot[pl.ds(FIELDS * rows + which, 1)]
                adds[index, pl.ds(at, 1), :] = 2.0 * diff[pl.ds(at, 1), :] * piece

    def slope_of(field):
        north = jnp.where(line == 0, 0.0, pltpu.roll(field, 1, 0))
        south = jnp.where(line == total - 1, 0.0, pltpu.roll(field, total - 1, 0))
        sides = pltpu.roll(field, 1, 1) + pltpu.roll(field, LANES - 1, 1)
        laplace = north + south + sides - 4.0 * field
        return diff[...] * laplace + grow[...] * field / (1.0 + field * field)

    def put_late(index, slab):
        to = slots.at[pl.ds((index * slabs + slab) * held, held)]
        for i, (what, row) in enumerate(late_rows(rows)):
            at, group = each + i // groups, i % groups
            place = slab * rows + row
            if what == "odd":
                piece = odds[group, pl.ds(8 + place, 1)]
            elif 0 <= place < total:
                piece = owns[index, pl.ds(place, 1)]
                piece = pltpu.roll(piece, group * share, 1) if group else piece
            else:
                piece = jnp.zeros((1, LANES), jnp.float32)
            if group:
                piece = jnp.where(lane[:1] >= group * share, piece, to[pl.ds(at, 1)])
            to[pl.ds(at, 1)] = piece

    field = None
    for index in range(blocks):
        beyond(index)
    for index in range(blocks):
        behind, twice = (index - 1) % blocks, (index - 2) % blocks
        odd, term = block(0, twice) + adds[twice], block(1, behind)
        even = odd + 4.0 * slope_of(odd) + term
        slope = slope_of(even)
        own = block(2, behind) + adds[behind]
        owns[index] = own
        odd = even + 4.0 * slope + own
        stepped = even + 8.0 * slope
        pair = odd + 4.0 * slope_of(odd) - stepped
        terms[index] = block(1, index) + pair
        if index == blocks - 1:
            field = stepped + terms[index]
    for index in range(blocks):
        slope = slope_of(field)
        odd = field + 4.0 * slope + owns[index]
        for group in range(groups):
            for to, value in ((padded, field), (odds, odd)):
                to[group, pl.ds(8, total), :] = (
                    pltpu.roll(value, group * share, 1) if group else value
                )
        for slab in range(slabs):
            start = 8 + slab * rows - UP_RIM
            value = padded[0, pl.ds(start, each), :]
            for group in range(1, groups):
                piece = padded[group, pl.ds(start + group * each, each), :]
                value = jnp.where(lane >= group * share, piece, value)
            slots[pl.ds((index * slabs + slab) * held, each), :] = value
            put_late(index, slab)
        if index < blocks - 1:
            field = field + 8.0 * slope + terms[index]


def up_kernel(
    share, arrived, next_forcing, late_a, late_b, core, coefs,
    out, fields, diff, grow, flat, ready, sems,
):
    rows, depth, _ = next_forcing.shape
    groups, each, held = packing(rows, share)
    take_coefs(rows, coefs, diff, grow)
    lane = lax.broadcasted_iota(jnp.int32, (depth, LANES), 1)

    def whole(line, group):
        value = None
        for part in range(groups):
            piece = arrived[pl.ds(part * held + line, depth, stride=groups * held), :]
            if part != group:
                piece = pltpu.roll(piece, ((part - group) * share) % LANES, 1)
            value = piece if value is None else jnp.where(lane >= part * share, piece, value)
        return value

    for row in range(rows + 2 * UP_RIM):
        fields[0, MARGIN - UP_RIM + row] = whole(row % each, row // each)
    for i, (what, row) in enumerate(late_rows(rows)):
        spot = 5 if what == "forcing" else 2
        fields[spot, MARGIN + row] = whole(each + i // groups, i % groups)
    fields[5, pl.ds(MARGIN, rows)] = next_forcing[...]
    for row, rim in ((0, 0), (rows - 1, rows + 1)):
        spot = pl.ds(MARGIN + row, 1)
        added = 2.0 * diff[spot] * late_a[pl.ds(rim, 1)]
        fields[5, spot] = next_forcing[pl.ds(row, 1)] + added
    odd_first = CORES.index("o0") * rows

    def first(at, n):
        mid, slope = growth_of(fields.at[0], at, n, diff[pl.ds(at, n)], grow[pl.ds(at, n)])
        fields[2, pl.ds(at, n)] = mid + 4.0 * slope + fields[5, pl.ds(at, n)]

    def second(at, n):
        d, g = diff[pl.ds(at, n)], grow[pl.ds(at, n)]
        for start, late in ((0, late_a), (2, late_b)):
            mid, slope = growth_of(fields.at[start], at, n, d, g)
            fields[start + 1, pl.ds(at, n)] = mid + 2.0 * slope + late[pl.ds(at - MARGIN + 1, n)]

    copies = []

    def emit(point, value):
        put_rows(flat, point * rows, value)
        for r in range(0, rows, 8):
            for c in range(depth):
                start = (point * rows + r) * depth + c
                ready[point, pl.ds(r, 8), pl.ds(c * LANES, LANES)] = flat[
                    pl.ds(start, 8, stride=depth), :
                ]
        copy = pltpu.make_async_copy(ready.at[point], out.at[point], sems.at[point])
        copy.start()
        copies.append(copy)

    def last(i):
        at, n = MARGIN, rows
        mid, slope = growth_of(fields.at[i], at, n, diff[pl.ds(at, n)], grow[pl.ds(at, n)])
        emit(2 * i + 1, mid + slope + core[pl.ds(odd_first + i * rows, n)])

    core_rows = pl.ds(MARGIN, rows)
    emit(0, fields[0, core_rows])
    over_rows(rows, 1, first)
    emit(4, fields[2, core_rows])
    over_rows(rows, 1, second)
    emit(2, fields[1, core_rows])
    emit(6, fields[3, core_rows])
    for i in (0, 2, 1, 3):
        last(i)
    for copy in copies:
        copy.wait()


def moved(array, blocks, slabs):
    tm, space = lax.axis_size("tm"), lax.axis_size("space")
    pairs = [
        (t * space + s, (t + blocks) % tm * space + (s + slabs) % space)
        for t in range(tm)
        for s in range(space)
    ]
    return lax.ppermute(array, ("tm", "space"), pairs)


def swapped(array, offset):
    tm, space = lax.axis_size("tm"), lax.axis_size("space")
    pairs = [
        (t * space + s, ((((t - offset) % tm) ^ 1) + offset) % tm * space + s)
        for t in range(tm)
        for s in range(space)
    ]
    return lax.ppermute(array, ("tm", "space"), pairs)


def rims(down, up, slant_down, slant_up):
    slanted = moved(slant_down, 1, 1), moved(slant_up, 1, -1)
    return moved(down, 0, 1), moved(up, 0, -1), *slanted


def body(initial, source, diffusivity, growth):
    points, rows, cols = initial.shape
    assert points == POINTS and lax.axis_size("tm") % 2 == 0 and rows % 8 == 0 and cols % LANES == 0
    depth = cols // LANES
    tm, space = lax.axis_size("tm"), lax.axis_size("space")
    devices = tm * space
    share = cols // devices
    assert share * devices == cols and LANES % share == 0
    assert reach_of() <= REACH and REACH + share + reach_of() <= LANES
    _, _, held = packing(rows, share)
    wide = rows + 2 * MARGIN

    def lines(n):
        return (n * depth, LANES)

    def field(n):
        return (n, depth, LANES)

    def as_rows(array):
        return array.reshape(-1, depth, LANES)

    window_rows = 2 * rows // depth
    assert window_rows * depth == 2 * rows
    raw = [(points // 2, rows, cols), source.shape, (2, rows, cols)]
    extra = window_rows if handed_on(space) else 0
    *sends, inward, outward, evens, terms, rates = call(
        functools.partial(pack_kernel, share),
        [lines(EDGE_0 + extra), lines(EDGE_0), lines(SLANT_0), lines(SLANT_0)]
        + [lines(rows + TURN)] * 2
        + raw,
        [lines(2 * SCRATCH * (CHAINS + 1)), lines(2 * rows), lines(3 * rows + 2)],
        initial, source, diffusivity, growth,
        place=pltpu.HBM, sems=points // 2 + 3,
    )
    core, *windows = call(
        functools.partial(core_kernel, share),
        [lines(len(CORES) * rows)] + [(2 * rows, LANES)] * len(sent_windows(space)),
        [],
        evens, terms, rates,
        cost=pl.CostEstimate(flops=0, transcendentals=0, bytes_accessed=CORE_COST),
    )
    sends, inward, outward = [as_rows(part) for part in sends], as_rows(inward), as_rows(outward)
    inward = swapped(inward, 0)
    inward, sends[2], sends[3] = lax.optimization_barrier((inward, sends[2], sends[3]))
    arrived = [*rims(*sends), inward, swapped(outward, 1)]
    windows = [as_rows(part) for part in windows]
    for i, by in enumerate(far_windows(space), 3):
        windows[i] = moved(windows[i], 0, by)
    core = as_rows(core)
    arrived, windows = lax.optimization_barrier((arrived, windows))

    buffers = [(wide, depth, LANES), (wide, depth, LANES)]
    turn, down, up, next_odd, last_odd, forcing, coefs, held_windows, next_first = call(
        level0_kernel,
        [
            field(2 * rows), field(EDGE_1 + window_rows + extra), field(EDGE_1 + window_rows),
            field(rows), field(rows), field(3 * rows), field(2 * (rows + 4)),
            field(window_rows * space), field(rows),
        ],
        [(len(CORES) + 2 + 3 * (POINTS // 2), wide, depth, LANES)] + buffers,
        core, *arrived, *windows,
    )
    above, below, ahead_terms = moved(down, 0, 1), moved(up, 0, -1), moved(turn, -1, 0)
    slot_rows = slot_lines(rows, share, reach_of())
    slots, next_forcing, late_a, late_b, windows = call(
        functools.partial(level1_kernel, share),
        [
            (devices * slot_rows, LANES),
            field(rows), field(rows + 2), field(rows + 2), field(window_rows * space),
        ],
        [(12, wide, depth, LANES)] + buffers + [((FIELDS * rows + 2) * depth, LANES)],
        next_odd, last_odd, forcing, coefs, next_first, held_windows, above, below, ahead_terms,
    )
    next_forcing = moved(next_forcing, 1, 0)
    slots = slots.reshape(devices, slot_rows, 1, LANES)
    slots = lax.all_to_all(slots, ("tm", "space"), 0, 0, tiled=True)
    slots = slots.reshape(devices * slot_rows, LANES)
    (slots,) = call(
        functools.partial(sweep_kernel, share, rows),
        [(devices * held, LANES)],
        [(space * rows, LANES)] * 2
        + [(tm, space * rows, LANES)] * 3
        + [(LANES // share, 8 + space * rows + 2 * rows + held, LANES)]
        + [(LANES // share, 16 + space * rows, LANES)],
        slots, windows.reshape(-1, LANES),
    )
    slots = slots.reshape(devices, held, 1, LANES)
    slots = lax.all_to_all(slots, ("tm", "space"), 0, 0, tiled=True)
    (out,) = call(
        functools.partial(up_kernel, share),
        [(points, rows, cols)],
        [(6, wide, depth, LANES)]
        + buffers
        + [(points * rows * depth, LANES), (points, rows, cols)],
        slots.reshape(devices * held, LANES), next_forcing, late_a, late_b, core, coefs,
        to=pltpu.HBM, sems=points,
    )
    return out


def solution(mesh):
    placed = (P("tm", "space", None), P("tm", "space", None), P("space", None), P("space", None))
    return jax.shard_map(
        body, mesh=mesh, in_specs=placed, out_specs=P("tm", "space", None), check_vma=False
    )
```

```python
import functools

import jax
import jax.numpy as jnp
from jax import lax
from jax.experimental import pallas as pl
from jax.experimental.pallas import tpu as pltpu
from jax.sharding import PartitionSpec as P

LANES = 128
MARGIN = 4
REACH = 32
UP_RIM = 2
POINTS = 8
FIELDS = 3
CORE_COST = 30_000_000
diffusion_number = 0.03
time_step = 0.02

CHAINS = POINTS // 2 - 1
EDGE_0 = 4 * CHAINS + 6
SLANT_0 = 4
TURN = 2
EDGE_1 = 8
CORES = ("e0", "e1", "e2", "o0", "o1", "o2", "o3", "s0", "s1", "s2", "s3", "d", "g")


def params(mib):
    return pltpu.CompilerParams(vmem_limit_bytes=int(mib * 2**20))


def call(
    kernel, outs, scratch, *args, mib=16, place=pltpu.VMEM, to=pltpu.VMEM, sems=0, cost=None
):
    if place == pltpu.HBM:
        args = [pltpu.with_memory_space_constraint(arg, place) for arg in args]
    return pl.pallas_call(
        kernel,
        out_shape=tuple(jax.ShapeDtypeStruct(shape, jnp.float32) for shape in outs),
        in_specs=[pl.BlockSpec(memory_space=place)] * len(args),
        out_specs=tuple(pl.BlockSpec(memory_space=to) for _ in outs),
        scratch_shapes=[pltpu.VMEM(shape, jnp.float32) for shape in scratch]
        + ([pltpu.SemaphoreType.DMA((sems,))] if sems else []),
        compiler_params=params(mib),
        cost_estimate=cost,
    )(*args)


def beside(mid):
    depth = mid.shape[1]
    lane = lax.broadcasted_iota(jnp.int32, mid.shape, 2)
    line = lax.broadcasted_iota(jnp.int32, mid.shape, 1)
    left = pltpu.roll(mid, 1, 2)
    left_turn = pltpu.roll(left, 1, 1)
    right = pltpu.roll(mid, LANES - 1, 2)
    right_turn = pltpu.roll(right, depth - 1, 1)
    left = jnp.where(lane == 0, jnp.where(line == 0, 0.0, left_turn), left)
    right = jnp.where(lane == LANES - 1, jnp.where(line == depth - 1, 0.0, right_turn), right)
    return left + right


def slope_of_rows(wide, diff, grow):
    mid = wide[1:-1]
    laplace = wide[:-2] + wide[2:] + beside(mid) - 4.0 * mid
    return mid, diff * laplace + grow * mid / (1.0 + mid * mid)


def growth_of(ref, at, rows, diff, grow):
    return slope_of_rows(ref[pl.ds(at - 1, rows + 2)], diff, grow)


def over_rows(rows, rim, body):
    body(MARGIN - rim, rows + 2 * rim)


def flags():
    slab = lax.axis_index("space")
    low = jnp.where(slab > 0, 1.0, 0.0).astype(jnp.float32)
    high = jnp.where(slab < lax.axis_size("space") - 1, 1.0, 0.0).astype(jnp.float32)
    return low, high


def rim_rows(rows, low, high):
    return (
        (lambda k: MARGIN - k, low),
        (lambda k: MARGIN + rows - 1 + k, high),
    )


def pieces(name, evens, source, diffusivity, growth):
    if name == "d":
        return lambda rows, cols: diffusivity[rows, cols] * diffusion_number
    if name == "g":
        return lambda rows, cols: growth[rows, cols] * time_step
    if name == "ep":
        return lambda rows, cols: evens[POINTS // 2 - 1, rows, cols]
    if name == "op":
        return lambda rows, cols: source[POINTS - 1, rows, cols]
    which = int(name[1])
    if name[0] == "e":
        return lambda rows, cols: evens[which, rows, cols]
    return lambda rows, cols: source[2 * which + (name[0] == "o"), rows, cols]


def fetch(initial_all, source_all, diffusivity_all, growth_all, evens, source, coefs, sems):
    pairs = [(initial_all.at[2 * i], evens.at[i]) for i in range(POINTS // 2)]
    pairs += [(diffusivity_all, coefs.at[0]), (growth_all, coefs.at[1]), (source_all, source)]
    copies = [pltpu.make_async_copy(*pair, sems.at[i]) for i, pair in enumerate(pairs)]
    for copy in copies:
        copy.start()
    return copies[:-1], copies[-1]


def target_of(by):
    slabs = lax.axis_size("space")
    return lax.axis_index("tm") * slabs + (lax.axis_index("space") + by) % slabs


SCRATCH = 10


def pack_kernel(
    share, initial_all, source_all, diffusivity_all, growth_all,
    down, up, slant_down, slant_up, inward, outward,
    evens, source, coefs, edge, cells, turn, sems,
):
    waits, last = fetch(
        initial_all, source_all, diffusivity_all, growth_all, evens, source, coefs, sems
    )
    _, rows, cols = coefs.shape
    depth = cols // LANES
    diffusivity, growth = coefs.at[0], coefs.at[1]

    def put(ref, at, name, first, count):
        get = pieces(name, evens, source, diffusivity, growth)
        for c in range(depth):
            place = pl.ds(at * depth + c, count, stride=depth)
            ref[place, :] = get(pl.ds(first, count), pl.ds(c * LANES, LANES))

    def rows_of(ref, at, count):
        return ref[pl.ds(at * depth, count * depth), :].reshape(count, depth, LANES)

    def coef_rows(which, first, count):
        return rows_of(cells, which * rows + first, count)

    chains = [(f"e{i}", f"o{i}", f"s{i + 1}", f"o{i + 1}") for i in range(CHAINS)]
    chains.append(("ep", "op", None, None))
    sides = ((down, slant_down, False), (up, slant_up, True))

    def near(upward, count):
        return 0 if upward else rows - count

    for wait in waits:
        wait.wait()
    for index, name in enumerate(("d", "g")):
        for r in range(0, rows, 8):
            put(cells, index * rows + r, name, r, 8)
    for side, (rim, slant, upward) in enumerate(sides):
        for i, (start, _, _, _) in enumerate(chains):
            put(edge, (2 * i + side) * SCRATCH, start, near(upward, 4), 4)
        put_rows(rim, 4 * CHAINS + 3, coef_rows(0, near(upward, 2), 2))
        put_rows(rim, 4 * CHAINS + 5, coef_rows(1, near(upward, 1), 1))
    end = EDGE_0 * depth
    if end < down.shape[0]:
        for index in range(2):
            get = lambda line: cells[pl.ds(index * rows * depth + line, rows, stride=depth), :]
            down[pl.ds(end + index * rows, rows), :] = window(get, target_of(2) * share, depth)
    put_rows(turn, 0, jnp.zeros((1, depth, LANES), jnp.float32))
    for r in range(0, rows, 8):
        put(turn, 1 + r, "ep", r, 8)
    put_rows(turn, rows + 1, jnp.zeros((1, depth, LANES), jnp.float32))
    last.wait()
    for side, (rim, slant, upward) in enumerate(sides):
        for i, (_, term, after, after_odd) in enumerate(chains):
            spot = (2 * i + side) * SCRATCH
            put(edge, spot + 4, term, near(upward, 3), 3)
            if after:
                put(edge, spot + 7, after, near(upward, 2), 2)
                put(edge, spot + 9, after_odd, near(upward, 1), 1)
        put(rim, 4 * CHAINS, "s0", near(upward, 2), 2)
        put(rim, 4 * CHAINS + 2, "o0", near(upward, 1), 1)
    for r in range(0, rows, 8):
        put(turn, rows + 2 + r, "op", r, 8)
        put(turn, 2 * rows + 2 + r, "s0", r, 8)
    ahead = lax.axis_index("tm") % 2 == 0
    wide = rows_of(turn, 0, rows + 2)
    mid, slope = slope_of_rows(wide, coef_rows(0, 0, rows), coef_rows(1, 0, rows))
    forward = mid + slope + rows_of(turn, rows + 2, rows)
    backward = rows_of(turn, 2 * rows + 2, rows)
    put_rows(inward, 0, jnp.where(ahead, forward, backward))
    put_rows(outward, 0, jnp.where(ahead, backward, forward))
    for i, row in enumerate((1, rows)):
        for to in (inward, outward):
            put_rows(to, rows + i, rows_of(turn, row, 1))
    for side, (rim, slant, upward) in enumerate(sides):
        n0, n1, inner = (0, 1, 1) if upward else (rows - 1, rows - 2, rows - 3)
        diff0, diff1, grow1 = coef_rows(0, n0, 1), coef_rows(0, n1, 1), coef_rows(1, n1, 1)
        nothing = jnp.zeros_like(diff0)

        def pick(value, k):
            place = k if upward else value.shape[0] - 1 - k
            return value[place : place + 1]

        for i, (_, _, after, _) in enumerate(chains):
            spot = (2 * i + side) * SCRATCH
            start, term = rows_of(edge, spot, 4), rows_of(edge, spot + 4, 3)
            mid, slope = slope_of_rows(start, coef_rows(0, inner, 2), coef_rows(1, inner, 2))
            inner_term = term[1:] if upward else term[:-1]
            odd = mid + slope + inner_term
            wide = [nothing, odd] if upward else [odd, nothing]
            mid, slope = slope_of_rows(jnp.concatenate(wide, axis=0), diff1, grow1)
            part = mid + slope
            odd1 = pick(odd, 0)
            to, at = (rim, 4 * i) if after else (slant, 0)
            put_rows(to, at, pick(start, 0))
            put_rows(to, at + 1, pick(term, 0) + diff0 * pick(start, 1))
            if after:
                follow = rows_of(edge, spot + 7, 2)
                put_rows(to, at + 2, pick(follow, 0) + diff0 * odd1)
                part = part + pick(follow, 1)
                put_rows(to, at + 3, rows_of(edge, spot + 9, 1) + diff0 * part)
            else:
                put_rows(to, at + 2, odd1)
                put_rows(to, at + 3, part)


def column_of(shape, offset):
    lane = lax.broadcasted_iota(jnp.int32, shape, len(shape) - 1)
    return jnp.where(lane < LANES - REACH, lane, lane - LANES) + offset


def window(get, first, depth):
    line, offset = first // LANES, first % LANES
    source = column_of(get(0).shape, offset)
    shift = (LANES - offset) % LANES
    before = jnp.where(line > 0, pltpu.roll(get(jnp.maximum(line - 1, 0)), shift, 1), 0.0)
    here = pltpu.roll(get(line), shift, 1)
    after = jnp.where(
        line < depth - 1, pltpu.roll(get(jnp.minimum(line + 1, depth - 1)), shift, 1), 0.0
    )
    return jnp.where(source < 0, before, jnp.where(source >= LANES, after, here))


def core_kernel(
    share, initial_all, source_all, diffusivity_all, growth_all, core, *refs
):
    *windows, evens, source, coefs, sems = refs
    waits, last = fetch(
        initial_all, source_all, diffusivity_all, growth_all, evens, source, coefs, sems
    )
    for wait in (*waits, last):
        wait.wait()
    _, rows, cols = coefs.shape
    depth = cols // LANES
    for index, name in enumerate(CORES):
        get = pieces(name, evens, source, coefs.at[0], coefs.at[1])
        for c in range(depth):
            for r in range(0, rows, 8):
                value = get(pl.ds(r, 8), pl.ds(c * LANES, LANES))
                core[pl.ds((index * rows + r) * depth + c, 8, stride=depth), :] = value
    for by, out in zip(sent_windows(lax.axis_size("space")), windows, strict=True):
        for which, name in enumerate(("d", "g")):
            start = CORES.index(name) * rows * depth
            get = lambda line: core[pl.ds(start + line, rows, stride=depth), :]
            out[pl.ds(which * rows, rows)] = window(get, target_of(by) * share, depth)


def handed_on(slabs):
    return slabs == 4


def far_windows(slabs):
    return [] if handed_on(slabs) else list(range(2, slabs - 1))


def sent_windows(slabs):
    return [0, 1, slabs - 1] + far_windows(slabs)


def level0_kernel(
    core, above, below, behind_above, behind_below, inward, outward, own, ahead_one, behind_one,
    *refs,
):
    distant = far_windows(lax.axis_size("space"))
    windows, refs = refs[: len(distant)], refs[len(distant) :]
    (
        turn, down, up, next_odd, last_odd, forcing, coefs, held, next_first,
        fields, diff, grow,
    ) = refs
    rows = core.shape[0] // len(CORES)
    low, high = flags()
    depth = core.shape[1]
    names = list(CORES) + ["ep", "op"]
    spots = {name: index for index, name in enumerate(names)}
    extra = len(names)
    halves = POINTS // 2
    odd = [extra + i for i in range(halves)]
    even = [extra + halves + i for i in range(halves)]
    image = [extra + 2 * halves + i for i in range(halves)]
    nothing = jnp.zeros((1, depth, LANES), jnp.float32)
    sides = rim_rows(rows, low, high)
    for (at, flag), rim, slant in zip(
        sides, (above, below), (behind_above, behind_below), strict=True
    ):

        def put(name, k, ref, row):
            fields[spots[name] if isinstance(name, str) else name, pl.ds(at(k), 1)] = (
                ref[pl.ds(row, 1)] * flag
            )

        for i in range(CHAINS):
            put(f"e{i}", 1, rim, 4 * i)
            put(f"o{i}", 1, rim, 4 * i + 1)
            put(f"s{i + 1}", 1, rim, 4 * i + 2)
            fields[spots[f"e{i}"], pl.ds(at(2), 1)] = nothing
            fields[odd[i + 1], pl.ds(at(2), 1)] = nothing
        put("ep", 1, slant, 0)
        put("op", 1, slant, 1)
        put(odd[0], 2, slant, 2)
        fields[spots["ep"], pl.ds(at(2), 1)] = nothing
        first_row = min(at(1), at(2))
        edge_at = 4 * CHAINS
        fields[spots["s0"], pl.ds(first_row, 2)] = rim[pl.ds(edge_at, 2)] * flag
        diff[pl.ds(first_row, 2)] = rim[pl.ds(edge_at + 3, 2)] * flag
        grow[pl.ds(at(1), 1)] = rim[pl.ds(edge_at + 5, 1)] * flag
        grow[pl.ds(at(2), 1)] = nothing
    for name in CORES:
        if name in ("d", "g"):
            buffer = diff if name == "d" else grow
        else:
            buffer = fields.at[spots[name]]
        buffer[pl.ds(MARGIN, rows)] = core[pl.ds(CORES.index(name) * rows, rows)]
    even_block = lax.axis_index("tm") % 2 == 0
    cells = pl.ds(0, rows)
    from_behind = jnp.where(even_block, outward[cells], inward[cells])
    ahead = jnp.where(even_block, inward[cells], outward[cells])
    fields[odd[0], pl.ds(MARGIN, rows)] = from_behind
    for (at, _), row, edge_row in zip(sides, (0, 1), (0, rows - 1), strict=True):
        edge = pl.ds(rows + row, 1)
        fields[spots["ep"], pl.ds(MARGIN + edge_row, 1)] = jnp.where(
            even_block, outward[edge], inward[edge]
        )
        near, first = pl.ds(at(1), 1), pl.ds(MARGIN + edge_row, 1)
        mid, slope = growth_of(fields.at[spots["ep"]], at(1), 1, diff[near], grow[near])
        fields[odd[0], near] = mid + slope + fields[spots["op"], near]
        fields[odd[0], first] = fields[odd[0], first] + diff[first] * mid

    def first(at, n):
        d, g = diff[pl.ds(at, n)], grow[pl.ds(at, n)]
        for i in range(CHAINS):
            mid, slope = growth_of(fields.at[spots[f"e{i}"]], at, n, d, g)
            fields[odd[i + 1], pl.ds(at, n)] = mid + slope + fields[spots[f"o{i}"], pl.ds(at, n)]

    def second(at, n):
        d, g = diff[pl.ds(at, n)], grow[pl.ds(at, n)]
        for i in range(halves):
            mid, slope = growth_of(fields.at[odd[i]], at, n, d, g)
            fields[even[i], pl.ds(at, n)] = mid + slope + fields[spots[f"s{i}"], pl.ds(at, n)]

    def third(at, n):
        d, g = diff[pl.ds(at, n)], grow[pl.ds(at, n)]
        for i in range(halves):
            mid, slope = growth_of(fields.at[even[i]], at, n, d, g)
            fields[odd[i], pl.ds(at, n)] = mid + slope + fields[spots[f"o{i}"], pl.ds(at, n)]
            fields[image[i], pl.ds(at, n)] = mid + 2.0 * slope

    def fourth(at, n):
        d, g = diff[pl.ds(at, n)], grow[pl.ds(at, n)]
        here = at - MARGIN
        for i in range(halves):
            mid, slope = growth_of(fields.at[odd[i]], at, n, d, g)
            pair = mid + slope - fields[image[i], pl.ds(at, n)]
            if i == halves - 1:
                next_first[...] = ahead + pair
            else:
                term = fields[spots[f"s{i + 1}"], pl.ds(at, n)] + pair
                forcing[pl.ds(i * rows + here, n)] = term
                if i < 2:
                    turn[pl.ds(i * rows + here, n)] = term
                if i == 0:
                    next_odd[...] = fields[image[0], pl.ds(at, n)] + term
                if i == halves - 2:
                    last_odd[...] = fields[image[i], pl.ds(at, n)] + term

    over_rows(rows, 1, first)
    over_rows(rows, 1, second)
    for (at, flag), rim, slant in zip(
        sides, (above, below), (behind_above, behind_below), strict=True
    ):
        near, far = pl.ds(at(1), 1), pl.ds(at(2), 1)
        for i in range(halves):
            place = 4 * CHAINS + 2 if i == 0 else 4 * i - 1
            fields[spots[f"o{i}"], near] = rim[pl.ds(place, 1)] * flag
            value = diff[far] * fields[odd[i], near]
            if i == 0:
                value = value + fields[spots["s0"], far] + slant[pl.ds(3, 1)] * flag
            fields[even[i], far] = value
    over_rows(rows, 1, third)
    over_rows(rows, 0, fourth)
    coefs[pl.ds(0, rows + 4)] = diff[pl.ds(MARGIN - 2, rows + 4)]
    coefs[pl.ds(rows + 4, rows + 4)] = grow[pl.ds(MARGIN - 2, rows + 4)]
    for rim, n0, n1 in ((down, rows - 1, rows - 2), (up, 0, 1)):

        def row(ref, first, n):
            return ref[pl.ds(first + n, 1)]

        diff0 = 2.0 * row(diff, MARGIN, n0)
        around = [
            slope_of_rows(
                ref[pl.ds(first + n1 - 1, 3)], row(diff, MARGIN, n1), row(grow, MARGIN, n1)
            )
            for ref, first in ((next_odd, 0), (last_odd, 0))
        ]
        (mid, slope), (mid_last, slope_last) = around
        even1 = mid + 2.0 * slope + row(forcing, rows, n1)
        g3 = row(forcing, 2 * rows, n0)
        rim[pl.ds(0, 1)] = row(next_odd, 0, n0)
        rim[pl.ds(1, 1)] = row(forcing, rows, n0) + diff0 * mid
        rim[pl.ds(2, 1)] = g3 + diff0 * even1
        rim[pl.ds(3, 1)] = g3
        rim[pl.ds(4, 1)] = row(forcing, 0, n0)
        rim[pl.ds(5, 1)] = row(last_odd, 0, n0)
        rim[pl.ds(6, 1)] = row(next_first, 0, n0) + diff0 * mid_last
        rim[pl.ds(7, 1)] = row(next_first, 0, n1) + mid_last + 2.0 * slope_last
    slab, slabs = lax.axis_index("space"), lax.axis_size("space")
    size = 2 * rows // depth
    down[pl.ds(EDGE_1, size)] = ahead_one[...]
    up[pl.ds(EDGE_1, size)] = behind_one[...]
    if handed_on(slabs):
        down[pl.ds(EDGE_1 + size, size)] = above[pl.ds(EDGE_0, size)]
    for by, part in zip([0] + distant, (own, *windows), strict=True):
        held[pl.ds((slab - by) % slabs * size, size)] = part[...]


def take_coefs(rows, coefs, diff, grow):
    diff[pl.ds(MARGIN - 2, rows + 4)] = coefs[pl.ds(0, rows + 4)]
    grow[pl.ds(MARGIN - 2, rows + 4)] = coefs[pl.ds(rows + 4, rows + 4)]


def level1_kernel(
    share, next_odd, last_odd, forcing, coefs, next_first, held, above, below, ahead_terms,
    slots, next_forcing, late_a, late_b, windows,
    fields, diff, grow, flat,
):
    rows = forcing.shape[0] // 3
    low, high = flags()
    take_coefs(rows, coefs, diff, grow)
    windows[...] = held[...]
    slab, slabs = lax.axis_index("space"), lax.axis_size("space")
    size = windows.shape[0] // slabs
    windows[pl.ds((slab - 1) % slabs * size, size)] = above[pl.ds(EDGE_1, size)]
    windows[pl.ds((slab + 1) % slabs * size, size)] = below[pl.ds(EDGE_1, size)]
    if handed_on(slabs):
        windows[pl.ds((slab - 2) % slabs * size, size)] = above[pl.ds(EDGE_1 + size, size)]
    g1, g3, g2, g0, before, after, even0, even1, image0, image1, odd0, odd1 = range(12)
    nothing = jnp.zeros((1, *forcing.shape[1:]), jnp.float32)
    sides = rim_rows(rows, low, high)
    core = pl.ds(MARGIN, rows)
    fields[after, core] = next_odd[...]
    fields[before, core] = last_odd[...]
    fields[g0, core] = next_first[...]
    fields[g1, core] = ahead_terms[pl.ds(0, rows)]
    fields[g2, core] = forcing[pl.ds(rows, rows)]
    fields[g3, core] = forcing[pl.ds(2 * rows, rows)]
    for (at, flag), rim in zip(sides, (above, below), strict=True):
        near, far = pl.ds(at(1), 1), pl.ds(at(2), 1)
        for spot, row in ((after, 0), (g2, 1), (g3, 2), (before, 5), (g0, 6)):
            fields[spot, near] = rim[pl.ds(row, 1)] * flag
        fields[even0, far] = rim[pl.ds(7, 1)] * flag
        fields[g1, near] = nothing
        for spot in (after, before, even1):
            fields[spot, far] = nothing

    def second(at, n):
        d, g = diff[pl.ds(at, n)], grow[pl.ds(at, n)]
        for start, term, end in ((before, g0, even0), (after, g2, even1)):
            mid, slope = growth_of(fields.at[start], at, n, d, g)
            fields[end, pl.ds(at, n)] = mid + 2.0 * slope + fields[term, pl.ds(at, n)]

    def third(at, n):
        d, g = diff[pl.ds(at, n)], grow[pl.ds(at, n)]
        for start, term, end, image in ((even0, g1, odd0, image0), (even1, g3, odd1, image1)):
            mid, slope = growth_of(fields.at[start], at, n, d, g)
            fields[end, pl.ds(at, n)] = mid + 2.0 * slope + fields[term, pl.ds(at, n)]
            fields[image, pl.ds(at, n)] = mid + 4.0 * slope

    def fourth(at, n):
        d, g = diff[pl.ds(at, n)], grow[pl.ds(at, n)]
        here = at - MARGIN
        mid, slope = growth_of(fields.at[odd1], at, n, d, g)
        pair1 = mid + 2.0 * slope - fields[image1, pl.ds(at, n)]
        put_rows(flat, rows, next_first[...] + pair1)
        mid, slope = growth_of(fields.at[odd0], at, n, d, g)
        image = fields[image0, pl.ds(at, n)]
        term = ahead_terms[pl.ds(rows, rows)] + (mid + 2.0 * slope - image)
        next_forcing[pl.ds(here, n)] = term
        put_rows(flat, 2 * rows, term)
        put_rows(flat, 0, image + term)

    over_rows(rows, 1, second)
    over_rows(rows, 1, third)
    over_rows(rows, 0, fourth)
    for late, which, row in ((late_a, 0, 4), (late_b, 2, 3)):
        late[pl.ds(1, rows)] = forcing[pl.ds(which * rows, rows)]
        late[pl.ds(0, 1)] = above[pl.ds(row, 1)] * low
        late[pl.ds(rows + 1, 1)] = below[pl.ds(row, 1)] * high
    depth = forcing.shape[1]
    put_rows(flat, FIELDS * rows, ahead_terms[pl.ds(0, 1)])
    put_rows(flat, FIELDS * rows + 1, ahead_terms[pl.ds(rows - 1, 1)])
    if folded(rows, share, reach_of()):
        pack_folded(slots, flat, rows, depth, reach_of())
    else:
        pack_windows(slots, flat, rows, depth, share)


def put_rows(flat, first, value):
    depth = value.shape[1]
    for i in range(value.shape[0]):
        flat[pl.ds((first + i) * depth, depth), :] = value[i]


def reach_of():
    return lax.axis_size("tm") + 2


def slot_lines(rows, share, reach):
    return (FIELDS * 8 + 8 if folded(rows, share, reach) else FIELDS * rows) + 2


def folded(rows, share, reach):
    return rows == 16 and 2 * share == LANES and FIELDS * 2 * reach <= share


def pack_folded(slots, flat, rows, depth, reach):
    lines = slot_lines(rows, LANES // 2, reach)
    devices = slots.shape[0] // lines
    lane = lax.broadcasted_iota(jnp.int32, (8, LANES), 1)
    place = lane % (LANES // 2)
    rims = [None] * devices
    for field in range(FIELDS):
        first = field * rows * depth
        cells = []
        for line in range(depth):
            top = flat[pl.ds(first + line, 8, stride=depth), :]
            low = flat[pl.ds(first + 8 * depth + line, 8, stride=depth), :]
            cells.append(jnp.where(lane < LANES // 2, top, pltpu.roll(low, LANES // 2, 1)))
            cells.append(jnp.where(lane < LANES // 2, pltpu.roll(top, LANES // 2, 1), low))
        for target in range(devices):
            slots[pl.ds(target * lines + field * 8, 8), :] = cells[target]
            left = cells[target - 1] if target > 0 else 0.0
            right = cells[target + 1] if target < devices - 1 else 0.0
            rim = jnp.where(
                place >= LANES // 2 - reach, left, jnp.where(place < reach, right, 0.0)
            )
            if field == 0:
                rims[target] = rim
            else:
                rims[target] = rims[target] + pltpu.roll(rim, 2 * reach * field, 1)
    for target in range(devices):
        slots[pl.ds(target * lines + FIELDS * 8, 8), :] = rims[target]
    top = flat[pl.ds(FIELDS * rows * depth, depth), :]
    low = flat[pl.ds((FIELDS * rows + 1) * depth, depth), :]
    lane = lax.broadcasted_iota(jnp.int32, (depth, LANES), 1)
    line = lax.broadcasted_iota(jnp.int32, (depth, LANES), 0)
    place = lane % (LANES // 2)
    evens = jnp.where(lane < LANES // 2, top, pltpu.roll(low, LANES // 2, 1))
    odds = jnp.where(lane < LANES // 2, pltpu.roll(top, LANES // 2, 1), low)
    before = jnp.where(line == 0, 0.0, pltpu.roll(odds, 1, 0))
    after = jnp.where(line == depth - 1, 0.0, pltpu.roll(evens, depth - 1, 0))
    for parity, cells, left, right in ((0, evens, before, odds), (1, odds, evens, after)):
        rim = jnp.where(place >= LANES // 2 - reach, left, jnp.where(place < reach, right, 0.0))
        for i, value in enumerate((cells, rim)):
            start = parity * lines + lines - 2 + i
            slots[pl.ds(start, depth, stride=2 * lines), :] = value


def unfold(slot, field, reach):
    cells, rims = slot[pl.ds(field * 8, 8)], slot[pl.ds(FIELDS * 8, 8)]
    lane = lax.broadcasted_iota(jnp.int32, (8, LANES), 1)
    half = LANES // 2
    back = 2 * reach * field
    top = pltpu.roll(rims, (half - back) % LANES, 1)
    low = pltpu.roll(rims, (-back) % LANES, 1) if back else rims
    return jnp.concatenate(
        [
            jnp.where(lane < half, cells, top),
            jnp.where(lane < half, pltpu.roll(cells, half, 1), low),
        ],
        axis=0,
    )


def unfold_row(slot, which):
    last = slot.shape[0] - 2
    cells, rims = slot[pl.ds(last, 1)], slot[pl.ds(last + 1, 1)]
    lane = lax.broadcasted_iota(jnp.int32, (1, LANES), 1)
    half = LANES // 2
    if which == 0:
        return jnp.where(lane < half, cells, pltpu.roll(rims, half, 1))
    return jnp.where(lane < half, pltpu.roll(cells, half, 1), rims)


def pack_windows(slots, flat, rows, depth, share):
    lines = slot_lines(rows, share, reach_of())
    for field in range(FIELDS + 1):
        first, count = field * rows * depth, rows if field < FIELDS else 2
        held = [flat[pl.ds(first + line, count, stride=depth), :] for line in range(depth)]
        for target in range(slots.shape[0] // lines):
            line, offset = target * share // LANES, target * share % LANES
            shift = (LANES - offset) % LANES
            place = column_of((count, LANES), offset)
            value = pltpu.roll(held[line], shift, 1)
            if offset < REACH:
                before = pltpu.roll(held[line - 1], shift, 1) if line > 0 else 0.0
                value = jnp.where(place < 0, before, value)
            if offset > REACH:
                after = pltpu.roll(held[line + 1], shift, 1) if line < depth - 1 else 0.0
                value = jnp.where(place >= LANES, after, value)
            slots[pl.ds(target * lines + field * rows, count), :] = value


def late_rows(rows):
    return (("forcing", rows), ("forcing", -1), ("odd", rows + 1), ("odd", -2))


def packing(rows, share):
    groups = LANES // share
    each = -(-(rows + 2 * UP_RIM) // groups)
    return groups, each, each + -(-4 // groups)


def sweep_kernel(share, rows, arrived, windows, slots, diff, grow, terms, owns, adds, padded, odds):
    slabs = lax.axis_size("space")
    reach = reach_of()
    lines = slot_lines(rows, share, reach)
    devices = arrived.shape[0] // lines
    blocks = devices // slabs
    total = slabs * rows
    groups, each, held = packing(rows, share)
    for slab in range(slabs):
        diff[pl.ds(slab * rows, rows), :] = windows[pl.ds(2 * slab * rows, rows), :]
        grow[pl.ds(slab * rows, rows), :] = windows[pl.ds((2 * slab + 1) * rows, rows), :]
    line = lax.broadcasted_iota(jnp.int32, (total, LANES), 0)
    lane = lax.broadcasted_iota(jnp.int32, (each, LANES), 1)
    padded[...] = jnp.zeros(padded.shape, jnp.float32)
    odds[...] = jnp.zeros(odds.shape, jnp.float32)

    def block(field, index):
        parts = []
        for slab in range(slabs):
            slot = arrived.at[pl.ds((index * slabs + slab) * lines, lines)]
            if folded(rows, share, reach):
                parts.append(unfold(slot, field, reach))
            else:
                parts.append(slot[pl.ds(field * rows, rows)])
        return jnp.concatenate(parts, axis=0)

    adds[...] = jnp.zeros(adds.shape, jnp.float32)

    def beyond(index):
        for slab in range(slabs):
            slot = arrived.at[pl.ds((index * slabs + slab) * lines, lines)]
            for which, at in ((0, slab * rows - 1), (1, (slab + 1) * rows)):
                if not 0 <= at < total:
                    continue
                if folded(rows, share, reach):
                    piece = unfold_row(slot, which)
                else:
                    piece = slot[pl.ds(FIELDS * rows + which, 1)]
                adds[index, pl.ds(at, 1), :] = 2.0 * diff[pl.ds(at, 1), :] * piece

    def slope_of(field):
        north = jnp.where(line == 0, 0.0, pltpu.roll(field, 1, 0))
        south = jnp.where(line == total - 1, 0.0, pltpu.roll(field, total - 1, 0))
        sides = pltpu.roll(field, 1, 1) + pltpu.roll(field, LANES - 1, 1)
        laplace = north + south + sides - 4.0 * field
        return diff[...] * laplace + grow[...] * field / (1.0 + field * field)

    def put_late(index, slab):
        to = slots.at[pl.ds((index * slabs + slab) * held, held)]
        for i, (what, row) in enumerate(late_rows(rows)):
            at, group = each + i // groups, i % groups
            place = slab * rows + row
            if what == "odd":
                piece = odds[group, pl.ds(8 + place, 1)]
            elif 0 <= place < total:
                piece = owns[index, pl.ds(place, 1)]
                piece = pltpu.roll(piece, group * share, 1) if group else piece
            else:
                piece = jnp.zeros((1, LANES), jnp.float32)
            if group:
                piece = jnp.where(lane[:1] >= group * share, piece, to[pl.ds(at, 1)])
            to[pl.ds(at, 1)] = piece

    field = None
    for index in range(blocks):
        beyond(index)
    last_term = block(1, blocks - 1)
    for index in range(blocks):
        behind, twice = (index - 1) % blocks, (index - 2) % blocks
        odd, term = block(0, twice) + adds[twice], last_term if index == 0 else next_term
        even = odd + 4.0 * slope_of(odd) + term
        slope = slope_of(even)
        own = block(2, behind) + adds[behind]
        owns[index] = own
        odd = even + 4.0 * slope + own
        stepped = even + 8.0 * slope
        pair = odd + 4.0 * slope_of(odd) - stepped
        next_term = block(1, index) if index < blocks - 1 else last_term
        terms[index] = next_term + pair
        if index == blocks - 1:
            field = stepped + terms[index]
    for index in range(blocks):
        slope = slope_of(field)
        odd = field + 4.0 * slope + owns[index]
        for group in range(groups):
            for to, value in ((padded, field), (odds, odd)):
                to[group, pl.ds(8, total), :] = (
                    pltpu.roll(value, group * share, 1) if group else value
                )
        for slab in range(slabs):
            start = 8 + slab * rows - UP_RIM
            value = padded[0, pl.ds(start, each), :]
            for group in range(1, groups):
                piece = padded[group, pl.ds(start + group * each, each), :]
                value = jnp.where(lane >= group * share, piece, value)
            slots[pl.ds((index * slabs + slab) * held, each), :] = value
            put_late(index, slab)
        if index < blocks - 1:
            field = field + 8.0 * slope + terms[index]


def up_kernel(
    share, arrived, next_forcing, late_a, late_b, core, coefs,
    out, fields, diff, grow, flat, ready, sems,
):
    rows, depth, _ = next_forcing.shape
    groups, each, held = packing(rows, share)
    take_coefs(rows, coefs, diff, grow)
    lane = lax.broadcasted_iota(jnp.int32, (depth, LANES), 1)

    def whole(line, group):
        value = None
        for part in range(groups):
            piece = arrived[pl.ds(part * held + line, depth, stride=groups * held), :]
            if part != group:
                piece = pltpu.roll(piece, ((part - group) * share) % LANES, 1)
            value = piece if value is None else jnp.where(lane >= part * share, piece, value)
        return value

    for row in range(rows + 2 * UP_RIM):
        fields[0, MARGIN - UP_RIM + row] = whole(row % each, row // each)
    for i, (what, row) in enumerate(late_rows(rows)):
        spot = 5 if what == "forcing" else 2
        fields[spot, MARGIN + row] = whole(each + i // groups, i % groups)
    fields[5, pl.ds(MARGIN, rows)] = next_forcing[...]
    for row, rim in ((0, 0), (rows - 1, rows + 1)):
        spot = pl.ds(MARGIN + row, 1)
        added = 2.0 * diff[spot] * late_a[pl.ds(rim, 1)]
        fields[5, spot] = next_forcing[pl.ds(row, 1)] + added
    odd_first = CORES.index("o0") * rows

    def first(at, n):
        mid, slope = growth_of(fields.at[0], at, n, diff[pl.ds(at, n)], grow[pl.ds(at, n)])
        fields[2, pl.ds(at, n)] = mid + 4.0 * slope + fields[5, pl.ds(at, n)]

    def second(at, n):
        d, g = diff[pl.ds(at, n)], grow[pl.ds(at, n)]
        for start, late in ((0, late_a), (2, late_b)):
            mid, slope = growth_of(fields.at[start], at, n, d, g)
            fields[start + 1, pl.ds(at, n)] = mid + 2.0 * slope + late[pl.ds(at - MARGIN + 1, n)]

    copies = []

    def emit(point, value):
        put_rows(flat, point * rows, value)
        for r in range(0, rows, 8):
            for c in range(depth):
                start = (point * rows + r) * depth + c
                ready[point, pl.ds(r, 8), pl.ds(c * LANES, LANES)] = flat[
                    pl.ds(start, 8, stride=depth), :
                ]
        copy = pltpu.make_async_copy(ready.at[point], out.at[point], sems.at[point])
        copy.start()
        copies.append(copy)

    def last(i):
        at, n = MARGIN, rows
        mid, slope = growth_of(fields.at[i], at, n, diff[pl.ds(at, n)], grow[pl.ds(at, n)])
        emit(2 * i + 1, mid + slope + core[pl.ds(odd_first + i * rows, n)])

    core_rows = pl.ds(MARGIN, rows)
    emit(0, fields[0, core_rows])
    over_rows(rows, 1, first)
    emit(4, fields[2, core_rows])
    over_rows(rows, 1, second)
    emit(2, fields[1, core_rows])
    emit(6, fields[3, core_rows])
    for i in (0, 2, 1, 3):
        last(i)
    for copy in copies:
        copy.wait()


def moved(array, blocks, slabs):
    tm, space = lax.axis_size("tm"), lax.axis_size("space")
    pairs = [
        (t * space + s, (t + blocks) % tm * space + (s + slabs) % space)
        for t in range(tm)
        for s in range(space)
    ]
    return lax.ppermute(array, ("tm", "space"), pairs)


def swapped(array, offset):
    tm, space = lax.axis_size("tm"), lax.axis_size("space")
    pairs = [
        (t * space + s, ((((t - offset) % tm) ^ 1) + offset) % tm * space + s)
        for t in range(tm)
        for s in range(space)
    ]
    return lax.ppermute(array, ("tm", "space"), pairs)


def rims(down, up, slant_down, slant_up):
    slanted = moved(slant_down, 1, 1), moved(slant_up, 1, -1)
    return moved(down, 0, 1), moved(up, 0, -1), *slanted


def body(initial, source, diffusivity, growth):
    points, rows, cols = initial.shape
    assert points == POINTS and lax.axis_size("tm") % 2 == 0 and rows % 8 == 0 and cols % LANES == 0
    depth = cols // LANES
    tm, space = lax.axis_size("tm"), lax.axis_size("space")
    devices = tm * space
    share = cols // devices
    assert share * devices == cols and LANES % share == 0
    assert reach_of() <= REACH and REACH + share + reach_of() <= LANES
    _, _, held = packing(rows, share)
    wide = rows + 2 * MARGIN

    def lines(n):
        return (n * depth, LANES)

    def field(n):
        return (n, depth, LANES)

    def as_rows(array):
        return array.reshape(-1, depth, LANES)

    window_rows = 2 * rows // depth
    assert window_rows * depth == 2 * rows
    raw = [(points // 2, rows, cols), source.shape, (2, rows, cols)]
    extra = window_rows if handed_on(space) else 0
    *sends, inward, outward = call(
        functools.partial(pack_kernel, share),
        [lines(EDGE_0 + extra), lines(EDGE_0), lines(SLANT_0), lines(SLANT_0)]
        + [lines(rows + TURN)] * 2,
        raw + [lines(2 * SCRATCH * (CHAINS + 1)), lines(2 * rows), lines(3 * rows + 2)],
        initial, source, diffusivity, growth,
        place=pltpu.HBM, sems=points // 2 + 3,
    )
    core, *windows = call(
        functools.partial(core_kernel, share),
        [lines(len(CORES) * rows)] + [(2 * rows, LANES)] * len(sent_windows(space)),
        raw,
        initial, source, diffusivity, growth,
        place=pltpu.HBM, sems=points // 2 + 3,
        cost=pl.CostEstimate(flops=0, transcendentals=0, bytes_accessed=CORE_COST),
    )
    sends, inward, outward = [as_rows(part) for part in sends], as_rows(inward), as_rows(outward)
    inward = swapped(inward, 0)
    inward, sends[2], sends[3] = lax.optimization_barrier((inward, sends[2], sends[3]))
    arrived = [*rims(*sends), inward, swapped(outward, 1)]
    windows = [as_rows(part) for part in windows]
    for i, by in enumerate(far_windows(space), 3):
        windows[i] = moved(windows[i], 0, by)
    core = as_rows(core)
    arrived, windows = lax.optimization_barrier((arrived, windows))

    buffers = [(wide, depth, LANES), (wide, depth, LANES)]
    turn, down, up, next_odd, last_odd, forcing, coefs, held_windows, next_first = call(
        level0_kernel,
        [
            field(2 * rows), field(EDGE_1 + window_rows + extra), field(EDGE_1 + window_rows),
            field(rows), field(rows), field(3 * rows), field(2 * (rows + 4)),
            field(window_rows * space), field(rows),
        ],
        [(len(CORES) + 2 + 3 * (POINTS // 2), wide, depth, LANES)] + buffers,
        core, *arrived, *windows,
    )
    above, below, ahead_terms = moved(down, 0, 1), moved(up, 0, -1), moved(turn, -1, 0)
    slot_rows = slot_lines(rows, share, reach_of())
    slots, next_forcing, late_a, late_b, windows = call(
        functools.partial(level1_kernel, share),
        [
            (devices * slot_rows, LANES),
            field(rows), field(rows + 2), field(rows + 2), field(window_rows * space),
        ],
        [(12, wide, depth, LANES)] + buffers + [((FIELDS * rows + 2) * depth, LANES)],
        next_odd, last_odd, forcing, coefs, next_first, held_windows, above, below, ahead_terms,
    )
    next_forcing = moved(next_forcing, 1, 0)
    slots = slots.reshape(devices, slot_rows, 1, LANES)
    slots = lax.all_to_all(slots, ("tm", "space"), 0, 0, tiled=True)
    slots = slots.reshape(devices * slot_rows, LANES)
    (slots,) = call(
        functools.partial(sweep_kernel, share, rows),
        [(devices * held, LANES)],
        [(space * rows, LANES)] * 2
        + [(tm, space * rows, LANES)] * 3
        + [(LANES // share, 8 + space * rows + 2 * rows + held, LANES)]
        + [(LANES // share, 16 + space * rows, LANES)],
        slots, windows.reshape(-1, LANES),
    )
    slots = slots.reshape(devices, held, 1, LANES)
    slots = lax.all_to_all(slots, ("tm", "space"), 0, 0, tiled=True)
    (out,) = call(
        functools.partial(up_kernel, share),
        [(points, rows, cols)],
        [(6, wide, depth, LANES)]
        + buffers
        + [(points * rows * depth, LANES), (points, rows, cols)],
        slots.reshape(devices * held, LANES), next_forcing, late_a, late_b, core, coefs,
        to=pltpu.HBM, sems=points,
    )
    return out


def solution(mesh):
    placed = (P("tm", "space", None), P("tm", "space", None), P("space", None), P("space", None))
    return jax.shard_map(
        body, mesh=mesh, in_specs=placed, out_specs=P("tm", "space", None), check_vma=False
    )
```
